32 devices in a mesh: lat: 4 (over z), lon: 8 (over y, x, core).
Axes of the slice: x: 2, y: 2, z: 4, core: 2. Of those that a mesh axis runs over, the one named last changes fastest.
Arguments:
- sigma: float32 [4, 512, 1024], P(None, 'lat', 'lon'), may hold values from 0.5 to 2
- east_coef: float32 [4, 512, 1024], P(None, 'lat', 'lon'), may hold values from 0.04 to 0.24
- north_coef: float32 [4, 512, 1024], P(None, 'lat', 'lon'), may hold values from 0.04 to 0.24
- mask: int32 [4, 512, 1024], P(None, 'lat', 'lon'), may hold values 0 or 1
- innovations: float32 [4096, 128], P(('lat', 'lon')), may hold values from -6 to 6
- cells: int32 [4096, 128], P(('lat', 'lon')), may hold values from 0 to 65535
- owner: int32 [4096, 1], P(('lat', 'lon')), may hold values from 0 to 31; in each aligned block of 128 rows (0 to 127, 128 to 255, ...) at most 8 rows name the same one
- obs_weights: float32 [4096, 128, 128], P(('lat', 'lon')), may hold values from 0 to 4, as said below
Outputs:
- increment: float32 [4, 512, 1024], P(None, 'lat', 'lon')
- residual: float32 [4, 512, 1024], P(None, 'lat', 'lon')
The draws below stay inside these ranges and needn't reach their ends.
Inputs may be any that keep to these rules, and one draw needn't show every extreme that they name: `owner`: within the 128 blocks held by one device, no tile is named by more than 8 blocks, a bound that some block reaches. `obs_weights`: each block is symmetric and positive definite.
All inputs are finite; a program needn't handle non-finite values. No bound on the sum of `mask` on one device may be relied on, other than what follows from the above.
Results may differ from the reference program's by a relative error of at most 0.0003.
Values sent between devices are 32-bit elements; how exact they have to be, the bound alone decides.
No kernel may reach another device: no remote copies, remote signals or barrier semaphores. Data moves between devices by JAX's collectives and lax.ppermute only.
A program may use at most 128 MiB of HBM per device.

```python
import math
import jax
import jax.numpy as jnp
import numpy as np
from jax import lax

LEVELS = 4
TILE_LAT = 128
TILE_LON = 128
BLOCKS_DEV = 128
BLOCK_OBS = 128
PASSES = 5
ITERS = 2
MOST = 8
NLAT = 512
NLON = 1024
BLOCKS = 4096
CELLS = 65536
N_LON = 8
DEVICES = 32


def draw_obs_weights(key, part):
    key_place = jax.random.fold_in(key, 11)
    key_scale = jax.random.fold_in(key, 12)
    key_extra = jax.random.fold_in(key, 13)
    positions = jax.random.uniform(key_place, (BLOCKS, BLOCK_OBS), jnp.float32) * BLOCK_OBS
    log_scale = jax.random.uniform(key_scale, (BLOCKS, BLOCK_OBS), jnp.float32, -0.7, 0.7)
    length_scale = 6.0
    nugget = jax.random.uniform(key_extra, (BLOCKS, BLOCK_OBS), jnp.float32, 0.2, 0.6)
    distance = jnp.abs(positions[:, :, None] - positions[:, None, :])
    kernel = 0.5 * jnp.exp(log_scale[:, :, None] + log_scale[:, None, :] - distance / length_scale)
    identity = jnp.eye(BLOCK_OBS, dtype=jnp.float32)
    return kernel + identity[None, :, :] * nugget[:, :, None]


def plant(array, stream_key, smallest, top_value):
    longest = array.shape.index(max(array.shape))
    spots = []
    for shift in (0, 1):
        where = [jax.random.randint(jax.random.fold_in(stream_key, axis), (), 0, length) for axis, length in enumerate(array.shape)]
        where[longest] = (where[longest] + shift) % array.shape[longest]
        spots.append(tuple(where))
    return array.at[spots[0]].set(smallest).at[spots[1]].set(top_value)


def shard_levels(rng, extent, shards, low, high):
    loudness = 1.0
    for dim, blocks in shards:
        draws = jax.random.uniform(jax.random.fold_in(jax.random.fold_in(rng, 6), dim), (blocks,), jnp.float32, low / len(shards), high / len(shards))
        loudness = loudness * jnp.repeat(jnp.exp(draws), extent[dim] // blocks).reshape((-1,) + (1,) * (len(extent) - 1 - dim))
    return loudness


def routed_block(rng, own, number, rows, amount, top, reach, skew):
    ranking = jax.random.permutation(rng, amount)
    heavy_load, ordinary = shares(amount, rows * top, reach, skew, True), shares(amount, rows * top, reach, skew, False)
    places = jnp.arange(amount)

    def named(lengths, rotation):
        used = int((lengths > 0).sum())
        fixed = max(1, used // 4)
        passed = fixed + (places - fixed + rotation * (used - fixed)) % max(1, amount - fixed)
        return jnp.zeros((amount,), jnp.int32).at[ranking[jnp.where(places < fixed, places, passed)]].set(jnp.asarray(lengths, jnp.int32))

    lengths = jnp.where(number % 4 == 0, named(heavy_load, number // 4), named(ordinary, number - number // 4 - 1))
    mixed = jax.random.permutation(jax.random.fold_in(own, 3), amount)
    donor, sink = mixed[0:amount // 2 * 2:2], mixed[1:amount // 2 * 2:2]
    room = jnp.minimum(lengths[donor] - 1, reach - lengths[sink]) // 2
    room = jnp.where((donor == ranking[0]) | (sink == ranking[0]) | (lengths[sink] == 0), 0, jnp.maximum(room, 0))
    passed = jax.random.randint(jax.random.fold_in(own, 4), (amount // 2,), 0, 1 << 20) % (room + 1)
    lengths = lengths.at[donor].add(-passed).at[sink].add(passed)
    members = jnp.searchsorted(jnp.cumsum(lengths), jnp.arange(rows * top), side="right").astype(jnp.int32)
    listing = members.reshape(top, rows).T
    listing = listing[jax.random.permutation(jax.random.fold_in(own, 1), rows)]
    rotation = jax.random.randint(jax.random.fold_in(own, 2), (rows, 1), 0, top)
    return jnp.take_along_axis(listing, (jnp.arange(top)[None, :] + rotation) % top, axis=1)


def shares(number_of, total, most, skew, full):
    portions = [(1 << 20) // math.isqrt(grade ** skew) + 1 for grade in range(1, number_of + 1)]
    largest = most if full else min(most, max(-(-total // number_of), total * portions[0] // sum(portions)))
    least = 1 if total - largest >= number_of - 1 else 0
    holding, rest = [largest] + [least] * (number_of - 1), total - largest - least * (number_of - 1)
    while rest > 0:
        movable = [i for i in range(1, number_of) if holding[i] < largest] or [i for i in range(1, number_of) if holding[i] < most]
        mass, left = sum([portions[i] for i in movable]), rest
        for i in movable:
            extra = min(most - holding[i], max(1, left * portions[i] // mass), rest)
            holding[i] = holding[i] + extra
            rest = rest - extra
    return np.array(holding)


def scatter_about(key, extent, deviation, limit, split=(), kind=jnp.bfloat16):
    entries = deviation * jax.random.normal(key, extent, jnp.float32)
    if split:
        entries = entries * shard_levels(key, extent, split, -0.22, 0.18)
    return jnp.clip(entries, -limit, limit).astype(kind)


def setup_inputs(seed: int = 0) -> dict:
    splits = jax.random.split(jax.random.key(seed), 9)
    sigma = jnp.clip(jnp.exp(math.log(2.0) - 1.3862944 * jax.random.uniform(splits[0], (LEVELS, NLAT, NLON), jnp.float32) ** shard_levels(splits[0], (LEVELS, NLAT, NLON), ((1, 4), (2, 8)), -0.2, 0.2)), 0.5, 2.0)
    east_coef = jnp.clip(0.04 + 0.19999999552965164 * jax.random.uniform(splits[1], (LEVELS, NLAT, NLON), jnp.float32) ** shard_levels(splits[1], (LEVELS, NLAT, NLON), ((1, 4), (2, 8)), -0.2, 0.2), 0.04, 0.24)
    north_coef = jnp.clip(0.04 + 0.19999999552965164 * jax.random.uniform(splits[2], (LEVELS, NLAT, NLON), jnp.float32) ** shard_levels(splits[2], (LEVELS, NLAT, NLON), ((1, 4), (2, 8)), -0.2, 0.2), 0.04, 0.24)
    mask = plant((jax.random.randint(splits[3], (LEVELS, NLAT, NLON), 0, 10) < 9).astype(jnp.int32), jax.random.fold_in(splits[3], 1), 0, 1)
    innovations = scatter_about(splits[4], (BLOCKS, BLOCK_OBS), 1.0, 6.0, ((0, 32),), jnp.float32)
    cells = plant(jax.random.randint(splits[5], (BLOCKS, BLOCK_OBS), 0, CELLS), jax.random.fold_in(splits[5], 1), 0, CELLS - 1).astype(jnp.int32)
    owner_keys = jax.random.split(jax.random.fold_in(splits[6], 1), BLOCKS // BLOCKS_DEV)
    owner_turns = jax.random.permutation(jax.random.fold_in(splits[6], 3), BLOCKS // BLOCKS_DEV)
    owner = jax.vmap(lambda own, number: routed_block(jax.random.fold_in(splits[6], 2), own, number, BLOCKS_DEV, DEVICES, 1, MOST, 2))(owner_keys, owner_turns).reshape((BLOCKS, 1))
    obs_weights = draw_obs_weights(jax.random.fold_in(splits[8], 71), 0)
    return dict(sigma=sigma, east_coef=east_coef, north_coef=north_coef, mask=mask, innovations=innovations, cells=cells, owner=owner, obs_weights=obs_weights)


def face_weights(mask, east_coef, north_coef):
    land = mask.astype(jnp.float32)
    east = east_coef * land * jnp.roll(land, -1, 2)
    west = jnp.roll(east, 1, 2)
    upper = jnp.concatenate([land[:, 1:], jnp.zeros_like(land[:, :1])], 1)
    north = north_coef * land * upper
    south = jnp.concatenate([jnp.zeros_like(north[:, :1]), north[:, :-1]], 1)
    return east, west, north, south


def diffuse(field, weights):
    east, west, north, south = weights
    above = jnp.concatenate([field[:, 1:], jnp.zeros_like(field[:, :1])], 1)
    below = jnp.concatenate([jnp.zeros_like(field[:, :1]), field[:, :-1]], 1)
    result = field + east * (jnp.roll(field, -1, 2) - field) + west * (jnp.roll(field, 1, 2) - field)
    return result + north * (above - field) + south * (below - field)


def smooth(field, weights):
    for sweep in range(PASSES):
        field = diffuse(field, weights)
    return field


def reference(sigma, east_coef, north_coef, mask, innovations, cells, owner, obs_weights):
    weights = face_weights(mask, east_coef, north_coef)
    target = owner[:, 0].astype(jnp.int32)
    lat_tile = target // N_LON
    lon_tile = target % N_LON
    level = cells // (TILE_LAT * TILE_LON)
    row_index = (cells // TILE_LON) % TILE_LAT + lat_tile[:, None] * TILE_LAT
    col_index = cells % TILE_LON + lon_tile[:, None] * TILE_LON
    flat = ((level * NLAT + row_index) * NLON + col_index).astype(jnp.int32)

    def adjoint(values):
        total = jnp.zeros((LEVELS * NLAT * NLON,), jnp.float32).at[flat.reshape(-1)].add(values.reshape(-1))
        return total.reshape(LEVELS, NLAT, NLON)

    def weigh(values):
        return jnp.einsum("kij,kj->ki", obs_weights, values, precision=lax.Precision.HIGHEST)

    def hessian(direction):
        field = sigma * smooth(direction, weights)
        seen = field.reshape(-1)[flat]
        return direction + smooth(sigma * adjoint(weigh(seen)), weights)

    right = smooth(sigma * adjoint(weigh(innovations)), weights)
    solution = jnp.zeros_like(right)
    residual = right
    direction = right
    norm_now = jnp.sum(residual * residual)
    for sweep in range(ITERS):
        image = hessian(direction)
        alpha = norm_now / jnp.sum(direction * image)
        solution = solution + alpha * direction
        residual = residual - alpha * image
        norm_next = jnp.sum(residual * residual)
        direction = residual + (norm_next / norm_now) * direction
        norm_now = norm_next
    increment = sigma * smooth(solution, weights)
    return increment, residual
```

```python
import functools

import jax
import jax.numpy as jnp
from jax import lax
from jax.experimental import pallas as pl
from jax.experimental.pallas import tpu as pltpu
from jax.sharding import PartitionSpec as P

PASSES = 5
HALO = 16
EDGE = 8
GROUP = 16
F32 = jnp.float32
BF16 = jnp.bfloat16
VMEM = pl.BlockSpec(memory_space=pltpu.VMEM)
SMEM = pl.BlockSpec(memory_space=pltpu.SMEM)
PARAMS = pltpu.CompilerParams(vmem_limit_bytes=48 * 1024 * 1024)


def parts(values):
    high = values.astype(BF16)
    low = (values - high.astype(F32)).astype(BF16)
    return high, low


def lane_of(rows):
    return lax.broadcasted_iota(jnp.int32, (rows, 128), 1)


def pack_sides(fields):
    lane = lane_of(fields[0].shape[0])
    packed = jnp.zeros_like(fields[0])
    for level, field in enumerate(fields):
        start = 2 * HALO * level
        left = pltpu.roll(field, start, 1) if start else field
        right = pltpu.roll(field, (start + 2 * HALO) % 128, 1)
        packed = jnp.where((lane >= start) & (lane < start + HALO), left, packed)
        packed = jnp.where((lane >= start + HALO) & (lane < start + 2 * HALO), right, packed)
    return packed


def put_strips(fields, top, bottom, sides, sides_top, sides_bottom):
    rows = fields[0].shape[0]
    for level, field in enumerate(fields):
        top[level] = field[:HALO]
        bottom[level] = field[rows - HALO :]
    packed = pack_sides(fields)
    sides[...] = packed
    sides_top[...] = packed[:HALO]
    sides_bottom[...] = packed[rows - HALO :]


def place_halo(put, levels, rows, own, halo):
    before, after, east, west, north_east, north_west, south_east, south_west = halo
    for level in range(levels):
        put(level, 0, HALO, 0, before(level))
        put(level, HALO, HALO + rows, 0, own(level))
        put(level, HALO + rows, 2 * HALO + rows, 0, after(level))
    spans = (
        (0, HALO, north_east, north_west),
        (HALO, HALO + rows, east, west),
        (HALO + rows, 2 * HALO + rows, south_east, south_west),
    )
    for start, stop, right, left in spans:
        lane = lane_of(stop - start)
        mixed = jnp.where((lane % (2 * HALO)) < HALO, right(), left())
        for level in range(levels):
            shift = 2 * HALO * level
            first = pltpu.roll(mixed, (128 - shift) % 128, 1) if shift else mixed
            back = (128 - 2 * HALO - shift) % 128
            last = pltpu.roll(mixed, back, 1) if back else mixed
            side = jnp.where(lane < HALO, first, jnp.where(lane >= 128 - HALO, last, 0.0))
            put(level, start, stop, 1, side)


def exchange(strips):
    top, bottom, sides, sides_top, sides_bottom = strips
    tall, wide = lax.axis_size("lat"), lax.axis_size("lon")

    def send(block, down, right):
        pairs = [
            (i * wide + j, (i + down) * wide + (j + right) % wide)
            for i in range(tall)
            for j in range(wide)
            if 0 <= i + down < tall
        ]
        return lax.ppermute(block, ("lat", "lon"), pairs)

    return (
        send(bottom, 1, 0),
        send(top, -1, 0),
        send(sides, 0, -1),
        send(sides, 0, 1),
        send(sides_bottom, 1, -1),
        send(sides_bottom, 1, 1),
        send(sides_top, -1, -1),
        send(sides_top, -1, 1),
    )


def face_strip_kernel(mask, east, north, top, bottom, sides, sides_top, sides_bottom):
    levels = mask.shape[0]
    for index, array in enumerate((mask, east, north)):
        fields = [array[level].astype(F32) for level in range(levels)]
        put_strips(
            fields,
            top.at[index],
            bottom.at[index],
            sides.at[index],
            sides_top.at[index],
            sides_bottom.at[index],
        )


def face_strips(mask, east, north):
    levels, rows, cols = mask.shape
    shapes = [
        (3, levels, HALO, cols),
        (3, levels, HALO, cols),
        (3, rows, cols),
        (3, HALO, cols),
        (3, HALO, cols),
    ]
    return pl.pallas_call(
        face_strip_kernel,
        out_shape=[jax.ShapeDtypeStruct(shape, F32) for shape in shapes],
        in_specs=[VMEM] * 3,
        out_specs=[VMEM] * 5,
        compiler_params=PARAMS,
        name="face_strips",
    )(mask, east, north)


def face_kernel(mask, east, north, *refs):
    halo, weights, padded, faces = refs[:8], refs[8], refs[9], refs[10]
    levels, rows, cols = mask.shape
    tall = rows + 2 * HALO
    zeros = jnp.zeros((EDGE, 2 * cols), F32)
    for index, array in enumerate((mask, east, north)):
        for level in range(levels):
            padded[index, level, 0:EDGE] = zeros
            padded[index, level, EDGE + tall :] = zeros

        def put(level, start, stop, half, value, index=index):
            padded[index, level, EDGE + start : EDGE + stop, half * cols : (half + 1) * cols] = value

        def pick(ref, index=index):
            if len(ref.shape) == 4:
                return lambda level: ref[index, level]
            return lambda: ref[index]

        place_halo(
            put,
            levels,
            rows,
            lambda level, array=array: array[level].astype(F32),
            [pick(ref) for ref in halo],
        )
    faces[0:EDGE] = zeros
    faces[EDGE + tall :] = zeros

    def one_level(level, carry):
        land = padded[0, level, EDGE : EDGE + tall]
        land_north = padded[0, level, EDGE + 1 : EDGE + 1 + tall]
        east_face = padded[1, level, EDGE : EDGE + tall] * land * pltpu.roll(land, 2 * cols - 1, 1)
        west_face = pltpu.roll(east_face, 1, 1)
        north_face = padded[2, level, EDGE : EDGE + tall] * land * land_north
        faces[EDGE : EDGE + tall] = north_face
        south_face = faces[EDGE - 1 : EDGE - 1 + tall]
        weights[0, level] = 1.0 - (((east_face + west_face) + north_face) + south_face)
        weights[1, level] = east_face
        weights[2, level] = west_face
        weights[3, level] = north_face
        weights[4, level] = south_face
        return carry

    lax.fori_loop(0, levels, one_level, 0)


def face_weights(mask, east, north, halo):
    levels, rows, cols = mask.shape
    tall = rows + 2 * HALO
    return pl.pallas_call(
        face_kernel,
        out_shape=jax.ShapeDtypeStruct((5, levels, tall, 2 * cols), F32),
        in_specs=[VMEM] * 11,
        out_specs=VMEM,
        scratch_shapes=[
            pltpu.VMEM((3, levels, tall + 2 * EDGE, 2 * cols), F32),
            pltpu.VMEM((tall + 2 * EDGE, 2 * cols), F32),
        ],
        compiler_params=PARAMS,
        name="face_weights",
    )(mask, east, north, *halo)


def load_field(field, halo, source):
    levels, rows, cols = source.shape
    tall = rows + 2 * HALO
    zeros = jnp.zeros((EDGE, 2 * cols), F32)
    for slot in range(2):
        for level in range(levels):
            field[slot, level, 0:EDGE] = zeros
            field[slot, level, EDGE + tall :] = zeros

    def put(level, start, stop, half, value):
        field[0, level, EDGE + start : EDGE + stop, half * cols : (half + 1) * cols] = value

    def pick(ref):
        if len(ref.shape) == 3:
            return lambda level: ref[level]
        return lambda: ref[...]

    place_halo(put, levels, rows, lambda level: source[level], [pick(ref) for ref in halo])


def sweep(field, weights, source, target, rows_from, rows_to):
    levels = field.shape[1]
    wide = field.shape[3]

    def one_level(level, carry):
        for start in range(rows_from, rows_to, 16):
            stop = min(start + 16, rows_to)
            here = field[source, level, EDGE + start : EDGE + stop]
            above = field[source, level, EDGE + start + 1 : EDGE + stop + 1]
            below = field[source, level, EDGE + start - 1 : EDGE + stop - 1]
            total = weights[0, level, start:stop] * here
            total += weights[1, level, start:stop] * pltpu.roll(here, wide - 1, 1)
            total += weights[2, level, start:stop] * pltpu.roll(here, 1, 1)
            total += weights[3, level, start:stop] * above
            total += weights[4, level, start:stop] * below
            field[target, level, EDGE + start : EDGE + stop] = total
        return carry

    lax.fori_loop(0, levels, one_level, 0)


def smooth(field, weights, slot, depth):
    tall = weights.shape[2]
    for step in range(PASSES):
        reach = depth + PASSES - 1 - step
        skip = (HALO - reach) // 8 * 8
        sweep(field, weights, slot, 1 - slot, skip, tall - skip)
        slot = 1 - slot
    return slot


def one_hot_iota(cells):
    return lax.broadcasted_iota(jnp.int32, (cells, 128), 0).astype(F32).astype(BF16)


def spread_row(row, count):
    return jnp.broadcast_to(jnp.broadcast_to(row, (16, 128)).astype(BF16)[0:1], (count, 128))


def scatter_into(total, load_rows, steps, half_rows, half_cols):
    row_iota = one_hot_iota(half_rows)
    col_iota = one_hot_iota(half_cols)
    total[...] = jnp.zeros_like(total)

    def step(index, carry):
        high_rows, low_rows, columns = [], [], []
        for row_index, col_index, value in load_rows(index):
            high, low = parts(jnp.broadcast_to(value, (16, 128)))
            hit = row_iota == spread_row(row_index, half_rows)
            zero = jnp.zeros((half_rows, 128), BF16)
            high_rows.append(jnp.where(hit, jnp.broadcast_to(high[0:1], (half_rows, 128)), zero))
            low_rows.append(jnp.where(hit, jnp.broadcast_to(low[0:1], (half_rows, 128)), zero))
            columns.append(
                jnp.where(
                    col_iota == spread_row(col_index, half_cols),
                    jnp.ones((half_cols, 128), BF16),
                    jnp.zeros((half_cols, 128), BF16),
                )
            )
        left = jnp.concatenate(
            [jnp.concatenate(high_rows, axis=1), jnp.concatenate(low_rows, axis=1)], axis=0
        )
        right = jnp.concatenate(columns, axis=1)
        total[...] += lax.dot_general(
            left, right, (((1,), (1,)), ((), ())), preferred_element_type=F32
        )
        return carry

    lax.fori_loop(0, steps, step, 0)


def split_cells(cells, rows, cols):
    level = cells // (rows * cols)
    row = (cells // cols) % rows
    col = cells % cols
    return (level // 2) * rows + row, (level % 2) * cols + col


def put_field(total, sigma, field, extra=None):
    levels, rows, cols = sigma.shape
    half = total.shape[0] // 2
    fields = []
    for level in range(levels):
        r, c = level // 2 * rows, level % 2 * cols
        value = total[r : r + rows, c : c + cols] + total[half + r : half + r + rows, c : c + cols]
        value = sigma[level] * value
        if extra is not None:
            value = value + extra(level)
        field[level] = value
        fields.append(value)
    return fields


def strip_shapes(levels, rows, cols):
    return [
        (levels, HALO, cols),
        (levels, HALO, cols),
        (rows, cols),
        (HALO, cols),
        (HALO, cols),
    ]


def scatter_first_kernel(capacity, arrived, sigma, row_at, col_at, field, *refs):
    strips, total = refs[:5], refs[5]
    levels, rows, cols = sigma.shape
    sources = arrived.shape[0]
    cells = jnp.concatenate([arrived[source, 0:capacity] for source in range(sources)], axis=0)
    row_index, col_index = split_cells(cells.astype(jnp.int32), rows, cols)
    row_at[...] = row_index.astype(F32)
    col_at[...] = col_index.astype(F32)

    def load(index):
        base = pl.multiple_of(index * GROUP, GROUP)
        row_block = row_at[pl.ds(base, GROUP)]
        col_block = col_at[pl.ds(base, GROUP)]
        for j in range(GROUP):
            source = index * (GROUP // capacity) + j // capacity
            slot = capacity + j % capacity
            yield row_block[j : j + 1], col_block[j : j + 1], arrived[source, slot : slot + 1]

    scatter_into(total, load, row_at.shape[0] // GROUP, levels // 2 * rows, 2 * cols)
    put_strips(put_field(total, sigma, field), *strips)


def scatter_first(arrived, sigma, capacity):
    levels, rows, cols = sigma.shape
    slots = arrived.shape[0] * capacity
    shapes = [(slots, 128), (slots, 128), (levels, rows, cols)] + strip_shapes(levels, rows, cols)
    out = pl.pallas_call(
        functools.partial(scatter_first_kernel, capacity),
        out_shape=[jax.ShapeDtypeStruct(shape, F32) for shape in shapes],
        in_specs=[VMEM] * 2,
        out_specs=[VMEM] * len(shapes),
        scratch_shapes=[pltpu.VMEM((levels * rows, 2 * cols), F32)],
        compiler_params=PARAMS,
        name="scatter_first",
    )(arrived, sigma)
    return out[0], out[1], out[2], out[3:]


def lane_value(block, lane):
    return jnp.sum(jnp.where(lane_of(block.shape[0]) == lane, block, 0.0))


def lanes(values, rows):
    lane = lane_of(rows)
    out = jnp.zeros((rows, 128), F32)
    for index, value in enumerate(values):
        out = jnp.where(lane == index, value, out)
    return out


def scatter_next_kernel(capacity, last, arrived, row_at, col_at, sigma, *refs):
    if last:
        previous, field, strips, sums, total = refs[0], refs[1], refs[2:7], refs[7], refs[8]
    else:
        previous, field, strips, sums, total = None, refs[0], refs[1:6], refs[6], refs[7]
    levels, rows, cols = sigma.shape
    sources = arrived.shape[0]
    gathered = jnp.concatenate(
        [arrived[source, capacity : capacity + 1] for source in range(sources)], axis=0
    )
    added = jnp.sum(gathered, axis=0, keepdims=True)
    sums[...] = jnp.broadcast_to(added, (8, 128))

    def load(index):
        base = pl.multiple_of(index * GROUP, GROUP)
        row_block = row_at[pl.ds(base, GROUP)]
        col_block = col_at[pl.ds(base, GROUP)]
        for j in range(GROUP):
            source = index * (GROUP // capacity) + j // capacity
            slot = j % capacity
            yield row_block[j : j + 1], col_block[j : j + 1], arrived[source, slot : slot + 1]

    scatter_into(total, load, row_at.shape[0] // GROUP, levels // 2 * rows, 2 * cols)
    extra = None
    if last:
        beta = lane_value(added, 1) / lane_value(added, 0)

        def extra(level):
            return beta * previous[level]

    put_strips(put_field(total, sigma, field, extra), *strips)


def scatter_next(arrived, row_at, col_at, sigma, capacity, previous=None):
    levels, rows, cols = sigma.shape
    last = previous is not None
    shapes = [(levels, rows, cols)] + strip_shapes(levels, rows, cols) + [(8, 128)]
    operands = [arrived, row_at, col_at, sigma] + ([previous] if last else [])
    out = pl.pallas_call(
        functools.partial(scatter_next_kernel, capacity, last),
        out_shape=[jax.ShapeDtypeStruct(shape, F32) for shape in shapes],
        in_specs=[VMEM] * len(operands),
        out_specs=[VMEM] * len(shapes),
        scratch_shapes=[pltpu.VMEM((levels * rows, 2 * cols), F32)],
        compiler_params=PARAMS,
        name="scatter_last" if last else "scatter_next",
    )(*operands)
    return out[0], out[1:6], out[6]


def gather_from(fields, row_at, col_at, seen, table):
    rows, cols = fields[0].shape
    half_rows, half_cols = len(fields) // 2 * rows, 2 * cols
    for level, field in enumerate(fields):
        high, low = parts(field.T)
        c, r = level % 2 * cols, level // 2 * rows
        table[c : c + cols, r : r + rows] = high
        table[half_cols + c : half_cols + c + cols, r : r + rows] = low
    row_iota = one_hot_iota(half_rows)
    col_iota = lax.broadcasted_iota(jnp.int32, (half_cols, 256), 0).astype(F32)

    def step(index, carry):
        base = pl.multiple_of(index * 8, 8)
        row_block = row_at[pl.ds(base, 8)]
        col_block = col_at[pl.ds(base, 8)]
        found = []
        for j in range(0, 8, 2):
            hot = jnp.concatenate(
                [
                    jnp.where(
                        row_iota == spread_row(row_block[i : i + 1], half_rows),
                        jnp.ones((half_rows, 128), BF16),
                        jnp.zeros((half_rows, 128), BF16),
                    )
                    for i in (j, j + 1)
                ],
                axis=1,
            )
            lines = jnp.dot(table[...], hot, preferred_element_type=F32)
            lines = lines[:half_cols] + lines[half_cols:]
            wanted = jnp.concatenate([col_block[j : j + 1], col_block[j + 1 : j + 2]], axis=1)
            value = jnp.sum(jnp.where(col_iota == wanted, lines, 0.0), axis=0, keepdims=True)
            found += [value[:, :128], value[:, 128:]]
        seen[pl.ds(base, 8)] = jnp.concatenate(found, axis=0)
        return carry

    lax.fori_loop(0, row_at.shape[0] // 8, step, 0)


def own_part(field, slot, level, rows, cols):
    return field[slot, level, EDGE + HALO : EDGE + HALO + rows, 0:cols]


def total_of(pairs):
    added = None
    for left, right in pairs:
        term = left * right
        added = term if added is None else added + term
    return jnp.sum(added)


def observe_first_kernel(source, *refs):
    halo, weights, sigma, row_at, col_at = refs[:8], refs[8], refs[9], refs[10], refs[11]
    seen, right, image, sums, field, table = refs[12:]
    levels, rows, cols = source.shape
    load_field(field, halo, source)
    slot = smooth(field, weights, 0, PASSES)
    right[...] = field[slot, :, EDGE : EDGE + rows + 2 * HALO]
    own = [own_part(field, slot, level, rows, cols) for level in range(levels)]
    sums[...] = lanes([total_of([(value, value) for value in own])], 8)
    slot = smooth(field, weights, slot, 0)
    fields = [sigma[level] * own_part(field, slot, level, rows, cols) for level in range(levels)]
    for level in range(levels):
        image[level] = fields[level]
    gather_from(fields, row_at, col_at, seen, table)


def observe_next_kernel(source, *refs):
    halo, weights, sigma, row_at, col_at = refs[:8], refs[8], refs[9], refs[10], refs[11]
    right, scalars = refs[12:14]
    seen, residual, image, sums, field, table = refs[14:]
    levels, rows, cols = source.shape
    tall = rows + 2 * HALO
    norm, product = lane_value(scalars[0:1], 0), lane_value(scalars[0:1], 1)
    alpha = norm / (norm + product)
    load_field(field, halo, source)
    slot = smooth(field, weights, 0, PASSES)

    def one_level(level, carry):
        first = right[level]
        field[slot, level, EDGE : EDGE + tall] = first - alpha * (
            first + field[slot, level, EDGE : EDGE + tall]
        )
        return carry

    lax.fori_loop(0, levels, one_level, 0)
    own = [own_part(field, slot, level, rows, cols) for level in range(levels)]
    first = [right[level, HALO : HALO + rows, 0:cols] for level in range(levels)]
    for level in range(levels):
        residual[level] = own[level]
    sums[...] = lanes(
        [total_of([(value, value) for value in own]), total_of(list(zip(own, first)))], 8
    )
    slot = smooth(field, weights, slot, 0)
    fields = [sigma[level] * own_part(field, slot, level, rows, cols) for level in range(levels)]
    for level in range(levels):
        image[level] = fields[level]
    gather_from(fields, row_at, col_at, seen, table)


def observe(source, halo, weights, sigma, row_at, col_at, right=None, scalars=None):
    levels, rows, cols = sigma.shape
    tall = rows + 2 * HALO
    slots = row_at.shape[0]
    first = right is None
    kept = (levels, tall, 2 * cols) if first else (levels, rows, cols)
    shapes = [(slots, 128), kept, (levels, rows, cols), (8, 128)]
    operands = [source, *halo, weights, sigma, row_at, col_at]
    operands += [] if first else [right, scalars]
    return pl.pallas_call(
        observe_first_kernel if first else observe_next_kernel,
        out_shape=[jax.ShapeDtypeStruct(shape, F32) for shape in shapes],
        in_specs=[VMEM] * len(operands),
        out_specs=[VMEM] * len(shapes),
        scratch_shapes=[
            pltpu.VMEM((2, levels, tall + 2 * EDGE, 2 * cols), F32),
            pltpu.VMEM((4 * cols, levels // 2 * rows), BF16),
        ],
        compiler_params=PARAMS,
        name="observe_first" if first else "observe_next",
    )(*operands)


def finish_kernel(source, *refs):
    halo, weights, right, residual_one, image_zero, image_one, scalars = refs[:8], *refs[8:14]
    increment, residual, field = refs[14:]
    levels, rows, cols = source.shape
    norm_zero, norm_one, cross, product_zero, product_one, product_cross = [
        lane_value(scalars[0:1], index) for index in range(6)
    ]
    alpha_zero = norm_zero / (norm_zero + product_zero)
    beta = norm_one / norm_zero
    square = norm_one + 2.0 * beta * cross + beta * beta * norm_zero
    seen = product_one + 2.0 * beta * product_cross + beta * beta * product_zero
    alpha_one = norm_one / (square + seen)
    for level in range(levels):
        direction = image_one[level] + beta * image_zero[level]
        increment[level] = alpha_zero * image_zero[level] + alpha_one * direction
    load_field(field, halo, source)
    slot = smooth(field, weights, 0, 0)
    for level in range(levels):
        here = residual_one[level]
        direction = here + beta * right[level, HALO : HALO + rows, 0:cols]
        image = direction + own_part(field, slot, level, rows, cols)
        residual[level] = here - alpha_one * image


def finish(source, halo, weights, right, residual_one, image_zero, image_one, scalars):
    levels, rows, cols = source.shape
    tall = rows + 2 * HALO
    return pl.pallas_call(
        finish_kernel,
        out_shape=[jax.ShapeDtypeStruct((levels, rows, cols), F32)] * 2,
        in_specs=[VMEM] * 15,
        out_specs=[VMEM] * 2,
        scratch_shapes=[pltpu.VMEM((2, levels, tall + 2 * EDGE, 2 * cols), F32)],
        compiler_params=PARAMS,
        name="finish",
    )(source, *halo, weights, right, residual_one, image_zero, image_one, scalars)


def apply_blocks(values, weights):
    high, low = parts(values)
    both = jnp.concatenate([high, low], axis=0)
    row = lax.broadcasted_iota(jnp.int32, (8, 128), 0)
    out = jnp.zeros((8, 128), F32)
    for k in range(8):
        matrix_high, matrix_low = parts(weights(k))
        product = jnp.dot(both, matrix_high, preferred_element_type=F32)
        product = product[:8] + product[8:]
        product = product + jnp.dot(both, matrix_low, preferred_element_type=F32)[:8]
        out = jnp.where(row == k, product, out)
    return out


def weigh_first_kernel(capacity, owner, cells, innovations, weights, parcel, place, count):
    step = pl.program_id(0)
    stride = 2 * capacity

    @pl.when(step == 0)
    def _():
        parcel[...] = jnp.zeros_like(parcel)

        def clear(index, carry):
            count[index] = 0
            return carry

        lax.fori_loop(0, count.shape[0], clear, 0)

    for group in range(GROUP // 8):
        block = pl.ds(group * 8, 8)
        here = innovations[block]
        result = apply_blocks(here, lambda k: weights[group * 8 + k])
        cell_rows = cells[block].astype(F32)
        for k in range(8):
            index = step * GROUP + group * 8 + k
            target = owner[index, 0]
            rank = count[target]
            count[target] = rank + 1
            place[index] = target * capacity + rank
            at = target * stride + rank
            parcel[pl.ds(at, 1), :] = cell_rows[k : k + 1]
            parcel[pl.ds(at + capacity, 1), :] = result[k : k + 1]


def weigh_first(owner, cells, innovations, weights, devices, capacity):
    held, width = cells.shape
    return pl.pallas_call(
        functools.partial(weigh_first_kernel, capacity),
        grid=(held // GROUP,),
        out_shape=[
            jax.ShapeDtypeStruct((devices * 2 * capacity, width), F32),
            jax.ShapeDtypeStruct((held,), jnp.int32),
        ],
        in_specs=[
            SMEM,
            pl.BlockSpec((GROUP, width), lambda i: (i, 0)),
            pl.BlockSpec((GROUP, width), lambda i: (i, 0)),
            pl.BlockSpec((GROUP, width, width), lambda i: (i, 0, 0)),
        ],
        out_specs=[
            pl.BlockSpec((devices * 2 * capacity, width), lambda i: (0, 0)),
            SMEM,
        ],
        scratch_shapes=[pltpu.SMEM((devices,), jnp.int32)],
        compiler_params=PARAMS,
        name="weigh_first",
    )(owner, cells, innovations, weights)


def weigh_next_kernel(capacity, stride, devices, last, place, returned, sums, weights, *refs):
    if last:
        sums_before, weighted_before, parcel, totals = refs
    else:
        parcel, weighted, totals = refs
    step = pl.program_id(0)

    @pl.when(step == 0)
    def _():
        parcel[...] = jnp.zeros_like(parcel)
        totals[...] = jnp.zeros_like(totals)

    for group in range(GROUP // 8):
        places = [place[step * GROUP + group * 8 + k] for k in range(8)]
        here = jnp.concatenate([returned[pl.ds(at, 1), :] for at in places], axis=0)
        result = apply_blocks(here, lambda k: weights[group * 8 + k])
        totals[0] += here * result
        if last:
            totals[1] += here * weighted_before[group * 8 : group * 8 + 8]
        else:
            weighted[group * 8 : group * 8 + 8] = result
        for k in range(8):
            target = places[k] // capacity
            at = target * stride + (places[k] - target * capacity)
            parcel[pl.ds(at, 1), :] = result[k : k + 1]

    @pl.when(step == pl.num_programs(0) - 1)
    def _():
        if last:
            scalars = [
                lane_value(sums_before[0:1], 0),
                lane_value(sums[0:1], 0),
                lane_value(sums[0:1], 1),
                lane_value(sums_before[0:1], 1),
                jnp.sum(totals[0]),
                jnp.sum(totals[1]),
            ]
            scalars[0] = scalars[0] / devices
            scalars[3] = scalars[3] / devices
        else:
            scalars = [lane_value(sums[0:1], 0), jnp.sum(totals[0])]
        row = lanes(scalars, 1)
        for target in range(devices):
            at = target * stride + capacity
            parcel[at : at + 1] = row


def weigh_next(place, returned, sums, weights, devices, capacity, stride, before=None):
    held, width = weights.shape[:2]
    last = before is not None
    resident = lambda shape: pl.BlockSpec(shape, lambda i: (0,) * len(shape))
    operands = [place, returned, sums, weights]
    in_specs = [
        SMEM,
        resident(returned.shape),
        resident((8, 128)),
        pl.BlockSpec((GROUP, width, width), lambda i: (i, 0, 0)),
    ]
    out_shape = [jax.ShapeDtypeStruct((devices * stride, width), F32)]
    out_specs = [resident((devices * stride, width))]
    if last:
        operands += list(before)
        in_specs += [resident((8, 128)), pl.BlockSpec((GROUP, width), lambda i: (i, 0))]
    else:
        out_shape += [jax.ShapeDtypeStruct((held, width), F32)]
        out_specs += [pl.BlockSpec((GROUP, width), lambda i: (i, 0))]
    return pl.pallas_call(
        functools.partial(weigh_next_kernel, capacity, stride, devices, last),
        grid=(held // GROUP,),
        out_shape=out_shape,
        in_specs=in_specs,
        out_specs=out_specs,
        scratch_shapes=[pltpu.VMEM((2, 8, 128), F32)],
        compiler_params=PARAMS,
        name="weigh_last" if last else "weigh_next",
    )(*operands)


def swap(block):
    return lax.all_to_all(block, ("lat", "lon"), split_axis=0, concat_axis=0, tiled=True)


def body(sigma, east_coef, north_coef, mask, innovations, cells, owner, obs_weights):
    devices = lax.axis_size("lat") * lax.axis_size("lon")
    held, width = cells.shape
    capacity = max(2, (2 * held + devices - 1) // devices)
    stride = (capacity + 8) // 8 * 8
    slots = devices * capacity

    face_halo = exchange(face_strips(mask, east_coef, north_coef))
    parcel, place = weigh_first(owner, cells, innovations, obs_weights, devices, capacity)
    arrived = swap(parcel.reshape(devices, 2 * capacity, width))
    weights = face_weights(mask, east_coef, north_coef, face_halo)

    row_at, col_at, field, strips = scatter_first(arrived, sigma, capacity)
    seen, right, image_zero, sums = observe(
        field, exchange(strips), weights, sigma, row_at, col_at
    )
    returned = swap(seen.reshape(devices, capacity, width)).reshape(slots, width)
    parcel, weighted = weigh_next(place, returned, sums, obs_weights, devices, capacity, stride)
    arrived = swap(parcel.reshape(devices, stride, width))

    field_zero, strips, scalars_zero = scatter_next(arrived, row_at, col_at, sigma, capacity)
    seen, residual_one, image_one, sums = observe(
        field_zero, exchange(strips), weights, sigma, row_at, col_at, right, scalars_zero
    )
    returned = swap(seen.reshape(devices, capacity, width)).reshape(slots, width)
    (parcel,) = weigh_next(
        place, returned, sums, obs_weights, devices, capacity, stride, (scalars_zero, weighted)
    )
    arrived = swap(parcel.reshape(devices, stride, width))

    field, strips, scalars = scatter_next(arrived, row_at, col_at, sigma, capacity, field_zero)
    increment, residual = finish(
        field, exchange(strips), weights, right, residual_one, image_zero, image_one, scalars
    )
    return (increment, residual)


def solution(mesh):
    return jax.shard_map(
        body,
        mesh=mesh,
        in_specs=(
            P(None, "lat", "lon"),
            P(None, "lat", "lon"),
            P(None, "lat", "lon"),
            P(None, "lat", "lon"),
            P(("lat", "lon"), None),
            P(("lat", "lon"), None),
            P(("lat", "lon"), None),
            P(("lat", "lon"), None, None),
        ),
        out_specs=(P(None, "lat", "lon"), P(None, "lat", "lon")),
        check_vma=False,
    )
```

```python
import functools

import jax
import jax.numpy as jnp
from jax import lax
from jax.experimental import pallas as pl
from jax.experimental.pallas import tpu as pltpu
from jax.sharding import PartitionSpec as P

PASSES = 5
HALO = 16
EDGE = 8
GROUP = 16
F32 = jnp.float32
BF16 = jnp.bfloat16
VMEM = pl.BlockSpec(memory_space=pltpu.VMEM)
SMEM = pl.BlockSpec(memory_space=pltpu.SMEM)
PARAMS = pltpu.CompilerParams(vmem_limit_bytes=48 * 1024 * 1024)


def parts(values):
    high = values.astype(BF16)
    low = (values - high.astype(F32)).astype(BF16)
    return high, low


def lane_of(rows):
    return lax.broadcasted_iota(jnp.int32, (rows, 128), 1)


def pack_sides(fields):
    lane = lane_of(fields[0].shape[0])
    packed = jnp.zeros_like(fields[0])
    for level, field in enumerate(fields):
        start = 2 * HALO * level
        left = pltpu.roll(field, start, 1) if start else field
        right = pltpu.roll(field, (start + 2 * HALO) % 128, 1)
        packed = jnp.where((lane >= start) & (lane < start + HALO), left, packed)
        packed = jnp.where((lane >= start + HALO) & (lane < start + 2 * HALO), right, packed)
    return packed


def place_halo(put, levels, rows, own, halo):
    before, after, mixed = halo
    for level in range(levels):
        put(level, 0, HALO, 0, before(level))
        put(level, HALO, HALO + rows, 0, own(level))
        put(level, HALO + rows, 2 * HALO + rows, 0, after(level))
    spans = (
        (0, HALO, before(levels)),
        (HALO, HALO + rows, mixed()),
        (HALO + rows, 2 * HALO + rows, after(levels)),
    )
    for start, stop, sides in spans:
        lane = lane_of(stop - start)
        for level in range(levels):
            shift = 2 * HALO * level
            first = pltpu.roll(sides, (128 - shift) % 128, 1) if shift else sides
            back = (128 - 2 * HALO - shift) % 128
            last = pltpu.roll(sides, back, 1) if back else sides
            side = jnp.where(lane < HALO, first, jnp.where(lane >= 128 - HALO, last, 0.0))
            put(level, start, stop, 1, side)


def turn_kernel(count, *refs):
    arrays, (from_east, from_west, mixed, down, up) = refs[:count], refs[count:]
    levels, rows, _ = arrays[0].shape
    for index, array in enumerate(arrays):
        at = (index,) if count > 1 else ()
        lane = lane_of(rows)
        sides = jnp.where(lane % (2 * HALO) < HALO, from_east[at + (...,)], from_west[at + (...,)])
        mixed[at + (...,)] = sides
        for level in range(levels):
            down[at + (level,)] = array[level, rows - HALO :].astype(F32)
            up[at + (level,)] = array[level, :HALO].astype(F32)
        down[at + (levels,)] = sides[rows - HALO :]
        up[at + (levels,)] = sides[:HALO]


def exchange(arrays, sides):
    count = len(arrays)
    levels, rows, cols = arrays[0].shape
    tall, wide = lax.axis_size("lat"), lax.axis_size("lon")
    east = [(i, (i + 1) % wide) for i in range(wide)]
    from_west = lax.ppermute(sides, "lon", east)
    from_east = lax.ppermute(sides, "lon", [(to, at) for at, to in east])
    lead = (count,) if count > 1 else ()
    shapes = [lead + (rows, cols)] + [lead + (levels + 1, HALO, cols)] * 2
    mixed, down, up = pl.pallas_call(
        functools.partial(turn_kernel, count),
        out_shape=[jax.ShapeDtypeStruct(shape, F32) for shape in shapes],
        in_specs=[VMEM] * (count + 2),
        out_specs=[VMEM] * 3,
        compiler_params=PARAMS,
        name="turn",
    )(*arrays, from_east, from_west)
    north = [(i, i + 1) for i in range(tall - 1)]
    before = lax.ppermute(down, "lat", north)
    after = lax.ppermute(up, "lat", [(to, at) for at, to in north])
    return before, after, mixed


def face_side_kernel(mask, east, north, sides):
    for index, array in enumerate((mask, east, north)):
        sides[index] = pack_sides([array[level].astype(F32) for level in range(mask.shape[0])])


def face_sides(mask, east, north):
    return pl.pallas_call(
        face_side_kernel,
        out_shape=jax.ShapeDtypeStruct((3,) + mask.shape[1:], F32),
        in_specs=[VMEM] * 3,
        out_specs=VMEM,
        compiler_params=PARAMS,
        name="face_sides",
    )(mask, east, north)


def face_kernel(mask, east, north, *refs):
    halo, weights, padded, faces = refs[:3], refs[3], refs[4], refs[5]
    levels, rows, cols = mask.shape
    tall = rows + 2 * HALO
    zeros = jnp.zeros((EDGE, 2 * cols), F32)
    for index, array in enumerate((mask, east, north)):
        for level in range(levels):
            padded[index, level, 0:EDGE] = zeros
            padded[index, level, EDGE + tall :] = zeros

        def put(level, start, stop, half, value, index=index):
            padded[index, level, EDGE + start : EDGE + stop, half * cols : (half + 1) * cols] = value

        def pick(ref, index=index):
            if len(ref.shape) == 4:
                return lambda level: ref[index, level]
            return lambda: ref[index]

        place_halo(
            put,
            levels,
            rows,
            lambda level, array=array: array[level].astype(F32),
            [pick(ref) for ref in halo],
        )
    faces[0:EDGE] = zeros
    faces[EDGE + tall :] = zeros

    def one_level(level, carry):
        land = padded[0, level, EDGE : EDGE + tall]
        land_north = padded[0, level, EDGE + 1 : EDGE + 1 + tall]
        east_face = padded[1, level, EDGE : EDGE + tall] * land * pltpu.roll(land, 2 * cols - 1, 1)
        west_face = pltpu.roll(east_face, 1, 1)
        north_face = padded[2, level, EDGE : EDGE + tall] * land * land_north
        faces[EDGE : EDGE + tall] = north_face
        south_face = faces[EDGE - 1 : EDGE - 1 + tall]
        weights[0, level] = 1.0 - (((east_face + west_face) + north_face) + south_face)
        weights[1, level] = east_face
        weights[2, level] = west_face
        weights[3, level] = north_face
        weights[4, level] = south_face
        return carry

    lax.fori_loop(0, levels, one_level, 0)


def face_weights(mask, east, north, halo):
    levels, rows, cols = mask.shape
    tall = rows + 2 * HALO
    return pl.pallas_call(
        face_kernel,
        out_shape=jax.ShapeDtypeStruct((5, levels, tall, 2 * cols), F32),
        in_specs=[VMEM] * 6,
        out_specs=VMEM,
        scratch_shapes=[
            pltpu.VMEM((3, levels, tall + 2 * EDGE, 2 * cols), F32),
            pltpu.VMEM((tall + 2 * EDGE, 2 * cols), F32),
        ],
        compiler_params=PARAMS,
        name="face_weights",
    )(mask, east, north, *halo)


def load_field(field, halo, source):
    levels, rows, cols = source.shape
    tall = rows + 2 * HALO
    zeros = jnp.zeros((EDGE, 2 * cols), F32)
    for slot in range(2):
        for level in range(levels):
            field[slot, level, 0:EDGE] = zeros
            field[slot, level, EDGE + tall :] = zeros

    def put(level, start, stop, half, value):
        field[0, level, EDGE + start : EDGE + stop, half * cols : (half + 1) * cols] = value

    def pick(ref):
        if len(ref.shape) == 3:
            return lambda level: ref[level]
        return lambda: ref[...]

    place_halo(put, levels, rows, lambda level: source[level], [pick(ref) for ref in halo])


def sweep(field, weights, source, target, rows_from, rows_to):
    levels = field.shape[1]
    wide = field.shape[3]

    def one_level(level, carry):
        for start in range(rows_from, rows_to, 16):
            stop = min(start + 16, rows_to)
            here = field[source, level, EDGE + start : EDGE + stop]
            above = field[source, level, EDGE + start + 1 : EDGE + stop + 1]
            below = field[source, level, EDGE + start - 1 : EDGE + stop - 1]
            total = weights[0, level, start:stop] * here
            total += weights[1, level, start:stop] * pltpu.roll(here, wide - 1, 1)
            total += weights[2, level, start:stop] * pltpu.roll(here, 1, 1)
            total += weights[3, level, start:stop] * above
            total += weights[4, level, start:stop] * below
            field[target, level, EDGE + start : EDGE + stop] = total
        return carry

    lax.fori_loop(0, levels, one_level, 0)


def smooth(field, weights, slot, depth):
    tall = weights.shape[2]
    for step in range(PASSES):
        reach = depth + PASSES - 1 - step
        skip = (HALO - reach) // 8 * 8
        sweep(field, weights, slot, 1 - slot, skip, tall - skip)
        slot = 1 - slot
    return slot


def one_hot_iota(cells):
    return lax.broadcasted_iota(jnp.int32, (cells, 128), 0).astype(F32).astype(BF16)


def spread_row(row, count):
    return jnp.broadcast_to(jnp.broadcast_to(row, (16, 128)).astype(BF16)[0:1], (count, 128))


def scatter_into(total, load_rows, steps, half_rows, half_cols):
    row_iota = one_hot_iota(half_rows)
    col_iota = one_hot_iota(half_cols)
    total[...] = jnp.zeros_like(total)

    def step(index, carry):
        high_rows, low_rows, columns = [], [], []
        for row_index, col_index, value in load_rows(index):
            high, low = parts(jnp.broadcast_to(value, (16, 128)))
            hit = row_iota == spread_row(row_index, half_rows)
            zero = jnp.zeros((half_rows, 128), BF16)
            high_rows.append(jnp.where(hit, jnp.broadcast_to(high[0:1], (half_rows, 128)), zero))
            low_rows.append(jnp.where(hit, jnp.broadcast_to(low[0:1], (half_rows, 128)), zero))
            columns.append(
                jnp.where(
                    col_iota == spread_row(col_index, half_cols),
                    jnp.ones((half_cols, 128), BF16),
                    jnp.zeros((half_cols, 128), BF16),
                )
            )
        left = jnp.concatenate(high_rows + low_rows, axis=1)
        right = jnp.concatenate(columns + columns, axis=1)
        total[...] += lax.dot_general(
            left, right, (((1,), (1,)), ((), ())), preferred_element_type=F32
        )
        return carry

    lax.fori_loop(0, steps, step, 0)


def split_cells(cells, rows, cols):
    level = cells // (rows * cols)
    row = (cells // cols) % rows
    col = cells % cols
    return (level // 2) * rows + row, (level % 2) * cols + col


def put_field(total, sigma, field, extra=None):
    levels, rows, cols = sigma.shape
    fields = []
    for level in range(levels):
        r, c = level // 2 * rows, level % 2 * cols
        value = sigma[level] * total[r : r + rows, c : c + cols]
        if extra is not None:
            value = value + extra(level)
        field[level] = value
        fields.append(value)
    return fields


def scatter_first_kernel(capacity, arrived, sigma, row_at, col_at, field, *refs):
    sides, total = refs
    levels, rows, cols = sigma.shape
    sources = arrived.shape[0]
    cells = jnp.concatenate([arrived[source, 0:capacity] for source in range(sources)], axis=0)
    row_index, col_index = split_cells(cells.astype(jnp.int32), rows, cols)
    row_at[...] = row_index.astype(F32)
    col_at[...] = col_index.astype(F32)

    def load(index):
        base = pl.multiple_of(index * GROUP, GROUP)
        row_block = row_at[pl.ds(base, GROUP)]
        col_block = col_at[pl.ds(base, GROUP)]
        for j in range(GROUP):
            source = index * (GROUP // capacity) + j // capacity
            slot = capacity + j % capacity
            yield row_block[j : j + 1], col_block[j : j + 1], arrived[source, slot : slot + 1]

    scatter_into(total, load, row_at.shape[0] // GROUP, levels // 2 * rows, 2 * cols)
    sides[...] = pack_sides(put_field(total, sigma, field))


def scatter_first(arrived, sigma, capacity):
    levels, rows, cols = sigma.shape
    slots = arrived.shape[0] * capacity
    shapes = [(slots, 128), (slots, 128), (levels, rows, cols), (rows, cols)]
    out = pl.pallas_call(
        functools.partial(scatter_first_kernel, capacity),
        out_shape=[jax.ShapeDtypeStruct(shape, F32) for shape in shapes],
        in_specs=[VMEM] * 2,
        out_specs=[VMEM] * len(shapes),
        scratch_shapes=[pltpu.VMEM((levels // 2 * rows, 2 * cols), F32)],
        compiler_params=PARAMS,
        name="scatter_first",
    )(arrived, sigma)
    return out


def lane_value(block, lane):
    return jnp.sum(jnp.where(lane_of(block.shape[0]) == lane, block, 0.0))


def lanes(values, rows):
    lane = lane_of(rows)
    out = jnp.zeros((rows, 128), F32)
    for index, value in enumerate(values):
        out = jnp.where(lane == index, value, out)
    return out


def scatter_next_kernel(capacity, last, arrived, row_at, col_at, sigma, *refs):
    if last:
        previous, field, sides, sums, total = refs
    else:
        previous, (field, sides, sums, total) = None, refs
    levels, rows, cols = sigma.shape
    sources = arrived.shape[0]
    gathered = jnp.concatenate(
        [arrived[source, capacity : capacity + 1] for source in range(sources)], axis=0
    )
    added = jnp.sum(gathered, axis=0, keepdims=True)
    sums[...] = jnp.broadcast_to(added, (8, 128))

    def load(index):
        base = pl.multiple_of(index * GROUP, GROUP)
        row_block = row_at[pl.ds(base, GROUP)]
        col_block = col_at[pl.ds(base, GROUP)]
        for j in range(GROUP):
            source = index * (GROUP // capacity) + j // capacity
            slot = j % capacity
            yield row_block[j : j + 1], col_block[j : j + 1], arrived[source, slot : slot + 1]

    scatter_into(total, load, row_at.shape[0] // GROUP, levels // 2 * rows, 2 * cols)
    extra = None
    if last:
        beta = lane_value(added, 1) / lane_value(added, 0)

        def extra(level):
            return beta * previous[level]

    sides[...] = pack_sides(put_field(total, sigma, field, extra))


def scatter_next(arrived, row_at, col_at, sigma, capacity, previous=None):
    levels, rows, cols = sigma.shape
    last = previous is not None
    shapes = [(levels, rows, cols), (rows, cols), (8, 128)]
    operands = [arrived, row_at, col_at, sigma] + ([previous] if last else [])
    out = pl.pallas_call(
        functools.partial(scatter_next_kernel, capacity, last),
        out_shape=[jax.ShapeDtypeStruct(shape, F32) for shape in shapes],
        in_specs=[VMEM] * len(operands),
        out_specs=[VMEM] * len(shapes),
        scratch_shapes=[pltpu.VMEM((levels // 2 * rows, 2 * cols), F32)],
        compiler_params=PARAMS,
        name="scatter_last" if last else "scatter_next",
    )(*operands)
    return out


def gather_from(fields, row_at, col_at, seen, table):
    rows, cols = fields[0].shape
    half_rows, half_cols = len(fields) // 2 * rows, 2 * cols
    for level, field in enumerate(fields):
        high, low = parts(field.T)
        c, r = level % 2 * cols, level // 2 * rows
        table[c : c + cols, r : r + rows] = high
        table[c : c + cols, half_rows + r : half_rows + r + rows] = low
    row_iota = one_hot_iota(half_rows)
    col_iota = lax.broadcasted_iota(jnp.int32, (half_cols, 256), 0).astype(F32)

    def step(index, carry):
        base = pl.multiple_of(index * 8, 8)
        row_block = row_at[pl.ds(base, 8)]
        col_block = col_at[pl.ds(base, 8)]
        found = []
        for j in range(0, 8, 2):
            hot = jnp.concatenate(
                [
                    jnp.where(
                        row_iota == spread_row(row_block[i : i + 1], half_rows),
                        jnp.ones((half_rows, 128), BF16),
                        jnp.zeros((half_rows, 128), BF16),
                    )
                    for i in (j, j + 1)
                ],
                axis=1,
            )
            lines = jnp.dot(
                table[...], jnp.concatenate([hot, hot], axis=0), preferred_element_type=F32
            )
            wanted = jnp.concatenate([col_block[j : j + 1], col_block[j + 1 : j + 2]], axis=1)
            value = jnp.sum(jnp.where(col_iota == wanted, lines, 0.0), axis=0, keepdims=True)
            found += [value[:, :128], value[:, 128:]]
        seen[pl.ds(base, 8)] = jnp.concatenate(found, axis=0)
        return carry

    lax.fori_loop(0, row_at.shape[0] // 8, step, 0)


def own_part(field, slot, level, rows, cols):
    return field[slot, level, EDGE + HALO : EDGE + HALO + rows, 0:cols]


def total_of(pairs):
    added = None
    for left, right in pairs:
        term = left * right
        added = term if added is None else added + term
    return jnp.sum(added)


def observe_first_kernel(source, *refs):
    halo, weights, sigma, row_at, col_at = refs[:3], refs[3], refs[4], refs[5], refs[6]
    seen, right, image, sums, field, table = refs[7:]
    levels, rows, cols = source.shape
    load_field(field, halo, source)
    slot = smooth(field, weights, 0, PASSES)
    right[...] = field[slot, :, EDGE : EDGE + rows + 2 * HALO]
    own = [own_part(field, slot, level, rows, cols) for level in range(levels)]
    sums[...] = lanes([total_of([(value, value) for value in own])], 8)
    slot = smooth(field, weights, slot, 0)
    fields = [sigma[level] * own_part(field, slot, level, rows, cols) for level in range(levels)]
    for level in range(levels):
        image[level] = fields[level]
    gather_from(fields, row_at, col_at, seen, table)


def observe_next_kernel(source, *refs):
    halo, weights, sigma, row_at, col_at = refs[:3], refs[3], refs[4], refs[5], refs[6]
    right, scalars = refs[7:9]
    seen, residual, image, sums, field, table = refs[9:]
    levels, rows, cols = source.shape
    tall = rows + 2 * HALO
    norm, product = lane_value(scalars[0:1], 0), lane_value(scalars[0:1], 1)
    alpha = norm / (norm + product)
    load_field(field, halo, source)
    slot = smooth(field, weights, 0, PASSES)

    def one_level(level, carry):
        first = right[level]
        field[slot, level, EDGE : EDGE + tall] = first - alpha * (
            first + field[slot, level, EDGE : EDGE + tall]
        )
        return carry

    lax.fori_loop(0, levels, one_level, 0)
    own = [own_part(field, slot, level, rows, cols) for level in range(levels)]
    first = [right[level, HALO : HALO + rows, 0:cols] for level in range(levels)]
    for level in range(levels):
        residual[level] = own[level]
    sums[...] = lanes(
        [total_of([(value, value) for value in own]), total_of(list(zip(own, first)))], 8
    )
    slot = smooth(field, weights, slot, 0)
    fields = [sigma[level] * own_part(field, slot, level, rows, cols) for level in range(levels)]
    for level in range(levels):
        image[level] = fields[level]
    gather_from(fields, row_at, col_at, seen, table)


def observe(source, halo, weights, sigma, row_at, col_at, right=None, scalars=None):
    levels, rows, cols = sigma.shape
    tall = rows + 2 * HALO
    slots = row_at.shape[0]
    first = right is None
    kept = (levels, tall, 2 * cols) if first else (levels, rows, cols)
    shapes = [(slots, 128), kept, (levels, rows, cols), (8, 128)]
    operands = [source, *halo, weights, sigma, row_at, col_at]
    operands += [] if first else [right, scalars]
    return pl.pallas_call(
        observe_first_kernel if first else observe_next_kernel,
        out_shape=[jax.ShapeDtypeStruct(shape, F32) for shape in shapes],
        in_specs=[VMEM] * len(operands),
        out_specs=[VMEM] * len(shapes),
        scratch_shapes=[
            pltpu.VMEM((2, levels, tall + 2 * EDGE, 2 * cols), F32),
            pltpu.VMEM((2 * cols, levels * rows), BF16),
        ],
        compiler_params=PARAMS,
        name="observe_first" if first else "observe_next",
    )(*operands)


def finish_kernel(source, *refs):
    halo, weights, right, residual_one, image_zero, image_one, scalars = refs[:3], *refs[3:9]
    increment, residual, field = refs[9:]
    levels, rows, cols = source.shape
    norm_zero, norm_one, cross, product_zero, product_one, product_cross = [
        lane_value(scalars[0:1], index) for index in range(6)
    ]
    alpha_zero = norm_zero / (norm_zero + product_zero)
    beta = norm_one / norm_zero
    square = norm_one + 2.0 * beta * cross + beta * beta * norm_zero
    seen = product_one + 2.0 * beta * product_cross + beta * beta * product_zero
    alpha_one = norm_one / (square + seen)
    for level in range(levels):
        direction = image_one[level] + beta * image_zero[level]
        increment[level] = alpha_zero * image_zero[level] + alpha_one * direction
    load_field(field, halo, source)
    slot = smooth(field, weights, 0, 0)
    for level in range(levels):
        here = residual_one[level]
        direction = here + beta * right[level, HALO : HALO + rows, 0:cols]
        image = direction + own_part(field, slot, level, rows, cols)
        residual[level] = here - alpha_one * image


def finish(source, halo, weights, right, residual_one, image_zero, image_one, scalars):
    levels, rows, cols = source.shape
    tall = rows + 2 * HALO
    return pl.pallas_call(
        finish_kernel,
        out_shape=[jax.ShapeDtypeStruct((levels, rows, cols), F32)] * 2,
        in_specs=[VMEM] * 10,
        out_specs=[VMEM] * 2,
        scratch_shapes=[pltpu.VMEM((2, levels, tall + 2 * EDGE, 2 * cols), F32)],
        compiler_params=PARAMS,
        name="finish",
    )(source, *halo, weights, right, residual_one, image_zero, image_one, scalars)


def apply_blocks(values, weights):
    high, low = parts(values)
    first = jnp.concatenate([high, low, jnp.zeros((128 - 2 * GROUP, 128), BF16)], axis=0)
    second = jnp.concatenate([high, jnp.zeros((128 - GROUP, 128), BF16)], axis=0)
    right = jnp.concatenate([first, second], axis=1)
    lane = lane_of(128)
    column = jnp.where(lane < 2 * GROUP, lane % GROUP, GROUP)
    kept = jnp.zeros((128, 128), F32)
    for start in range(0, GROUP, 4):
        left = jnp.concatenate(parts(weights[start : start + 4].reshape(4 * 128, 128)), axis=1)
        product = lax.dot_general(left, right, (((1,), (1,)), ((), ())), preferred_element_type=F32)
        for k in range(4):
            kept = jnp.where(column == start + k, product[k * 128 : (k + 1) * 128], kept)
    kept = kept.T
    return kept[:GROUP] + kept[GROUP : 2 * GROUP]


def weigh_first_kernel(capacity, owner, cells, innovations, weights, parcel, place, count):
    step = pl.program_id(0)
    stride = 2 * capacity

    @pl.when(step == 0)
    def _():
        parcel[...] = jnp.zeros_like(parcel)

        def clear(index, carry):
            count[index] = 0
            return carry

        lax.fori_loop(0, count.shape[0], clear, 0)

    result = apply_blocks(innovations[...], weights)
    cell_rows = cells[...].astype(F32)
    for k in range(GROUP):
        index = step * GROUP + k
        target = owner[index, 0]
        rank = count[target]
        count[target] = rank + 1
        place[index] = target * capacity + rank
        at = target * stride + rank
        parcel[pl.ds(at, 1), :] = cell_rows[k : k + 1]
        parcel[pl.ds(at + capacity, 1), :] = result[k : k + 1]


def weigh_first(owner, cells, innovations, weights, devices, capacity):
    held, width = cells.shape
    return pl.pallas_call(
        functools.partial(weigh_first_kernel, capacity),
        grid=(held // GROUP,),
        out_shape=[
            jax.ShapeDtypeStruct((devices * 2 * capacity, width), F32),
            jax.ShapeDtypeStruct((held,), jnp.int32),
        ],
        in_specs=[
            SMEM,
            pl.BlockSpec((GROUP, width), lambda i: (i, 0)),
            pl.BlockSpec((GROUP, width), lambda i: (i, 0)),
            pl.BlockSpec((GROUP, width, width), lambda i: (i, 0, 0)),
        ],
        out_specs=[
            pl.BlockSpec((devices * 2 * capacity, width), lambda i: (0, 0)),
            SMEM,
        ],
        scratch_shapes=[pltpu.SMEM((devices,), jnp.int32)],
        compiler_params=PARAMS,
        name="weigh_first",
    )(owner, cells, innovations, weights)


def weigh_next_kernel(capacity, stride, devices, last, place, returned, sums, weights, *refs):
    if last:
        sums_before, weighted_before, parcel, totals = refs
    else:
        parcel, weighted, totals = refs
    step = pl.program_id(0)

    @pl.when(step == 0)
    def _():
        parcel[...] = jnp.zeros_like(parcel)
        totals[...] = jnp.zeros_like(totals)

    places = [place[step * GROUP + k] for k in range(GROUP)]
    here = jnp.concatenate([returned[pl.ds(at, 1), :] for at in places], axis=0)
    result = apply_blocks(here, weights)
    totals[0] += here * result
    if last:
        totals[1] += here * weighted_before[...]
    else:
        weighted[...] = result
    for k in range(GROUP):
        target = places[k] // capacity
        at = target * stride + (places[k] - target * capacity)
        parcel[pl.ds(at, 1), :] = result[k : k + 1]

    @pl.when(step == pl.num_programs(0) - 1)
    def _():
        if last:
            scalars = [
                lane_value(sums_before[0:1], 0),
                lane_value(sums[0:1], 0),
                lane_value(sums[0:1], 1),
                lane_value(sums_before[0:1], 1),
                jnp.sum(totals[0]),
                jnp.sum(totals[1]),
            ]
            scalars[0] = scalars[0] / devices
            scalars[3] = scalars[3] / devices
        else:
            scalars = [lane_value(sums[0:1], 0), jnp.sum(totals[0])]
        row = lanes(scalars, 1)
        for target in range(devices):
            at = target * stride + capacity
            parcel[at : at + 1] = row


def weigh_next(place, returned, sums, weights, devices, capacity, stride, before=None):
    held, width = weights.shape[:2]
    last = before is not None
    resident = lambda shape: pl.BlockSpec(shape, lambda i: (0,) * len(shape))
    operands = [place, returned, sums, weights]
    in_specs = [
        SMEM,
        resident(returned.shape),
        resident((8, 128)),
        pl.BlockSpec((GROUP, width, width), lambda i: (i, 0, 0)),
    ]
    out_shape = [jax.ShapeDtypeStruct((devices * stride, width), F32)]
    out_specs = [resident((devices * stride, width))]
    if last:
        operands += list(before)
        in_specs += [resident((8, 128)), pl.BlockSpec((GROUP, width), lambda i: (i, 0))]
    else:
        out_shape += [jax.ShapeDtypeStruct((held, width), F32)]
        out_specs += [pl.BlockSpec((GROUP, width), lambda i: (i, 0))]
    return pl.pallas_call(
        functools.partial(weigh_next_kernel, capacity, stride, devices, last),
        grid=(held // GROUP,),
        out_shape=out_shape,
        in_specs=in_specs,
        out_specs=out_specs,
        scratch_shapes=[pltpu.VMEM((2, GROUP, 128), F32)],
        compiler_params=PARAMS,
        name="weigh_last" if last else "weigh_next",
    )(*operands)


def swap(block):
    return lax.all_to_all(block, ("lat", "lon"), split_axis=0, concat_axis=0, tiled=True)


def body(sigma, east_coef, north_coef, mask, innovations, cells, owner, obs_weights):
    devices = lax.axis_size("lat") * lax.axis_size("lon")
    held, width = cells.shape
    capacity = max(2, (2 * held + devices - 1) // devices)
    stride = (capacity + 8) // 8 * 8
    slots = devices * capacity

    face_halo = exchange([mask, east_coef, north_coef], face_sides(mask, east_coef, north_coef))
    parcel, place = weigh_first(owner, cells, innovations, obs_weights, devices, capacity)
    arrived = swap(parcel.reshape(devices, 2 * capacity, width))
    weights = face_weights(mask, east_coef, north_coef, face_halo)

    row_at, col_at, field, sides = scatter_first(arrived, sigma, capacity)
    seen, right, image_zero, sums = observe(
        field, exchange([field], sides), weights, sigma, row_at, col_at
    )
    returned = swap(seen.reshape(devices, capacity, width)).reshape(slots, width)
    parcel, weighted = weigh_next(place, returned, sums, obs_weights, devices, capacity, stride)
    arrived = swap(parcel.reshape(devices, stride, width))

    field_zero, sides, scalars_zero = scatter_next(arrived, row_at, col_at, sigma, capacity)
    seen, residual_one, image_one, sums = observe(
        field_zero, exchange([field_zero], sides), weights, sigma, row_at, col_at, right, scalars_zero
    )
    returned = swap(seen.reshape(devices, capacity, width)).reshape(slots, width)
    (parcel,) = weigh_next(
        place, returned, sums, obs_weights, devices, capacity, stride, (scalars_zero, weighted)
    )
    arrived = swap(parcel.reshape(devices, stride, width))

    field, sides, scalars = scatter_next(arrived, row_at, col_at, sigma, capacity, field_zero)
    increment, residual = finish(
        field, exchange([field], sides), weights, right, residual_one, image_zero, image_one, scalars
    )
    return (increment, residual)


def solution(mesh):
    return jax.shard_map(
        body,
        mesh=mesh,
        in_specs=(
            P(None, "lat", "lon"),
            P(None, "lat", "lon"),
            P(None, "lat", "lon"),
            P(None, "lat", "lon"),
            P(("lat", "lon"), None),
            P(("lat", "lon"), None),
            P(("lat", "lon"), None),
            P(("lat", "lon"), None, None),
        ),
        out_specs=(P(None, "lat", "lon"), P(None, "lat", "lon")),
        check_vma=False,
    )
```

```python
import functools

import jax
import jax.numpy as jnp
from jax import lax
from jax.experimental import pallas as pl
from jax.experimental.pallas import tpu as pltpu
from jax.sharding import PartitionSpec as P

PASSES = 5
HALO = 16
EDGE = 8
GROUP = 16
F32 = jnp.float32
BF16 = jnp.bfloat16
VMEM = pl.BlockSpec(memory_space=pltpu.VMEM)
HBM = pl.BlockSpec(memory_space=pltpu.HBM)
SMEM = pl.BlockSpec(memory_space=pltpu.SMEM)
PARAMS = pltpu.CompilerParams(vmem_limit_bytes=32 * 1024 * 1024)


def parts(values):
    high = values.astype(BF16)
    low = (values - high.astype(F32)).astype(BF16)
    return high, low


def lane_of(rows):
    return lax.broadcasted_iota(jnp.int32, (rows, 128), 1)


def pack_sides(fields):
    lane = lane_of(fields[0].shape[0])
    packed = jnp.zeros_like(fields[0])
    for level, field in enumerate(fields):
        start = 2 * HALO * level
        left = pltpu.roll(field, start, 1) if start else field
        right = pltpu.roll(field, (start + 2 * HALO) % 128, 1)
        packed = jnp.where((lane >= start) & (lane < start + HALO), left, packed)
        packed = jnp.where((lane >= start + HALO) & (lane < start + 2 * HALO), right, packed)
    return packed


def place_halo(put, levels, rows, own, halo):
    before, after, mixed = halo
    for level in range(levels):
        put(level, 0, HALO, 0, before(level))
        put(level, HALO, HALO + rows, 0, own(level))
        put(level, HALO + rows, 2 * HALO + rows, 0, after(level))
    spans = (
        (0, HALO, before(levels)),
        (HALO, HALO + rows, mixed()),
        (HALO + rows, 2 * HALO + rows, after(levels)),
    )
    for start, stop, sides in spans:
        lane = lane_of(stop - start)
        for level in range(levels):
            shift = 2 * HALO * level
            first = pltpu.roll(sides, (128 - shift) % 128, 1) if shift else sides
            back = (128 - 2 * HALO - shift) % 128
            last = pltpu.roll(sides, back, 1) if back else sides
            side = jnp.where(lane < HALO, first, jnp.where(lane >= 128 - HALO, last, 0.0))
            put(level, start, stop, 1, side)


def turn_kernel(count, *refs):
    arrays, (from_east, from_west, mixed, down, up) = refs[:count], refs[count:]
    levels, rows, _ = arrays[0].shape
    for index, array in enumerate(arrays):
        at = (index,) if count > 1 else ()
        lane = lane_of(rows)
        sides = jnp.where(lane % (2 * HALO) < HALO, from_east[at + (...,)], from_west[at + (...,)])
        mixed[at + (...,)] = sides
        for level in range(levels):
            down[at + (level,)] = array[level, rows - HALO :].astype(F32)
            up[at + (level,)] = array[level, :HALO].astype(F32)
        down[at + (levels,)] = sides[rows - HALO :]
        up[at + (levels,)] = sides[:HALO]


def exchange(arrays, sides):
    mixed, down, up = exchange_columns(arrays, sides)
    return exchange_rows(down, up) + (mixed,)


def exchange_columns(arrays, sides):
    count = len(arrays)
    levels, rows, cols = arrays[0].shape
    wide = lax.axis_size("lon")
    east = [(i, (i + 1) % wide) for i in range(wide)]
    from_west = lax.ppermute(sides, "lon", east)
    from_east = lax.ppermute(sides, "lon", [(to, at) for at, to in east])
    lead = (count,) if count > 1 else ()
    shapes = [lead + (rows, cols)] + [lead + (levels + 1, HALO, cols)] * 2
    return pl.pallas_call(
        functools.partial(turn_kernel, count),
        out_shape=[jax.ShapeDtypeStruct(shape, F32) for shape in shapes],
        in_specs=[VMEM] * (count + 2),
        out_specs=[VMEM] * 3,
        compiler_params=PARAMS,
        name="turn",
    )(*arrays, from_east, from_west)


def exchange_rows(down, up):
    north = [(i, i + 1) for i in range(lax.axis_size("lat") - 1)]
    before = lax.ppermute(down, "lat", north)
    after = lax.ppermute(up, "lat", [(to, at) for at, to in north])
    return before, after


def face_side_kernel(mask, east, north, sides):
    for index, array in enumerate((mask, east, north)):
        sides[index] = pack_sides([array[level].astype(F32) for level in range(mask.shape[0])])


def face_sides(mask, east, north):
    return pl.pallas_call(
        face_side_kernel,
        out_shape=jax.ShapeDtypeStruct((3,) + mask.shape[1:], F32),
        in_specs=[VMEM] * 3,
        out_specs=VMEM,
        compiler_params=PARAMS,
        name="face_sides",
    )(mask, east, north)


def face_kernel(mask, east, north, *refs):
    halo, weights, padded, faces = refs[:3], refs[3], refs[4], refs[5]
    levels, rows, cols = mask.shape
    tall = rows + 2 * HALO
    zeros = jnp.zeros((EDGE, 2 * cols), F32)
    for index, array in enumerate((mask, east, north)):
        for level in range(levels):
            padded[index, level, 0:EDGE] = zeros
            padded[index, level, EDGE + tall :] = zeros

        def put(level, start, stop, half, value, index=index):
            padded[index, level, EDGE + start : EDGE + stop, half * cols : (half + 1) * cols] = value

        def pick(ref, index=index):
            if len(ref.shape) == 4:
                return lambda level: ref[index, level]
            return lambda: ref[index]

        place_halo(
            put,
            levels,
            rows,
            lambda level, array=array: array[level].astype(F32),
            [pick(ref) for ref in halo],
        )
    faces[0:EDGE] = zeros
    faces[EDGE + tall :] = zeros

    def one_level(level, carry):
        land = padded[0, level, EDGE : EDGE + tall]
        land_north = padded[0, level, EDGE + 1 : EDGE + 1 + tall]
        east_face = padded[1, level, EDGE : EDGE + tall] * land * pltpu.roll(land, 2 * cols - 1, 1)
        west_face = pltpu.roll(east_face, 1, 1)
        north_face = padded[2, level, EDGE : EDGE + tall] * land * land_north
        faces[EDGE : EDGE + tall] = north_face
        south_face = faces[EDGE - 1 : EDGE - 1 + tall]
        weights[0, level] = 1.0 - (((east_face + west_face) + north_face) + south_face)
        weights[1, level] = east_face
        weights[2, level] = west_face
        weights[3, level] = north_face
        weights[4, level] = south_face
        return carry

    lax.fori_loop(0, levels, one_level, 0)


def face_weights(mask, east, north, halo):
    levels, rows, cols = mask.shape
    tall = rows + 2 * HALO
    return pl.pallas_call(
        face_kernel,
        out_shape=jax.ShapeDtypeStruct((5, levels, tall, 2 * cols), F32),
        in_specs=[VMEM] * 6,
        out_specs=VMEM,
        scratch_shapes=[
            pltpu.VMEM((3, levels, tall + 2 * EDGE, 2 * cols), F32),
            pltpu.VMEM((tall + 2 * EDGE, 2 * cols), F32),
        ],
        compiler_params=PARAMS,
        name="face_weights",
    )(mask, east, north, *halo)


def load_field(field, halo, source):
    levels, rows, cols = source.shape
    tall = rows + 2 * HALO
    zeros = jnp.zeros((EDGE, 2 * cols), F32)
    for slot in range(2):
        for level in range(levels):
            field[slot, level, 0:EDGE] = zeros
            field[slot, level, EDGE + tall :] = zeros

    def put(level, start, stop, half, value):
        field[0, level, EDGE + start : EDGE + stop, half * cols : (half + 1) * cols] = value

    def pick(ref):
        if len(ref.shape) == 3:
            return lambda level: ref[level]
        return lambda: ref[...]

    place_halo(put, levels, rows, lambda level: source[level], [pick(ref) for ref in halo])


def sweep(field, weights, source, target, rows_from, rows_to):
    levels = field.shape[1]
    wide = field.shape[3]

    def one_level(level, carry):
        for start in range(rows_from, rows_to, 16):
            stop = min(start + 16, rows_to)
            here = field[source, level, EDGE + start : EDGE + stop]
            above = field[source, level, EDGE + start + 1 : EDGE + stop + 1]
            below = field[source, level, EDGE + start - 1 : EDGE + stop - 1]
            total = weights[0, level, start:stop] * here
            total += weights[1, level, start:stop] * pltpu.roll(here, wide - 1, 1)
            total += weights[2, level, start:stop] * pltpu.roll(here, 1, 1)
            total += weights[3, level, start:stop] * above
            total += weights[4, level, start:stop] * below
            field[target, level, EDGE + start : EDGE + stop] = total
        return carry

    lax.fori_loop(0, levels, one_level, 0)


def smooth(field, weights, slot, depth):
    tall = weights.shape[2]
    for step in range(PASSES):
        reach = depth + PASSES - 1 - step
        skip = (HALO - reach) // 8 * 8
        sweep(field, weights, slot, 1 - slot, skip, tall - skip)
        slot = 1 - slot
    return slot


def index_iota(cells):
    return lax.broadcasted_iota(jnp.int32, (cells, 128), 0).astype(F32).astype(BF16)


def spread_row(row, count):
    return jnp.broadcast_to(jnp.broadcast_to(row, (16, 128)).astype(BF16)[0:1], (count, 128))


def one_hot(iota, row, form):
    count = iota.shape[0]
    if form == "ramp":
        return jnp.maximum(1.0 - jnp.abs(iota - spread_row(row, count)), 0.0).astype(BF16)
    return jnp.where(
        iota == spread_row(row, count), jnp.ones((count, 128), BF16), jnp.zeros((count, 128), BF16)
    )


def scatter_into(total, load_rows, slots, half_rows, half_cols, group, form):
    row_iota = index_iota(half_rows)
    col_iota = index_iota(half_cols)
    total[...] = jnp.zeros_like(total)

    def step(index, carry):
        high_rows, low_rows, columns = [], [], []
        for row_index, col_index, value in load_rows(index):
            high, low = parts(jnp.broadcast_to(value, (16, 128)))
            high = jnp.broadcast_to(high[0:1], (half_rows, 128))
            low = jnp.broadcast_to(low[0:1], (half_rows, 128))
            if form == "ramp":
                hot = one_hot(row_iota, row_index, form)
                high_rows.append(hot * high)
                low_rows.append(hot * low)
            else:
                hit = row_iota == spread_row(row_index, half_rows)
                zero = jnp.zeros((half_rows, 128), BF16)
                high_rows.append(jnp.where(hit, high, zero))
                low_rows.append(jnp.where(hit, low, zero))
            columns.append(one_hot(col_iota, col_index, form))
        left = jnp.concatenate(high_rows + low_rows, axis=1)
        right = jnp.concatenate(columns + columns, axis=1)
        total[...] += lax.dot_general(
            left, right, (((1,), (1,)), ((), ())), preferred_element_type=F32
        )
        return carry

    lax.fori_loop(0, slots // group, step, 0)


def load_group(index, group, capacity, row_at, col_at, arrived, first_slot):
    base = pl.multiple_of(index * group, group)
    if group < 8:
        base = pl.multiple_of(index * group // 8 * 8, 8)
    row_block = row_at[pl.ds(base, max(group, 8))]
    col_block = col_at[pl.ds(base, max(group, 8))]
    for j in range(group):
        source = index * (group // capacity) + j // capacity
        slot = first_slot + j % capacity
        yield row_block[j : j + 1], col_block[j : j + 1], arrived[source, pl.ds(slot, 1)]


def split_cells(cells, rows, cols):
    level = cells // (rows * cols)
    row = (cells // cols) % rows
    col = cells % cols
    return (level // 2) * rows + row, (level % 2) * cols + col


def put_field(total, sigma, field, extra=None):
    levels, rows, cols = sigma.shape
    fields = []
    for level in range(levels):
        r, c = level // 2 * rows, level % 2 * cols
        value = sigma[level] * total[r : r + rows, c : c + cols]
        if extra is not None:
            value = value + extra(level)
        field[level] = value
        fields.append(value)
    return fields


def scatter_first_kernel(capacity, arrived, sigma, row_at, col_at, field, *refs):
    sides, total = refs
    levels, rows, cols = sigma.shape
    sources = arrived.shape[0]
    cells = jnp.concatenate([arrived[source, 0:capacity] for source in range(sources)], axis=0)
    row_index, col_index = split_cells(cells.astype(jnp.int32), rows, cols)
    row_at[...] = row_index.astype(F32)
    col_at[...] = col_index.astype(F32)

    def load(index):
        return load_group(index, 16, capacity, row_at, col_at, arrived, capacity)

    scatter_into(total, load, row_at.shape[0], levels // 2 * rows, 2 * cols, 16, "ramp")
    sides[...] = pack_sides(put_field(total, sigma, field))


def scatter_first(arrived, sigma, capacity):
    levels, rows, cols = sigma.shape
    slots = arrived.shape[0] * capacity
    shapes = [(slots, 128), (slots, 128), (levels, rows, cols), (rows, cols)]
    out = pl.pallas_call(
        functools.partial(scatter_first_kernel, capacity),
        out_shape=[jax.ShapeDtypeStruct(shape, F32) for shape in shapes],
        in_specs=[VMEM] * 2,
        out_specs=[VMEM] * len(shapes),
        scratch_shapes=[pltpu.VMEM((levels // 2 * rows, 2 * cols), F32)],
        compiler_params=PARAMS,
        name="scatter_first",
    )(arrived, sigma)
    return out


def lane_value(block, lane):
    return jnp.sum(jnp.where(lane_of(block.shape[0]) == lane, block, 0.0))


def lanes(values, rows):
    lane = lane_of(rows)
    out = jnp.zeros((rows, 128), F32)
    for index, value in enumerate(values):
        out = jnp.where(lane == index, value, out)
    return out


def scatter_next_kernel(capacity, last, arrived, row_at, col_at, sigma, *refs):
    if last:
        previous, field, sides, sums, total = refs
    else:
        previous, (field, sides, sums, total) = None, refs
    levels, rows, cols = sigma.shape
    sources = arrived.shape[0]
    gathered = jnp.concatenate(
        [arrived[source, capacity : capacity + 1] for source in range(sources)], axis=0
    )
    added = jnp.sum(gathered, axis=0, keepdims=True)
    sums[...] = jnp.broadcast_to(added, (8, 128))

    group = 8 if last else 16

    def load(index):
        return load_group(index, group, capacity, row_at, col_at, arrived, 0)

    scatter_into(
        total, load, row_at.shape[0], levels // 2 * rows, 2 * cols, group, "ramp" if last else "hit"
    )
    extra = None
    if last:
        beta = lane_value(added, 1) / lane_value(added, 0)

        def extra(level):
            return beta * previous[level]

    sides[...] = pack_sides(put_field(total, sigma, field, extra))


def scatter_next(arrived, row_at, col_at, sigma, capacity, previous=None):
    levels, rows, cols = sigma.shape
    last = previous is not None
    shapes = [(levels, rows, cols), (rows, cols), (8, 128)]
    operands = [arrived, row_at, col_at, sigma] + ([previous] if last else [])
    out = pl.pallas_call(
        functools.partial(scatter_next_kernel, capacity, last),
        out_shape=[jax.ShapeDtypeStruct(shape, F32) for shape in shapes],
        in_specs=[VMEM] * len(operands),
        out_specs=[VMEM] * len(shapes),
        scratch_shapes=[pltpu.VMEM((levels // 2 * rows, 2 * cols), F32)],
        compiler_params=PARAMS,
        name="scatter_last" if last else "scatter_next",
    )(*operands)
    return out


def gather_from(fields, row_at, col_at, seen, table, form):
    rows, cols = fields[0].shape
    half_rows, half_cols = len(fields) // 2 * rows, 2 * cols
    for level, field in enumerate(fields):
        high, low = parts(field.T)
        c, r = level % 2 * cols, level // 2 * rows
        table[c : c + cols, r : r + rows] = high
        table[c : c + cols, half_rows + r : half_rows + r + rows] = low
    row_iota = index_iota(half_rows)
    sublane = lax.broadcasted_iota(jnp.int32, (8, 256), 0)

    def step(index, carry):
        base = pl.multiple_of(index * 8, 8)
        row_block = row_at[pl.ds(base, 8)]
        col_block = col_at[pl.ds(base, 8)].astype(jnp.int32)
        found = []
        for j in range(0, 8, 2):
            hot = jnp.concatenate(
                [one_hot(row_iota, row_block[i : i + 1], form) for i in (j, j + 1)], axis=1
            )
            lines = jnp.dot(
                table[...], jnp.concatenate([hot, hot], axis=0), preferred_element_type=F32
            )
            wanted = jnp.concatenate([col_block[j : j + 1], col_block[j + 1 : j + 2]], axis=1)
            wanted = jnp.broadcast_to(wanted, (8, 256))
            tiles = [lines[i : i + 8] for i in range(0, half_cols, 8)]
            bit = 8
            while len(tiles) > 1:
                upper = (wanted & bit) != 0
                tiles = [
                    jnp.where(upper, tiles[i + 1], tiles[i]) for i in range(0, len(tiles), 2)
                ]
                bit = bit * 2
            value = jnp.sum(
                jnp.where((wanted & 7) == sublane, tiles[0], 0.0), axis=0, keepdims=True
            )
            found += [value[:, :128], value[:, 128:]]
        seen[pl.ds(base, 8)] = jnp.concatenate(found, axis=0)
        return carry

    lax.fori_loop(0, row_at.shape[0] // 8, step, 0)


def own_part(field, slot, level, rows, cols):
    return field[slot, level, EDGE + HALO : EDGE + HALO + rows, 0:cols]


def total_of(pairs):
    added = None
    for left, right in pairs:
        term = left * right
        added = term if added is None else added + term
    return jnp.sum(added)


def observe_first_kernel(source, *refs):
    halo, weights, sigma, row_at, col_at = refs[:3], refs[3], refs[4], refs[5], refs[6]
    seen, right, image, sums, field, table = refs[7:]
    levels, rows, cols = source.shape
    load_field(field, halo, source)
    slot = smooth(field, weights, 0, PASSES)
    right[...] = field[slot, :, EDGE : EDGE + rows + 2 * HALO]
    own = [own_part(field, slot, level, rows, cols) for level in range(levels)]
    sums[...] = lanes([total_of([(value, value) for value in own])], 8)
    slot = smooth(field, weights, slot, 0)
    fields = [sigma[level] * own_part(field, slot, level, rows, cols) for level in range(levels)]
    for level in range(levels):
        image[level] = fields[level]
    gather_from(fields, row_at, col_at, seen, table, "hit")


def observe_next_kernel(source, *refs):
    halo, weights, sigma, row_at, col_at = refs[:3], refs[3], refs[4], refs[5], refs[6]
    right, scalars = refs[7:9]
    seen, residual, image, sums, field, table = refs[9:]
    levels, rows, cols = source.shape
    tall = rows + 2 * HALO
    norm, product = lane_value(scalars[0:1], 0), lane_value(scalars[0:1], 1)
    alpha = norm / (norm + product)
    load_field(field, halo, source)
    slot = smooth(field, weights, 0, PASSES)

    def one_level(level, carry):
        first = right[level]
        field[slot, level, EDGE : EDGE + tall] = first - alpha * (
            first + field[slot, level, EDGE : EDGE + tall]
        )
        return carry

    lax.fori_loop(0, levels, one_level, 0)
    own = [own_part(field, slot, level, rows, cols) for level in range(levels)]
    first = [right[level, HALO : HALO + rows, 0:cols] for level in range(levels)]
    for level in range(levels):
        residual[level] = own[level]
    sums[...] = lanes(
        [total_of([(value, value) for value in own]), total_of(list(zip(own, first)))], 8
    )
    slot = smooth(field, weights, slot, 0)
    fields = [sigma[level] * own_part(field, slot, level, rows, cols) for level in range(levels)]
    for level in range(levels):
        image[level] = fields[level]
    gather_from(fields, row_at, col_at, seen, table, "ramp")


def observe(source, halo, weights, sigma, row_at, col_at, right=None, scalars=None):
    levels, rows, cols = sigma.shape
    tall = rows + 2 * HALO
    slots = row_at.shape[0]
    first = right is None
    kept = (levels, tall, 2 * cols) if first else (levels, rows, cols)
    shapes = [(slots, 128), kept, (levels, rows, cols), (8, 128)]
    operands = [source, *halo, weights, sigma, row_at, col_at]
    operands += [] if first else [right, scalars]
    return pl.pallas_call(
        observe_first_kernel if first else observe_next_kernel,
        out_shape=[jax.ShapeDtypeStruct(shape, F32) for shape in shapes],
        in_specs=[VMEM] * len(operands),
        out_specs=[VMEM] * len(shapes),
        scratch_shapes=[
            pltpu.VMEM((2, levels, tall + 2 * EDGE, 2 * cols), F32),
            pltpu.VMEM((2 * cols, levels * rows), BF16),
        ],
        compiler_params=PARAMS,
        name="observe_first" if first else "observe_next",
    )(*operands)


def finish_kernel(source, *refs):
    halo, weights, right, residual_one, image_zero, image_one, scalars = refs[:3], *refs[3:9]
    increment, residual, field = refs[9:]
    levels, rows, cols = source.shape
    norm_zero, norm_one, cross, product_zero, product_one, product_cross = [
        lane_value(scalars[0:1], index) for index in range(6)
    ]
    alpha_zero = norm_zero / (norm_zero + product_zero)
    beta = norm_one / norm_zero
    square = norm_one + 2.0 * beta * cross + beta * beta * norm_zero
    seen = product_one + 2.0 * beta * product_cross + beta * beta * product_zero
    alpha_one = norm_one / (square + seen)
    for level in range(levels):
        direction = image_one[level] + beta * image_zero[level]
        increment[level] = alpha_zero * image_zero[level] + alpha_one * direction
    load_field(field, halo, source)
    slot = smooth(field, weights, 0, 0)
    for level in range(levels):
        here = residual_one[level]
        direction = here + beta * right[level, HALO : HALO + rows, 0:cols]
        image = direction + own_part(field, slot, level, rows, cols)
        residual[level] = here - alpha_one * image


def finish(source, halo, weights, right, residual_one, image_zero, image_one, scalars):
    levels, rows, cols = source.shape
    tall = rows + 2 * HALO
    return pl.pallas_call(
        finish_kernel,
        out_shape=[jax.ShapeDtypeStruct((levels, rows, cols), F32)] * 2,
        in_specs=[VMEM] * 10,
        out_specs=[VMEM] * 2,
        scratch_shapes=[pltpu.VMEM((2, levels, tall + 2 * EDGE, 2 * cols), F32)],
        compiler_params=PARAMS,
        name="finish",
    )(source, *halo, weights, right, residual_one, image_zero, image_one, scalars)


def apply_blocks(values, weights, at):
    high, low = parts(values)
    first = jnp.concatenate([high, low, jnp.zeros((128 - 2 * GROUP, 128), BF16)], axis=0)
    second = jnp.concatenate([high, jnp.zeros((128 - GROUP, 128), BF16)], axis=0)
    right = jnp.concatenate([first, second], axis=1)
    lane = lane_of(128)
    column = jnp.where(lane < 2 * GROUP, lane % GROUP, GROUP)
    kept = jnp.zeros((128, 128), F32)
    for start in range(0, GROUP, 4):
        left = jnp.concatenate(parts(weights[at + start : at + start + 4].reshape(4 * 128, 128)), axis=1)
        product = lax.dot_general(left, right, (((1,), (1,)), ((), ())), preferred_element_type=F32)
        for k in range(4):
            kept = jnp.where(column == start + k, product[k * 128 : (k + 1) * 128], kept)
    kept = kept.T
    return kept[:GROUP] + kept[GROUP : 2 * GROUP]


def weigh_first_kernel(capacity, owner, cells, innovations, weights, parcel, place, *scratch):
    count, held_cells, held_values, held_weights, small, large = scratch
    stride = 2 * capacity
    held = held_cells.shape[0]
    steps = held // GROUP
    copies = [
        pltpu.make_async_copy(innovations, held_values, small.at[0]),
        pltpu.make_async_copy(cells, held_cells, small.at[1]),
    ]
    for step in range(steps):
        block = pl.ds(step * GROUP, GROUP)
        copies.append(
            pltpu.make_async_copy(weights.at[block], held_weights.at[block], large.at[step])
        )
    for copy in copies:
        copy.start()
    parcel[...] = jnp.zeros_like(parcel)
    for index in range(count.shape[0]):
        count[index] = 0
    copies[0].wait()
    copies[1].wait()

    for step in range(steps):
        copies[2 + step].wait()
        block = slice(step * GROUP, (step + 1) * GROUP)
        result = apply_blocks(held_values[block], held_weights, step * GROUP)
        cell_rows = held_cells[block].astype(F32)
        for k in range(GROUP):
            index = step * GROUP + k
            target = owner[index]
            rank = count[target]
            count[target] = rank + 1
            place[index] = target * capacity + rank
            at = target * stride + rank
            parcel[pl.ds(at, 1), :] = cell_rows[k : k + 1]
            parcel[pl.ds(at + capacity, 1), :] = result[k : k + 1]


def weigh_first(owner, cells, innovations, weights, devices, capacity):
    held, width = cells.shape
    return pl.pallas_call(
        functools.partial(weigh_first_kernel, capacity),
        out_shape=[
            jax.ShapeDtypeStruct((devices * 2 * capacity, width), F32),
            jax.ShapeDtypeStruct((held,), jnp.int32),
        ],
        in_specs=[SMEM, HBM, HBM, HBM],
        out_specs=[VMEM, SMEM],
        scratch_shapes=[
            pltpu.SMEM((devices,), jnp.int32),
            pltpu.VMEM((held, width), jnp.int32),
            pltpu.VMEM((held, width), F32),
            pltpu.VMEM((held, width, width), F32),
            pltpu.SemaphoreType.DMA((2,)),
            pltpu.SemaphoreType.DMA((held // GROUP,)),
        ],
        compiler_params=PARAMS,
        name="weigh_first",
    )(owner, cells, innovations, weights)


def weigh_next_kernel(capacity, stride, devices, last, place, returned, sums, weights, *refs):
    if last:
        sums_before, weighted_before, parcel = refs
    else:
        parcel, weighted = refs
    parcel[...] = jnp.zeros_like(parcel)
    total = jnp.zeros((GROUP, 128), F32)
    total_cross = jnp.zeros((GROUP, 128), F32)
    for first in range(0, weights.shape[0], GROUP):
        places = [place[first + k] for k in range(GROUP)]
        here = jnp.concatenate([returned[pl.ds(at, 1), :] for at in places], axis=0)
        result = apply_blocks(here, weights, first)
        total += here * result
        if last:
            total_cross += here * weighted_before[first : first + GROUP]
        else:
            weighted[first : first + GROUP] = result
        for k in range(GROUP):
            target = places[k] // capacity
            at = target * stride + (places[k] - target * capacity)
            parcel[pl.ds(at, 1), :] = result[k : k + 1]
    if last:
        scalars = [
            lane_value(sums_before[0:1], 0) / devices,
            lane_value(sums[0:1], 0),
            lane_value(sums[0:1], 1),
            lane_value(sums_before[0:1], 1) / devices,
            jnp.sum(total),
            jnp.sum(total_cross),
        ]
    else:
        scalars = [lane_value(sums[0:1], 0), jnp.sum(total)]
    row = lanes(scalars, 1)
    for target in range(devices):
        at = target * stride + capacity
        parcel[at : at + 1] = row


def weigh_next(place, returned, sums, weights, devices, capacity, stride, before=None):
    held, width = weights.shape[:2]
    last = before is not None
    operands = [place, returned, sums, weights] + (list(before) if last else [])
    out_shape = [jax.ShapeDtypeStruct((devices * stride, width), F32)]
    if not last:
        out_shape += [jax.ShapeDtypeStruct((held, width), F32)]
    return pl.pallas_call(
        functools.partial(weigh_next_kernel, capacity, stride, devices, last),
        out_shape=out_shape,
        in_specs=[SMEM] + [VMEM] * (len(operands) - 1),
        out_specs=[VMEM] * len(out_shape),
        compiler_params=PARAMS,
        name="weigh_last" if last else "weigh_next",
    )(*operands)


def swap(block):
    return lax.all_to_all(block, ("lat", "lon"), split_axis=0, concat_axis=0, tiled=True)


def body(sigma, east_coef, north_coef, mask, innovations, cells, owner, obs_weights):
    devices = lax.axis_size("lat") * lax.axis_size("lon")
    held, width = cells.shape
    capacity = max(2, (2 * held + devices - 1) // devices)
    stride = (capacity + 8) // 8 * 8
    slots = devices * capacity

    faces = [mask, east_coef, north_coef]
    sides, innovations = lax.optimization_barrier((face_sides(*faces), innovations))
    mixed, down, up = exchange_columns(faces, sides)
    parcel, place = weigh_first(
        owner.reshape(held), cells, innovations, obs_weights, devices, capacity
    )
    parcel, down, up = lax.optimization_barrier((parcel, down, up))
    face_halo = exchange_rows(down, up) + (mixed,)
    arrived = swap(parcel.reshape(devices, 2 * capacity, width))
    weights = face_weights(mask, east_coef, north_coef, face_halo)

    row_at, col_at, field, sides = scatter_first(arrived, sigma, capacity)
    seen, right, image_zero, sums = observe(
        field, exchange([field], sides), weights, sigma, row_at, col_at
    )
    returned = swap(seen.reshape(devices, capacity, width)).reshape(slots, width)
    parcel, weighted = weigh_next(place, returned, sums, obs_weights, devices, capacity, stride)
    arrived = swap(parcel.reshape(devices, stride, width))

    field_zero, sides, scalars_zero = scatter_next(arrived, row_at, col_at, sigma, capacity)
    seen, residual_one, image_one, sums = observe(
        field_zero, exchange([field_zero], sides), weights, sigma, row_at, col_at, right, scalars_zero
    )
    returned = swap(seen.reshape(devices, capacity, width)).reshape(slots, width)
    (parcel,) = weigh_next(
        place, returned, sums, obs_weights, devices, capacity, stride, (scalars_zero, weighted)
    )
    arrived = swap(parcel.reshape(devices, stride, width))

    field, sides, scalars = scatter_next(arrived, row_at, col_at, sigma, capacity, field_zero)
    increment, residual = finish(
        field, exchange([field], sides), weights, right, residual_one, image_zero, image_one, scalars
    )
    return (increment, residual)


def solution(mesh):
    return jax.shard_map(
        body,
        mesh=mesh,
        in_specs=(
            P(None, "lat", "lon"),
            P(None, "lat", "lon"),
            P(None, "lat", "lon"),
            P(None, "lat", "lon"),
            P(("lat", "lon"), None),
            P(("lat", "lon"), None),
            P(("lat", "lon"), None),
            P(("lat", "lon"), None, None),
        ),
        out_specs=(P(None, "lat", "lon"), P(None, "lat", "lon")),
        check_vma=False,
    )
```

```python
import functools

import jax
import jax.numpy as jnp
from jax import lax
from jax.experimental import pallas as pl
from jax.experimental.pallas import tpu as pltpu
from jax.sharding import PartitionSpec as P

PASSES = 5
HALO = 16
EDGE = 8
GROUP = 16
F32 = jnp.float32
BF16 = jnp.bfloat16
VMEM = pl.BlockSpec(memory_space=pltpu.VMEM)
HBM = pl.BlockSpec(memory_space=pltpu.HBM)
SMEM = pl.BlockSpec(memory_space=pltpu.SMEM)
PARAMS = pltpu.CompilerParams(vmem_limit_bytes=32 * 1024 * 1024)

ROOMLESS = pltpu.CompilerParams(vmem_limit_bytes=60 * 1024 * 1024)


def parts(values):
    high = values.astype(BF16)
    low = (values - high.astype(F32)).astype(BF16)
    return high, low


def lane_of(rows):
    return lax.broadcasted_iota(jnp.int32, (rows, 128), 1)


def pack_sides(fields):
    lane = lane_of(fields[0].shape[0])
    packed = jnp.zeros_like(fields[0])
    for level, field in enumerate(fields):
        start = 2 * HALO * level
        left = pltpu.roll(field, start, 1) if start else field
        right = pltpu.roll(field, (start + 2 * HALO) % 128, 1)
        packed = jnp.where((lane >= start) & (lane < start + HALO), left, packed)
        packed = jnp.where((lane >= start + HALO) & (lane < start + 2 * HALO), right, packed)
    return packed


def place_halo(put, levels, rows, own, halo):
    before, after, mixed = halo
    for level in range(levels):
        put(level, 0, HALO, 0, before(level))
        put(level, HALO, HALO + rows, 0, own(level))
        put(level, HALO + rows, 2 * HALO + rows, 0, after(level))
    spans = (
        (0, HALO, before(levels)),
        (HALO, HALO + rows, mixed()),
        (HALO + rows, 2 * HALO + rows, after(levels)),
    )
    for start, stop, sides in spans:
        lane = lane_of(stop - start)
        for level in range(levels):
            shift = 2 * HALO * level
            first = pltpu.roll(sides, (128 - shift) % 128, 1) if shift else sides
            back = (128 - 2 * HALO - shift) % 128
            last = pltpu.roll(sides, back, 1) if back else sides
            side = jnp.where(lane < HALO, first, jnp.where(lane >= 128 - HALO, last, 0.0))
            put(level, start, stop, 1, side)


def turn_kernel(count, *refs):
    even, arrays, refs = refs[0], refs[1 : 1 + count], refs[1 + count :]
    from_east, from_west, mixed, down, up = refs
    levels, rows, _ = arrays[0].shape
    lane = lane_of(rows)
    eastern = lane % (2 * HALO) < HALO
    if even is not None:
        eastern = eastern == (even[0] == 1)
    for index, array in enumerate(arrays):
        at = (index,) if count > 1 else ()
        sides = jnp.where(eastern, from_east[at + (...,)], from_west[at + (...,)])
        mixed[at + (...,)] = sides
        for level in range(levels):
            down[at + (level,)] = array[level, rows - HALO :].astype(F32)
            up[at + (level,)] = array[level, :HALO].astype(F32)
        down[at + (levels,)] = sides[rows - HALO :]
        up[at + (levels,)] = sides[:HALO]


def pairs_of(size, ring):
    first = [(i, i + 1) for i in range(0, size - 1, 2)]
    second = [(i, (i + 1) % size) for i in range(1, size if ring else size - 1, 2)]
    both_ways = lambda pairs: pairs + [(to, at) for at, to in pairs]
    return both_ways(first), both_ways(second)


def exchange(arrays, sides, form="step"):
    mixed, down, up = exchange_columns(arrays, sides, form)
    return exchange_rows(down, up, form) + (mixed,)


def exchange_columns(arrays, sides, form="step"):
    count = len(arrays)
    levels, rows, cols = arrays[0].shape
    wide = lax.axis_size("lon")
    even = None
    if form == "pair":
        even = (lax.axis_index("lon") % 2 == 0).astype(jnp.int32).reshape(1)
        first, second = pairs_of(wide, True)
        from_east = lax.ppermute(sides, "lon", first)
        from_west = lax.ppermute(sides, "lon", second)
    else:
        east = [(i, (i + 1) % wide) for i in range(wide)]
        from_west = lax.ppermute(sides, "lon", east)
        from_east = lax.ppermute(sides, "lon", [(to, at) for at, to in east])
    lead = (count,) if count > 1 else ()
    shapes = [lead + (rows, cols)] + [lead + (levels + 1, HALO, cols)] * 2
    kernel = functools.partial(turn_kernel, count)
    operands = [*arrays, from_east, from_west]
    if even is None:
        kernel = functools.partial(turn_kernel, count, None)
    else:
        operands = [even] + operands
    return pl.pallas_call(
        kernel,
        out_shape=[jax.ShapeDtypeStruct(shape, F32) for shape in shapes],
        in_specs=([] if even is None else [SMEM]) + [VMEM] * (count + 2),
        out_specs=[VMEM] * 3,
        compiler_params=PARAMS,
        cost_estimate=pl.CostEstimate(flops=0, bytes_accessed=1800000, transcendentals=0),
        name="turn",
    )(*operands)


def exchange_rows(down, up, form="step"):
    tall, me = lax.axis_size("lat"), lax.axis_index("lat")
    if form == "pair":
        first, second = pairs_of(tall, False)
        even = me % 2 == 0
        one = lax.ppermute(jnp.where(even, down, up), "lat", first)
        two = lax.ppermute(jnp.where(even, up, down), "lat", second)
        return jnp.where(even, two, one), jnp.where(even, one, two)
    if form == "swap":
        at = jnp.arange(tall).reshape(tall, 1, 1, 1)
        parcel = jnp.where(at == me + 1, down, jnp.where(at == me - 1, up, 0.0))
        got = lax.all_to_all(parcel, "lat", split_axis=0, concat_axis=0, tiled=True)
        return (
            jnp.sum(jnp.where(at == me - 1, got, 0.0), axis=0),
            jnp.sum(jnp.where(at == me + 1, got, 0.0), axis=0),
        )
    north = [(i, i + 1) for i in range(tall - 1)]
    before = lax.ppermute(down, "lat", north)
    after = lax.ppermute(up, "lat", [(to, at) for at, to in north])
    return before, after


def next_column(halves):
    lane = lane_of(halves[0].shape[0])
    return [
        pltpu.roll(jnp.where(lane == 0, halves[1 - half], halves[half]), 127, 1) for half in range(2)
    ]


def previous_column(halves):
    lane = lane_of(halves[0].shape[0])
    return [
        pltpu.roll(jnp.where(lane == 127, halves[1 - half], halves[half]), 1, 1)
        for half in range(2)
    ]


def face_side_kernel(mask, east, north, sides, held_mask, held, arrived):
    copies = [
        pltpu.make_async_copy(mask, held_mask, arrived.at[0]),
        pltpu.make_async_copy(east, held.at[0], arrived.at[1]),
        pltpu.make_async_copy(north, held.at[1], arrived.at[2]),
    ]
    for copy in copies:
        copy.start()
    for index, copy in enumerate(copies):
        copy.wait()
        array = held.at[index - 1] if index else held_mask
        sides[index] = pack_sides([array[level].astype(F32) for level in range(mask.shape[0])])


def face_sides(mask, east, north):
    return pl.pallas_call(
        face_side_kernel,
        out_shape=jax.ShapeDtypeStruct((3,) + mask.shape[1:], F32),
        in_specs=[HBM] * 3,
        out_specs=VMEM,
        scratch_shapes=[
            pltpu.VMEM(mask.shape, jnp.int32),
            pltpu.VMEM((2,) + mask.shape, F32),
            pltpu.SemaphoreType.DMA((3,)),
        ],
        compiler_params=ROOMLESS,
        cost_estimate=pl.CostEstimate(flops=0, bytes_accessed=3600000, transcendentals=0),
        name="face_sides",
    )(mask, east, north)


def face_kernel(mask, east, north, *refs):
    halo, weights, padded, faces = refs[:3], refs[3], refs[4], refs[5]
    levels, rows, cols = mask.shape
    tall = rows + 2 * HALO
    zeros = jnp.zeros((EDGE, cols), F32)
    for index, array in enumerate((mask, east, north)):
        for level in range(levels):
            for half in range(2):
                padded[index, level, half, 0:EDGE] = zeros
                padded[index, level, half, EDGE + tall :] = zeros

        def put(level, start, stop, half, value, index=index):
            padded[index, level, half, EDGE + start : EDGE + stop] = value

        def pick(ref, index=index):
            if len(ref.shape) == 4:
                return lambda level: ref[index, level]
            return lambda: ref[index]

        place_halo(
            put,
            levels,
            rows,
            lambda level, array=array: array[level].astype(F32),
            [pick(ref) for ref in halo],
        )
    for half in range(2):
        faces[half, 0:EDGE] = zeros
        faces[half, EDGE + tall :] = zeros
    own_rows = slice(EDGE, EDGE + tall)

    def one_level(level, carry):
        land = [padded[0, level, half, own_rows] for half in range(2)]
        east_face = [
            padded[1, level, half, own_rows] * land[half] * next_column(land)[half]
            for half in range(2)
        ]
        west_face = previous_column(east_face)
        for half in range(2):
            land_north = padded[0, level, half, EDGE + 1 : EDGE + 1 + tall]
            north_face = padded[2, level, half, own_rows] * land[half] * land_north
            faces[half, own_rows] = north_face
            south_face = faces[half, EDGE - 1 : EDGE - 1 + tall]
            weights[0, level, half] = 1.0 - (
                ((east_face[half] + west_face[half]) + north_face) + south_face
            )
            weights[1, level, half] = east_face[half]
            weights[2, level, half] = west_face[half]
            weights[3, level, half] = north_face
            weights[4, level, half] = south_face
        return carry

    lax.fori_loop(0, levels, one_level, 0)


def face_weights(mask, east, north, halo):
    levels, rows, cols = mask.shape
    tall = rows + 2 * HALO
    return pl.pallas_call(
        face_kernel,
        out_shape=jax.ShapeDtypeStruct((5, levels, 2, tall, cols), F32),
        in_specs=[VMEM] * 6,
        out_specs=VMEM,
        scratch_shapes=[
            pltpu.VMEM((3, levels, 2, tall + 2 * EDGE, cols), F32),
            pltpu.VMEM((2, tall + 2 * EDGE, cols), F32),
        ],
        compiler_params=PARAMS,
        cost_estimate=pl.CostEstimate(flops=0, bytes_accessed=4320000, transcendentals=0),
        name="face_weights",
    )(mask, east, north, *halo)


def load_field(field, halo, source):
    levels, rows, cols = source.shape
    tall = rows + 2 * HALO
    zeros = jnp.zeros((EDGE, cols), F32)
    for slot in range(2):
        for level in range(levels):
            for half in range(2):
                field[slot, level, half, 0:EDGE] = zeros
                field[slot, level, half, EDGE + tall :] = zeros

    def put(level, start, stop, half, value):
        field[0, level, half, EDGE + start : EDGE + stop] = value

    def pick(ref):
        if len(ref.shape) == 3:
            return lambda level: ref[level]
        return lambda: ref[...]

    place_halo(put, levels, rows, lambda level: source[level], [pick(ref) for ref in halo])


def sweep(field, weights, source, target, rows_from, rows_to):
    def one_level(level, carry):
        for start in range(rows_from, rows_to, 16):
            stop = min(start + 16, rows_to)
            here = [field[source, level, half, EDGE + start : EDGE + stop] for half in range(2)]
            east, west = next_column(here), previous_column(here)
            for half in range(2):
                above = field[source, level, half, EDGE + start + 1 : EDGE + stop + 1]
                below = field[source, level, half, EDGE + start - 1 : EDGE + stop - 1]
                total = weights[0, level, half, start:stop] * here[half]
                total += weights[1, level, half, start:stop] * east[half]
                total += weights[2, level, half, start:stop] * west[half]
                total += weights[3, level, half, start:stop] * above
                total += weights[4, level, half, start:stop] * below
                field[target, level, half, EDGE + start : EDGE + stop] = total
        return carry

    lax.fori_loop(0, field.shape[1], one_level, 0)


def smooth(field, weights, slot, depth):
    tall = weights.shape[3]
    for step in range(PASSES):
        reach = depth + PASSES - 1 - step
        skip = (HALO - reach) // 8 * 8
        sweep(field, weights, slot, 1 - slot, skip, tall - skip)
        slot = 1 - slot
    return slot


def index_iota(cells):
    return lax.broadcasted_iota(jnp.int32, (cells, 128), 0).astype(F32).astype(BF16)


def spread_row(row, count):
    return jnp.broadcast_to(jnp.broadcast_to(row, (16, 128)).astype(BF16)[0:1], (count, 128))


def one_hot(iota, row, form):
    count = iota.shape[0]
    if form == "ramp":
        return jnp.maximum(1.0 - jnp.abs(iota - spread_row(row, count)), 0.0).astype(BF16)
    return jnp.where(
        iota == spread_row(row, count), jnp.ones((count, 128), BF16), jnp.zeros((count, 128), BF16)
    )


def scatter_into(total, load_rows, slots, half_rows, half_cols, group, form):
    row_iota = index_iota(half_rows)
    col_iota = index_iota(half_cols)
    total[...] = jnp.zeros_like(total)

    def step(index, carry):
        high_rows, low_rows, columns = [], [], []
        for row_index, col_index, value in load_rows(index):
            high, low = parts(jnp.broadcast_to(value, (16, 128)))
            high = jnp.broadcast_to(high[0:1], (half_rows, 128))
            low = jnp.broadcast_to(low[0:1], (half_rows, 128))
            if form == "ramp":
                hot = one_hot(row_iota, row_index, form)
                high_rows.append(hot * high)
                low_rows.append(hot * low)
            else:
                hit = row_iota == spread_row(row_index, half_rows)
                zero = jnp.zeros((half_rows, 128), BF16)
                high_rows.append(jnp.where(hit, high, zero))
                low_rows.append(jnp.where(hit, low, zero))
            columns.append(one_hot(col_iota, col_index, form))
        left = jnp.concatenate(high_rows + low_rows, axis=1)
        right = jnp.concatenate(columns + columns, axis=1)
        total[...] += lax.dot_general(
            left, right, (((1,), (1,)), ((), ())), preferred_element_type=F32
        )
        return carry

    lax.fori_loop(0, slots // group, step, 0)


def load_group(index, group, capacity, row_at, col_at, arrived, first_slot):
    base = pl.multiple_of(index * group, group)
    if group < 8:
        base = pl.multiple_of(index * group // 8 * 8, 8)
    row_block = row_at[pl.ds(base, max(group, 8))]
    col_block = col_at[pl.ds(base, max(group, 8))]
    for j in range(group):
        source = index * (group // capacity) + j // capacity
        slot = first_slot + j % capacity
        yield row_block[j : j + 1], col_block[j : j + 1], arrived[source, pl.ds(slot, 1)]


def split_cells(cells, rows, cols):
    level = cells // (rows * cols)
    row = (cells // cols) % rows
    col = cells % cols
    return (level // 2) * rows + row, (level % 2) * cols + col


def put_field(total, sigma, field, extra=None):
    levels, rows, cols = sigma.shape
    fields = []
    for level in range(levels):
        r, c = level // 2 * rows, level % 2 * cols
        value = sigma[level] * total[r : r + rows, c : c + cols]
        if extra is not None:
            value = value + extra(level)
        field[level] = value
        fields.append(value)
    return fields


def scatter_first_kernel(capacity, arrived, sigma, row_at, col_at, field, *refs):
    sides, total = refs
    levels, rows, cols = sigma.shape
    sources = arrived.shape[0]
    cells = jnp.concatenate([arrived[source, 0:capacity] for source in range(sources)], axis=0)
    row_index, col_index = split_cells(cells.astype(jnp.int32), rows, cols)
    row_at[...] = row_index.astype(F32)
    col_at[...] = col_index.astype(F32)

    def load(index):
        return load_group(index, 32, capacity, row_at, col_at, arrived, capacity)

    scatter_into(total, load, row_at.shape[0], levels // 2 * rows, 2 * cols, 32, "hit")
    sides[...] = pack_sides(put_field(total, sigma, field))


def scatter_first(arrived, sigma, capacity):
    levels, rows, cols = sigma.shape
    slots = arrived.shape[0] * capacity
    shapes = [(slots, 128), (slots, 128), (levels, rows, cols), (rows, cols)]
    out = pl.pallas_call(
        functools.partial(scatter_first_kernel, capacity),
        out_shape=[jax.ShapeDtypeStruct(shape, F32) for shape in shapes],
        in_specs=[VMEM] * 2,
        out_specs=[VMEM] * len(shapes),
        scratch_shapes=[pltpu.VMEM((levels // 2 * rows, 2 * cols), F32)],
        compiler_params=PARAMS,
        cost_estimate=pl.CostEstimate(flops=0, bytes_accessed=39600000, transcendentals=0),
        name="scatter_first",
    )(arrived, sigma)
    return out


def lane_value(block, lane):
    return jnp.sum(jnp.where(lane_of(block.shape[0]) == lane, block, 0.0))


def lanes(values, rows):
    lane = lane_of(rows)
    out = jnp.zeros((rows, 128), F32)
    for index, value in enumerate(values):
        out = jnp.where(lane == index, value, out)
    return out


def scatter_next_kernel(capacity, last, arrived, row_at, col_at, sigma, *refs):
    if last:
        previous, field, sides, sums, total = refs
    else:
        previous, (field, sides, sums, total) = None, refs
    levels, rows, cols = sigma.shape
    sources = arrived.shape[0]
    gathered = jnp.concatenate(
        [arrived[source, capacity : capacity + 1] for source in range(sources)], axis=0
    )
    added = jnp.sum(gathered, axis=0, keepdims=True)
    sums[...] = jnp.broadcast_to(added, (8, 128))

    group = 32 if last else 64

    def load(index):
        return load_group(index, group, capacity, row_at, col_at, arrived, 0)

    scatter_into(
        total, load, row_at.shape[0], levels // 2 * rows, 2 * cols, group, "hit"
    )
    extra = None
    if last:
        beta = lane_value(added, 1) / lane_value(added, 0)

        def extra(level):
            return beta * previous[level]

    sides[...] = pack_sides(put_field(total, sigma, field, extra))


def scatter_next(arrived, row_at, col_at, sigma, capacity, previous=None):
    levels, rows, cols = sigma.shape
    last = previous is not None
    shapes = [(levels, rows, cols), (rows, cols), (8, 128)]
    operands = [arrived, row_at, col_at, sigma] + ([previous] if last else [])
    out = pl.pallas_call(
        functools.partial(scatter_next_kernel, capacity, last),
        out_shape=[jax.ShapeDtypeStruct(shape, F32) for shape in shapes],
        in_specs=[VMEM] * len(operands),
        out_specs=[VMEM] * len(shapes),
        scratch_shapes=[pltpu.VMEM((levels // 2 * rows, 2 * cols), F32)],
        compiler_params=PARAMS,
        cost_estimate=pl.CostEstimate(flops=0, bytes_accessed=39600000, transcendentals=0),
        name="scatter_last" if last else "scatter_next",
    )(*operands)
    return out


def gather_from(fields, row_at, col_at, seen, table, group):
    rows, cols = fields[0].shape
    half_rows, half_cols = len(fields) // 2 * rows, 2 * cols
    for level, field in enumerate(fields):
        high, low = parts(field.T)
        c, r = level % 2 * cols, level // 2 * rows
        table[c : c + cols, r : r + rows] = high
        table[c : c + cols, half_rows + r : half_rows + r + rows] = low
    row_iota = index_iota(half_rows)
    sublane = lax.broadcasted_iota(jnp.int32, (8, 256), 0)

    def step(index, carry):
        base = pl.multiple_of(index * group, group)
        row_block = row_at[pl.ds(base, group)]
        col_block = col_at[pl.ds(base, group)].astype(jnp.int32)
        found = []
        for j in range(0, group, 2):
            hot = jnp.concatenate(
                [one_hot(row_iota, row_block[i : i + 1], "hit") for i in (j, j + 1)], axis=1
            )
            lines = jnp.dot(
                table[...], jnp.concatenate([hot, hot], axis=0), preferred_element_type=F32
            )
            wanted = jnp.concatenate([col_block[j : j + 1], col_block[j + 1 : j + 2]], axis=1)
            wanted = jnp.broadcast_to(wanted, (8, 256))
            tiles = [lines[i : i + 8] for i in range(0, half_cols, 8)]
            bit = 8
            while len(tiles) > 1:
                upper = (wanted & bit) != 0
                tiles = [
                    jnp.where(upper, tiles[i + 1], tiles[i]) for i in range(0, len(tiles), 2)
                ]
                bit = bit * 2
            value = jnp.sum(
                jnp.where((wanted & 7) == sublane, tiles[0], 0.0), axis=0, keepdims=True
            )
            found += [value[:, :128], value[:, 128:]]
        seen[pl.ds(base, group)] = jnp.concatenate(found, axis=0)
        return carry

    lax.fori_loop(0, row_at.shape[0] // group, step, 0)


def own_part(field, slot, level, rows, cols):
    return field[slot, level, 0, EDGE + HALO : EDGE + HALO + rows]


def total_of(pairs):
    added = None
    for left, right in pairs:
        term = left * right
        added = term if added is None else added + term
    return jnp.sum(added)


def observe_first_kernel(source, *refs):
    halo, weights, sigma, row_at, col_at = refs[:3], refs[3], refs[4], refs[5], refs[6]
    seen, right, image, sums, field, table = refs[7:]
    levels, rows, cols = source.shape
    load_field(field, halo, source)
    slot = smooth(field, weights, 0, PASSES)
    right[...] = field[slot, :, :, EDGE : EDGE + rows + 2 * HALO]
    own = [own_part(field, slot, level, rows, cols) for level in range(levels)]
    sums[...] = lanes([total_of([(value, value) for value in own])], 8)
    slot = smooth(field, weights, slot, 0)
    fields = [sigma[level] * own_part(field, slot, level, rows, cols) for level in range(levels)]
    for level in range(levels):
        image[level] = fields[level]
    gather_from(fields, row_at, col_at, seen, table, 32)


def observe_next_kernel(source, *refs):
    halo, weights, sigma, row_at, col_at = refs[:3], refs[3], refs[4], refs[5], refs[6]
    right, scalars = refs[7:9]
    seen, residual, image, sums, field, table = refs[9:]
    levels, rows, cols = source.shape
    tall = rows + 2 * HALO
    norm, product = lane_value(scalars[0:1], 0), lane_value(scalars[0:1], 1)
    alpha = norm / (norm + product)
    load_field(field, halo, source)
    slot = smooth(field, weights, 0, PASSES)

    def one_level(level, carry):
        first = right[level]
        field[slot, level, :, EDGE : EDGE + tall] = first - alpha * (
            first + field[slot, level, :, EDGE : EDGE + tall]
        )
        return carry

    lax.fori_loop(0, levels, one_level, 0)
    own = [own_part(field, slot, level, rows, cols) for level in range(levels)]
    first = [right[level, 0, HALO : HALO + rows] for level in range(levels)]
    for level in range(levels):
        residual[level] = own[level]
    sums[...] = lanes(
        [total_of([(value, value) for value in own]), total_of(list(zip(own, first)))], 8
    )
    slot = smooth(field, weights, slot, 0)
    fields = [sigma[level] * own_part(field, slot, level, rows, cols) for level in range(levels)]
    for level in range(levels):
        image[level] = fields[level]
    gather_from(fields, row_at, col_at, seen, table, 64)


def observe(source, halo, weights, sigma, row_at, col_at, right=None, scalars=None):
    levels, rows, cols = sigma.shape
    tall = rows + 2 * HALO
    slots = row_at.shape[0]
    first = right is None
    kept = (levels, 2, tall, cols) if first else (levels, rows, cols)
    shapes = [(slots, 128), kept, (levels, rows, cols), (8, 128)]
    operands = [source, *halo, weights, sigma, row_at, col_at]
    operands += [] if first else [right, scalars]
    return pl.pallas_call(
        observe_first_kernel if first else observe_next_kernel,
        out_shape=[jax.ShapeDtypeStruct(shape, F32) for shape in shapes],
        in_specs=[VMEM] * len(operands),
        out_specs=[VMEM] * len(shapes),
        scratch_shapes=[
            pltpu.VMEM((2, levels, 2, tall + 2 * EDGE, cols), F32),
            pltpu.VMEM((2 * cols, levels * rows), BF16),
        ],
        compiler_params=PARAMS,
        cost_estimate=pl.CostEstimate(flops=0, bytes_accessed=57600000, transcendentals=0),
        name="observe_first" if first else "observe_next",
    )(*operands)


def finish_kernel(source, *refs):
    halo, weights, right, residual_one, image_zero, image_one, scalars = refs[:3], *refs[3:9]
    increment, residual, field = refs[9:]
    levels, rows, cols = source.shape
    norm_zero, norm_one, cross, product_zero, product_one, product_cross = [
        lane_value(scalars[0:1], index) for index in range(6)
    ]
    alpha_zero = norm_zero / (norm_zero + product_zero)
    beta = norm_one / norm_zero
    square = norm_one + 2.0 * beta * cross + beta * beta * norm_zero
    seen = product_one + 2.0 * beta * product_cross + beta * beta * product_zero
    alpha_one = norm_one / (square + seen)
    for level in range(levels):
        direction = image_one[level] + beta * image_zero[level]
        increment[level] = alpha_zero * image_zero[level] + alpha_one * direction
    load_field(field, halo, source)
    slot = smooth(field, weights, 0, 0)
    for level in range(levels):
        here = residual_one[level]
        direction = here + beta * right[level, 0, HALO : HALO + rows]
        image = direction + own_part(field, slot, level, rows, cols)
        residual[level] = here - alpha_one * image


def finish(source, halo, weights, right, residual_one, image_zero, image_one, scalars):
    levels, rows, cols = source.shape
    tall = rows + 2 * HALO
    return pl.pallas_call(
        finish_kernel,
        out_shape=[jax.ShapeDtypeStruct((levels, rows, cols), F32)] * 2,
        in_specs=[VMEM] * 10,
        out_specs=[VMEM] * 2,
        scratch_shapes=[pltpu.VMEM((2, levels, 2, tall + 2 * EDGE, cols), F32)],
        compiler_params=PARAMS,
        cost_estimate=pl.CostEstimate(flops=0, bytes_accessed=10800000, transcendentals=0),
        name="finish",
    )(source, *halo, weights, right, residual_one, image_zero, image_one, scalars)


def apply_blocks(values, weights, at):
    high, low = parts(values)
    first = jnp.concatenate([high, low, jnp.zeros((128 - 2 * GROUP, 128), BF16)], axis=0)
    second = jnp.concatenate([high, jnp.zeros((128 - GROUP, 128), BF16)], axis=0)
    right = jnp.concatenate([first, second], axis=1)
    lane = lane_of(128)
    column = jnp.where(lane < 2 * GROUP, lane % GROUP, GROUP)
    kept = jnp.zeros((128, 128), F32)
    for start in range(0, GROUP, 4):
        left = jnp.concatenate(parts(weights[at + start : at + start + 4].reshape(4 * 128, 128)), axis=1)
        product = lax.dot_general(left, right, (((1,), (1,)), ((), ())), preferred_element_type=F32)
        for k in range(4):
            kept = jnp.where(column == start + k, product[k * 128 : (k + 1) * 128], kept)
    kept = kept.T
    return kept[:GROUP] + kept[GROUP : 2 * GROUP]


def weigh_first_kernel(capacity, owner, cells, innovations, weights, parcel, place, *scratch):
    count, held_cells, held_values, held_weights, small, large = scratch
    stride = 2 * capacity
    held = held_cells.shape[0]
    steps = held // GROUP
    copies = [
        pltpu.make_async_copy(innovations, held_values, small.at[0]),
        pltpu.make_async_copy(cells, held_cells, small.at[1]),
    ]
    for step in range(steps):
        block = pl.ds(step * GROUP, GROUP)
        copies.append(
            pltpu.make_async_copy(weights.at[block], held_weights.at[block], large.at[step])
        )
    for copy in copies:
        copy.start()
    parcel[...] = jnp.zeros_like(parcel)
    for index in range(count.shape[0]):
        count[index] = 0
    copies[0].wait()
    copies[1].wait()

    for step in range(steps):
        copies[2 + step].wait()
        block = slice(step * GROUP, (step + 1) * GROUP)
        result = apply_blocks(held_values[block], held_weights, step * GROUP)
        cell_rows = held_cells[block].astype(F32)
        for k in range(GROUP):
            index = step * GROUP + k
            target = owner[index]
            rank = count[target]
            count[target] = rank + 1
            place[index] = target * capacity + rank
            at = target * stride + rank
            parcel[pl.ds(at, 1), :] = cell_rows[k : k + 1]
            parcel[pl.ds(at + capacity, 1), :] = result[k : k + 1]


def weigh_first(owner, cells, innovations, weights, devices, capacity):
    held, width = cells.shape
    return pl.pallas_call(
        functools.partial(weigh_first_kernel, capacity),
        out_shape=[
            jax.ShapeDtypeStruct((devices * 2 * capacity, width), F32),
            jax.ShapeDtypeStruct((held,), jnp.int32),
        ],
        in_specs=[SMEM, HBM, HBM, HBM],
        out_specs=[VMEM, SMEM],
        scratch_shapes=[
            pltpu.SMEM((devices,), jnp.int32),
            pltpu.VMEM((held, width), jnp.int32),
            pltpu.VMEM((held, width), F32),
            pltpu.VMEM((held, width, width), F32),
            pltpu.SemaphoreType.DMA((2,)),
            pltpu.SemaphoreType.DMA((held // GROUP,)),
        ],
        compiler_params=ROOMLESS,
        cost_estimate=pl.CostEstimate(flops=0, bytes_accessed=21600000, transcendentals=0),
        name="weigh_first",
    )(owner, cells, innovations, weights)


def weigh_next_kernel(capacity, stride, devices, last, place, returned, sums, weights, *refs):
    if last:
        sums_before, weighted_before, parcel = refs
    else:
        parcel, weighted = refs
    parcel[...] = jnp.zeros_like(parcel)
    total = jnp.zeros((GROUP, 128), F32)
    total_cross = jnp.zeros((GROUP, 128), F32)
    for first in range(0, weights.shape[0], GROUP):
        places = [place[first + k] for k in range(GROUP)]
        here = jnp.concatenate([returned[pl.ds(at, 1), :] for at in places], axis=0)
        result = apply_blocks(here, weights, first)
        total += here * result
        if last:
            total_cross += here * weighted_before[first : first + GROUP]
        else:
            weighted[first : first + GROUP] = result
        for k in range(GROUP):
            target = places[k] // capacity
            at = target * stride + (places[k] - target * capacity)
            parcel[pl.ds(at, 1), :] = result[k : k + 1]
    if last:
        scalars = [
            lane_value(sums_before[0:1], 0) / devices,
            lane_value(sums[0:1], 0),
            lane_value(sums[0:1], 1),
            lane_value(sums_before[0:1], 1) / devices,
            jnp.sum(total),
            jnp.sum(total_cross),
        ]
    else:
        scalars = [lane_value(sums[0:1], 0), jnp.sum(total)]
    row = lanes(scalars, 1)
    for target in range(devices):
        at = target * stride + capacity
        parcel[at : at + 1] = row


def weigh_next(place, returned, sums, weights, devices, capacity, stride, before=None):
    held, width = weights.shape[:2]
    last = before is not None
    operands = [place, returned, sums, weights] + (list(before) if last else [])
    out_shape = [jax.ShapeDtypeStruct((devices * stride, width), F32)]
    if not last:
        out_shape += [jax.ShapeDtypeStruct((held, width), F32)]
    return pl.pallas_call(
        functools.partial(weigh_next_kernel, capacity, stride, devices, last),
        out_shape=out_shape,
        in_specs=[SMEM] + [VMEM] * (len(operands) - 1),
        out_specs=[VMEM] * len(out_shape),
        compiler_params=PARAMS,
        cost_estimate=pl.CostEstimate(flops=0, bytes_accessed=11520000, transcendentals=0),
        name="weigh_last" if last else "weigh_next",
    )(*operands)


def swap(block):
    return lax.all_to_all(block, ("lat", "lon"), split_axis=0, concat_axis=0, tiled=True)


def body(sigma, east_coef, north_coef, mask, innovations, cells, owner, obs_weights):
    devices = lax.axis_size("lat") * lax.axis_size("lon")
    held, width = cells.shape
    capacity = max(2, (2 * held + devices - 1) // devices)
    stride = (capacity + 8) // 8 * 8
    slots = devices * capacity

    faces = [mask, east_coef, north_coef]
    sides, innovations = lax.optimization_barrier((face_sides(*faces), innovations))
    mixed, down, up = exchange_columns(faces, sides)
    parcel, place = weigh_first(
        owner.reshape(held), cells, innovations, obs_weights, devices, capacity
    )
    parcel, down, up = lax.optimization_barrier((parcel, down, up))
    face_halo = exchange_rows(down, up) + (mixed,)
    arrived = swap(parcel.reshape(devices, 2 * capacity, width))
    weights = face_weights(mask, east_coef, north_coef, face_halo)

    row_at, col_at, field, sides = scatter_first(arrived, sigma, capacity)
    seen, right, image_zero, sums = observe(
        field, exchange([field], sides), weights, sigma, row_at, col_at
    )
    returned = swap(seen.reshape(devices, capacity, width)).reshape(slots, width)
    parcel, weighted = weigh_next(place, returned, sums, obs_weights, devices, capacity, stride)
    arrived = swap(parcel.reshape(devices, stride, width))

    field_zero, sides, scalars_zero = scatter_next(arrived, row_at, col_at, sigma, capacity)
    seen, residual_one, image_one, sums = observe(
        field_zero, exchange([field_zero], sides, "pair"), weights, sigma, row_at, col_at, right, scalars_zero
    )
    returned = swap(seen.reshape(devices, capacity, width)).reshape(slots, width)
    (parcel,) = weigh_next(
        place, returned, sums, obs_weights, devices, capacity, stride, (scalars_zero, weighted)
    )
    arrived = swap(parcel.reshape(devices, stride, width))

    field, sides, scalars = scatter_next(arrived, row_at, col_at, sigma, capacity, field_zero)
    increment, residual = finish(
        field, exchange([field], sides, "swap"), weights, right, residual_one, image_zero, image_one, scalars
    )
    return (increment, residual)


def solution(mesh):
    return jax.shard_map(
        body,
        mesh=mesh,
        in_specs=(
            P(None, "lat", "lon"),
            P(None, "lat", "lon"),
            P(None, "lat", "lon"),
            P(None, "lat", "lon"),
            P(("lat", "lon"), None),
            P(("lat", "lon"), None),
            P(("lat", "lon"), None),
            P(("lat", "lon"), None, None),
        ),
        out_specs=(P(None, "lat", "lon"), P(None, "lat", "lon")),
        check_vma=False,
    )
```

```python
import functools

import jax
import jax.numpy as jnp
from jax import lax
from jax.experimental import pallas as pl
from jax.experimental.pallas import tpu as pltpu
from jax.sharding import PartitionSpec as P

PASSES = 5
HALO = 16
EDGE = 8
GROUP = 16
F32 = jnp.float32
BF16 = jnp.bfloat16
VMEM = pl.BlockSpec(memory_space=pltpu.VMEM)
HBM = pl.BlockSpec(memory_space=pltpu.HBM)
SMEM = pl.BlockSpec(memory_space=pltpu.SMEM)
PARAMS = pltpu.CompilerParams(vmem_limit_bytes=32 * 1024 * 1024)

ROOMLESS = pltpu.CompilerParams(vmem_limit_bytes=60 * 1024 * 1024)

SNUG = pltpu.CompilerParams(vmem_limit_bytes=44 * 1024 * 1024)


def parts(values):
    high = values.astype(BF16)
    low = (values - high.astype(F32)).astype(BF16)
    return high, low


def lane_of(rows):
    return lax.broadcasted_iota(jnp.int32, (rows, 128), 1)


def pack_sides(fields):
    lane = lane_of(fields[0].shape[0])
    packed = jnp.zeros_like(fields[0])
    for level, field in enumerate(fields):
        start = 2 * HALO * level
        left = pltpu.roll(field, start, 1) if start else field
        right = pltpu.roll(field, (start + 2 * HALO) % 128, 1)
        packed = jnp.where((lane >= start) & (lane < start + HALO), left, packed)
        packed = jnp.where((lane >= start + HALO) & (lane < start + 2 * HALO), right, packed)
    return packed


def place_halo(put, levels, rows, own, halo):
    before, after, mixed = halo
    for level in range(levels):
        put(level, 0, HALO, 0, before(level))
        put(level, HALO, HALO + rows, 0, own(level))
        put(level, HALO + rows, 2 * HALO + rows, 0, after(level))
    spans = (
        (0, HALO, before(levels)),
        (HALO, HALO + rows, mixed()),
        (HALO + rows, 2 * HALO + rows, after(levels)),
    )
    for start, stop, sides in spans:
        lane = lane_of(stop - start)
        for level in range(levels):
            shift = 2 * HALO * level
            first = pltpu.roll(sides, (128 - shift) % 128, 1) if shift else sides
            back = (128 - 2 * HALO - shift) % 128
            last = pltpu.roll(sides, back, 1) if back else sides
            side = jnp.where(lane < HALO, first, jnp.where(lane >= 128 - HALO, last, 0.0))
            put(level, start, stop, 1, side)


def turn_kernel(count, *refs):
    arrays, (from_east, from_west, mixed, down, up) = refs[:count], refs[count:]
    levels, rows, _ = arrays[0].shape
    eastern = lane_of(rows) % (2 * HALO) < HALO
    for index, array in enumerate(arrays):
        at = (index,) if count > 1 else ()
        sides = jnp.where(eastern, from_east[at + (...,)], from_west[at + (...,)])
        mixed[at + (...,)] = sides
        for level in range(levels):
            down[at + (level,)] = array[level, rows - HALO :].astype(F32)
            up[at + (level,)] = array[level, :HALO].astype(F32)
        down[at + (levels,)] = sides[rows - HALO :]
        up[at + (levels,)] = sides[:HALO]


def exchange(arrays, sides):
    mixed, down, up = exchange_columns(arrays, sides)
    return exchange_rows(down, up) + (mixed,)


def exchange_columns(arrays, sides):
    count = len(arrays)
    levels, rows, cols = arrays[0].shape
    wide = lax.axis_size("lon")
    east = [(i, (i + 1) % wide) for i in range(wide)]
    from_west = lax.ppermute(sides, "lon", east)
    from_east = lax.ppermute(sides, "lon", [(to, at) for at, to in east])
    lead = (count,) if count > 1 else ()
    shapes = [lead + (rows, cols)] + [lead + (levels + 1, HALO, cols)] * 2
    return pl.pallas_call(
        functools.partial(turn_kernel, count),
        out_shape=[jax.ShapeDtypeStruct(shape, F32) for shape in shapes],
        in_specs=[VMEM] * (count + 2),
        out_specs=[VMEM] * 3,
        compiler_params=PARAMS,
        name="turn",
    )(*arrays, from_east, from_west)


def exchange_rows(down, up):
    tall = lax.axis_size("lat")
    first = [(i, i + 1) for i in range(0, tall - 1, 2)]
    second = [(i, i + 1) for i in range(1, tall - 1, 2)]
    even = lax.axis_index("lat") % 2 == 0
    one = lax.ppermute(
        jnp.where(even, down, up), "lat", first + [(to, at) for at, to in first]
    )
    two = lax.ppermute(
        jnp.where(even, up, down), "lat", second + [(to, at) for at, to in second]
    )
    return jnp.where(even, two, one), jnp.where(even, one, two)


def next_column(halves):
    lane = lane_of(halves[0].shape[0])
    return [
        pltpu.roll(jnp.where(lane == 0, halves[1 - half], halves[half]), 127, 1) for half in range(2)
    ]


def previous_column(halves):
    lane = lane_of(halves[0].shape[0])
    return [
        pltpu.roll(jnp.where(lane == 127, halves[1 - half], halves[half]), 1, 1)
        for half in range(2)
    ]


def face_side_kernel(mask, east, north, sides, held_mask, held, arrived):
    copies = [
        pltpu.make_async_copy(mask, held_mask, arrived.at[0]),
        pltpu.make_async_copy(east, held.at[0], arrived.at[1]),
        pltpu.make_async_copy(north, held.at[1], arrived.at[2]),
    ]
    for copy in copies:
        copy.start()
    for index, copy in enumerate(copies):
        copy.wait()
        array = held.at[index - 1] if index else held_mask
        sides[index] = pack_sides([array[level].astype(F32) for level in range(mask.shape[0])])


def face_sides(mask, east, north):
    return pl.pallas_call(
        face_side_kernel,
        out_shape=jax.ShapeDtypeStruct((3,) + mask.shape[1:], F32),
        in_specs=[HBM] * 3,
        out_specs=VMEM,
        scratch_shapes=[
            pltpu.VMEM(mask.shape, jnp.int32),
            pltpu.VMEM((2,) + mask.shape, F32),
            pltpu.SemaphoreType.DMA((3,)),
        ],
        compiler_params=ROOMLESS,
        name="face_sides",
    )(mask, east, north)


def face_kernel(mask, east, north, *refs):
    halo, weights, padded, faces = refs[:3], refs[3], refs[4], refs[5]
    levels, rows, cols = mask.shape
    tall = rows + 2 * HALO
    zeros = jnp.zeros((EDGE, cols), F32)
    for index, array in enumerate((mask, east, north)):
        for level in range(levels):
            for half in range(2):
                padded[index, level, half, 0:EDGE] = zeros
                padded[index, level, half, EDGE + tall :] = zeros

        def put(level, start, stop, half, value, index=index):
            padded[index, level, half, EDGE + start : EDGE + stop] = value

        def pick(ref, index=index):
            if len(ref.shape) == 4:
                return lambda level: ref[index, level]
            return lambda: ref[index]

        place_halo(
            put,
            levels,
            rows,
            lambda level, array=array: array[level].astype(F32),
            [pick(ref) for ref in halo],
        )
    for half in range(2):
        faces[half, 0:EDGE] = zeros
        faces[half, EDGE + tall :] = zeros
    own_rows = slice(EDGE, EDGE + tall)

    def one_level(level, carry):
        land = [padded[0, level, half, own_rows] for half in range(2)]
        east_face = [
            padded[1, level, half, own_rows] * land[half] * next_column(land)[half]
            for half in range(2)
        ]
        west_face = previous_column(east_face)
        for half in range(2):
            land_north = padded[0, level, half, EDGE + 1 : EDGE + 1 + tall]
            north_face = padded[2, level, half, own_rows] * land[half] * land_north
            faces[half, own_rows] = north_face
            south_face = faces[half, EDGE - 1 : EDGE - 1 + tall]
            weights[0, level, half] = 1.0 - (
                ((east_face[half] + west_face[half]) + north_face) + south_face
            )
            weights[1, level, half] = east_face[half]
            weights[2, level, half] = west_face[half]
            weights[3, level, half] = north_face
            weights[4, level, half] = south_face
        return carry

    lax.fori_loop(0, levels, one_level, 0)


def face_weights(mask, east, north, halo):
    levels, rows, cols = mask.shape
    tall = rows + 2 * HALO
    return pl.pallas_call(
        face_kernel,
        out_shape=jax.ShapeDtypeStruct((5, levels, 2, tall, cols), F32),
        in_specs=[VMEM] * 6,
        out_specs=VMEM,
        scratch_shapes=[
            pltpu.VMEM((3, levels, 2, tall + 2 * EDGE, cols), F32),
            pltpu.VMEM((2, tall + 2 * EDGE, cols), F32),
        ],
        compiler_params=PARAMS,
        name="face_weights",
    )(mask, east, north, *halo)


def load_field(field, spare, halo, source):
    levels, rows, cols = source.shape
    tall = rows + 2 * HALO
    zeros = jnp.zeros((EDGE, cols), F32)
    for ref in (field, spare):
        for level in range(levels):
            for half in range(2):
                ref[level, half, 0:EDGE] = zeros
                ref[level, half, EDGE + tall :] = zeros

    def put(level, start, stop, half, value):
        field[level, half, EDGE + start : EDGE + stop] = value

    def pick(ref):
        if len(ref.shape) == 3:
            return lambda level: ref[level]
        return lambda: ref[...]

    place_halo(put, levels, rows, lambda level: source[level], [pick(ref) for ref in halo])


def sweep(source, target, weights, rows_from, rows_to):
    def one_level(level, carry):
        for start in range(rows_from, rows_to, 16):
            stop = min(start + 16, rows_to)
            here = [source[level, half, EDGE + start : EDGE + stop] for half in range(2)]
            east, west = next_column(here), previous_column(here)
            for half in range(2):
                above = source[level, half, EDGE + start + 1 : EDGE + stop + 1]
                below = source[level, half, EDGE + start - 1 : EDGE + stop - 1]
                total = weights[0, level, half, start:stop] * here[half]
                total += weights[1, level, half, start:stop] * east[half]
                total += weights[2, level, half, start:stop] * west[half]
                total += weights[3, level, half, start:stop] * above
                total += weights[4, level, half, start:stop] * below
                target[level, half, EDGE + start : EDGE + stop] = total
        return carry

    lax.fori_loop(0, source.shape[0], one_level, 0)


def smooth(field, spare, weights, depth):
    tall = weights.shape[3]
    for step in range(PASSES):
        reach = depth + PASSES - 1 - step
        skip = (HALO - reach) // 8 * 8
        sweep(field, spare, weights, skip, tall - skip)
        field, spare = spare, field
    return spare, field


def index_iota(cells):
    return lax.broadcasted_iota(jnp.int32, (cells, 128), 0).astype(F32).astype(BF16)


def spread_row(row, count):
    return jnp.broadcast_to(jnp.broadcast_to(row, (16, 128)).astype(BF16)[0:1], (count, 128))


def one_hot(iota, row, form):
    count = iota.shape[0]
    if form == "ramp":
        return jnp.maximum(1.0 - jnp.abs(iota - spread_row(row, count)), 0.0).astype(BF16)
    return jnp.where(
        iota == spread_row(row, count), jnp.ones((count, 128), BF16), jnp.zeros((count, 128), BF16)
    )


def scatter_into(total, load_rows, slots, half_rows, half_cols, group, form):
    row_iota = index_iota(half_rows)
    col_iota = index_iota(half_cols)
    total[...] = jnp.zeros_like(total)

    def step(index, carry):
        high_rows, low_rows, columns = [], [], []
        for row_index, col_index, value in load_rows(index):
            high, low = parts(jnp.broadcast_to(value, (16, 128)))
            high = jnp.broadcast_to(high[0:1], (half_rows, 128))
            low = jnp.broadcast_to(low[0:1], (half_rows, 128))
            if form == "ramp":
                hot = one_hot(row_iota, row_index, form)
                high_rows.append(hot * high)
                low_rows.append(hot * low)
            else:
                hit = row_iota == spread_row(row_index, half_rows)
                zero = jnp.zeros((half_rows, 128), BF16)
                high_rows.append(jnp.where(hit, high, zero))
                low_rows.append(jnp.where(hit, low, zero))
            columns.append(one_hot(col_iota, col_index, form))
        left = jnp.concatenate(high_rows + low_rows, axis=1)
        right = jnp.concatenate(columns + columns, axis=1)
        total[...] += lax.dot_general(
            left, right, (((1,), (1,)), ((), ())), preferred_element_type=F32
        )
        return carry

    lax.fori_loop(0, slots // group, step, 0)


def load_group(index, group, capacity, row_at, col_at, arrived, first_slot):
    base = pl.multiple_of(index * group, group)
    if group < 8:
        base = pl.multiple_of(index * group // 8 * 8, 8)
    row_block = row_at[pl.ds(base, max(group, 8))]
    col_block = col_at[pl.ds(base, max(group, 8))]
    for j in range(group):
        source = index * (group // capacity) + j // capacity
        slot = first_slot + j % capacity
        yield row_block[j : j + 1], col_block[j : j + 1], arrived[source, pl.ds(slot, 1)]


def split_cells(cells, rows, cols):
    level = cells // (rows * cols)
    row = (cells // cols) % rows
    col = cells % cols
    return (level // 2) * rows + row, (level % 2) * cols + col


def put_field(total, sigma, field, extra=None):
    levels, rows, cols = sigma.shape
    fields = []
    for level in range(levels):
        r, c = level // 2 * rows, level % 2 * cols
        value = sigma[level] * total[r : r + rows, c : c + cols]
        if extra is not None:
            value = value + extra(level)
        field[level] = value
        fields.append(value)
    return fields


def scatter_first_kernel(capacity, arrived, sigma, row_at, col_at, field, *refs):
    sides, total = refs
    levels, rows, cols = sigma.shape
    sources = arrived.shape[0]
    cells = jnp.concatenate([arrived[source, 0:capacity] for source in range(sources)], axis=0)
    row_index, col_index = split_cells(cells.astype(jnp.int32), rows, cols)
    row_at[...] = row_index.astype(F32)
    col_at[...] = col_index.astype(F32)

    def load(index):
        return load_group(index, 64, capacity, row_at, col_at, arrived, capacity)

    scatter_into(total, load, row_at.shape[0], levels // 2 * rows, 2 * cols, 64, "hit")
    sides[...] = pack_sides(put_field(total, sigma, field))


def scatter_first(arrived, sigma, capacity):
    levels, rows, cols = sigma.shape
    slots = arrived.shape[0] * capacity
    shapes = [(slots, 128), (slots, 128), (levels, rows, cols), (rows, cols)]
    out = pl.pallas_call(
        functools.partial(scatter_first_kernel, capacity),
        out_shape=[jax.ShapeDtypeStruct(shape, F32) for shape in shapes],
        in_specs=[VMEM] * 2,
        out_specs=[VMEM] * len(shapes),
        scratch_shapes=[pltpu.VMEM((levels // 2 * rows, 2 * cols), F32)],
        compiler_params=PARAMS,
        name="scatter_first",
    )(arrived, sigma)
    return out


def lane_value(block, lane):
    return jnp.sum(jnp.where(lane_of(block.shape[0]) == lane, block, 0.0))


def lanes(values, rows):
    lane = lane_of(rows)
    out = jnp.zeros((rows, 128), F32)
    for index, value in enumerate(values):
        out = jnp.where(lane == index, value, out)
    return out


def scatter_next_kernel(capacity, last, arrived, row_at, col_at, sigma, *refs):
    if last:
        previous, field, sides, sums, total = refs
    else:
        previous, (field, sides, sums, total) = None, refs
    levels, rows, cols = sigma.shape
    sources = arrived.shape[0]
    gathered = jnp.concatenate(
        [arrived[source, capacity : capacity + 1] for source in range(sources)], axis=0
    )
    added = jnp.sum(gathered, axis=0, keepdims=True)
    sums[...] = jnp.broadcast_to(added, (8, 128))

    group = 128 if last else 64

    def load(index):
        return load_group(index, group, capacity, row_at, col_at, arrived, 0)

    scatter_into(
        total, load, row_at.shape[0], levels // 2 * rows, 2 * cols, group, "hit"
    )
    extra = None
    if last:
        beta = lane_value(added, 1) / lane_value(added, 0)

        def extra(level):
            return beta * previous[level]

    sides[...] = pack_sides(put_field(total, sigma, field, extra))


def scatter_next(arrived, row_at, col_at, sigma, capacity, previous=None):
    levels, rows, cols = sigma.shape
    last = previous is not None
    shapes = [(levels, rows, cols), (rows, cols), (8, 128)]
    operands = [arrived, row_at, col_at, sigma] + ([previous] if last else [])
    out = pl.pallas_call(
        functools.partial(scatter_next_kernel, capacity, last),
        out_shape=[jax.ShapeDtypeStruct(shape, F32) for shape in shapes],
        in_specs=[VMEM] * len(operands),
        out_specs=[VMEM] * len(shapes),
        scratch_shapes=[pltpu.VMEM((levels // 2 * rows, 2 * cols), F32)],
        compiler_params=PARAMS,
        name="scatter_last" if last else "scatter_next",
    )(*operands)
    return out


def gather_from(fields, row_at, col_at, seen, table, group):
    rows, cols = fields[0].shape
    half_rows, half_cols = len(fields) // 2 * rows, 2 * cols
    for level, field in enumerate(fields):
        high, low = parts(field.T)
        c, r = level % 2 * cols, level // 2 * rows
        table[c : c + cols, r : r + rows] = high
        table[c : c + cols, half_rows + r : half_rows + r + rows] = low
    row_iota = index_iota(half_rows)
    sublane = lax.broadcasted_iota(jnp.int32, (8, 256), 0)

    def step(index, carry):
        base = pl.multiple_of(index * group, group)
        row_block = row_at[pl.ds(base, group)]
        col_block = col_at[pl.ds(base, group)].astype(jnp.int32)
        found = []
        for j in range(0, group, 2):
            hot = jnp.concatenate(
                [one_hot(row_iota, row_block[i : i + 1], "hit") for i in (j, j + 1)], axis=1
            )
            lines = jnp.dot(
                table[...], jnp.concatenate([hot, hot], axis=0), preferred_element_type=F32
            )
            wanted = jnp.concatenate([col_block[j : j + 1], col_block[j + 1 : j + 2]], axis=1)
            wanted = jnp.broadcast_to(wanted, (8, 256))
            tiles = [lines[i : i + 8] for i in range(0, half_cols, 8)]
            bit = 8
            while len(tiles) > 1:
                upper = (wanted & bit) != 0
                tiles = [
                    jnp.where(upper, tiles[i + 1], tiles[i]) for i in range(0, len(tiles), 2)
                ]
                bit = bit * 2
            value = jnp.sum(
                jnp.where((wanted & 7) == sublane, tiles[0], 0.0), axis=0, keepdims=True
            )
            found += [value[:, :128], value[:, 128:]]
        seen[pl.ds(base, group)] = jnp.concatenate(found, axis=0)
        return carry

    lax.fori_loop(0, row_at.shape[0] // group, step, 0)


def own_part(field, level, rows):
    return field[level, 0, EDGE + HALO : EDGE + HALO + rows]


def total_of(pairs):
    added = None
    for left, right in pairs:
        term = left * right
        added = term if added is None else added + term
    return jnp.sum(added)


def observe_first_kernel(source, *refs):
    halo, weights, sigma, row_at, col_at = refs[:3], refs[3], refs[4], refs[5], refs[6]
    seen, right, image, sums, field, spare, table = refs[7:]
    levels, rows, cols = source.shape
    load_field(field, spare, halo, source)
    spare, field = smooth(field, spare, weights, PASSES)
    right[...] = field[:, :, EDGE : EDGE + rows + 2 * HALO]
    own = [own_part(field, level, rows) for level in range(levels)]
    sums[...] = lanes([total_of([(value, value) for value in own])], 8)
    spare, field = smooth(field, spare, weights, 0)
    fields = [sigma[level] * own_part(field, level, rows) for level in range(levels)]
    for level in range(levels):
        image[level] = fields[level]
    gather_from(fields, row_at, col_at, seen, table, 64)


def observe_next_kernel(source, *refs):
    halo, weights, sigma, row_at, col_at = refs[:3], refs[3], refs[4], refs[5], refs[6]
    right, scalars = refs[7:9]
    seen, residual, image, sums, field, spare, table = refs[9:]
    levels, rows, cols = source.shape
    tall = rows + 2 * HALO
    norm, product = lane_value(scalars[0:1], 0), lane_value(scalars[0:1], 1)
    alpha = norm / (norm + product)
    load_field(field, spare, halo, source)
    spare, field = smooth(field, spare, weights, PASSES)

    def one_level(level, carry):
        first = right[level]
        field[level, :, EDGE : EDGE + tall] = first - alpha * (
            first + field[level, :, EDGE : EDGE + tall]
        )
        return carry

    lax.fori_loop(0, levels, one_level, 0)
    own = [own_part(field, level, rows) for level in range(levels)]
    first = [right[level, 0, HALO : HALO + rows] for level in range(levels)]
    for level in range(levels):
        residual[level] = own[level]
    sums[...] = lanes(
        [total_of([(value, value) for value in own]), total_of(list(zip(own, first)))], 8
    )
    spare, field = smooth(field, spare, weights, 0)
    fields = [sigma[level] * own_part(field, level, rows) for level in range(levels)]
    for level in range(levels):
        image[level] = fields[level]
    gather_from(fields, row_at, col_at, seen, table, 128)


def observe(source, halo, weights, sigma, row_at, col_at, right=None, scalars=None):
    levels, rows, cols = sigma.shape
    tall = rows + 2 * HALO
    slots = row_at.shape[0]
    first = right is None
    kept = (levels, 2, tall, cols) if first else (levels, rows, cols)
    shapes = [(slots, 128), kept, (levels, rows, cols), (8, 128)]
    operands = [source, *halo, weights, sigma, row_at, col_at]
    operands += [] if first else [right, scalars]
    return pl.pallas_call(
        observe_first_kernel if first else observe_next_kernel,
        out_shape=[jax.ShapeDtypeStruct(shape, F32) for shape in shapes],
        in_specs=[VMEM] * len(operands),
        out_specs=[VMEM] * len(shapes),
        scratch_shapes=[
            pltpu.VMEM((levels, 2, tall + 2 * EDGE, cols), F32),
            pltpu.VMEM((levels, 2, tall + 2 * EDGE, cols), F32),
            pltpu.VMEM((2 * cols, levels * rows), BF16),
        ],
        compiler_params=PARAMS,
        name="observe_first" if first else "observe_next",
    )(*operands)


def finish_kernel(source, *refs):
    halo, weights, right, residual_one, image_zero, image_one, scalars = refs[:3], *refs[3:9]
    increment, residual, field, spare = refs[9:]
    levels, rows, cols = source.shape
    norm_zero, norm_one, cross, product_zero, product_one, product_cross = [
        lane_value(scalars[0:1], index) for index in range(6)
    ]
    alpha_zero = norm_zero / (norm_zero + product_zero)
    beta = norm_one / norm_zero
    square = norm_one + 2.0 * beta * cross + beta * beta * norm_zero
    seen = product_one + 2.0 * beta * product_cross + beta * beta * product_zero
    alpha_one = norm_one / (square + seen)
    for level in range(levels):
        direction = image_one[level] + beta * image_zero[level]
        increment[level] = alpha_zero * image_zero[level] + alpha_one * direction
    load_field(field, spare, halo, source)
    spare, field = smooth(field, spare, weights, 0)
    for level in range(levels):
        here = residual_one[level]
        direction = here + beta * right[level, 0, HALO : HALO + rows]
        image = direction + own_part(field, level, rows)
        residual[level] = here - alpha_one * image


def finish(source, halo, weights, right, residual_one, image_zero, image_one, scalars):
    levels, rows, cols = source.shape
    tall = rows + 2 * HALO
    return pl.pallas_call(
        finish_kernel,
        out_shape=[jax.ShapeDtypeStruct((levels, rows, cols), F32)] * 2,
        in_specs=[VMEM] * 10,
        out_specs=[VMEM] * 2,
        scratch_shapes=[pltpu.VMEM((levels, 2, tall + 2 * EDGE, cols), F32),
            pltpu.VMEM((levels, 2, tall + 2 * EDGE, cols), F32)],
        compiler_params=PARAMS,
        name="finish",
    )(source, *halo, weights, right, residual_one, image_zero, image_one, scalars)


def apply_blocks(values, split_rows):
    high, low = parts(values)
    first = jnp.concatenate([high, low, jnp.zeros((128 - 2 * GROUP, 128), BF16)], axis=0)
    second = jnp.concatenate([high, jnp.zeros((128 - GROUP, 128), BF16)], axis=0)
    right = jnp.concatenate([first, second], axis=1)
    lane = lane_of(128)
    column = jnp.where(lane < 2 * GROUP, lane % GROUP, GROUP)
    kept = jnp.zeros((128, 128), F32)
    for start in range(0, GROUP, 4):
        product = lax.dot_general(split_rows(start), right, (((1,), (1,)), ((), ())), preferred_element_type=F32)
        for k in range(4):
            kept = jnp.where(column == start + k, product[k * 128 : (k + 1) * 128], kept)
    kept = kept.T
    return kept[:GROUP] + kept[GROUP : 2 * GROUP]


def weigh_first_kernel(capacity, stride, owner, cells, innovations, weights, *refs):
    parcel, split, place, count, held_cells, held_values, held_weights, small, large = refs
    held = held_cells.shape[0]
    steps = held // GROUP
    copies = [
        pltpu.make_async_copy(innovations, held_values, small.at[0]),
        pltpu.make_async_copy(cells, held_cells, small.at[1]),
    ]
    for step in range(steps):
        block = pl.ds(step * GROUP, GROUP)
        copies.append(
            pltpu.make_async_copy(weights.at[block], held_weights.at[block], large.at[step])
        )
    for copy in copies:
        copy.start()
    parcel[...] = jnp.zeros_like(parcel)
    for index in range(count.shape[0]):
        count[index] = 0
    for index in range(held):
        target = owner[index]
        rank = count[target]
        count[target] = rank + 1
        place[index] = target * capacity + rank
        place[held + index] = target * stride + rank
    copies[0].wait()
    copies[1].wait()

    for step in range(steps):
        copies[2 + step].wait()
        first = step * GROUP

        def split_rows(start):
            blocks = slice(first + start, first + start + 4)
            both = jnp.concatenate(parts(held_weights[blocks].reshape(4 * 128, 128)), axis=1)
            split[blocks] = both.reshape(4, 128, 256)
            return both

        result = apply_blocks(held_values[first : first + GROUP], split_rows)
        cell_rows = held_cells[first : first + GROUP].astype(F32)
        for k in range(GROUP):
            at = place[first + k] + owner[first + k] * capacity
            parcel[pl.ds(at, 1), :] = cell_rows[k : k + 1]
            parcel[pl.ds(at + capacity, 1), :] = result[k : k + 1]


def weigh_first(owner, cells, innovations, weights, devices, capacity, stride):
    held, width = cells.shape
    return pl.pallas_call(
        functools.partial(weigh_first_kernel, capacity, stride),
        out_shape=[
            jax.ShapeDtypeStruct((devices * 2 * capacity, width), F32),
            jax.ShapeDtypeStruct((held, width, 2 * width), BF16),
            jax.ShapeDtypeStruct((2 * held,), jnp.int32),
        ],
        in_specs=[SMEM, HBM, HBM, HBM],
        out_specs=[VMEM, VMEM, SMEM],
        scratch_shapes=[
            pltpu.SMEM((devices,), jnp.int32),
            pltpu.VMEM((held, width), jnp.int32),
            pltpu.VMEM((held, width), F32),
            pltpu.VMEM((held, width, width), F32),
            pltpu.SemaphoreType.DMA((2,)),
            pltpu.SemaphoreType.DMA((held // GROUP,)),
        ],
        compiler_params=SNUG,
        name="weigh_first",
    )(owner, cells, innovations, weights)


def weigh_next_kernel(capacity, stride, devices, last, place, returned, sums, split, *refs):
    if last:
        sums_before, weighted_before, parcel = refs
    else:
        parcel, weighted = refs
    parcel[...] = jnp.zeros_like(parcel)
    total = jnp.zeros((GROUP, 128), F32)
    total_cross = jnp.zeros((GROUP, 128), F32)
    held = split.shape[0]
    for first in range(0, held, GROUP):
        here = jnp.concatenate(
            [returned[pl.ds(place[first + k], 1), :] for k in range(GROUP)], axis=0
        )
        result = apply_blocks(
            here, lambda start: split[first + start : first + start + 4].reshape(4 * 128, 256)
        )
        total += here * result
        if last:
            total_cross += here * weighted_before[first : first + GROUP]
        else:
            weighted[first : first + GROUP] = result
        for k in range(GROUP):
            parcel[pl.ds(place[held + first + k], 1), :] = result[k : k + 1]
    if last:
        scalars = [
            lane_value(sums_before[0:1], 0) / devices,
            lane_value(sums[0:1], 0),
            lane_value(sums[0:1], 1),
            lane_value(sums_before[0:1], 1) / devices,
            jnp.sum(total),
            jnp.sum(total_cross),
        ]
    else:
        scalars = [lane_value(sums[0:1], 0), jnp.sum(total)]
    row = lanes(scalars, 1)
    for target in range(devices):
        at = target * stride + capacity
        parcel[at : at + 1] = row


def weigh_next(place, returned, sums, split, devices, capacity, stride, before=None):
    held, width = split.shape[:2]
    last = before is not None
    operands = [place, returned, sums, split] + (list(before) if last else [])
    out_shape = [jax.ShapeDtypeStruct((devices * stride, width), F32)]
    if not last:
        out_shape += [jax.ShapeDtypeStruct((held, width), F32)]
    return pl.pallas_call(
        functools.partial(weigh_next_kernel, capacity, stride, devices, last),
        out_shape=out_shape,
        in_specs=[SMEM] + [VMEM] * (len(operands) - 1),
        out_specs=[VMEM] * len(out_shape),
        compiler_params=PARAMS,
        name="weigh_last" if last else "weigh_next",
    )(*operands)


def swap(block):
    return lax.all_to_all(block, ("lat", "lon"), split_axis=0, concat_axis=0, tiled=True)


def body(sigma, east_coef, north_coef, mask, innovations, cells, owner, obs_weights):
    devices = lax.axis_size("lat") * lax.axis_size("lon")
    held, width = cells.shape
    capacity = max(2, (2 * held + devices - 1) // devices)
    stride = (capacity + 8) // 8 * 8
    slots = devices * capacity

    faces = [mask, east_coef, north_coef]
    sides, innovations = lax.optimization_barrier((face_sides(*faces), innovations))
    mixed, down, up = exchange_columns(faces, sides)
    parcel, split, place = weigh_first(
        owner.reshape(held), cells, innovations, obs_weights, devices, capacity, stride
    )
    parcel, down, up = lax.optimization_barrier((parcel, down, up))
    face_halo = exchange_rows(down, up) + (mixed,)
    arrived = swap(parcel.reshape(devices, 2 * capacity, width))
    weights = face_weights(mask, east_coef, north_coef, face_halo)

    row_at, col_at, field, sides = scatter_first(arrived, sigma, capacity)
    seen, right, image_zero, sums = observe(
        field, exchange([field], sides), weights, sigma, row_at, col_at
    )
    returned = swap(seen.reshape(devices, capacity, width)).reshape(slots, width)
    parcel, weighted = weigh_next(place, returned, sums, split, devices, capacity, stride)
    arrived = swap(parcel.reshape(devices, stride, width))

    field_zero, sides, scalars_zero = scatter_next(arrived, row_at, col_at, sigma, capacity)
    seen, residual_one, image_one, sums = observe(
        field_zero, exchange([field_zero], sides), weights, sigma, row_at, col_at, right, scalars_zero
    )
    returned = swap(seen.reshape(devices, capacity, width)).reshape(slots, width)
    (parcel,) = weigh_next(
        place, returned, sums, split, devices, capacity, stride, (scalars_zero, weighted)
    )
    arrived = swap(parcel.reshape(devices, stride, width))

    field, sides, scalars = scatter_next(arrived, row_at, col_at, sigma, capacity, field_zero)
    increment, residual = finish(
        field, exchange([field], sides), weights, right, residual_one, image_zero, image_one, scalars
    )
    return (increment, residual)


def solution(mesh):
    return jax.shard_map(
        body,
        mesh=mesh,
        in_specs=(
            P(None, "lat", "lon"),
            P(None, "lat", "lon"),
            P(None, "lat", "lon"),
            P(None, "lat", "lon"),
            P(("lat", "lon"), None),
            P(("lat", "lon"), None),
            P(("lat", "lon"), None),
            P(("lat", "lon"), None, None),
        ),
        out_specs=(P(None, "lat", "lon"), P(None, "lat", "lon")),
        check_vma=False,
    )
```

```python
import functools

import jax
import jax.numpy as jnp
from jax import lax
from jax.experimental import pallas as pl
from jax.experimental.pallas import tpu as pltpu
from jax.sharding import PartitionSpec as P

PASSES = 5
HALO = 16
EDGE = 8
GROUP = 16
F32 = jnp.float32
BF16 = jnp.bfloat16
VMEM = pl.BlockSpec(memory_space=pltpu.VMEM)
HBM = pl.BlockSpec(memory_space=pltpu.HBM)
SMEM = pl.BlockSpec(memory_space=pltpu.SMEM)
PARAMS = pltpu.CompilerParams(vmem_limit_bytes=32 * 1024 * 1024)

ROOMLESS = pltpu.CompilerParams(vmem_limit_bytes=60 * 1024 * 1024)


def parts(values):
    high = values.astype(BF16)
    low = (values - high.astype(F32)).astype(BF16)
    return high, low


def lane_of(rows):
    return lax.broadcasted_iota(jnp.int32, (rows, 128), 1)


def pack_sides(fields):
    lane = lane_of(fields[0].shape[0])
    packed = jnp.zeros_like(fields[0])
    for level, field in enumerate(fields):
        start = 2 * HALO * level
        turned = pltpu.roll(field, (start + HALO) % 128, 1)
        packed = jnp.where((lane >= start) & (lane < start + 2 * HALO), turned, packed)
    return packed


def turn_kernel(fields, from_east, from_west, mixed, down, up):
    levels, rows, _ = fields.shape[-3:]
    western = lane_of(rows) % (2 * HALO) < HALO
    for index in range(fields.shape[0] if len(fields.shape) == 4 else 1):
        at = (index,) if len(fields.shape) == 4 else ()
        sides = jnp.where(western, from_west[at + (...,)], from_east[at + (...,)])
        mixed[at + (...,)] = sides
        for level in range(levels):
            down[at + (level,)] = fields[at + (level, slice(rows - HALO, rows))]
            up[at + (level,)] = fields[at + (level, slice(0, HALO))]
        down[at + (levels,)] = sides[rows - HALO :]
        up[at + (levels,)] = sides[:HALO]


def exchange(fields, sides):
    mixed, down, up = exchange_columns(fields, sides)
    return exchange_rows(down, up) + (mixed,)


def exchange_columns(fields, sides):
    *lead, levels, rows, cols = fields.shape
    wide = lax.axis_size("lon")
    east = [(i, (i + 1) % wide) for i in range(wide)]
    from_west = lax.ppermute(sides, "lon", east)
    from_east = lax.ppermute(sides, "lon", [(to, at) for at, to in east])
    shapes = [(*lead, rows, cols)] + [(*lead, levels + 1, HALO, cols)] * 2
    return pl.pallas_call(
        turn_kernel,
        out_shape=[jax.ShapeDtypeStruct(shape, F32) for shape in shapes],
        in_specs=[VMEM] * 3,
        out_specs=[VMEM] * 3,
        compiler_params=PARAMS,
        name="turn",
    )(fields, from_east, from_west)


def exchange_rows(down, up):
    tall = lax.axis_size("lat")
    first = [(i, i + 1) for i in range(0, tall - 1, 2)]
    second = [(i, i + 1) for i in range(1, tall - 1, 2)]
    even = lax.axis_index("lat") % 2 == 0
    one = lax.ppermute(
        jnp.where(even, down, up), "lat", first + [(to, at) for at, to in first]
    )
    two = lax.ppermute(
        jnp.where(even, up, down), "lat", second + [(to, at) for at, to in second]
    )
    return jnp.where(even, two, one), jnp.where(even, one, two)


def neighbours(tiles):
    *own, side = tiles
    lane = lane_of(side.shape[0])
    side_next, side_previous = side, side
    after, before = [], []
    for level, field in enumerate(own):
        middle = 2 * HALO * level + HALO
        turned_side = pltpu.roll(side, 128 - middle, 1)
        turned_own = pltpu.roll(field, middle, 1)
        after.append(pltpu.roll(jnp.where(lane == 0, turned_side, field), 127, 1))
        before.append(pltpu.roll(jnp.where(lane == 127, turned_side, field), 1, 1))
        side_next = jnp.where(lane == middle, turned_own, side_next)
        side_previous = jnp.where(lane == middle - 1, turned_own, side_previous)
    after.append(pltpu.roll(side_next, 127, 1))
    before.append(pltpu.roll(side_previous, 1, 1))
    return after, before


def place(target, own, halo, lead=()):
    before, after, mixed = halo
    levels = before.shape[-3] - 1
    rows = mixed.shape[-2]
    for tile in range(levels + 1):
        at = lead + (tile,)
        blank = jnp.zeros((EDGE, 128), F32)
        middle = mixed[lead + (...,)] if tile == levels else own[at + (...,)]
        target[at + (slice(0, EDGE),)] = blank
        target[at + (slice(EDGE, EDGE + HALO),)] = before[at + (...,)]
        target[at + (slice(EDGE + HALO, EDGE + HALO + rows),)] = middle
        target[at + (slice(EDGE + HALO + rows, EDGE + 2 * HALO + rows),)] = after[at + (...,)]
        target[at + (slice(EDGE + 2 * HALO + rows, 2 * EDGE + 2 * HALO + rows),)] = blank


def clear_margins(target):
    blank = jnp.zeros((target.shape[0], EDGE, 128), F32)
    target[:, 0:EDGE] = blank
    target[:, target.shape[1] - EDGE :] = blank


def face_kernel(products, before, after, mixed, weights, padded, faces):
    tiles, tall = weights.shape[1:3]
    for index in range(2):
        place(padded, products, (before, after, mixed), (index,))
    inner = slice(EDGE, EDGE + tall)
    faces[:, 0:EDGE] = jnp.zeros((tiles, EDGE, 128), F32)
    faces[:, EDGE + tall :] = jnp.zeros((tiles, EDGE, 128), F32)
    land = [(padded[0, tile, inner] > 0.0).astype(F32) for tile in range(tiles)]
    land_east, _ = neighbours(land)
    east_face = [padded[0, tile, inner] * land_east[tile] for tile in range(tiles)]
    _, west_face = neighbours(east_face)
    for tile in range(tiles):
        land_north = (padded[0, tile, EDGE + 1 : EDGE + 1 + tall] > 0.0).astype(F32)
        north_face = padded[1, tile, inner] * land_north
        faces[tile, inner] = north_face
        south_face = faces[tile, EDGE - 1 : EDGE - 1 + tall]
        weights[0, tile] = 1.0 - (
            ((east_face[tile] + west_face[tile]) + north_face) + south_face
        )
        weights[1, tile] = east_face[tile]
        weights[2, tile] = west_face[tile]
        weights[3, tile] = north_face
        weights[4, tile] = south_face


def face_weights(products, halo):
    _, levels, rows, cols = products.shape
    tall = rows + 2 * HALO
    return pl.pallas_call(
        face_kernel,
        out_shape=jax.ShapeDtypeStruct((5, levels + 1, tall, cols), F32),
        in_specs=[VMEM] * 4,
        out_specs=VMEM,
        scratch_shapes=[
            pltpu.VMEM((2, levels + 1, tall + 2 * EDGE, cols), F32),
            pltpu.VMEM((levels + 1, tall + 2 * EDGE, cols), F32),
        ],
        compiler_params=PARAMS,
        name="face_weights",
    )(products, *halo)


def sweep(source, target, weights, rows_from, rows_to, sides):
    tiles = source.shape[0]
    for start in range(rows_from, rows_to, 16):
        stop = min(start + 16, rows_to)
        here = [source[tile, EDGE + start : EDGE + stop] for tile in range(tiles)]
        east, west = neighbours(here)
        for tile in range(tiles if sides else tiles - 1):
            above = source[tile, EDGE + start + 1 : EDGE + stop + 1]
            below = source[tile, EDGE + start - 1 : EDGE + stop - 1]
            total = weights[0, tile, start:stop] * here[tile]
            total += weights[1, tile, start:stop] * east[tile]
            total += weights[2, tile, start:stop] * west[tile]
            total += weights[3, tile, start:stop] * above
            total += weights[4, tile, start:stop] * below
            target[tile, EDGE + start : EDGE + stop] = total


def smooth(field, spare, weights, depth):
    tall = weights.shape[2]
    for step in range(PASSES):
        reach = depth + PASSES - 1 - step
        skip = (HALO - reach) // 8 * 8
        sweep(field, spare, weights, skip, tall - skip, reach > 0)
        field, spare = spare, field
    return spare, field


def index_iota(cells):
    return lax.broadcasted_iota(jnp.int32, (cells, 128), 0).astype(F32).astype(BF16)


def spread_row(row, count):
    return jnp.broadcast_to(jnp.broadcast_to(row, (16, 128)).astype(BF16)[0:1], (count, 128))


def one_hot(iota, row):
    count = iota.shape[0]
    return jnp.where(
        iota == spread_row(row, count), jnp.ones((count, 128), BF16), jnp.zeros((count, 128), BF16)
    )


def scatter_into(total, load_rows, slots, half_rows, half_cols, group):
    row_iota = index_iota(half_rows)
    col_iota = index_iota(half_cols)
    total[...] = jnp.zeros_like(total)

    def step(index, carry):
        high_rows, low_rows, columns = [], [], []
        for row_index, col_index, value in load_rows(index):
            high, low = parts(jnp.broadcast_to(value, (16, 128)))
            high = jnp.broadcast_to(high[0:1], (half_rows, 128))
            low = jnp.broadcast_to(low[0:1], (half_rows, 128))
            hit = row_iota == spread_row(row_index, half_rows)
            zero = jnp.zeros((half_rows, 128), BF16)
            high_rows.append(jnp.where(hit, high, zero))
            low_rows.append(jnp.where(hit, low, zero))
            columns.append(one_hot(col_iota, col_index))
        if total.shape[0] == half_rows:
            left = jnp.concatenate(high_rows + low_rows, axis=1)
            right = jnp.concatenate(columns + columns, axis=1)
        else:
            left = jnp.concatenate(
                [jnp.concatenate(high_rows, axis=1), jnp.concatenate(low_rows, axis=1)], axis=0
            )
            right = jnp.concatenate(columns, axis=1)
        total[...] += lax.dot_general(
            left, right, (((1,), (1,)), ((), ())), preferred_element_type=F32
        )
        return carry

    lax.fori_loop(0, slots // group, step, 0)


def load_group(index, group, capacity, row_at, col_at, arrived, stride, first_slot):
    base = pl.multiple_of(index * group, group)
    row_block = row_at[pl.ds(base, group)]
    col_block = col_at[pl.ds(base, group)]
    for j in range(group):
        source = index * (group // capacity) + j // capacity
        at = source * stride + first_slot + j % capacity
        yield row_block[j : j + 1], col_block[j : j + 1], arrived[pl.ds(at, 1)]


def split_cells(cells, rows, cols):
    level = cells // (rows * cols)
    row = (cells // cols) % rows
    col = cells % cols
    return (level // 2) * rows + row, (level % 2) * cols + col


def put_field(total, sigma, field, extra=None):
    levels, rows, cols = sigma.shape
    fields = []
    for level in range(levels):
        r, c = level // 2 * rows, level % 2 * cols
        value = total[r : r + rows, c : c + cols]
        if total.shape[0] > levels // 2 * rows:
            low = r + levels // 2 * rows
            value = value + total[low : low + rows, c : c + cols]
        value = sigma[level] * value
        if extra is not None:
            value = value + extra(level)
        field[level] = value
        fields.append(value)
    return fields


def scatter_first_kernel(capacity, arrived, sigma, row_at, col_at, field, *refs):
    sides, total = refs
    levels, rows, cols = sigma.shape
    stride = 2 * capacity
    cells = jnp.concatenate(
        [arrived[at : at + capacity] for at in range(0, arrived.shape[0], stride)], axis=0
    )
    row_index, col_index = split_cells(cells.astype(jnp.int32), rows, cols)
    row_at[...] = row_index.astype(F32)
    col_at[...] = col_index.astype(F32)

    def load(index):
        return load_group(index, 64, capacity, row_at, col_at, arrived, stride, capacity)

    scatter_into(total, load, row_at.shape[0], levels // 2 * rows, 2 * cols, 64)
    sides[...] = pack_sides(put_field(total, sigma, field))


def scatter_first(arrived, sigma, capacity):
    levels, rows, cols = sigma.shape
    slots = arrived.shape[0] // 2
    shapes = [(slots, 128), (slots, 128), (levels, rows, cols), (rows, cols)]
    out = pl.pallas_call(
        functools.partial(scatter_first_kernel, capacity),
        out_shape=[jax.ShapeDtypeStruct(shape, F32) for shape in shapes],
        in_specs=[VMEM] * 2,
        out_specs=[VMEM] * len(shapes),
        scratch_shapes=[pltpu.VMEM((levels // 2 * rows, 2 * cols), F32)],
        compiler_params=PARAMS,
        name="scatter_first",
    )(arrived, sigma)
    return out


def lane_value(block, lane):
    return jnp.sum(jnp.where(lane_of(block.shape[0]) == lane, block, 0.0))


def lanes(values, rows):
    lane = lane_of(rows)
    out = jnp.zeros((rows, 128), F32)
    for index, value in enumerate(values):
        out = jnp.where(lane == index, value, out)
    return out


def scatter_next_kernel(capacity, last, arrived, row_at, col_at, sigma, *refs):
    if last:
        previous, field, sides, sums, total = refs
    else:
        previous, (field, sides, sums, total) = None, refs
    levels, rows, cols = sigma.shape
    stride = capacity + 1
    gathered = jnp.concatenate(
        [arrived[at : at + 1] for at in range(capacity, arrived.shape[0], stride)], axis=0
    )
    added = jnp.sum(gathered, axis=0, keepdims=True)
    sums[...] = jnp.broadcast_to(added, (8, 128))

    group = 128 if last else 64

    def load(index):
        return load_group(index, group, capacity, row_at, col_at, arrived, stride, 0)

    scatter_into(
        total, load, row_at.shape[0], levels // 2 * rows, 2 * cols, group
    )
    extra = None
    if last:
        beta = lane_value(added, 1) / lane_value(added, 0)

        def extra(level):
            return beta * previous[level]

    sides[...] = pack_sides(put_field(total, sigma, field, extra))


def scatter_next(arrived, row_at, col_at, sigma, capacity, previous=None):
    levels, rows, cols = sigma.shape
    last = previous is not None
    shapes = [(levels, rows, cols), (rows, cols), (8, 128)]
    operands = [arrived, row_at, col_at, sigma] + ([previous] if last else [])
    out = pl.pallas_call(
        functools.partial(scatter_next_kernel, capacity, last),
        out_shape=[jax.ShapeDtypeStruct(shape, F32) for shape in shapes],
        in_specs=[VMEM] * len(operands),
        out_specs=[VMEM] * len(shapes),
        scratch_shapes=[pltpu.VMEM((levels // 2 * rows * (1 if last else 2), 2 * cols), F32)],
        compiler_params=PARAMS,
        name="scatter_last" if last else "scatter_next",
    )(*operands)
    return out


def gather_from(fields, row_at, col_at, seen, table, group):
    rows, cols = fields[0].shape
    half_rows, half_cols = len(fields) // 2 * rows, 2 * cols
    for level, field in enumerate(fields):
        high, low = parts(field.T)
        c, r = level % 2 * cols, level // 2 * rows
        if table.shape[0] == half_cols:
            table[c : c + cols, r : r + rows] = high
            table[c : c + cols, half_rows + r : half_rows + r + rows] = low
        else:
            for i in range(0, cols, 16):
                at = 2 * (c + i)
                table[at : at + 16, r : r + rows] = high[i : i + 16]
                table[at + 16 : at + 32, r : r + rows] = low[i : i + 16]
    row_iota = index_iota(half_rows)
    sublane = lax.broadcasted_iota(jnp.int32, (8, 256), 0)

    def step(index, carry):
        base = pl.multiple_of(index * group, group)
        row_block = row_at[pl.ds(base, group)]
        col_block = col_at[pl.ds(base, group)].astype(jnp.int32)
        found = []
        for j in range(0, group, 2):
            hot = jnp.concatenate(
                [one_hot(row_iota, row_block[i : i + 1]) for i in (j, j + 1)], axis=1
            )
            if table.shape[0] == half_cols:
                hot = jnp.concatenate([hot, hot], axis=0)
            lines = jnp.dot(table[...], hot, preferred_element_type=F32)
            wanted = jnp.concatenate([col_block[j : j + 1], col_block[j + 1 : j + 2]], axis=1)
            wanted = jnp.broadcast_to(wanted, (8, 256))
            if table.shape[0] == half_cols:
                tiles = [lines[i : i + 8] for i in range(0, half_cols, 8)]
            else:
                tiles = [
                    lines[i + j : i + j + 8] + lines[i + j + 16 : i + j + 24]
                    for i in range(0, 2 * half_cols, 32)
                    for j in (0, 8)
                ]
            bit = 8
            while len(tiles) > 1:
                upper = (wanted & bit) != 0
                tiles = [
                    jnp.where(upper, tiles[i + 1], tiles[i]) for i in range(0, len(tiles), 2)
                ]
                bit = bit * 2
            value = jnp.sum(
                jnp.where((wanted & 7) == sublane, tiles[0], 0.0), axis=0, keepdims=True
            )
            found += [value[:, :128], value[:, 128:]]
        seen[pl.ds(base, group)] = jnp.concatenate(found, axis=0)
        return carry

    lax.fori_loop(0, row_at.shape[0] // group, step, 0)


def own_part(field, level, rows):
    return field[level, EDGE + HALO : EDGE + HALO + rows]


def total_of(pairs):
    added = None
    for left, right in pairs:
        term = left * right
        added = term if added is None else added + term
    return jnp.sum(added)


def observe_first_kernel(source, *refs):
    halo, weights, sigma, row_at, col_at = refs[:3], refs[3], refs[4], refs[5], refs[6]
    seen, right, image, sums, field, spare, table = refs[7:]
    levels, rows, cols = source.shape
    place(field, source, halo)
    clear_margins(spare)
    spare, field = smooth(field, spare, weights, PASSES)
    right[...] = field[:, EDGE : EDGE + rows + 2 * HALO]
    own = [own_part(field, level, rows) for level in range(levels)]
    sums[...] = lanes([total_of([(value, value) for value in own])], 8)
    spare, field = smooth(field, spare, weights, 0)
    fields = [sigma[level] * own_part(field, level, rows) for level in range(levels)]
    for level in range(levels):
        image[level] = fields[level]
    gather_from(fields, row_at, col_at, seen, table, 64)


def observe_next_kernel(source, *refs):
    halo, weights, sigma, row_at, col_at = refs[:3], refs[3], refs[4], refs[5], refs[6]
    right, scalars = refs[7:9]
    seen, residual, image, sums, field, spare, table = refs[9:]
    levels, rows, cols = source.shape
    tall = rows + 2 * HALO
    norm, product = lane_value(scalars[0:1], 0), lane_value(scalars[0:1], 1)
    alpha = norm / (norm + product)
    place(field, source, halo)
    clear_margins(spare)
    spare, field = smooth(field, spare, weights, PASSES)

    for tile in range(levels + 1):
        first = right[tile]
        field[tile, EDGE : EDGE + tall] = first - alpha * (first + field[tile, EDGE : EDGE + tall])
    own = [own_part(field, level, rows) for level in range(levels)]
    first = [right[level, HALO : HALO + rows] for level in range(levels)]
    for level in range(levels):
        residual[level] = own[level]
    sums[...] = lanes(
        [total_of([(value, value) for value in own]), total_of(list(zip(own, first)))], 8
    )
    spare, field = smooth(field, spare, weights, 0)
    fields = [sigma[level] * own_part(field, level, rows) for level in range(levels)]
    for level in range(levels):
        image[level] = fields[level]
    gather_from(fields, row_at, col_at, seen, table, 128)


def observe(source, halo, weights, sigma, row_at, col_at, right=None, scalars=None):
    levels, rows, cols = sigma.shape
    tall = rows + 2 * HALO
    slots = row_at.shape[0]
    first = right is None
    kept = (levels + 1, tall, cols) if first else (levels, rows, cols)
    shapes = [(slots, 128), kept, (levels, rows, cols), (8, 128)]
    operands = [source, *halo, weights, sigma, row_at, col_at]
    operands += [] if first else [right, scalars]
    return pl.pallas_call(
        observe_first_kernel if first else observe_next_kernel,
        out_shape=[jax.ShapeDtypeStruct(shape, F32) for shape in shapes],
        in_specs=[VMEM] * len(operands),
        out_specs=[VMEM] * len(shapes),
        scratch_shapes=[
            pltpu.VMEM((levels + 1, tall + 2 * EDGE, cols), F32),
            pltpu.VMEM((levels + 1, tall + 2 * EDGE, cols), F32),
            pltpu.VMEM(
                (4 * cols, levels // 2 * rows) if first else (2 * cols, levels * rows), BF16
            ),
        ],
        compiler_params=PARAMS,
        name="observe_first" if first else "observe_next",
    )(*operands)


def finish_kernel(source, *refs):
    halo, weights, right, residual_one, image_zero, image_one, scalars = refs[:3], *refs[3:9]
    increment, residual, field, spare = refs[9:]
    levels, rows, cols = source.shape
    norm_zero, norm_one, cross, product_zero, product_one, product_cross = [
        lane_value(scalars[0:1], index) for index in range(6)
    ]
    alpha_zero = norm_zero / (norm_zero + product_zero)
    beta = norm_one / norm_zero
    square = norm_one + 2.0 * beta * cross + beta * beta * norm_zero
    seen = product_one + 2.0 * beta * product_cross + beta * beta * product_zero
    alpha_one = norm_one / (square + seen)
    for level in range(levels):
        direction = image_one[level] + beta * image_zero[level]
        increment[level] = alpha_zero * image_zero[level] + alpha_one * direction
    place(field, source, halo)
    clear_margins(spare)
    spare, field = smooth(field, spare, weights, 0)
    for level in range(levels):
        here = residual_one[level]
        direction = here + beta * right[level, HALO : HALO + rows]
        image = direction + own_part(field, level, rows)
        residual[level] = here - alpha_one * image


def finish(source, halo, weights, right, residual_one, image_zero, image_one, scalars):
    levels, rows, cols = source.shape
    tall = rows + 2 * HALO
    return pl.pallas_call(
        finish_kernel,
        out_shape=[jax.ShapeDtypeStruct((levels, rows, cols), F32)] * 2,
        in_specs=[VMEM] * 10,
        out_specs=[VMEM] * 2,
        scratch_shapes=[pltpu.VMEM((levels + 1, tall + 2 * EDGE, cols), F32),
            pltpu.VMEM((levels + 1, tall + 2 * EDGE, cols), F32)],
        compiler_params=PARAMS,
        name="finish",
    )(source, *halo, weights, right, residual_one, image_zero, image_one, scalars)


def apply_blocks(values, weights, at):
    high, low = parts(values)
    first = jnp.concatenate([high, low, jnp.zeros((128 - 2 * GROUP, 128), BF16)], axis=0)
    second = jnp.concatenate([high, jnp.zeros((128 - GROUP, 128), BF16)], axis=0)
    right = jnp.concatenate([first, second], axis=1)
    lane = lane_of(128)
    column = jnp.where(lane < 2 * GROUP, lane % GROUP, GROUP)
    kept = jnp.zeros((128, 128), F32)
    for start in range(0, GROUP, 4):
        matrix = weights[at + start : at + start + 4].reshape(4 * 128, 128)
        left = jnp.concatenate(parts(matrix), axis=1)
        product = lax.dot_general(left, right, (((1,), (1,)), ((), ())), preferred_element_type=F32)
        for k in range(4):
            kept = jnp.where(column == start + k, product[k * 128 : (k + 1) * 128], kept)
    kept = kept.T
    return kept[:GROUP] + kept[GROUP : 2 * GROUP]


def start_kernel(capacity, owner, cells, innovations, weights, mask, east, north, *refs):
    parcel, places, products, sides = refs[:4]
    count, held_cells, held_values, held_weights, held_mask, held_faces, arrived = refs[4:]
    held = held_cells.shape[0]
    levels = mask.shape[0]
    steps = held // GROUP
    moves = [
        (innovations, held_values),
        (cells, held_cells),
        (mask, held_mask),
        (east, held_faces.at[0]),
        (north, held_faces.at[1]),
    ]
    for step in range(steps):
        block = pl.ds(step * GROUP, GROUP)
        moves.append((weights.at[block], held_weights.at[block]))
    copies = [
        pltpu.make_async_copy(source, target, arrived.at[index])
        for index, (source, target) in enumerate(moves)
    ]
    for copy in copies:
        copy.start()
    parcel[...] = jnp.zeros_like(parcel)
    for index in range(count.shape[0]):
        count[index] = 0
    for index in range(held):
        target = owner[index]
        rank = count[target]
        count[target] = rank + 1
        places[index] = target * capacity + rank
        places[held + index] = target * (capacity + 1) + rank
    copies[0].wait()
    copies[1].wait()
    for step in range(steps):
        copies[5 + step].wait()
        first = step * GROUP
        result = apply_blocks(held_values[first : first + GROUP], held_weights, first)
        cell_rows = held_cells[first : first + GROUP].astype(F32)
        for k in range(GROUP):
            at = places[first + k] + owner[first + k] * capacity
            parcel[pl.ds(at, 1), :] = cell_rows[k : k + 1]
            parcel[pl.ds(at + capacity, 1), :] = result[k : k + 1]
    for copy in copies[2:5]:
        copy.wait()
    for index in range(2):
        fields = [held_mask[level].astype(F32) * held_faces[index, level] for level in range(levels)]
        for level in range(levels):
            products[index, level] = fields[level]
        sides[index] = pack_sides(fields)


def start(owner, cells, innovations, weights, mask, east, north, devices, capacity):
    held, width = cells.shape
    shapes = [(devices * 2 * capacity, width), (2 * held,), (2,) + mask.shape, (2,) + mask.shape[1:]]
    types = [F32, jnp.int32, F32, F32]
    return pl.pallas_call(
        functools.partial(start_kernel, capacity),
        out_shape=[jax.ShapeDtypeStruct(shape, kind) for shape, kind in zip(shapes, types)],
        in_specs=[SMEM] + [HBM] * 6,
        out_specs=[VMEM, SMEM, VMEM, VMEM],
        scratch_shapes=[
            pltpu.SMEM((devices,), jnp.int32),
            pltpu.VMEM((held, width), jnp.int32),
            pltpu.VMEM((held, width), F32),
            pltpu.VMEM((held, width, width), F32),
            pltpu.VMEM(mask.shape, jnp.int32),
            pltpu.VMEM((2,) + mask.shape, F32),
            pltpu.SemaphoreType.DMA((5 + held // GROUP,)),
        ],
        compiler_params=ROOMLESS,
        name="start",
    )(owner, cells, innovations, weights, mask, east, north)


def weigh_next_kernel(capacity, devices, last, places, returned, sums, weights, *refs):
    if last:
        sums_before, weighted_before, parcel = refs
    else:
        parcel, weighted = refs
    parcel[...] = jnp.zeros_like(parcel)
    total = jnp.zeros((GROUP, 128), F32)
    total_cross = jnp.zeros((GROUP, 128), F32)
    held = weights.shape[0]
    for first in range(0, held, GROUP):
        here = jnp.concatenate(
            [returned[pl.ds(places[first + k], 1), :] for k in range(GROUP)], axis=0
        )
        result = apply_blocks(here, weights, first)
        total += here * result
        if last:
            total_cross += here * weighted_before[first : first + GROUP]
        else:
            weighted[first : first + GROUP] = result
        for k in range(GROUP):
            parcel[pl.ds(places[held + first + k], 1), :] = result[k : k + 1]
    if last:
        scalars = [
            lane_value(sums_before[0:1], 0) / devices,
            lane_value(sums[0:1], 0),
            lane_value(sums[0:1], 1),
            lane_value(sums_before[0:1], 1) / devices,
            jnp.sum(total),
            jnp.sum(total_cross),
        ]
    else:
        scalars = [lane_value(sums[0:1], 0), jnp.sum(total)]
    row = lanes(scalars, 1)
    for target in range(devices):
        at = target * (capacity + 1) + capacity
        parcel[at : at + 1] = row


def weigh_next(places, returned, sums, weights, devices, capacity, before=None):
    held, width = weights.shape[:2]
    last = before is not None
    operands = [places, returned, sums, weights] + (list(before) if last else [])
    out_shape = [jax.ShapeDtypeStruct((devices * (capacity + 1), width), F32)]
    if not last:
        out_shape += [jax.ShapeDtypeStruct((held, width), F32)]
    return pl.pallas_call(
        functools.partial(weigh_next_kernel, capacity, devices, last),
        out_shape=out_shape,
        in_specs=[SMEM] + [VMEM] * (len(operands) - 1),
        out_specs=[VMEM] * len(out_shape),
        compiler_params=PARAMS,
        name="weigh_last" if last else "weigh_next",
    )(*operands)


def swap(block):
    devices = lax.axis_size("lat") * lax.axis_size("lon")
    shares = block.reshape(devices, block.shape[0] // devices, 1, block.shape[1])
    got = lax.all_to_all(shares, ("lat", "lon"), split_axis=0, concat_axis=0, tiled=True)
    return got.reshape(block.shape)


def body(sigma, east_coef, north_coef, mask, innovations, cells, owner, obs_weights):
    devices = lax.axis_size("lat") * lax.axis_size("lon")
    held, width = cells.shape
    capacity = max(2, (2 * held + devices - 1) // devices)

    parcel, places, products, sides = start(
        owner.reshape(held),
        cells,
        innovations,
        obs_weights,
        mask,
        east_coef,
        north_coef,
        devices,
        capacity,
    )
    mixed, down, up = exchange_columns(products, sides)
    arrived = swap(parcel)
    weights = face_weights(products, exchange_rows(down, up) + (mixed,))

    row_at, col_at, field, sides = scatter_first(arrived, sigma, capacity)
    seen, right, image_zero, sums = observe(
        field, exchange(field, sides), weights, sigma, row_at, col_at
    )
    returned = swap(seen)
    parcel, weighted = weigh_next(places, returned, sums, obs_weights, devices, capacity)
    arrived = swap(parcel)

    field_zero, sides, scalars_zero = scatter_next(arrived, row_at, col_at, sigma, capacity)
    seen, residual_one, image_one, sums = observe(
        field_zero, exchange(field_zero, sides), weights, sigma, row_at, col_at, right, scalars_zero
    )
    returned = swap(seen)
    (parcel,) = weigh_next(
        places, returned, sums, obs_weights, devices, capacity, (scalars_zero, weighted)
    )
    arrived = swap(parcel)

    field, sides, scalars = scatter_next(arrived, row_at, col_at, sigma, capacity, field_zero)
    increment, residual = finish(
        field, exchange(field, sides), weights, right, residual_one, image_zero, image_one, scalars
    )
    return (increment, residual)


def solution(mesh):
    return jax.shard_map(
        body,
        mesh=mesh,
        in_specs=(
            P(None, "lat", "lon"),
            P(None, "lat", "lon"),
            P(None, "lat", "lon"),
            P(None, "lat", "lon"),
            P(("lat", "lon"), None),
            P(("lat", "lon"), None),
            P(("lat", "lon"), None),
            P(("lat", "lon"), None, None),
        ),
        out_specs=(P(None, "lat", "lon"), P(None, "lat", "lon")),
        check_vma=False,
    )
```

```python
import functools

import jax
import jax.numpy as jnp
from jax import lax
from jax.experimental import pallas as pl
from jax.experimental.pallas import tpu as pltpu
from jax.sharding import PartitionSpec as P

PASSES = 5
HALO = 16
EDGE = 8
GROUP = 16
F32 = jnp.float32
BF16 = jnp.bfloat16
VMEM = pl.BlockSpec(memory_space=pltpu.VMEM)
HBM = pl.BlockSpec(memory_space=pltpu.HBM)
SMEM = pl.BlockSpec(memory_space=pltpu.SMEM)
PARAMS = pltpu.CompilerParams(vmem_limit_bytes=32 * 1024 * 1024)

ROOMLESS = pltpu.CompilerParams(vmem_limit_bytes=60 * 1024 * 1024)


SNUG = pltpu.CompilerParams(vmem_limit_bytes=52 * 1024 * 1024)


def parts(values):
    high = values.astype(BF16)
    low = (values - high.astype(F32)).astype(BF16)
    return high, low


def lane_of(rows):
    return lax.broadcasted_iota(jnp.int32, (rows, 128), 1)


def pack_sides(fields):
    lane = lane_of(fields[0].shape[0])
    packed = jnp.zeros_like(fields[0])
    for level, field in enumerate(fields):
        start = 2 * HALO * level
        turned = pltpu.roll(field, (start + HALO) % 128, 1)
        packed = jnp.where((lane >= start) & (lane < start + 2 * HALO), turned, packed)
    return packed


def turn_kernel(fields, from_east, from_west, mixed, down, up, *kept):
    levels, rows, _ = fields.shape[-3:]
    for ref in kept:
        ref[...] = fields[...]
    western = lane_of(rows) % (2 * HALO) < HALO
    for index in range(fields.shape[0] if len(fields.shape) == 4 else 1):
        at = (index,) if len(fields.shape) == 4 else ()
        sides = jnp.where(western, from_west[at + (...,)], from_east[at + (...,)])
        mixed[at + (...,)] = sides
        for level in range(levels):
            down[at + (level,)] = fields[at + (level, slice(rows - HALO, rows))]
            up[at + (level,)] = fields[at + (level, slice(0, HALO))]
        down[at + (levels,)] = sides[rows - HALO :]
        up[at + (levels,)] = sides[:HALO]


def exchange(fields, sides):
    mixed, down, up = exchange_columns(fields, sides)
    return exchange_rows(down, up) + (mixed,)


def exchange_columns(fields, sides, keep=False):
    *lead, levels, rows, cols = fields.shape
    wide = lax.axis_size("lon")
    east = [(i, (i + 1) % wide) for i in range(wide)]
    from_west = lax.ppermute(sides, "lon", east)
    from_east = lax.ppermute(sides, "lon", [(to, at) for at, to in east])
    shapes = [(*lead, rows, cols)] + [(*lead, levels + 1, HALO, cols)] * 2
    shapes += [fields.shape] if keep else []
    return pl.pallas_call(
        turn_kernel,
        out_shape=[jax.ShapeDtypeStruct(shape, F32) for shape in shapes],
        in_specs=[VMEM] * 3,
        out_specs=[VMEM] * len(shapes),
        compiler_params=PARAMS,
        name="turn",
    )(fields, from_east, from_west)


def exchange_rows(down, up):
    tall = lax.axis_size("lat")
    first = [(i, i + 1) for i in range(0, tall - 1, 2)]
    second = [(i, i + 1) for i in range(1, tall - 1, 2)]
    even = lax.axis_index("lat") % 2 == 0
    one = lax.ppermute(
        jnp.where(even, down, up), "lat", first + [(to, at) for at, to in first]
    )
    two = lax.ppermute(
        jnp.where(even, up, down), "lat", second + [(to, at) for at, to in second]
    )
    return jnp.where(even, two, one), jnp.where(even, one, two)


def neighbours(tiles):
    *own, side = tiles
    lane = lane_of(side.shape[0])
    side_next, side_previous = side, side
    after, before = [], []
    for level, field in enumerate(own):
        middle = 2 * HALO * level + HALO
        turned_side = pltpu.roll(side, 128 - middle, 1)
        turned_own = pltpu.roll(field, middle, 1)
        after.append(pltpu.roll(jnp.where(lane == 0, turned_side, field), 127, 1))
        before.append(pltpu.roll(jnp.where(lane == 127, turned_side, field), 1, 1))
        side_next = jnp.where(lane == middle, turned_own, side_next)
        side_previous = jnp.where(lane == middle - 1, turned_own, side_previous)
    after.append(pltpu.roll(side_next, 127, 1))
    before.append(pltpu.roll(side_previous, 1, 1))
    return after, before


def place(target, own, halo, lead=()):
    before, after, mixed = halo
    levels = before.shape[-3] - 1
    rows = mixed.shape[-2]
    for tile in range(levels + 1):
        at = lead + (tile,)
        blank = jnp.zeros((EDGE, 128), F32)
        middle = mixed[lead + (...,)] if tile == levels else own[at + (...,)]
        target[at + (slice(0, EDGE),)] = blank
        target[at + (slice(EDGE, EDGE + HALO),)] = before[at + (...,)]
        target[at + (slice(EDGE + HALO, EDGE + HALO + rows),)] = middle
        target[at + (slice(EDGE + HALO + rows, EDGE + 2 * HALO + rows),)] = after[at + (...,)]
        target[at + (slice(EDGE + 2 * HALO + rows, 2 * EDGE + 2 * HALO + rows),)] = blank


def clear_margins(target):
    blank = jnp.zeros((target.shape[0], EDGE, 128), F32)
    target[:, 0:EDGE] = blank
    target[:, target.shape[1] - EDGE :] = blank


def face_kernel(products, before, after, mixed, weights, padded, faces):
    tiles, tall = weights.shape[1:3]
    for index in range(2):
        place(padded, products, (before, after, mixed), (index,))
    inner = slice(EDGE, EDGE + tall)
    faces[:, 0:EDGE] = jnp.zeros((tiles, EDGE, 128), F32)
    faces[:, EDGE + tall :] = jnp.zeros((tiles, EDGE, 128), F32)
    land = [(padded[0, tile, inner] > 0.0).astype(F32) for tile in range(tiles)]
    land_east, _ = neighbours(land)
    east_face = [padded[0, tile, inner] * land_east[tile] for tile in range(tiles)]
    _, west_face = neighbours(east_face)
    for tile in range(tiles):
        land_north = (padded[0, tile, EDGE + 1 : EDGE + 1 + tall] > 0.0).astype(F32)
        north_face = padded[1, tile, inner] * land_north
        faces[tile, inner] = north_face
        south_face = faces[tile, EDGE - 1 : EDGE - 1 + tall]
        weights[0, tile] = 1.0 - (
            ((east_face[tile] + west_face[tile]) + north_face) + south_face
        )
        weights[1, tile] = east_face[tile]
        weights[2, tile] = west_face[tile]
        weights[3, tile] = north_face
        weights[4, tile] = south_face


def face_weights(products, halo):
    _, levels, rows, cols = products.shape
    tall = rows + 2 * HALO
    return pl.pallas_call(
        face_kernel,
        out_shape=jax.ShapeDtypeStruct((5, levels + 1, tall, cols), F32),
        in_specs=[VMEM] * 4,
        out_specs=VMEM,
        scratch_shapes=[
            pltpu.VMEM((2, levels + 1, tall + 2 * EDGE, cols), F32),
            pltpu.VMEM((levels + 1, tall + 2 * EDGE, cols), F32),
        ],
        compiler_params=PARAMS,
        name="face_weights",
    )(products, *halo)


def sweep(source, target, weights, rows_from, rows_to, block):
    tiles = source.shape[0]

    def step(index, carry):
        first = pl.multiple_of(rows_from + index * block, 8)
        for start in range(0, block, 16):
            count = min(16, block - start)
            at = pl.multiple_of(first + EDGE + start, 8)
            inner = pl.ds(pl.multiple_of(first + start, 8), count)
            here = [source[tile, pl.ds(at, count)] for tile in range(tiles)]
            east, west = neighbours(here)
            for tile in range(tiles):
                above = source[tile, pl.ds(at + 1, count)]
                below = source[tile, pl.ds(at - 1, count)]
                total = weights[0, tile, inner] * here[tile]
                total += weights[1, tile, inner] * east[tile]
                total += weights[2, tile, inner] * west[tile]
                total += weights[3, tile, inner] * above
                total += weights[4, tile, inner] * below
                target[tile, pl.ds(at, count)] = total
        return carry

    lax.fori_loop(0, (rows_to - rows_from) // block, step, 0)


def smooth(field, spare, weights, skip, block, paired):
    tall = weights.shape[2]

    def two(index, carry):
        sweep(field, spare, weights, skip, tall - skip, block)
        sweep(spare, field, weights, skip, tall - skip, block)
        return carry

    if paired:
        lax.fori_loop(0, PASSES // 2, two, 0)
    else:
        for index in range(PASSES // 2):
            two(index, 0)
    sweep(field, spare, weights, skip, tall - skip, block)
    return field, spare


def index_iota(cells):
    return lax.broadcasted_iota(jnp.int32, (cells, 128), 0).astype(F32).astype(BF16)


def spread_row(row, count):
    return jnp.broadcast_to(jnp.broadcast_to(row, (16, 128)).astype(BF16)[0:1], (count, 128))


def one_hot(iota, row):
    count = iota.shape[0]
    return jnp.where(
        iota == spread_row(row, count), jnp.ones((count, 128), BF16), jnp.zeros((count, 128), BF16)
    )


def scatter_into(total, load_rows, slots, half_rows, half_cols, group):
    row_iota = index_iota(half_rows)
    col_iota = index_iota(half_cols)
    total[...] = jnp.zeros_like(total)

    def step(index, carry):
        high_rows, low_rows, columns = [], [], []
        for row_index, col_index, value in load_rows(index):
            high, low = parts(jnp.broadcast_to(value, (16, 128)))
            high = jnp.broadcast_to(high[0:1], (half_rows, 128))
            low = jnp.broadcast_to(low[0:1], (half_rows, 128))
            hit = row_iota == spread_row(row_index, half_rows)
            zero = jnp.zeros((half_rows, 128), BF16)
            high_rows.append(jnp.where(hit, high, zero))
            low_rows.append(jnp.where(hit, low, zero))
            columns.append(one_hot(col_iota, col_index))
        left = jnp.concatenate(high_rows + low_rows, axis=1)
        right = jnp.concatenate(columns + columns, axis=1)
        total[...] += lax.dot_general(
            left, right, (((1,), (1,)), ((), ())), preferred_element_type=F32
        )
        return carry

    lax.fori_loop(0, slots // group, step, 0)


def load_group(index, group, capacity, row_at, col_at, arrived, stride, first_slot):
    base = pl.multiple_of(index * group, group)
    row_block = row_at[pl.ds(base, group)]
    col_block = col_at[pl.ds(base, group)]
    for j in range(group):
        source = index * (group // capacity) + j // capacity
        at = source * stride + first_slot + j % capacity
        yield row_block[j : j + 1], col_block[j : j + 1], arrived[pl.ds(at, 1)]


def split_cells(cells, rows, cols):
    level = cells // (rows * cols)
    row = (cells // cols) % rows
    col = cells % cols
    return (level // 2) * rows + row, (level % 2) * cols + col


def put_field(total, sigma, field, extra=None):
    levels, rows, cols = sigma.shape
    fields = []
    for level in range(levels):
        r, c = level // 2 * rows, level % 2 * cols
        value = total[r : r + rows, c : c + cols]
        value = sigma[level] * value
        if extra is not None:
            value = value + extra(level)
        field[level] = value
        fields.append(value)
    return fields


def scatter_first_kernel(capacity, arrived, sigma, row_at, col_at, field, *refs):
    sides, total = refs
    levels, rows, cols = sigma.shape
    stride = 2 * capacity
    cells = jnp.concatenate(
        [arrived[at : at + capacity] for at in range(0, arrived.shape[0], stride)], axis=0
    )
    row_index, col_index = split_cells(cells.astype(jnp.int32), rows, cols)
    row_at[...] = row_index.astype(F32)
    col_at[...] = col_index.astype(F32)

    def load(index):
        return load_group(index, 64, capacity, row_at, col_at, arrived, stride, capacity)

    scatter_into(total, load, row_at.shape[0], levels // 2 * rows, 2 * cols, 64)
    sides[...] = pack_sides(put_field(total, sigma, field))


def scatter_first(arrived, sigma, capacity):
    levels, rows, cols = sigma.shape
    slots = arrived.shape[0] // 2
    shapes = [(slots, 128), (slots, 128), (levels, rows, cols), (rows, cols)]
    out = pl.pallas_call(
        functools.partial(scatter_first_kernel, capacity),
        out_shape=[jax.ShapeDtypeStruct(shape, F32) for shape in shapes],
        in_specs=[VMEM] * 2,
        out_specs=[VMEM] * len(shapes),
        scratch_shapes=[pltpu.VMEM((levels // 2 * rows, 2 * cols), F32)],
        compiler_params=PARAMS,
        name="scatter_first",
    )(arrived, sigma)
    return out


def lane_value(block, lane):
    return jnp.sum(jnp.where(lane_of(block.shape[0]) == lane, block, 0.0))


def lanes(values, rows):
    lane = lane_of(rows)
    out = jnp.zeros((rows, 128), F32)
    for index, value in enumerate(values):
        out = jnp.where(lane == index, value, out)
    return out


def scatter_next_kernel(capacity, last, arrived, row_at, col_at, sigma, *refs):
    if last:
        previous, field, sides, sums, total = refs
    else:
        previous, (field, sides, sums, total) = None, refs
    levels, rows, cols = sigma.shape
    stride = capacity + 1
    gathered = jnp.concatenate(
        [arrived[at : at + 1] for at in range(capacity, arrived.shape[0], stride)], axis=0
    )
    added = jnp.sum(gathered, axis=0, keepdims=True)
    sums[...] = jnp.broadcast_to(added, (8, 128))

    group = 128 if last else 64

    def load(index):
        return load_group(index, group, capacity, row_at, col_at, arrived, stride, 0)

    scatter_into(
        total, load, row_at.shape[0], levels // 2 * rows, 2 * cols, group
    )
    extra = None
    if last:
        beta = lane_value(added, 1) / lane_value(added, 0)

        def extra(level):
            return beta * previous[level]

    sides[...] = pack_sides(put_field(total, sigma, field, extra))


def scatter_next(arrived, row_at, col_at, sigma, capacity, previous=None):
    levels, rows, cols = sigma.shape
    last = previous is not None
    shapes = [(levels, rows, cols), (rows, cols), (8, 128)]
    operands = [arrived, row_at, col_at, sigma] + ([previous] if last else [])
    out = pl.pallas_call(
        functools.partial(scatter_next_kernel, capacity, last),
        out_shape=[jax.ShapeDtypeStruct(shape, F32) for shape in shapes],
        in_specs=[VMEM] * len(operands),
        out_specs=[VMEM] * len(shapes),
        scratch_shapes=[pltpu.VMEM((levels // 2 * rows, 2 * cols), F32)],
        compiler_params=PARAMS,
        name="scatter_last" if last else "scatter_next",
    )(*operands)
    return out


def gather_from(fields, row_at, col_at, seen, table, group):
    rows, cols = fields[0].shape
    half_rows, half_cols = len(fields) // 2 * rows, 2 * cols
    for level, field in enumerate(fields):
        high, low = parts(field.T)
        c, r = level % 2 * cols, level // 2 * rows
        table[c : c + cols, r : r + rows] = high
        table[c : c + cols, half_rows + r : half_rows + r + rows] = low
    row_iota = index_iota(half_rows)
    sublane = lax.broadcasted_iota(jnp.int32, (8, 256), 0)

    def step(index, carry):
        base = pl.multiple_of(index * group, group)
        row_block = row_at[pl.ds(base, group)]
        col_block = col_at[pl.ds(base, group)].astype(jnp.int32)
        found = []
        for j in range(0, group, 2):
            hot = jnp.concatenate(
                [one_hot(row_iota, row_block[i : i + 1]) for i in (j, j + 1)], axis=1
            )
            hot = jnp.concatenate([hot, hot], axis=0)
            lines = jnp.dot(table[...], hot, preferred_element_type=F32)
            wanted = jnp.concatenate([col_block[j : j + 1], col_block[j + 1 : j + 2]], axis=1)
            wanted = jnp.broadcast_to(wanted, (8, 256))
            tiles = [lines[i : i + 8] for i in range(0, half_cols, 8)]
            bit = 8
            while len(tiles) > 1:
                upper = (wanted & bit) != 0
                tiles = [
                    jnp.where(upper, tiles[i + 1], tiles[i]) for i in range(0, len(tiles), 2)
                ]
                bit = bit * 2
            value = jnp.sum(
                jnp.where((wanted & 7) == sublane, tiles[0], 0.0), axis=0, keepdims=True
            )
            found += [value[:, :128], value[:, 128:]]
        seen[pl.ds(base, group)] = jnp.concatenate(found, axis=0)
        return carry

    lax.fori_loop(0, row_at.shape[0] // group, step, 0)


def own_part(field, level, rows):
    return field[level, EDGE + HALO : EDGE + HALO + rows]


def total_of(pairs):
    added = None
    for left, right in pairs:
        term = left * right
        added = term if added is None else added + term
    return jnp.sum(added)


def observe_first_kernel(source, *refs):
    halo, weights, sigma, row_at, col_at = refs[:3], refs[3], refs[4], refs[5], refs[6]
    seen, right, image, sums, field, spare, table = refs[7:]
    levels, rows, cols = source.shape
    place(field, source, halo)
    clear_margins(spare)
    spare, field = smooth(field, spare, weights, 0, 80, False)
    right[...] = field[:, EDGE : EDGE + rows + 2 * HALO]
    own = [own_part(field, level, rows) for level in range(levels)]
    sums[...] = lanes([total_of([(value, value) for value in own])], 8)
    spare, field = smooth(field, spare, weights, 8, 72, False)
    fields = [sigma[level] * own_part(field, level, rows) for level in range(levels)]
    for level in range(levels):
        image[level] = fields[level]
    gather_from(fields, row_at, col_at, seen, table, 64)


def observe_next_kernel(source, *refs):
    halo, weights, sigma, row_at, col_at = refs[:3], refs[3], refs[4], refs[5], refs[6]
    right, scalars = refs[7:9]
    seen, residual, image, sums, field, spare, table = refs[9:]
    levels, rows, cols = source.shape
    tall = rows + 2 * HALO
    norm, product = lane_value(scalars[0:1], 0), lane_value(scalars[0:1], 1)
    alpha = norm / (norm + product)
    place(field, source, halo)
    clear_margins(spare)
    spare, field = smooth(field, spare, weights, 0, 32, True)

    for tile in range(levels + 1):
        first = right[tile]
        field[tile, EDGE : EDGE + tall] = first - alpha * (first + field[tile, EDGE : EDGE + tall])
    own = [own_part(field, level, rows) for level in range(levels)]
    first = [right[level, HALO : HALO + rows] for level in range(levels)]
    for level in range(levels):
        residual[level] = own[level]
    sums[...] = lanes(
        [total_of([(value, value) for value in own]), total_of(list(zip(own, first)))], 8
    )
    spare, field = smooth(field, spare, weights, 8, 48, True)
    fields = [sigma[level] * own_part(field, level, rows) for level in range(levels)]
    for level in range(levels):
        image[level] = fields[level]
    gather_from(fields, row_at, col_at, seen, table, 128)


def observe(source, halo, weights, sigma, row_at, col_at, right=None, scalars=None):
    levels, rows, cols = sigma.shape
    tall = rows + 2 * HALO
    slots = row_at.shape[0]
    first = right is None
    kept = (levels + 1, tall, cols) if first else (levels, rows, cols)
    shapes = [(slots, 128), kept, (levels, rows, cols), (8, 128)]
    operands = [source, *halo, weights, sigma, row_at, col_at]
    operands += [] if first else [right, scalars]
    return pl.pallas_call(
        observe_first_kernel if first else observe_next_kernel,
        out_shape=[jax.ShapeDtypeStruct(shape, F32) for shape in shapes],
        in_specs=[VMEM] * len(operands),
        out_specs=[VMEM] * len(shapes),
        scratch_shapes=[
            pltpu.VMEM((levels + 1, tall + 2 * EDGE, cols), F32),
            pltpu.VMEM((levels + 1, tall + 2 * EDGE, cols), F32),
            pltpu.VMEM(
                (2 * cols, levels * rows), BF16
            ),
        ],
        compiler_params=PARAMS,
        name="observe_first" if first else "observe_next",
    )(*operands)


def finish_kernel(source, *refs):
    halo, weights, right, residual_one, image_zero, image_one, scalars = refs[:3], *refs[3:9]
    increment, residual, field, spare = refs[9:]
    levels, rows, cols = source.shape
    norm_zero, norm_one, cross, product_zero, product_one, product_cross = [
        lane_value(scalars[0:1], index) for index in range(6)
    ]
    alpha_zero = norm_zero / (norm_zero + product_zero)
    beta = norm_one / norm_zero
    square = norm_one + 2.0 * beta * cross + beta * beta * norm_zero
    seen = product_one + 2.0 * beta * product_cross + beta * beta * product_zero
    alpha_one = norm_one / (square + seen)
    for level in range(levels):
        direction = image_one[level] + beta * image_zero[level]
        increment[level] = alpha_zero * image_zero[level] + alpha_one * direction
    place(field, source, halo)
    clear_margins(spare)
    spare, field = smooth(field, spare, weights, 8, 48, False)
    for level in range(levels):
        here = residual_one[level]
        direction = here + beta * right[level, HALO : HALO + rows]
        image = direction + own_part(field, level, rows)
        residual[level] = here - alpha_one * image


def finish(source, halo, weights, right, residual_one, image_zero, image_one, scalars):
    levels, rows, cols = source.shape
    tall = rows + 2 * HALO
    return pl.pallas_call(
        finish_kernel,
        out_shape=[jax.ShapeDtypeStruct((levels, rows, cols), F32)] * 2,
        in_specs=[VMEM] * 10,
        out_specs=[VMEM] * 2,
        scratch_shapes=[pltpu.VMEM((levels + 1, tall + 2 * EDGE, cols), F32),
            pltpu.VMEM((levels + 1, tall + 2 * EDGE, cols), F32)],
        compiler_params=PARAMS,
        name="finish",
    )(source, *halo, weights, right, residual_one, image_zero, image_one, scalars)


def apply_blocks(values, weights, at):
    high, low = parts(values)
    first = jnp.concatenate([high, low, jnp.zeros((128 - 2 * GROUP, 128), BF16)], axis=0)
    second = jnp.concatenate([high, jnp.zeros((128 - GROUP, 128), BF16)], axis=0)
    right = jnp.concatenate([first, second], axis=1)
    lane = lane_of(128)
    column = jnp.where(lane < 2 * GROUP, lane % GROUP, GROUP)
    kept = jnp.zeros((128, 128), F32)
    for start in range(0, GROUP, 4):
        matrix = weights[at + start : at + start + 4].reshape(4 * 128, 128)
        left = jnp.concatenate(parts(matrix), axis=1)
        product = lax.dot_general(left, right, (((1,), (1,)), ((), ())), preferred_element_type=F32)
        for k in range(4):
            kept = jnp.where(column == start + k, product[k * 128 : (k + 1) * 128], kept)
    kept = kept.T
    return kept[:GROUP] + kept[GROUP : 2 * GROUP]


def start_kernel(capacity, owner, cells, innovations, weights, mask, east, north, *refs):
    parcel, places, products, sides = refs[:4]
    count, held_cells, held_values, held_weights, held_mask, held_faces, arrived = refs[4:]
    held = held_cells.shape[0]
    levels = mask.shape[0]
    steps = held // GROUP
    moves = [
        (innovations, held_values),
        (cells, held_cells),
        (mask, held_mask),
        (east, held_faces.at[0]),
        (north, held_faces.at[1]),
    ]
    for step in range(steps):
        block = pl.ds(step * GROUP, GROUP)
        moves.append((weights.at[block], held_weights.at[block]))
    copies = [
        pltpu.make_async_copy(source, target, arrived.at[index])
        for index, (source, target) in enumerate(moves)
    ]
    for copy in copies:
        copy.start()
    parcel[...] = jnp.zeros_like(parcel)
    for index in range(count.shape[0]):
        count[index] = 0
    for index in range(held):
        target = owner[index]
        rank = count[target]
        count[target] = rank + 1
        places[index] = target * capacity + rank
        places[held + index] = target * (capacity + 1) + rank
    copies[0].wait()
    copies[1].wait()
    for step in range(steps):
        copies[5 + step].wait()
        first = step * GROUP
        result = apply_blocks(held_values[first : first + GROUP], held_weights, first)
        cell_rows = held_cells[first : first + GROUP].astype(F32)
        for k in range(GROUP):
            at = places[first + k] + owner[first + k] * capacity
            parcel[pl.ds(at, 1), :] = cell_rows[k : k + 1]
            parcel[pl.ds(at + capacity, 1), :] = result[k : k + 1]
    for copy in copies[2:5]:
        copy.wait()
    for index in range(2):
        fields = [held_mask[level].astype(F32) * held_faces[index, level] for level in range(levels)]
        for level in range(levels):
            products[index, level] = fields[level]
        sides[index] = pack_sides(fields)


def start(owner, cells, innovations, weights, mask, east, north, devices, capacity):
    held, width = cells.shape
    shapes = [(devices * 2 * capacity, width), (2 * held,), (2,) + mask.shape, (2,) + mask.shape[1:]]
    types = [F32, jnp.int32, F32, F32]
    return pl.pallas_call(
        functools.partial(start_kernel, capacity),
        out_shape=[jax.ShapeDtypeStruct(shape, kind) for shape, kind in zip(shapes, types)],
        in_specs=[SMEM] + [HBM] * 6,
        out_specs=[VMEM, SMEM, VMEM, VMEM],
        scratch_shapes=[
            pltpu.SMEM((devices,), jnp.int32),
            pltpu.VMEM((held, width), jnp.int32),
            pltpu.VMEM((held, width), F32),
            pltpu.VMEM((held, width, width), F32),
            pltpu.VMEM(mask.shape, jnp.int32),
            pltpu.VMEM((2,) + mask.shape, F32),
            pltpu.SemaphoreType.DMA((5 + held // GROUP,)),
        ],
        compiler_params=ROOMLESS,
        name="start",
    )(owner, cells, innovations, weights, mask, east, north)


def weigh_next_kernel(capacity, devices, last, places, returned, sums, weights, *refs):
    held = weights.shape[0]
    copies = []
    if last:
        sums_before, weighted_before, parcel = refs
    else:
        parcel, weighted, held_weights, arrived = refs
        for step in range(held // GROUP):
            block = pl.ds(step * GROUP, GROUP)
            copies.append(
                pltpu.make_async_copy(
                    weights.at[block], held_weights.at[block], arrived.at[step]
                )
            )
            copies[-1].start()
        weights = held_weights
    parcel[...] = jnp.zeros_like(parcel)
    total = jnp.zeros((GROUP, 128), F32)
    total_cross = jnp.zeros((GROUP, 128), F32)
    for first in range(0, held, GROUP):
        here = jnp.concatenate(
            [returned[pl.ds(places[first + k], 1), :] for k in range(GROUP)], axis=0
        )
        if copies:
            copies[first // GROUP].wait()
        result = apply_blocks(here, weights, first)
        total += here * result
        if last:
            total_cross += here * weighted_before[first : first + GROUP]
        else:
            weighted[first : first + GROUP] = result
        for k in range(GROUP):
            parcel[pl.ds(places[held + first + k], 1), :] = result[k : k + 1]
    if last:
        scalars = [
            lane_value(sums_before[0:1], 0) / devices,
            lane_value(sums[0:1], 0),
            lane_value(sums[0:1], 1),
            lane_value(sums_before[0:1], 1) / devices,
            jnp.sum(total),
            jnp.sum(total_cross),
        ]
    else:
        scalars = [lane_value(sums[0:1], 0), jnp.sum(total)]
    row = lanes(scalars, 1)
    for target in range(devices):
        at = target * (capacity + 1) + capacity
        parcel[at : at + 1] = row


def weigh_next(places, returned, sums, weights, devices, capacity, before=None):
    held, width = weights.shape[:2]
    last = before is not None
    operands = [places, returned, sums, weights] + (list(before) if last else [])
    out_shape = [jax.ShapeDtypeStruct((devices * (capacity + 1), width), F32)]
    if not last:
        out_shape += [jax.ShapeDtypeStruct((held, width), F32)]
    return pl.pallas_call(
        functools.partial(weigh_next_kernel, capacity, devices, last),
        out_shape=out_shape,
        in_specs=[SMEM, VMEM, VMEM, VMEM if last else HBM] + [VMEM] * (len(operands) - 4),
        out_specs=[VMEM] * len(out_shape),
        scratch_shapes=[]
        if last
        else [pltpu.VMEM(weights.shape, F32), pltpu.SemaphoreType.DMA((held // GROUP,))],
        compiler_params=PARAMS if last else SNUG,
        name="weigh_last" if last else "weigh_next",
    )(*operands)


def swap(block):
    devices = lax.axis_size("lat") * lax.axis_size("lon")
    shares = block.reshape(devices, block.shape[0] // devices, 1, block.shape[1])
    got = lax.all_to_all(shares, ("lat", "lon"), split_axis=0, concat_axis=0, tiled=True)
    return got.reshape(block.shape)


def body(sigma, east_coef, north_coef, mask, innovations, cells, owner, obs_weights):
    devices = lax.axis_size("lat") * lax.axis_size("lon")
    held, width = cells.shape
    capacity = max(2, (2 * held + devices - 1) // devices)

    parcel, places, products, sides = start(
        owner.reshape(held),
        cells,
        innovations,
        obs_weights,
        mask,
        east_coef,
        north_coef,
        devices,
        capacity,
    )
    mixed, down, up, products = exchange_columns(products, sides, True)
    arrived = swap(parcel)
    weights = face_weights(products, exchange_rows(down, up) + (mixed,))

    row_at, col_at, field, sides = scatter_first(arrived, sigma, capacity)
    seen, right, image_zero, sums = observe(
        field, exchange(field, sides), weights, sigma, row_at, col_at
    )
    returned = swap(seen)
    parcel, weighted = weigh_next(places, returned, sums, obs_weights, devices, capacity)
    arrived = swap(parcel)

    field_zero, sides, scalars_zero = scatter_next(arrived, row_at, col_at, sigma, capacity)
    seen, residual_one, image_one, sums = observe(
        field_zero, exchange(field_zero, sides), weights, sigma, row_at, col_at, right, scalars_zero
    )
    returned = swap(seen)
    (parcel,) = weigh_next(
        places, returned, sums, obs_weights, devices, capacity, (scalars_zero, weighted)
    )
    arrived = swap(parcel)

    field, sides, scalars = scatter_next(arrived, row_at, col_at, sigma, capacity, field_zero)
    increment, residual = finish(
        field, exchange(field, sides), weights, right, residual_one, image_zero, image_one, scalars
    )
    return (increment, residual)


def solution(mesh):
    return jax.shard_map(
        body,
        mesh=mesh,
        in_specs=(
            P(None, "lat", "lon"),
            P(None, "lat", "lon"),
            P(None, "lat", "lon"),
            P(None, "lat", "lon"),
            P(("lat", "lon"), None),
            P(("lat", "lon"), None),
            P(("lat", "lon"), None),
            P(("lat", "lon"), None, None),
        ),
        out_specs=(P(None, "lat", "lon"), P(None, "lat", "lon")),
        check_vma=False,
    )
```

```python
import functools

import jax
import jax.numpy as jnp
from jax import lax
from jax.experimental import pallas as pl
from jax.experimental.pallas import tpu as pltpu
from jax.sharding import PartitionSpec as P

PASSES = 5
HALO = 16
EDGE = 8
GROUP = 16
AHEAD = 3
F32 = jnp.float32
BF16 = jnp.bfloat16
VMEM = pl.BlockSpec(memory_space=pltpu.VMEM)
HBM = pl.BlockSpec(memory_space=pltpu.HBM)
SMEM = pl.BlockSpec(memory_space=pltpu.SMEM)
PARAMS = pltpu.CompilerParams(vmem_limit_bytes=32 * 1024 * 1024)

ROOMLESS = pltpu.CompilerParams(vmem_limit_bytes=60 * 1024 * 1024)


SNUG = pltpu.CompilerParams(vmem_limit_bytes=52 * 1024 * 1024)


def parts(values):
    high = values.astype(BF16)
    low = (values - high.astype(F32)).astype(BF16)
    return high, low


def lane_of(rows):
    return lax.broadcasted_iota(jnp.int32, (rows, 128), 1)


def pack_sides(fields):
    lane = lane_of(fields[0].shape[0])
    packed = jnp.zeros_like(fields[0])
    for level, field in enumerate(fields):
        start = 2 * HALO * level
        turned = pltpu.roll(field, (start + HALO) % 128, 1)
        packed = jnp.where((lane >= start) & (lane < start + 2 * HALO), turned, packed)
    return packed


def turn_kernel(fields, from_east, from_west, mixed, down, up, *kept):
    levels, rows, _ = fields.shape[-3:]
    for ref in kept:
        ref[...] = fields[...]
    western = lane_of(rows) % (2 * HALO) < HALO
    for index in range(fields.shape[0] if len(fields.shape) == 4 else 1):
        at = (index,) if len(fields.shape) == 4 else ()
        sides = jnp.where(western, from_west[at + (...,)], from_east[at + (...,)])
        mixed[at + (...,)] = sides
        for level in range(levels):
            down[at + (level,)] = fields[at + (level, slice(rows - HALO, rows))]
            up[at + (level,)] = fields[at + (level, slice(0, HALO))]
        down[at + (levels,)] = sides[rows - HALO :]
        up[at + (levels,)] = sides[:HALO]


def exchange(fields, sides):
    mixed, down, up = exchange_columns(fields, sides)
    return exchange_rows(down, up) + (mixed,)


def exchange_columns(fields, sides, keep=False):
    *lead, levels, rows, cols = fields.shape
    wide = lax.axis_size("lon")
    east = [(i, (i + 1) % wide) for i in range(wide)]
    from_west = lax.ppermute(sides, "lon", east)
    from_east = lax.ppermute(sides, "lon", [(to, at) for at, to in east])
    shapes = [(*lead, rows, cols)] + [(*lead, levels + 1, HALO, cols)] * 2
    shapes += [fields.shape] if keep else []
    return pl.pallas_call(
        turn_kernel,
        out_shape=[jax.ShapeDtypeStruct(shape, F32) for shape in shapes],
        in_specs=[VMEM] * 3,
        out_specs=[VMEM] * len(shapes),
        compiler_params=PARAMS,
        name="turn",
    )(fields, from_east, from_west)


def exchange_rows(down, up):
    tall = lax.axis_size("lat")
    first = [(i, i + 1) for i in range(0, tall - 1, 2)]
    second = [(i, i + 1) for i in range(1, tall - 1, 2)]
    even = lax.axis_index("lat") % 2 == 0
    one = lax.ppermute(
        jnp.where(even, down, up), "lat", first + [(to, at) for at, to in first]
    )
    two = lax.ppermute(
        jnp.where(even, up, down), "lat", second + [(to, at) for at, to in second]
    )
    return jnp.where(even, two, one), jnp.where(even, one, two)


def neighbours(tiles):
    lane = lane_of(tiles[0].shape[0])
    later, earlier = tiles[1:] + tiles[:1], tiles[-1:] + tiles[:-1]
    after = [
        pltpu.roll(jnp.where(lane == 0, other, tile), 127, 1) for tile, other in zip(tiles, later)
    ]
    before = [
        pltpu.roll(jnp.where(lane == 127, other, tile), 1, 1) for tile, other in zip(tiles, earlier)
    ]
    return after, before


def lay_out(fields, side):
    lane = lane_of(side.shape[0])
    width = 2 * HALO
    turned = [pltpu.roll(field, width * level + HALO, 1) for level, field in enumerate(fields)]
    tiles = []
    for tile in range(len(fields) + 1):
        left, right = width * tile - HALO, width * tile + HALO
        before = turned[tile - 1] if tile else turned[0]
        after = turned[tile] if tile < len(fields) else turned[-1]
        value = jnp.where(lane < left, before, after)
        tiles.append(jnp.where((lane >= left) & (lane < right), side, value))
    return tiles


def pick_out(first, second, level):
    start = 2 * HALO * level + HALO
    return pltpu.roll(jnp.where(lane_of(first.shape[0]) >= start, first, second), 128 - start, 1)


def place(target, own, halo, lead=()):
    before, after, mixed = halo
    levels = before.shape[-3] - 1
    rows = mixed.shape[-2]
    spans = (
        (EDGE, before, before[lead + (levels,)]),
        (EDGE + HALO, own, mixed[lead + (...,)]),
        (EDGE + HALO + rows, after, after[lead + (levels,)]),
    )
    for start, source, side in spans:
        tiles = lay_out([source[lead + (level,)] for level in range(levels)], side)
        for tile, value in enumerate(tiles):
            target[lead + (tile, slice(start, start + side.shape[0]))] = value
    blank = jnp.zeros((EDGE, 128), F32)
    for tile in range(levels + 1):
        target[lead + (tile, slice(0, EDGE))] = blank
        target[lead + (tile, slice(EDGE + 2 * HALO + rows, 2 * EDGE + 2 * HALO + rows))] = blank


def clear_margins(target):
    blank = jnp.zeros((target.shape[0], EDGE, 128), F32)
    target[:, 0:EDGE] = blank
    target[:, target.shape[1] - EDGE :] = blank


def face_kernel(products, before, after, mixed, weights, padded, faces):
    tiles, tall = weights.shape[1:3]
    for index in range(2):
        place(padded, products, (before, after, mixed), (index,))
    inner = slice(EDGE, EDGE + tall)
    faces[:, 0:EDGE] = jnp.zeros((tiles, EDGE, 128), F32)
    faces[:, EDGE + tall :] = jnp.zeros((tiles, EDGE, 128), F32)
    land = [(padded[0, tile, inner] > 0.0).astype(F32) for tile in range(tiles)]
    land_east, _ = neighbours(land)
    east_face = [padded[0, tile, inner] * land_east[tile] for tile in range(tiles)]
    _, west_face = neighbours(east_face)
    for tile in range(tiles):
        land_north = (padded[0, tile, EDGE + 1 : EDGE + 1 + tall] > 0.0).astype(F32)
        north_face = padded[1, tile, inner] * land_north
        faces[tile, inner] = north_face
        south_face = faces[tile, EDGE - 1 : EDGE - 1 + tall]
        weights[0, tile] = 1.0 - (
            ((east_face[tile] + west_face[tile]) + north_face) + south_face
        )
        weights[1, tile] = east_face[tile]
        weights[2, tile] = west_face[tile]
        weights[3, tile] = north_face
        weights[4, tile] = south_face


def face_weights(products, halo):
    _, levels, rows, cols = products.shape
    tall = rows + 2 * HALO
    return pl.pallas_call(
        face_kernel,
        out_shape=jax.ShapeDtypeStruct((5, levels + 1, tall, cols), F32),
        in_specs=[VMEM] * 4,
        out_specs=VMEM,
        scratch_shapes=[
            pltpu.VMEM((2, levels + 1, tall + 2 * EDGE, cols), F32),
            pltpu.VMEM((levels + 1, tall + 2 * EDGE, cols), F32),
        ],
        compiler_params=PARAMS,
        name="face_weights",
    )(products, *halo)


def sweep(source, target, weights, rows_from, rows_to, block):
    tiles = source.shape[0]

    def step(index, carry):
        first = pl.multiple_of(rows_from + index * block, 8)
        for start in range(0, block, 16):
            count = min(16, block - start)
            at = pl.multiple_of(first + EDGE + start, 8)
            inner = pl.ds(pl.multiple_of(first + start, 8), count)
            here = [source[tile, pl.ds(at, count)] for tile in range(tiles)]
            east, west = neighbours(here)
            for tile in range(tiles):
                above = source[tile, pl.ds(at + 1, count)]
                below = source[tile, pl.ds(at - 1, count)]
                total = weights[0, tile, inner] * here[tile]
                total += weights[1, tile, inner] * east[tile]
                total += weights[2, tile, inner] * west[tile]
                total += weights[3, tile, inner] * above
                total += weights[4, tile, inner] * below
                target[tile, pl.ds(at, count)] = total
        return carry

    lax.fori_loop(0, (rows_to - rows_from) // block, step, 0)


def smooth(field, spare, weights, skip, block, paired):
    tall = weights.shape[2]

    def two(index, carry):
        sweep(field, spare, weights, skip, tall - skip, block)
        sweep(spare, field, weights, skip, tall - skip, block)
        return carry

    if paired:
        lax.fori_loop(0, PASSES // 2, two, 0)
    else:
        for index in range(PASSES // 2):
            two(index, 0)
    sweep(field, spare, weights, skip, tall - skip, block)
    return field, spare


def index_iota(cells):
    return lax.broadcasted_iota(jnp.int32, (cells, 128), 0).astype(F32).astype(BF16)


def spread_row(row, count):
    return jnp.broadcast_to(jnp.broadcast_to(row, (16, 128)).astype(BF16)[0:1], (count, 128))


def one_hot(iota, row):
    count = iota.shape[0]
    return jnp.where(
        iota == spread_row(row, count), jnp.ones((count, 128), BF16), jnp.zeros((count, 128), BF16)
    )


def scatter_into(total, load_rows, slots, half_rows, half_cols, group, buffers=()):
    row_iota = index_iota(half_rows)
    col_iota = index_iota(half_cols)
    total[...] = jnp.zeros_like(total)

    def hots(index):
        high_rows, low_rows, columns = [], [], []
        for row_index, col_index, value in load_rows(index):
            high, low = parts(jnp.broadcast_to(value, (16, 128)))
            high = jnp.broadcast_to(high[0:1], (half_rows, 128))
            low = jnp.broadcast_to(low[0:1], (half_rows, 128))
            hit = row_iota == spread_row(row_index, half_rows)
            zero = jnp.zeros((half_rows, 128), BF16)
            high_rows.append(jnp.where(hit, high, zero))
            low_rows.append(jnp.where(hit, low, zero))
            columns.append(one_hot(col_iota, col_index))
        return high_rows + low_rows, columns + columns

    def add(left, right):
        total[...] += lax.dot_general(
            left, right, (((1,), (1,)), ((), ())), preferred_element_type=F32
        )

    def step(index, carry):
        left, right = hots(index)
        add(jnp.concatenate(left, axis=1), jnp.concatenate(right, axis=1))
        return carry

    if not buffers:
        lax.fori_loop(0, slots // group, step, 0)
        return
    left_one, right_one, left_two, right_two = buffers
    steps = slots // group

    def build(index, left, right):
        lefts, rights = hots(index)
        for j, value in enumerate(lefts):
            left[:, j * 128 : (j + 1) * 128] = value
        for j, value in enumerate(rights):
            right[:, j * 128 : (j + 1) * 128] = value

    def two(index, carry):
        build(2 * index + 1, left_two, right_two)
        add(left_one[...], right_one[...])
        build(jnp.minimum(2 * index + 2, steps - 1), left_one, right_one)
        add(left_two[...], right_two[...])
        return carry

    build(0, left_one, right_one)
    lax.fori_loop(0, steps // 2, two, 0)


def load_group(index, group, capacity, row_at, col_at, arrived, stride, first_slot):
    base = pl.multiple_of(index * group, group)
    row_block = row_at[pl.ds(base, group)]
    col_block = col_at[pl.ds(base, group)]
    for j in range(group):
        source = index * (group // capacity) + j // capacity
        at = source * stride + first_slot + j % capacity
        yield row_block[j : j + 1], col_block[j : j + 1], arrived[pl.ds(at, 1)]


def split_cells(cells, rows, cols):
    level = cells // (rows * cols)
    row = (cells // cols) % rows
    col = cells % cols
    return (level // 2) * rows + row, (level % 2) * cols + col


def put_field(total, sigma, field, extra=None):
    levels, rows, cols = sigma.shape
    fields = []
    for level in range(levels):
        r, c = level // 2 * rows, level % 2 * cols
        value = total[r : r + rows, c : c + cols]
        value = sigma[level] * value
        if extra is not None:
            value = value + extra(level)
        field[level] = value
        fields.append(value)
    return fields


def scatter_first_kernel(capacity, arrived, sigma, row_at, col_at, field, *refs):
    sides, total = refs
    levels, rows, cols = sigma.shape
    stride = 2 * capacity
    cells = jnp.concatenate(
        [arrived[at : at + capacity] for at in range(0, arrived.shape[0], stride)], axis=0
    )
    row_index, col_index = split_cells(cells.astype(jnp.int32), rows, cols)
    row_at[...] = row_index.astype(F32)
    col_at[...] = col_index.astype(F32)

    def load(index):
        return load_group(index, 64, capacity, row_at, col_at, arrived, stride, capacity)

    scatter_into(total, load, row_at.shape[0], levels // 2 * rows, 2 * cols, 64)
    sides[...] = pack_sides(put_field(total, sigma, field))


def scatter_first(arrived, sigma, capacity):
    levels, rows, cols = sigma.shape
    slots = arrived.shape[0] // 2
    shapes = [(slots, 128), (slots, 128), (levels, rows, cols), (rows, cols)]
    out = pl.pallas_call(
        functools.partial(scatter_first_kernel, capacity),
        out_shape=[jax.ShapeDtypeStruct(shape, F32) for shape in shapes],
        in_specs=[VMEM] * 2,
        out_specs=[VMEM] * len(shapes),
        scratch_shapes=[pltpu.VMEM((levels // 2 * rows, 2 * cols), F32)],
        compiler_params=PARAMS,
        name="scatter_first",
    )(arrived, sigma)
    return out


def lane_value(block, lane):
    return jnp.sum(jnp.where(lane_of(block.shape[0]) == lane, block, 0.0))


def lanes(values, rows):
    lane = lane_of(rows)
    out = jnp.zeros((rows, 128), F32)
    for index, value in enumerate(values):
        out = jnp.where(lane == index, value, out)
    return out


def scatter_next_kernel(capacity, last, arrived, row_at, col_at, sigma, *refs):
    if last:
        previous, field, sides, sums, total, *buffers = refs
    else:
        previous, (field, sides, sums, total, *buffers) = None, refs
    levels, rows, cols = sigma.shape
    stride = capacity + 1
    gathered = jnp.concatenate(
        [arrived[at : at + 1] for at in range(capacity, arrived.shape[0], stride)], axis=0
    )
    added = jnp.sum(gathered, axis=0, keepdims=True)
    sums[...] = jnp.broadcast_to(added, (8, 128))

    group = 32 if last else 16

    def load(index):
        return load_group(index, group, capacity, row_at, col_at, arrived, stride, 0)

    scatter_into(
        total, load, row_at.shape[0], levels // 2 * rows, 2 * cols, group, buffers
    )
    extra = None
    if last:
        beta = lane_value(added, 1) / lane_value(added, 0)

        def extra(level):
            return beta * previous[level]

    sides[...] = pack_sides(put_field(total, sigma, field, extra))


def scatter_next(arrived, row_at, col_at, sigma, capacity, previous=None):
    levels, rows, cols = sigma.shape
    last = previous is not None
    shapes = [(levels, rows, cols), (rows, cols), (8, 128)]
    operands = [arrived, row_at, col_at, sigma] + ([previous] if last else [])
    out = pl.pallas_call(
        functools.partial(scatter_next_kernel, capacity, last),
        out_shape=[jax.ShapeDtypeStruct(shape, F32) for shape in shapes],
        in_specs=[VMEM] * len(operands),
        out_specs=[VMEM] * len(shapes),
        scratch_shapes=[pltpu.VMEM((levels // 2 * rows, 2 * cols), F32)]
        + [
            pltpu.VMEM((levels // 2 * rows, 2 * 128 * (32 if last else 16)), BF16),
            pltpu.VMEM((2 * cols, 2 * 128 * (32 if last else 16)), BF16),
        ]
        * 2,
        compiler_params=PARAMS,
        name="scatter_last" if last else "scatter_next",
    )(*operands)
    return out


def gather_from(fields, row_at, col_at, seen, table, group):
    rows, cols = fields[0].shape
    half_rows, half_cols = len(fields) // 2 * rows, 2 * cols
    for level, field in enumerate(fields):
        high, low = parts(field.T)
        c, r = level % 2 * cols, level // 2 * rows
        table[c : c + cols, r : r + rows] = high
        table[c : c + cols, half_rows + r : half_rows + r + rows] = low
    row_iota = index_iota(half_rows)
    sublane = lax.broadcasted_iota(jnp.int32, (8, 256), 0)

    def step(index, carry):
        base = pl.multiple_of(index * group, group)
        row_block = row_at[pl.ds(base, group)]
        col_block = col_at[pl.ds(base, group)].astype(jnp.int32)
        found = []
        for j in range(0, group, 2):
            hot = jnp.concatenate(
                [one_hot(row_iota, row_block[i : i + 1]) for i in (j, j + 1)], axis=1
            )
            hot = jnp.concatenate([hot, hot], axis=0)
            lines = jnp.dot(table[...], hot, preferred_element_type=F32)
            wanted = jnp.concatenate([col_block[j : j + 1], col_block[j + 1 : j + 2]], axis=1)
            wanted = jnp.broadcast_to(wanted, (8, 256))
            tiles = [lines[i : i + 8] for i in range(0, half_cols, 8)]
            bit = 8
            while len(tiles) > 1:
                upper = (wanted & bit) != 0
                tiles = [
                    jnp.where(upper, tiles[i + 1], tiles[i]) for i in range(0, len(tiles), 2)
                ]
                bit = bit * 2
            value = jnp.sum(
                jnp.where((wanted & 7) == sublane, tiles[0], 0.0), axis=0, keepdims=True
            )
            found += [value[:, :128], value[:, 128:]]
        seen[pl.ds(base, group)] = jnp.concatenate(found, axis=0)
        return carry

    lax.fori_loop(0, row_at.shape[0] // group, step, 0)


def own_part(field, level, rows):
    inner = slice(EDGE + HALO, EDGE + HALO + rows)
    return pick_out(field[level, inner], field[level + 1, inner], level)


def total_of(pairs):
    added = None
    for left, right in pairs:
        term = left * right
        added = term if added is None else added + term
    return jnp.sum(added)


def observe_first_kernel(source, *refs):
    halo, weights, sigma, row_at, col_at = refs[:3], refs[3], refs[4], refs[5], refs[6]
    seen, right, image, sums, field, spare, table = refs[7:]
    levels, rows, cols = source.shape
    place(field, source, halo)
    clear_margins(spare)
    spare, field = smooth(field, spare, weights, 0, 32, True)
    right[...] = field[:, EDGE : EDGE + rows + 2 * HALO]
    own = [own_part(field, level, rows) for level in range(levels)]
    sums[...] = lanes([total_of([(value, value) for value in own])], 8)
    spare, field = smooth(field, spare, weights, 8, 48, True)
    fields = [sigma[level] * own_part(field, level, rows) for level in range(levels)]
    for level in range(levels):
        image[level] = fields[level]
    gather_from(fields, row_at, col_at, seen, table, 32)


def observe_next_kernel(source, *refs):
    halo, weights, sigma, row_at, col_at = refs[:3], refs[3], refs[4], refs[5], refs[6]
    right, scalars = refs[7:9]
    seen, residual, image, sums, field, spare, table = refs[9:]
    levels, rows, cols = source.shape
    tall = rows + 2 * HALO
    norm, product = lane_value(scalars[0:1], 0), lane_value(scalars[0:1], 1)
    alpha = norm / (norm + product)
    place(field, source, halo)
    clear_margins(spare)
    spare, field = smooth(field, spare, weights, 0, 32, True)

    for tile in range(levels + 1):
        first = right[tile]
        field[tile, EDGE : EDGE + tall] = first - alpha * (first + field[tile, EDGE : EDGE + tall])
    own = [own_part(field, level, rows) for level in range(levels)]
    first = [pick_out(
            right[level, HALO : HALO + rows], right[level + 1, HALO : HALO + rows], level
        ) for level in range(levels)]
    for level in range(levels):
        residual[level] = own[level]
    sums[...] = lanes(
        [total_of([(value, value) for value in own]), total_of(list(zip(own, first)))], 8
    )
    spare, field = smooth(field, spare, weights, 8, 48, True)
    fields = [sigma[level] * own_part(field, level, rows) for level in range(levels)]
    for level in range(levels):
        image[level] = fields[level]
    gather_from(fields, row_at, col_at, seen, table, 64)


def observe(source, halo, weights, sigma, row_at, col_at, right=None, scalars=None):
    levels, rows, cols = sigma.shape
    tall = rows + 2 * HALO
    slots = row_at.shape[0]
    first = right is None
    kept = (levels + 1, tall, cols) if first else (levels, rows, cols)
    shapes = [(slots, 128), kept, (levels, rows, cols), (8, 128)]
    operands = [source, *halo, weights, sigma, row_at, col_at]
    operands += [] if first else [right, scalars]
    return pl.pallas_call(
        observe_first_kernel if first else observe_next_kernel,
        out_shape=[jax.ShapeDtypeStruct(shape, F32) for shape in shapes],
        in_specs=[VMEM] * len(operands),
        out_specs=[VMEM] * len(shapes),
        scratch_shapes=[
            pltpu.VMEM((levels + 1, tall + 2 * EDGE, cols), F32),
            pltpu.VMEM((levels + 1, tall + 2 * EDGE, cols), F32),
            pltpu.VMEM(
                (2 * cols, levels * rows), BF16
            ),
        ],
        compiler_params=PARAMS,
        name="observe_first" if first else "observe_next",
    )(*operands)


def finish_kernel(source, *refs):
    halo, weights, right, residual_one, image_zero, image_one, scalars = refs[:3], *refs[3:9]
    increment, residual, field, spare = refs[9:]
    levels, rows, cols = source.shape
    norm_zero, norm_one, cross, product_zero, product_one, product_cross = [
        lane_value(scalars[0:1], index) for index in range(6)
    ]
    alpha_zero = norm_zero / (norm_zero + product_zero)
    beta = norm_one / norm_zero
    square = norm_one + 2.0 * beta * cross + beta * beta * norm_zero
    seen = product_one + 2.0 * beta * product_cross + beta * beta * product_zero
    alpha_one = norm_one / (square + seen)
    for level in range(levels):
        direction = image_one[level] + beta * image_zero[level]
        increment[level] = alpha_zero * image_zero[level] + alpha_one * direction
    place(field, source, halo)
    clear_margins(spare)
    spare, field = smooth(field, spare, weights, 8, 48, True)
    for level in range(levels):
        here = residual_one[level]
        direction = here + beta * pick_out(
            right[level, HALO : HALO + rows], right[level + 1, HALO : HALO + rows], level
        )
        image = direction + own_part(field, level, rows)
        residual[level] = here - alpha_one * image


def finish(source, halo, weights, right, residual_one, image_zero, image_one, scalars):
    levels, rows, cols = source.shape
    tall = rows + 2 * HALO
    return pl.pallas_call(
        finish_kernel,
        out_shape=[jax.ShapeDtypeStruct((levels, rows, cols), F32)] * 2,
        in_specs=[VMEM] * 10,
        out_specs=[VMEM] * 2,
        scratch_shapes=[pltpu.VMEM((levels + 1, tall + 2 * EDGE, cols), F32),
            pltpu.VMEM((levels + 1, tall + 2 * EDGE, cols), F32)],
        compiler_params=PARAMS,
        name="finish",
    )(source, *halo, weights, right, residual_one, image_zero, image_one, scalars)


def apply_blocks(values, weights, at):
    high, low = parts(values)
    first = jnp.concatenate([high, low, jnp.zeros((128 - 2 * GROUP, 128), BF16)], axis=0)
    second = jnp.concatenate([high, jnp.zeros((128 - GROUP, 128), BF16)], axis=0)
    right = jnp.concatenate([first, second], axis=1)
    lane = lane_of(128)
    column = jnp.where(lane < 2 * GROUP, lane % GROUP, GROUP)
    kept = jnp.zeros((128, 128), F32)
    for start in range(0, GROUP, 4):
        matrix = weights[at + start : at + start + 4].reshape(4 * 128, 128)
        left = jnp.concatenate(parts(matrix), axis=1)
        product = lax.dot_general(left, right, (((1,), (1,)), ((), ())), preferred_element_type=F32)
        for k in range(4):
            kept = jnp.where(column == start + k, product[k * 128 : (k + 1) * 128], kept)
    kept = kept.T
    return kept[:GROUP] + kept[GROUP : 2 * GROUP]


def start_kernel(capacity, owner, cells, innovations, weights, mask, east, north, *refs):
    parcel, places, products, sides = refs[:4]
    count, held_cells, held_values, held_weights, held_mask, held_faces, arrived = refs[4:]
    held = held_cells.shape[0]
    levels = mask.shape[0]
    steps = held // GROUP
    moves = [
        (innovations, held_values),
        (cells, held_cells),
        (mask, held_mask),
        (east, held_faces.at[0]),
        (north, held_faces.at[1]),
    ]
    for step in range(steps):
        block = pl.ds(step * GROUP, GROUP)
        moves.append((weights.at[block], held_weights.at[block]))
    copies = [
        pltpu.make_async_copy(source, target, arrived.at[index])
        for index, (source, target) in enumerate(moves)
    ]
    for copy in copies[: 5 + AHEAD]:
        copy.start()
    parcel[...] = jnp.zeros_like(parcel)
    for index in range(count.shape[0]):
        count[index] = 0
    for index in range(held):
        target = owner[index]
        rank = count[target]
        count[target] = rank + 1
        places[index] = target * capacity + rank
        places[held + index] = target * (capacity + 1) + rank
    copies[0].wait()
    copies[1].wait()
    for step in range(steps):
        copies[5 + step].wait()
        if step + AHEAD < steps:
            copies[5 + step + AHEAD].start()
        first = step * GROUP
        result = apply_blocks(held_values[first : first + GROUP], held_weights, first)
        cell_rows = held_cells[first : first + GROUP].astype(F32)
        for k in range(GROUP):
            at = places[first + k] + owner[first + k] * capacity
            parcel[pl.ds(at, 1), :] = cell_rows[k : k + 1]
            parcel[pl.ds(at + capacity, 1), :] = result[k : k + 1]
    for copy in copies[2:5]:
        copy.wait()
    for index in range(2):
        fields = [held_mask[level].astype(F32) * held_faces[index, level] for level in range(levels)]
        for level in range(levels):
            products[index, level] = fields[level]
        sides[index] = pack_sides(fields)


def start(owner, cells, innovations, weights, mask, east, north, devices, capacity):
    held, width = cells.shape
    shapes = [(devices * 2 * capacity, width), (2 * held,), (2,) + mask.shape, (2,) + mask.shape[1:]]
    types = [F32, jnp.int32, F32, F32]
    return pl.pallas_call(
        functools.partial(start_kernel, capacity),
        out_shape=[jax.ShapeDtypeStruct(shape, kind) for shape, kind in zip(shapes, types)],
        in_specs=[SMEM] + [HBM] * 6,
        out_specs=[VMEM, SMEM, VMEM, VMEM],
        scratch_shapes=[
            pltpu.SMEM((devices,), jnp.int32),
            pltpu.VMEM((held, width), jnp.int32),
            pltpu.VMEM((held, width), F32),
            pltpu.VMEM((held, width, width), F32),
            pltpu.VMEM(mask.shape, jnp.int32),
            pltpu.VMEM((2,) + mask.shape, F32),
            pltpu.SemaphoreType.DMA((5 + held // GROUP,)),
        ],
        compiler_params=ROOMLESS,
        name="start",
    )(owner, cells, innovations, weights, mask, east, north)


def weigh_next_kernel(capacity, devices, last, places, returned, sums, weights, *refs):
    held = weights.shape[0]
    copies = []
    if last:
        sums_before, weighted_before, parcel = refs
    else:
        parcel, weighted, held_weights, arrived = refs
        for step in range(held // GROUP):
            block = pl.ds(step * GROUP, GROUP)
            copies.append(
                pltpu.make_async_copy(
                    weights.at[block], held_weights.at[block], arrived.at[step]
                )
            )
        for copy in copies[:AHEAD]:
            copy.start()
        weights = held_weights
    parcel[...] = jnp.zeros_like(parcel)
    total = jnp.zeros((GROUP, 128), F32)
    total_cross = jnp.zeros((GROUP, 128), F32)
    for first in range(0, held, GROUP):
        here = jnp.concatenate(
            [returned[pl.ds(places[first + k], 1), :] for k in range(GROUP)], axis=0
        )
        if copies:
            step = first // GROUP
            copies[step].wait()
            if step + AHEAD < len(copies):
                copies[step + AHEAD].start()
        result = apply_blocks(here, weights, first)
        total += here * result
        if last:
            total_cross += here * weighted_before[first : first + GROUP]
        else:
            weighted[first : first + GROUP] = result
        for k in range(GROUP):
            parcel[pl.ds(places[held + first + k], 1), :] = result[k : k + 1]
    if last:
        scalars = [
            lane_value(sums_before[0:1], 0) / devices,
            lane_value(sums[0:1], 0),
            lane_value(sums[0:1], 1),
            lane_value(sums_before[0:1], 1) / devices,
            jnp.sum(total),
            jnp.sum(total_cross),
        ]
    else:
        scalars = [lane_value(sums[0:1], 0), jnp.sum(total)]
    row = lanes(scalars, 1)
    for target in range(devices):
        at = target * (capacity + 1) + capacity
        parcel[at : at + 1] = row


def weigh_next(places, returned, sums, weights, devices, capacity, before=None):
    held, width = weights.shape[:2]
    last = before is not None
    operands = [places, returned, sums, weights] + (list(before) if last else [])
    out_shape = [jax.ShapeDtypeStruct((devices * (capacity + 1), width), F32)]
    if not last:
        out_shape += [jax.ShapeDtypeStruct((held, width), F32)]
    return pl.pallas_call(
        functools.partial(weigh_next_kernel, capacity, devices, last),
        out_shape=out_shape,
        in_specs=[SMEM, VMEM, VMEM, VMEM if last else HBM] + [VMEM] * (len(operands) - 4),
        out_specs=[VMEM] * len(out_shape),
        scratch_shapes=[]
        if last
        else [pltpu.VMEM(weights.shape, F32), pltpu.SemaphoreType.DMA((held // GROUP,))],
        compiler_params=PARAMS if last else SNUG,
        name="weigh_last" if last else "weigh_next",
    )(*operands)


def swap(block):
    devices = lax.axis_size("lat") * lax.axis_size("lon")
    shares = block.reshape(devices, block.shape[0] // devices, 1, block.shape[1])
    got = lax.all_to_all(shares, ("lat", "lon"), split_axis=0, concat_axis=0, tiled=True)
    return got.reshape(block.shape)


def body(sigma, east_coef, north_coef, mask, innovations, cells, owner, obs_weights):
    devices = lax.axis_size("lat") * lax.axis_size("lon")
    held, width = cells.shape
    capacity = max(2, (2 * held + devices - 1) // devices)

    parcel, places, products, sides = start(
        owner.reshape(held),
        cells,
        innovations,
        obs_weights,
        mask,
        east_coef,
        north_coef,
        devices,
        capacity,
    )
    mixed, down, up, products = exchange_columns(products, sides, True)
    arrived = swap(parcel)
    weights = face_weights(products, exchange_rows(down, up) + (mixed,))

    row_at, col_at, field, sides = scatter_first(arrived, sigma, capacity)
    seen, right, image_zero, sums = observe(
        field, exchange(field, sides), weights, sigma, row_at, col_at
    )
    returned = swap(seen)
    parcel, weighted = weigh_next(places, returned, sums, obs_weights, devices, capacity)
    arrived = swap(parcel)

    field_zero, sides, scalars_zero = scatter_next(arrived, row_at, col_at, sigma, capacity)
    seen, residual_one, image_one, sums = observe(
        field_zero, exchange(field_zero, sides), weights, sigma, row_at, col_at, right, scalars_zero
    )
    returned = swap(seen)
    (parcel,) = weigh_next(
        places, returned, sums, obs_weights, devices, capacity, (scalars_zero, weighted)
    )
    arrived = swap(parcel)

    field, sides, scalars = scatter_next(arrived, row_at, col_at, sigma, capacity, field_zero)
    increment, residual = finish(
        field, exchange(field, sides), weights, right, residual_one, image_zero, image_one, scalars
    )
    return (increment, residual)


def solution(mesh):
    return jax.shard_map(
        body,
        mesh=mesh,
        in_specs=(
            P(None, "lat", "lon"),
            P(None, "lat", "lon"),
            P(None, "lat", "lon"),
            P(None, "lat", "lon"),
            P(("lat", "lon"), None),
            P(("lat", "lon"), None),
            P(("lat", "lon"), None),
            P(("lat", "lon"), None, None),
        ),
        out_specs=(P(None, "lat", "lon"), P(None, "lat", "lon")),
        check_vma=False,
    )
```

```python
import functools

import jax
import jax.numpy as jnp
from jax import lax
from jax.experimental import pallas as pl
from jax.experimental.pallas import tpu as pltpu
from jax.sharding import PartitionSpec as P

PASSES = 5
HALO = 16
EDGE = 8
GROUP = 16
CHUNK = 32
AHEAD = 2
F32 = jnp.float32
BF16 = jnp.bfloat16
VMEM = pl.BlockSpec(memory_space=pltpu.VMEM)
HBM = pl.BlockSpec(memory_space=pltpu.HBM)
SMEM = pl.BlockSpec(memory_space=pltpu.SMEM)
PARAMS = pltpu.CompilerParams(vmem_limit_bytes=32 * 1024 * 1024)

ROOMLESS = pltpu.CompilerParams(vmem_limit_bytes=60 * 1024 * 1024)


SNUG = pltpu.CompilerParams(vmem_limit_bytes=52 * 1024 * 1024)


def parts(values):
    high = values.astype(BF16)
    low = (values - high.astype(F32)).astype(BF16)
    return high, low


def lane_of(rows):
    return lax.broadcasted_iota(jnp.int32, (rows, 128), 1)


def pack_sides(fields):
    lane = lane_of(fields[0].shape[0])
    packed = jnp.zeros_like(fields[0])
    for level, field in enumerate(fields):
        start = 2 * HALO * level
        turned = pltpu.roll(field, (start + HALO) % 128, 1)
        packed = jnp.where((lane >= start) & (lane < start + 2 * HALO), turned, packed)
    return packed


def turn_kernel(fields, from_east, from_west, mixed, down, up, *kept):
    levels, rows, _ = fields.shape[-3:]
    for ref in kept:
        ref[...] = fields[...]
    western = lane_of(rows) % (2 * HALO) < HALO
    for index in range(fields.shape[0] if len(fields.shape) == 4 else 1):
        at = (index,) if len(fields.shape) == 4 else ()
        sides = jnp.where(western, from_west[at + (...,)], from_east[at + (...,)])
        mixed[at + (...,)] = sides
        for level in range(levels):
            down[at + (level,)] = fields[at + (level, slice(rows - HALO, rows))]
            up[at + (level,)] = fields[at + (level, slice(0, HALO))]
        down[at + (levels,)] = sides[rows - HALO :]
        up[at + (levels,)] = sides[:HALO]


def exchange(fields, sides):
    mixed, down, up = exchange_columns(fields, sides)
    return exchange_rows(down, up) + (mixed,)


def exchange_columns(fields, sides, keep=False):
    *lead, levels, rows, cols = fields.shape
    wide = lax.axis_size("lon")
    east = [(i, (i + 1) % wide) for i in range(wide)]
    from_west = lax.ppermute(sides, "lon", east)
    from_east = lax.ppermute(sides, "lon", [(to, at) for at, to in east])
    shapes = [(*lead, rows, cols)] + [(*lead, levels + 1, HALO, cols)] * 2
    shapes += [fields.shape] if keep else []
    return pl.pallas_call(
        turn_kernel,
        out_shape=[jax.ShapeDtypeStruct(shape, F32) for shape in shapes],
        in_specs=[VMEM] * 3,
        out_specs=[VMEM] * len(shapes),
        compiler_params=PARAMS,
        name="turn",
    )(fields, from_east, from_west)


def exchange_rows(down, up):
    tall = lax.axis_size("lat")
    first = [(i, i + 1) for i in range(0, tall - 1, 2)]
    second = [(i, i + 1) for i in range(1, tall - 1, 2)]
    even = lax.axis_index("lat") % 2 == 0
    one = lax.ppermute(
        jnp.where(even, down, up), "lat", first + [(to, at) for at, to in first]
    )
    two = lax.ppermute(
        jnp.where(even, up, down), "lat", second + [(to, at) for at, to in second]
    )
    return jnp.where(even, two, one), jnp.where(even, one, two)


def neighbours(tiles):
    lane = lane_of(tiles[0].shape[0])
    later, earlier = tiles[1:] + tiles[:1], tiles[-1:] + tiles[:-1]
    after = [
        pltpu.roll(jnp.where(lane == 0, other, tile), 127, 1) for tile, other in zip(tiles, later)
    ]
    before = [
        pltpu.roll(jnp.where(lane == 127, other, tile), 1, 1) for tile, other in zip(tiles, earlier)
    ]
    return after, before


def lay_out(fields, side):
    lane = lane_of(side.shape[0])
    width = 2 * HALO
    turned = [pltpu.roll(field, width * level + HALO, 1) for level, field in enumerate(fields)]
    tiles = []
    for tile in range(len(fields) + 1):
        left, right = width * tile - HALO, width * tile + HALO
        before = turned[tile - 1] if tile else turned[0]
        after = turned[tile] if tile < len(fields) else turned[-1]
        value = jnp.where(lane < left, before, after)
        tiles.append(jnp.where((lane >= left) & (lane < right), side, value))
    return tiles


def pick_out(first, second, level):
    start = 2 * HALO * level + HALO
    return pltpu.roll(jnp.where(lane_of(first.shape[0]) >= start, first, second), 128 - start, 1)


def place(target, own, halo, lead=()):
    before, after, mixed = halo
    levels = before.shape[-3] - 1
    rows = mixed.shape[-2]
    spans = (
        (EDGE, before, before[lead + (levels,)]),
        (EDGE + HALO, own, mixed[lead + (...,)]),
        (EDGE + HALO + rows, after, after[lead + (levels,)]),
    )
    for start, source, side in spans:
        tiles = lay_out([source[lead + (level,)] for level in range(levels)], side)
        for tile, value in enumerate(tiles):
            target[lead + (tile, slice(start, start + side.shape[0]))] = value
    blank = jnp.zeros((EDGE, 128), F32)
    for tile in range(levels + 1):
        target[lead + (tile, slice(0, EDGE))] = blank
        target[lead + (tile, slice(EDGE + 2 * HALO + rows, 2 * EDGE + 2 * HALO + rows))] = blank


def clear_margins(target):
    blank = jnp.zeros((target.shape[0], EDGE, 128), F32)
    target[:, 0:EDGE] = blank
    target[:, target.shape[1] - EDGE :] = blank


def face_kernel(products, before, after, mixed, weights, padded, faces):
    tiles, tall = weights.shape[1:3]
    for index in range(2):
        place(padded, products, (before, after, mixed), (index,))
    inner = slice(EDGE, EDGE + tall)
    faces[:, 0:EDGE] = jnp.zeros((tiles, EDGE, 128), F32)
    faces[:, EDGE + tall :] = jnp.zeros((tiles, EDGE, 128), F32)
    land = [(padded[0, tile, inner] > 0.0).astype(F32) for tile in range(tiles)]
    land_east, _ = neighbours(land)
    east_face = [padded[0, tile, inner] * land_east[tile] for tile in range(tiles)]
    _, west_face = neighbours(east_face)
    for tile in range(tiles):
        land_north = (padded[0, tile, EDGE + 1 : EDGE + 1 + tall] > 0.0).astype(F32)
        north_face = padded[1, tile, inner] * land_north
        faces[tile, inner] = north_face
        south_face = faces[tile, EDGE - 1 : EDGE - 1 + tall]
        weights[0, tile] = 1.0 - (
            ((east_face[tile] + west_face[tile]) + north_face) + south_face
        )
        weights[1, tile] = east_face[tile]
        weights[2, tile] = west_face[tile]
        weights[3, tile] = north_face
        weights[4, tile] = south_face


def face_weights(products, halo):
    _, levels, rows, cols = products.shape
    tall = rows + 2 * HALO
    return pl.pallas_call(
        face_kernel,
        out_shape=jax.ShapeDtypeStruct((5, levels + 1, tall, cols), F32),
        in_specs=[VMEM] * 4,
        out_specs=VMEM,
        scratch_shapes=[
            pltpu.VMEM((2, levels + 1, tall + 2 * EDGE, cols), F32),
            pltpu.VMEM((levels + 1, tall + 2 * EDGE, cols), F32),
        ],
        compiler_params=PARAMS,
        name="face_weights",
    )(products, *halo)


def sweep(source, target, weights, rows_from, rows_to, block):
    tiles = source.shape[0]

    def step(index, carry):
        first = pl.multiple_of(rows_from + index * block, 8)
        for start in range(0, block, 16):
            count = min(16, block - start)
            at = pl.multiple_of(first + EDGE + start, 8)
            inner = pl.ds(pl.multiple_of(first + start, 8), count)
            here = [source[tile, pl.ds(at, count)] for tile in range(tiles)]
            east, west = neighbours(here)
            for tile in range(tiles):
                above = source[tile, pl.ds(at + 1, count)]
                below = source[tile, pl.ds(at - 1, count)]
                total = weights[0, tile, inner] * here[tile]
                total += weights[1, tile, inner] * east[tile]
                total += weights[2, tile, inner] * west[tile]
                total += weights[3, tile, inner] * above
                total += weights[4, tile, inner] * below
                target[tile, pl.ds(at, count)] = total
        return carry

    lax.fori_loop(0, (rows_to - rows_from) // block, step, 0)


def smooth(field, spare, weights, skip, block, paired):
    tall = weights.shape[2]

    def two(index, carry):
        sweep(field, spare, weights, skip, tall - skip, block)
        sweep(spare, field, weights, skip, tall - skip, block)
        return carry

    if paired:
        lax.fori_loop(0, PASSES // 2, two, 0)
    else:
        for index in range(PASSES // 2):
            two(index, 0)
    sweep(field, spare, weights, skip, tall - skip, block)
    return field, spare


def index_iota(cells):
    return lax.broadcasted_iota(jnp.int32, (cells, 128), 0).astype(F32).astype(BF16)


def spread_row(row, count):
    return jnp.broadcast_to(jnp.broadcast_to(row, (16, 128)).astype(BF16)[0:1], (count, 128))


def one_hot(iota, row):
    count = iota.shape[0]
    return jnp.where(
        iota == spread_row(row, count), jnp.ones((count, 128), BF16), jnp.zeros((count, 128), BF16)
    )


def scatter_into(total, load_rows, slots, half_rows, half_cols, group):
    row_iota = index_iota(half_rows)
    col_iota = index_iota(half_cols)
    total[...] = jnp.zeros_like(total)

    def step(index, carry):
        high_rows, low_rows, columns = [], [], []
        for row_index, col_index, value in load_rows(index):
            high, low = parts(jnp.broadcast_to(value, (16, 128)))
            high = jnp.broadcast_to(high[0:1], (half_rows, 128))
            low = jnp.broadcast_to(low[0:1], (half_rows, 128))
            hit = row_iota == spread_row(row_index, half_rows)
            zero = jnp.zeros((half_rows, 128), BF16)
            high_rows.append(jnp.where(hit, high, zero))
            low_rows.append(jnp.where(hit, low, zero))
            columns.append(one_hot(col_iota, col_index))
        left = jnp.concatenate(high_rows + low_rows, axis=1)
        right = jnp.concatenate(columns + columns, axis=1)
        total[...] += lax.dot_general(
            left, right, (((1,), (1,)), ((), ())), preferred_element_type=F32
        )
        return carry

    lax.fori_loop(0, slots // group, step, 0)


def load_group(index, group, capacity, row_at, col_at, arrived, stride, first_slot):
    base = pl.multiple_of(index * group, group)
    row_block = row_at[pl.ds(base, group)]
    col_block = col_at[pl.ds(base, group)]
    for j in range(group):
        source = index * (group // capacity) + j // capacity
        at = source * stride + first_slot + j % capacity
        yield row_block[j : j + 1], col_block[j : j + 1], arrived[pl.ds(at, 1)]


def split_cells(cells, rows, cols):
    level = cells // (rows * cols)
    row = (cells // cols) % rows
    col = cells % cols
    return (level // 2) * rows + row, (level % 2) * cols + col


def put_field(total, sigma, field, extra=None):
    levels, rows, cols = sigma.shape
    fields = []
    for level in range(levels):
        r, c = level // 2 * rows, level % 2 * cols
        value = total[r : r + rows, c : c + cols]
        value = sigma[level] * value
        if extra is not None:
            value = value + extra(level)
        field[level] = value
        fields.append(value)
    return fields


def scatter_first_kernel(capacity, arrived, sigma, row_at, col_at, field, *refs):
    sides, total = refs
    levels, rows, cols = sigma.shape
    stride = 2 * capacity
    cells = jnp.concatenate(
        [arrived[at : at + capacity] for at in range(0, arrived.shape[0], stride)], axis=0
    )
    row_index, col_index = split_cells(cells.astype(jnp.int32), rows, cols)
    row_at[...] = row_index.astype(F32)
    col_at[...] = col_index.astype(F32)

    def load(index):
        return load_group(index, 64, capacity, row_at, col_at, arrived, stride, capacity)

    scatter_into(total, load, row_at.shape[0], levels // 2 * rows, 2 * cols, 64)
    sides[...] = pack_sides(put_field(total, sigma, field))


def scatter_first(arrived, sigma, capacity):
    levels, rows, cols = sigma.shape
    slots = arrived.shape[0] // 2
    shapes = [(slots, 128), (slots, 128), (levels, rows, cols), (rows, cols)]
    out = pl.pallas_call(
        functools.partial(scatter_first_kernel, capacity),
        out_shape=[jax.ShapeDtypeStruct(shape, F32) for shape in shapes],
        in_specs=[VMEM] * 2,
        out_specs=[VMEM] * len(shapes),
        scratch_shapes=[pltpu.VMEM((levels // 2 * rows, 2 * cols), F32)],
        compiler_params=PARAMS,
        name="scatter_first",
    )(arrived, sigma)
    return out


def lane_value(block, lane):
    return jnp.sum(jnp.where(lane_of(block.shape[0]) == lane, block, 0.0))


def lanes(values, rows):
    lane = lane_of(rows)
    out = jnp.zeros((rows, 128), F32)
    for index, value in enumerate(values):
        out = jnp.where(lane == index, value, out)
    return out


def scatter_next_kernel(capacity, last, arrived, row_at, col_at, sigma, *refs):
    if last:
        previous, field, sides, sums, total = refs
    else:
        previous, (field, sides, sums, total) = None, refs
    levels, rows, cols = sigma.shape
    stride = capacity + 1
    gathered = jnp.concatenate(
        [arrived[at : at + 1] for at in range(capacity, arrived.shape[0], stride)], axis=0
    )
    added = jnp.sum(gathered, axis=0, keepdims=True)
    sums[...] = jnp.broadcast_to(added, (8, 128))

    group = 128 if last else 64

    def load(index):
        return load_group(index, group, capacity, row_at, col_at, arrived, stride, 0)

    scatter_into(
        total, load, row_at.shape[0], levels // 2 * rows, 2 * cols, group
    )
    extra = None
    if last:
        beta = lane_value(added, 1) / lane_value(added, 0)

        def extra(level):
            return beta * previous[level]

    sides[...] = pack_sides(put_field(total, sigma, field, extra))


def scatter_next(arrived, row_at, col_at, sigma, capacity, previous=None):
    levels, rows, cols = sigma.shape
    last = previous is not None
    shapes = [(levels, rows, cols), (rows, cols), (8, 128)]
    operands = [arrived, row_at, col_at, sigma] + ([previous] if last else [])
    out = pl.pallas_call(
        functools.partial(scatter_next_kernel, capacity, last),
        out_shape=[jax.ShapeDtypeStruct(shape, F32) for shape in shapes],
        in_specs=[VMEM] * len(operands),
        out_specs=[VMEM] * len(shapes),
        scratch_shapes=[pltpu.VMEM((levels // 2 * rows, 2 * cols), F32)],
        compiler_params=PARAMS,
        name="scatter_last" if last else "scatter_next",
    )(*operands)
    return out


def gather_from(fields, row_at, col_at, seen, table, group, wide):
    rows, cols = fields[0].shape
    half_rows, half_cols = len(fields) // 2 * rows, 2 * cols
    for level, field in enumerate(fields):
        high, low = parts(field.T)
        c, r = level % 2 * cols, level // 2 * rows
        table[c : c + cols, r : r + rows] = high
        table[c : c + cols, half_rows + r : half_rows + r + rows] = low
    row_iota = index_iota(half_rows)
    sublane = lax.broadcasted_iota(jnp.int32, (8, 128 * wide), 0)

    def step(index, carry):
        base = pl.multiple_of(index * group, group)
        row_block = row_at[pl.ds(base, group)]
        col_block = col_at[pl.ds(base, group)].astype(jnp.int32)
        found = []
        for j in range(0, group, wide):
            hot = jnp.concatenate(
                [one_hot(row_iota, row_block[i : i + 1]) for i in range(j, j + wide)], axis=1
            )
            hot = jnp.concatenate([hot, hot], axis=0)
            lines = jnp.dot(table[...], hot, preferred_element_type=F32)
            wanted = jnp.concatenate([col_block[i : i + 1] for i in range(j, j + wide)], axis=1)
            wanted = jnp.broadcast_to(wanted, (8, 128 * wide))
            tiles = [lines[i : i + 8] for i in range(0, half_cols, 8)]
            bit = 8
            while len(tiles) > 1:
                upper = (wanted & bit) != 0
                tiles = [
                    jnp.where(upper, tiles[i + 1], tiles[i]) for i in range(0, len(tiles), 2)
                ]
                bit = bit * 2
            value = jnp.sum(
                jnp.where((wanted & 7) == sublane, tiles[0], 0.0), axis=0, keepdims=True
            )
            found += [value[:, 128 * i : 128 * (i + 1)] for i in range(wide)]
        seen[pl.ds(base, group)] = jnp.concatenate(found, axis=0)
        return carry

    lax.fori_loop(0, row_at.shape[0] // group, step, 0)


def own_part(field, level, rows):
    inner = slice(EDGE + HALO, EDGE + HALO + rows)
    return pick_out(field[level, inner], field[level + 1, inner], level)


def total_of(pairs):
    added = None
    for left, right in pairs:
        term = left * right
        added = term if added is None else added + term
    return jnp.sum(added)


def observe_first_kernel(source, *refs):
    halo, weights, sigma, row_at, col_at = refs[:3], refs[3], refs[4], refs[5], refs[6]
    seen, right, image, sums, field, spare, table = refs[7:]
    levels, rows, cols = source.shape
    place(field, source, halo)
    clear_margins(spare)
    spare, field = smooth(field, spare, weights, 0, 32, True)
    right[...] = field[:, EDGE : EDGE + rows + 2 * HALO]
    own = [own_part(field, level, rows) for level in range(levels)]
    sums[...] = lanes([total_of([(value, value) for value in own])], 8)
    spare, field = smooth(field, spare, weights, 8, 48, True)
    fields = [sigma[level] * own_part(field, level, rows) for level in range(levels)]
    for level in range(levels):
        image[level] = fields[level]
    gather_from(fields, row_at, col_at, seen, table, 32, 4)


def observe_next_kernel(source, *refs):
    halo, weights, sigma, row_at, col_at = refs[:3], refs[3], refs[4], refs[5], refs[6]
    right, scalars = refs[7:9]
    seen, residual, image, sums, field, spare, table = refs[9:]
    levels, rows, cols = source.shape
    tall = rows + 2 * HALO
    norm, product = lane_value(scalars[0:1], 0), lane_value(scalars[0:1], 1)
    alpha = norm / (norm + product)
    place(field, source, halo)
    clear_margins(spare)
    spare, field = smooth(field, spare, weights, 0, 32, True)

    for tile in range(levels + 1):
        first = right[tile]
        field[tile, EDGE : EDGE + tall] = first - alpha * (first + field[tile, EDGE : EDGE + tall])
    own = [own_part(field, level, rows) for level in range(levels)]
    first = [pick_out(
            right[level, HALO : HALO + rows], right[level + 1, HALO : HALO + rows], level
        ) for level in range(levels)]
    for level in range(levels):
        residual[level] = own[level]
    sums[...] = lanes(
        [total_of([(value, value) for value in own]), total_of(list(zip(own, first)))], 8
    )
    spare, field = smooth(field, spare, weights, 8, 48, True)
    fields = [sigma[level] * own_part(field, level, rows) for level in range(levels)]
    for level in range(levels):
        image[level] = fields[level]
    gather_from(fields, row_at, col_at, seen, table, 64, 8)


def observe(source, halo, weights, sigma, row_at, col_at, right=None, scalars=None):
    levels, rows, cols = sigma.shape
    tall = rows + 2 * HALO
    slots = row_at.shape[0]
    first = right is None
    kept = (levels + 1, tall, cols) if first else (levels, rows, cols)
    shapes = [(slots, 128), kept, (levels, rows, cols), (8, 128)]
    operands = [source, *halo, weights, sigma, row_at, col_at]
    operands += [] if first else [right, scalars]
    return pl.pallas_call(
        observe_first_kernel if first else observe_next_kernel,
        out_shape=[jax.ShapeDtypeStruct(shape, F32) for shape in shapes],
        in_specs=[VMEM] * len(operands),
        out_specs=[VMEM] * len(shapes),
        scratch_shapes=[
            pltpu.VMEM((levels + 1, tall + 2 * EDGE, cols), F32),
            pltpu.VMEM((levels + 1, tall + 2 * EDGE, cols), F32),
            pltpu.VMEM(
                (2 * cols, levels * rows), BF16
            ),
        ],
        compiler_params=PARAMS,
        name="observe_first" if first else "observe_next",
    )(*operands)


def finish_kernel(source, *refs):
    halo, weights, right, residual_one, image_zero, image_one, scalars = refs[:3], *refs[3:9]
    increment, residual, field, spare = refs[9:]
    levels, rows, cols = source.shape
    norm_zero, norm_one, cross, product_zero, product_one, product_cross = [
        lane_value(scalars[0:1], index) for index in range(6)
    ]
    alpha_zero = norm_zero / (norm_zero + product_zero)
    beta = norm_one / norm_zero
    square = norm_one + 2.0 * beta * cross + beta * beta * norm_zero
    seen = product_one + 2.0 * beta * product_cross + beta * beta * product_zero
    alpha_one = norm_one / (square + seen)
    for level in range(levels):
        direction = image_one[level] + beta * image_zero[level]
        increment[level] = alpha_zero * image_zero[level] + alpha_one * direction
    place(field, source, halo)
    clear_margins(spare)
    spare, field = smooth(field, spare, weights, 8, 48, True)
    for level in range(levels):
        here = residual_one[level]
        direction = here + beta * pick_out(
            right[level, HALO : HALO + rows], right[level + 1, HALO : HALO + rows], level
        )
        image = direction + own_part(field, level, rows)
        residual[level] = here - alpha_one * image


def finish(source, halo, weights, right, residual_one, image_zero, image_one, scalars):
    levels, rows, cols = source.shape
    tall = rows + 2 * HALO
    return pl.pallas_call(
        finish_kernel,
        out_shape=[jax.ShapeDtypeStruct((levels, rows, cols), F32)] * 2,
        in_specs=[VMEM] * 10,
        out_specs=[VMEM] * 2,
        scratch_shapes=[pltpu.VMEM((levels + 1, tall + 2 * EDGE, cols), F32),
            pltpu.VMEM((levels + 1, tall + 2 * EDGE, cols), F32)],
        compiler_params=PARAMS,
        name="finish",
    )(source, *halo, weights, right, residual_one, image_zero, image_one, scalars)


def apply_blocks(values, weights, at):
    high, low = parts(values)
    first = jnp.concatenate([high, low, jnp.zeros((128 - 2 * GROUP, 128), BF16)], axis=0)
    second = jnp.concatenate([high, jnp.zeros((128 - GROUP, 128), BF16)], axis=0)
    right = jnp.concatenate([first, second], axis=1)
    lane = lane_of(128)
    column = jnp.where(lane < 2 * GROUP, lane % GROUP, GROUP)
    kept = jnp.zeros((128, 128), F32)
    for start in range(0, GROUP, 4):
        matrix = weights[at + start : at + start + 4].reshape(4 * 128, 128)
        left = jnp.concatenate(parts(matrix), axis=1)
        product = lax.dot_general(left, right, (((1,), (1,)), ((), ())), preferred_element_type=F32)
        for k in range(4):
            kept = jnp.where(column == start + k, product[k * 128 : (k + 1) * 128], kept)
    kept = kept.T
    return kept[:GROUP] + kept[GROUP : 2 * GROUP]


def start_kernel(capacity, owner, cells, innovations, weights, mask, east, north, *refs):
    parcel, places, products, sides = refs[:4]
    count, held_cells, held_values, held_weights, held_mask, held_faces, arrived = refs[4:]
    held = held_cells.shape[0]
    levels = mask.shape[0]
    steps = held // CHUNK
    moves = [
        (innovations, held_values),
        (cells, held_cells),
        (mask, held_mask),
        (east, held_faces.at[0]),
        (north, held_faces.at[1]),
    ]
    for step in range(steps):
        block = pl.ds(step * CHUNK, CHUNK)
        moves.append((weights.at[block], held_weights.at[block]))
    copies = [
        pltpu.make_async_copy(source, target, arrived.at[index])
        for index, (source, target) in enumerate(moves)
    ]
    for copy in copies[: 5 + AHEAD]:
        copy.start()
    parcel[...] = jnp.zeros_like(parcel)
    for index in range(count.shape[0]):
        count[index] = 0
    for index in range(held):
        target = owner[index]
        rank = count[target]
        count[target] = rank + 1
        places[index] = target * capacity + rank
        places[held + index] = target * (capacity + 1) + rank
    copies[0].wait()
    copies[1].wait()
    for first in range(0, held, GROUP):
        if first % CHUNK == 0:
            step = first // CHUNK
            copies[5 + step].wait()
            if step + AHEAD < steps:
                copies[5 + step + AHEAD].start()
        result = apply_blocks(held_values[first : first + GROUP], held_weights, first)
        cell_rows = held_cells[first : first + GROUP].astype(F32)
        for k in range(GROUP):
            at = places[first + k] + owner[first + k] * capacity
            parcel[pl.ds(at, 1), :] = cell_rows[k : k + 1]
            parcel[pl.ds(at + capacity, 1), :] = result[k : k + 1]
    for copy in copies[2:5]:
        copy.wait()
    for index in range(2):
        fields = [held_mask[level].astype(F32) * held_faces[index, level] for level in range(levels)]
        for level in range(levels):
            products[index, level] = fields[level]
        sides[index] = pack_sides(fields)


def start(owner, cells, innovations, weights, mask, east, north, devices, capacity):
    held, width = cells.shape
    shapes = [(devices * 2 * capacity, width), (2 * held,), (2,) + mask.shape, (2,) + mask.shape[1:]]
    types = [F32, jnp.int32, F32, F32]
    return pl.pallas_call(
        functools.partial(start_kernel, capacity),
        out_shape=[jax.ShapeDtypeStruct(shape, kind) for shape, kind in zip(shapes, types)],
        in_specs=[SMEM] + [HBM] * 6,
        out_specs=[VMEM, SMEM, VMEM, VMEM],
        scratch_shapes=[
            pltpu.SMEM((devices,), jnp.int32),
            pltpu.VMEM((held, width), jnp.int32),
            pltpu.VMEM((held, width), F32),
            pltpu.VMEM((held, width, width), F32),
            pltpu.VMEM(mask.shape, jnp.int32),
            pltpu.VMEM((2,) + mask.shape, F32),
            pltpu.SemaphoreType.DMA((5 + held // CHUNK,)),
        ],
        compiler_params=ROOMLESS,
        name="start",
    )(owner, cells, innovations, weights, mask, east, north)


def weigh_next_kernel(capacity, devices, last, places, returned, sums, weights, *refs):
    held = weights.shape[0]
    copies = []
    if last:
        sums_before, weighted_before, parcel = refs
    else:
        parcel, weighted, held_weights, arrived = refs
        for step in range(held // CHUNK):
            block = pl.ds(step * CHUNK, CHUNK)
            copies.append(
                pltpu.make_async_copy(
                    weights.at[block], held_weights.at[block], arrived.at[step]
                )
            )
        for copy in copies[:AHEAD]:
            copy.start()
        weights = held_weights
    parcel[...] = jnp.zeros_like(parcel)
    total = jnp.zeros((GROUP, 128), F32)
    total_cross = jnp.zeros((GROUP, 128), F32)
    for first in range(0, held, GROUP):
        here = jnp.concatenate(
            [returned[pl.ds(places[first + k], 1), :] for k in range(GROUP)], axis=0
        )
        if copies and first % CHUNK == 0:
            step = first // CHUNK
            copies[step].wait()
            if step + AHEAD < len(copies):
                copies[step + AHEAD].start()
        result = apply_blocks(here, weights, first)
        total += here * result
        if last:
            total_cross += here * weighted_before[first : first + GROUP]
        else:
            weighted[first : first + GROUP] = result
        for k in range(GROUP):
            parcel[pl.ds(places[held + first + k], 1), :] = result[k : k + 1]
    if last:
        scalars = [
            lane_value(sums_before[0:1], 0) / devices,
            lane_value(sums[0:1], 0),
            lane_value(sums[0:1], 1),
            lane_value(sums_before[0:1], 1) / devices,
            jnp.sum(total),
            jnp.sum(total_cross),
        ]
    else:
        scalars = [lane_value(sums[0:1], 0), jnp.sum(total)]
    row = lanes(scalars, 1)
    for target in range(devices):
        at = target * (capacity + 1) + capacity
        parcel[at : at + 1] = row


def weigh_next(places, returned, sums, weights, devices, capacity, before=None):
    held, width = weights.shape[:2]
    last = before is not None
    operands = [places, returned, sums, weights] + (list(before) if last else [])
    out_shape = [jax.ShapeDtypeStruct((devices * (capacity + 1), width), F32)]
    if not last:
        out_shape += [jax.ShapeDtypeStruct((held, width), F32)]
    return pl.pallas_call(
        functools.partial(weigh_next_kernel, capacity, devices, last),
        out_shape=out_shape,
        in_specs=[SMEM, VMEM, VMEM, VMEM if last else HBM] + [VMEM] * (len(operands) - 4),
        out_specs=[VMEM] * len(out_shape),
        scratch_shapes=[]
        if last
        else [pltpu.VMEM(weights.shape, F32), pltpu.SemaphoreType.DMA((held // CHUNK,))],
        compiler_params=PARAMS if last else SNUG,
        name="weigh_last" if last else "weigh_next",
    )(*operands)


def swap(block):
    devices = lax.axis_size("lat") * lax.axis_size("lon")
    shares = block.reshape(devices, block.shape[0] // devices, 1, block.shape[1])
    got = lax.all_to_all(shares, ("lat", "lon"), split_axis=0, concat_axis=0, tiled=True)
    return got.reshape(block.shape)


def body(sigma, east_coef, north_coef, mask, innovations, cells, owner, obs_weights):
    devices = lax.axis_size("lat") * lax.axis_size("lon")
    held, width = cells.shape
    capacity = max(2, (2 * held + devices - 1) // devices)

    parcel, places, products, sides = start(
        owner.reshape(held),
        cells,
        innovations,
        obs_weights,
        mask,
        east_coef,
        north_coef,
        devices,
        capacity,
    )
    mixed, down, up, products = exchange_columns(products, sides, True)
    arrived = swap(parcel)
    weights = face_weights(products, exchange_rows(down, up) + (mixed,))

    row_at, col_at, field, sides = scatter_first(arrived, sigma, capacity)
    seen, right, image_zero, sums = observe(
        field, exchange(field, sides), weights, sigma, row_at, col_at
    )
    returned = swap(seen)
    parcel, weighted = weigh_next(places, returned, sums, obs_weights, devices, capacity)
    arrived = swap(parcel)

    field_zero, sides, scalars_zero = scatter_next(arrived, row_at, col_at, sigma, capacity)
    seen, residual_one, image_one, sums = observe(
        field_zero, exchange(field_zero, sides), weights, sigma, row_at, col_at, right, scalars_zero
    )
    returned = swap(seen)
    (parcel,) = weigh_next(
        places, returned, sums, obs_weights, devices, capacity, (scalars_zero, weighted)
    )
    arrived = swap(parcel)

    field, sides, scalars = scatter_next(arrived, row_at, col_at, sigma, capacity, field_zero)
    increment, residual = finish(
        field, exchange(field, sides), weights, right, residual_one, image_zero, image_one, scalars
    )
    return (increment, residual)


def solution(mesh):
    return jax.shard_map(
        body,
        mesh=mesh,
        in_specs=(
            P(None, "lat", "lon"),
            P(None, "lat", "lon"),
            P(None, "lat", "lon"),
            P(None, "lat", "lon"),
            P(("lat", "lon"), None),
            P(("lat", "lon"), None),
            P(("lat", "lon"), None),
            P(("lat", "lon"), None, None),
        ),
        out_specs=(P(None, "lat", "lon"), P(None, "lat", "lon")),
        check_vma=False,
    )
```

```python
import functools

import jax
import jax.numpy as jnp
from jax import lax
from jax.experimental import pallas as pl
from jax.experimental.pallas import tpu as pltpu
from jax.sharding import PartitionSpec as P

PASSES = 5
HALO = 16
EDGE = 8
GROUP = 16
CHUNK = 32
AHEAD = 2
F32 = jnp.float32
BF16 = jnp.bfloat16
VMEM = pl.BlockSpec(memory_space=pltpu.VMEM)
HBM = pl.BlockSpec(memory_space=pltpu.HBM)
SMEM = pl.BlockSpec(memory_space=pltpu.SMEM)
PARAMS = pltpu.CompilerParams(vmem_limit_bytes=32 * 1024 * 1024)

ROOMLESS = pltpu.CompilerParams(vmem_limit_bytes=60 * 1024 * 1024)


def parts(values):
    high = values.astype(BF16)
    low = (values - high.astype(F32)).astype(BF16)
    return high, low


def lane_of(rows):
    return lax.broadcasted_iota(jnp.int32, (rows, 128), 1)


def pack_sides(fields):
    lane = lane_of(fields[0].shape[0])
    packed = jnp.zeros_like(fields[0])
    for level, field in enumerate(fields):
        start = 2 * HALO * level
        turned = pltpu.roll(field, (start + HALO) % 128, 1)
        packed = jnp.where((lane >= start) & (lane < start + 2 * HALO), turned, packed)
    return packed


def turn_kernel(fields, from_east, from_west, mixed, down, up, *kept):
    levels, rows, _ = fields.shape[-3:]
    for ref in kept:
        ref[...] = fields[...]
    western = lane_of(rows) % (2 * HALO) < HALO
    for index in range(fields.shape[0] if len(fields.shape) == 4 else 1):
        at = (index,) if len(fields.shape) == 4 else ()
        sides = jnp.where(western, from_west[at + (...,)], from_east[at + (...,)])
        mixed[at + (...,)] = sides
        for level in range(levels):
            down[at + (level,)] = fields[at + (level, slice(rows - HALO, rows))]
            up[at + (level,)] = fields[at + (level, slice(0, HALO))]
        down[at + (levels,)] = sides[rows - HALO :]
        up[at + (levels,)] = sides[:HALO]


def exchange(fields, sides, middle_first=False):
    mixed, down, up = exchange_columns(fields, sides)
    return exchange_rows(down, up, middle_first) + (mixed,)


def exchange_columns(fields, sides, keep=False):
    *lead, levels, rows, cols = fields.shape
    wide = lax.axis_size("lon")
    east = [(i, (i + 1) % wide) for i in range(wide)]
    from_west = lax.ppermute(sides, "lon", east)
    from_east = lax.ppermute(sides, "lon", [(to, at) for at, to in east])
    shapes = [(*lead, rows, cols)] + [(*lead, levels + 1, HALO, cols)] * 2
    shapes += [fields.shape] if keep else []
    return pl.pallas_call(
        turn_kernel,
        out_shape=[jax.ShapeDtypeStruct(shape, F32) for shape in shapes],
        in_specs=[VMEM] * 3,
        out_specs=[VMEM] * len(shapes),
        compiler_params=PARAMS,
        name="turn",
    )(fields, from_east, from_west)


def exchange_rows(down, up, middle_first=False):
    tall = lax.axis_size("lat")
    first = [(i, i + 1) for i in range(0, tall - 1, 2)]
    second = [(i, i + 1) for i in range(1, tall - 1, 2)]
    even = lax.axis_index("lat") % 2 == 0
    pairings = [(first, jnp.where(even, down, up)), (second, jnp.where(even, up, down))]
    got = {}
    for index in (1, 0) if middle_first else (0, 1):
        pairs, block = pairings[index]
        got[index] = lax.ppermute(block, "lat", pairs + [(to, at) for at, to in pairs])
    one, two = got[0], got[1]
    return jnp.where(even, two, one), jnp.where(even, one, two)


def neighbours(tiles):
    lane = lane_of(tiles[0].shape[0])
    later, earlier = tiles[1:] + tiles[:1], tiles[-1:] + tiles[:-1]
    after = [
        pltpu.roll(jnp.where(lane == 0, other, tile), 127, 1) for tile, other in zip(tiles, later)
    ]
    before = [
        pltpu.roll(jnp.where(lane == 127, other, tile), 1, 1) for tile, other in zip(tiles, earlier)
    ]
    return after, before


def lay_out(fields, side):
    lane = lane_of(side.shape[0])
    width = 2 * HALO
    turned = [pltpu.roll(field, width * level + HALO, 1) for level, field in enumerate(fields)]
    tiles = []
    for tile in range(len(fields) + 1):
        left, right = width * tile - HALO, width * tile + HALO
        before = turned[tile - 1] if tile else turned[0]
        after = turned[tile] if tile < len(fields) else turned[-1]
        value = jnp.where(lane < left, before, after)
        tiles.append(jnp.where((lane >= left) & (lane < right), side, value))
    return tiles


def pick_out(first, second, level):
    start = 2 * HALO * level + HALO
    return pltpu.roll(jnp.where(lane_of(first.shape[0]) >= start, first, second), 128 - start, 1)


def place(target, own, halo, lead=()):
    before, after, mixed = halo
    levels = before.shape[-3] - 1
    rows = mixed.shape[-2]
    spans = (
        (EDGE, before, before[lead + (levels,)]),
        (EDGE + HALO, own, mixed[lead + (...,)]),
        (EDGE + HALO + rows, after, after[lead + (levels,)]),
    )
    for start, source, side in spans:
        tiles = lay_out([source[lead + (level,)] for level in range(levels)], side)
        for tile, value in enumerate(tiles):
            target[lead + (tile, slice(start, start + side.shape[0]))] = value
    blank = jnp.zeros((EDGE, 128), F32)
    for tile in range(levels + 1):
        target[lead + (tile, slice(0, EDGE))] = blank
        target[lead + (tile, slice(EDGE + 2 * HALO + rows, 2 * EDGE + 2 * HALO + rows))] = blank


def clear_margins(target):
    blank = jnp.zeros((target.shape[0], EDGE, 128), F32)
    target[:, 0:EDGE] = blank
    target[:, target.shape[1] - EDGE :] = blank


def face_kernel(products, before, after, mixed, weights, padded, faces):
    tiles, tall = weights.shape[1:3]
    for index in range(2):
        place(padded, products, (before, after, mixed), (index,))
    inner = slice(EDGE, EDGE + tall)
    faces[:, 0:EDGE] = jnp.zeros((tiles, EDGE, 128), F32)
    faces[:, EDGE + tall :] = jnp.zeros((tiles, EDGE, 128), F32)
    land = [(padded[0, tile, inner] > 0.0).astype(F32) for tile in range(tiles)]
    land_east, _ = neighbours(land)
    east_face = [padded[0, tile, inner] * land_east[tile] for tile in range(tiles)]
    _, west_face = neighbours(east_face)
    for tile in range(tiles):
        land_north = (padded[0, tile, EDGE + 1 : EDGE + 1 + tall] > 0.0).astype(F32)
        north_face = padded[1, tile, inner] * land_north
        faces[tile, inner] = north_face
        south_face = faces[tile, EDGE - 1 : EDGE - 1 + tall]
        weights[0, tile] = 1.0 - (
            ((east_face[tile] + west_face[tile]) + north_face) + south_face
        )
        weights[1, tile] = east_face[tile]
        weights[2, tile] = west_face[tile]
        weights[3, tile] = north_face
        weights[4, tile] = south_face


def face_weights(products, halo):
    _, levels, rows, cols = products.shape
    tall = rows + 2 * HALO
    return pl.pallas_call(
        face_kernel,
        out_shape=jax.ShapeDtypeStruct((5, levels + 1, tall, cols), F32),
        in_specs=[VMEM] * 4,
        out_specs=VMEM,
        scratch_shapes=[
            pltpu.VMEM((2, levels + 1, tall + 2 * EDGE, cols), F32),
            pltpu.VMEM((levels + 1, tall + 2 * EDGE, cols), F32),
        ],
        compiler_params=PARAMS,
        name="face_weights",
    )(products, *halo)


def sweep(source, target, weights, rows_from, rows_to, block):
    tiles = source.shape[0]

    def step(index, carry):
        first = pl.multiple_of(rows_from + index * block, 8)
        for start in range(0, block, 16):
            count = min(16, block - start)
            at = pl.multiple_of(first + EDGE + start, 8)
            inner = pl.ds(pl.multiple_of(first + start, 8), count)
            here = [source[tile, pl.ds(at, count)] for tile in range(tiles)]
            east, west = neighbours(here)
            for tile in range(tiles):
                above = source[tile, pl.ds(at + 1, count)]
                below = source[tile, pl.ds(at - 1, count)]
                total = weights[0, tile, inner] * here[tile]
                total += weights[1, tile, inner] * east[tile]
                total += weights[2, tile, inner] * west[tile]
                total += weights[3, tile, inner] * above
                total += weights[4, tile, inner] * below
                target[tile, pl.ds(at, count)] = total
        return carry

    lax.fori_loop(0, (rows_to - rows_from) // block, step, 0)


def smooth(field, spare, weights, skip, block, paired):
    tall = weights.shape[2]

    def two(index, carry):
        sweep(field, spare, weights, skip, tall - skip, block)
        sweep(spare, field, weights, skip, tall - skip, block)
        return carry

    if paired:
        lax.fori_loop(0, PASSES // 2, two, 0)
    else:
        for index in range(PASSES // 2):
            two(index, 0)
    sweep(field, spare, weights, skip, tall - skip, block)
    return field, spare


def index_iota(cells):
    return lax.broadcasted_iota(jnp.int32, (cells, 128), 0).astype(F32).astype(BF16)


def spread_row(row, count):
    return jnp.broadcast_to(jnp.broadcast_to(row, (16, 128)).astype(BF16)[0:1], (count, 128))


def one_hot(iota, row):
    count = iota.shape[0]
    return jnp.where(
        iota == spread_row(row, count), jnp.ones((count, 128), BF16), jnp.zeros((count, 128), BF16)
    )


def scatter_into(total, load_rows, slots, half_rows, half_cols, group):
    row_iota = index_iota(half_rows)
    col_iota = index_iota(half_cols)
    total[...] = jnp.zeros_like(total)

    def step(index, carry):
        high_rows, low_rows, columns = [], [], []
        for row_index, col_index, value in load_rows(index):
            high, low = parts(jnp.broadcast_to(value, (16, 128)))
            high = jnp.broadcast_to(high[0:1], (half_rows, 128))
            low = jnp.broadcast_to(low[0:1], (half_rows, 128))
            hit = row_iota == spread_row(row_index, half_rows)
            zero = jnp.zeros((half_rows, 128), BF16)
            high_rows.append(jnp.where(hit, high, zero))
            low_rows.append(jnp.where(hit, low, zero))
            columns.append(one_hot(col_iota, col_index))
        left = jnp.concatenate(high_rows + low_rows, axis=1)
        right = jnp.concatenate(columns + columns, axis=1)
        total[...] += lax.dot_general(
            left, right, (((1,), (1,)), ((), ())), preferred_element_type=F32
        )
        return carry

    lax.fori_loop(0, slots // group, step, 0)


def load_group(index, group, capacity, row_at, col_at, arrived, stride, first_slot):
    base = pl.multiple_of(index * group, group)
    row_block = row_at[pl.ds(base, group)]
    col_block = col_at[pl.ds(base, group)]
    for j in range(group):
        source = index * (group // capacity) + j // capacity
        at = source * stride + first_slot + j % capacity
        yield row_block[j : j + 1], col_block[j : j + 1], arrived[pl.ds(at, 1)]


def split_cells(cells, rows, cols):
    level = cells // (rows * cols)
    row = (cells // cols) % rows
    col = cells % cols
    return (level // 2) * rows + row, (level % 2) * cols + col


def put_field(total, sigma, field, extra=None):
    levels, rows, cols = sigma.shape
    fields = []
    for level in range(levels):
        r, c = level // 2 * rows, level % 2 * cols
        value = total[r : r + rows, c : c + cols]
        value = sigma[level] * value
        if extra is not None:
            value = value + extra(level)
        field[level] = value
        fields.append(value)
    return fields


def scatter_first_kernel(capacity, arrived, sigma, row_at, col_at, field, *refs):
    sides, total = refs
    levels, rows, cols = sigma.shape
    stride = 2 * capacity
    cells = jnp.concatenate(
        [arrived[at : at + capacity] for at in range(0, arrived.shape[0], stride)], axis=0
    )
    row_index, col_index = split_cells(cells.astype(jnp.int32), rows, cols)
    row_at[...] = row_index.astype(F32)
    col_at[...] = col_index.astype(F32)

    def load(index):
        return load_group(index, 64, capacity, row_at, col_at, arrived, stride, capacity)

    scatter_into(total, load, row_at.shape[0], levels // 2 * rows, 2 * cols, 64)
    sides[...] = pack_sides(put_field(total, sigma, field))


def scatter_first(arrived, sigma, capacity):
    levels, rows, cols = sigma.shape
    slots = arrived.shape[0] // 2
    shapes = [(slots, 128), (slots, 128), (levels, rows, cols), (rows, cols)]
    out = pl.pallas_call(
        functools.partial(scatter_first_kernel, capacity),
        out_shape=[jax.ShapeDtypeStruct(shape, F32) for shape in shapes],
        in_specs=[VMEM] * 2,
        out_specs=[VMEM] * len(shapes),
        scratch_shapes=[pltpu.VMEM((levels // 2 * rows, 2 * cols), F32)],
        compiler_params=PARAMS,
        name="scatter_first",
    )(arrived, sigma)
    return out


def lane_value(block, lane):
    return jnp.sum(jnp.where(lane_of(block.shape[0]) == lane, block, 0.0))


def lanes(values, rows):
    lane = lane_of(rows)
    out = jnp.zeros((rows, 128), F32)
    for index, value in enumerate(values):
        out = jnp.where(lane == index, value, out)
    return out


def scatter_next_kernel(capacity, last, arrived, row_at, col_at, sigma, *refs):
    if last:
        previous, field, sides, sums, total = refs
    else:
        previous, (field, sides, sums, total) = None, refs
    levels, rows, cols = sigma.shape
    stride = capacity + 1
    gathered = jnp.concatenate(
        [arrived[at : at + 1] for at in range(capacity, arrived.shape[0], stride)], axis=0
    )
    added = jnp.sum(gathered, axis=0, keepdims=True)
    sums[...] = jnp.broadcast_to(added, (8, 128))

    group = 128 if last else 64

    def load(index):
        return load_group(index, group, capacity, row_at, col_at, arrived, stride, 0)

    scatter_into(
        total, load, row_at.shape[0], levels // 2 * rows, 2 * cols, group
    )
    extra = None
    if last:
        beta = lane_value(added, 1) / lane_value(added, 0)

        def extra(level):
            return beta * previous[level]

    sides[...] = pack_sides(put_field(total, sigma, field, extra))


def scatter_next(arrived, row_at, col_at, sigma, capacity, previous=None):
    levels, rows, cols = sigma.shape
    last = previous is not None
    shapes = [(levels, rows, cols), (rows, cols), (8, 128)]
    operands = [arrived, row_at, col_at, sigma] + ([previous] if last else [])
    out = pl.pallas_call(
        functools.partial(scatter_next_kernel, capacity, last),
        out_shape=[jax.ShapeDtypeStruct(shape, F32) for shape in shapes],
        in_specs=[VMEM] * len(operands),
        out_specs=[VMEM] * len(shapes),
        scratch_shapes=[pltpu.VMEM((levels // 2 * rows, 2 * cols), F32)],
        compiler_params=PARAMS,
        name="scatter_last" if last else "scatter_next",
    )(*operands)
    return out


def gather_from(fields, row_at, col_at, seen, table, group, wide):
    rows, cols = fields[0].shape
    half_rows, half_cols = len(fields) // 2 * rows, 2 * cols
    for level, field in enumerate(fields):
        high, low = parts(field.T)
        c, r = level % 2 * cols, level // 2 * rows
        table[c : c + cols, r : r + rows] = high
        table[c : c + cols, half_rows + r : half_rows + r + rows] = low
    row_iota = index_iota(half_rows)
    sublane = lax.broadcasted_iota(jnp.int32, (8, 128 * wide), 0)

    def step(index, carry):
        base = pl.multiple_of(index * group, group)
        row_block = row_at[pl.ds(base, group)]
        col_block = col_at[pl.ds(base, group)].astype(jnp.int32)
        found = []
        for j in range(0, group, wide):
            hot = jnp.concatenate(
                [one_hot(row_iota, row_block[i : i + 1]) for i in range(j, j + wide)], axis=1
            )
            hot = jnp.concatenate([hot, hot], axis=0)
            lines = jnp.dot(table[...], hot, preferred_element_type=F32)
            wanted = jnp.concatenate([col_block[i : i + 1] for i in range(j, j + wide)], axis=1)
            wanted = jnp.broadcast_to(wanted, (8, 128 * wide))
            tiles = [lines[i : i + 8] for i in range(0, half_cols, 8)]
            bit = 8
            while len(tiles) > 1:
                upper = (wanted & bit) != 0
                tiles = [
                    jnp.where(upper, tiles[i + 1], tiles[i]) for i in range(0, len(tiles), 2)
                ]
                bit = bit * 2
            value = jnp.sum(
                jnp.where((wanted & 7) == sublane, tiles[0], 0.0), axis=0, keepdims=True
            )
            found += [value[:, 128 * i : 128 * (i + 1)] for i in range(wide)]
        seen[pl.ds(base, group)] = jnp.concatenate(found, axis=0)
        return carry

    lax.fori_loop(0, row_at.shape[0] // group, step, 0)


def own_part(field, level, rows):
    inner = slice(EDGE + HALO, EDGE + HALO + rows)
    return pick_out(field[level, inner], field[level + 1, inner], level)


def total_of(pairs):
    added = None
    for left, right in pairs:
        term = left * right
        added = term if added is None else added + term
    return jnp.sum(added)


def observe_first_kernel(source, *refs):
    halo, weights, sigma, row_at, col_at = refs[:3], refs[3], refs[4], refs[5], refs[6]
    seen, right, image, sums, field, spare, table = refs[7:]
    levels, rows, cols = source.shape
    place(field, source, halo)
    clear_margins(spare)
    spare, field = smooth(field, spare, weights, 0, 32, True)
    right[...] = field[:, EDGE : EDGE + rows + 2 * HALO]
    own = [own_part(field, level, rows) for level in range(levels)]
    sums[...] = lanes([total_of([(value, value) for value in own])], 8)
    spare, field = smooth(field, spare, weights, 8, 48, True)
    fields = [sigma[level] * own_part(field, level, rows) for level in range(levels)]
    for level in range(levels):
        image[level] = fields[level]
    gather_from(fields, row_at, col_at, seen, table, 32, 4)


def observe_next_kernel(source, *refs):
    halo, weights, sigma, row_at, col_at = refs[:3], refs[3], refs[4], refs[5], refs[6]
    right, scalars = refs[7:9]
    seen, residual, image, sums, field, spare, table = refs[9:]
    levels, rows, cols = source.shape
    tall = rows + 2 * HALO
    norm, product = lane_value(scalars[0:1], 0), lane_value(scalars[0:1], 1)
    alpha = norm / (norm + product)
    place(field, source, halo)
    clear_margins(spare)
    spare, field = smooth(field, spare, weights, 0, 32, True)

    for tile in range(levels + 1):
        first = right[tile]
        field[tile, EDGE : EDGE + tall] = first - alpha * (first + field[tile, EDGE : EDGE + tall])
    own = [own_part(field, level, rows) for level in range(levels)]
    first = [pick_out(
            right[level, HALO : HALO + rows], right[level + 1, HALO : HALO + rows], level
        ) for level in range(levels)]
    for level in range(levels):
        residual[level] = own[level]
    sums[...] = lanes(
        [total_of([(value, value) for value in own]), total_of(list(zip(own, first)))], 8
    )
    spare, field = smooth(field, spare, weights, 8, 48, True)
    fields = [sigma[level] * own_part(field, level, rows) for level in range(levels)]
    for level in range(levels):
        image[level] = fields[level]
    gather_from(fields, row_at, col_at, seen, table, 64, 8)


def observe(source, halo, weights, sigma, row_at, col_at, right=None, scalars=None):
    levels, rows, cols = sigma.shape
    tall = rows + 2 * HALO
    slots = row_at.shape[0]
    first = right is None
    kept = (levels + 1, tall, cols) if first else (levels, rows, cols)
    shapes = [(slots, 128), kept, (levels, rows, cols), (8, 128)]
    operands = [source, *halo, weights, sigma, row_at, col_at]
    operands += [] if first else [right, scalars]
    return pl.pallas_call(
        observe_first_kernel if first else observe_next_kernel,
        out_shape=[jax.ShapeDtypeStruct(shape, F32) for shape in shapes],
        in_specs=[VMEM] * len(operands),
        out_specs=[VMEM] * len(shapes),
        scratch_shapes=[
            pltpu.VMEM((levels + 1, tall + 2 * EDGE, cols), F32),
            pltpu.VMEM((levels + 1, tall + 2 * EDGE, cols), F32),
            pltpu.VMEM(
                (2 * cols, levels * rows), BF16
            ),
        ],
        compiler_params=PARAMS,
        name="observe_first" if first else "observe_next",
    )(*operands)


def finish_kernel(source, *refs):
    halo, weights, right, residual_one, image_zero, image_one, scalars = refs[:3], *refs[3:9]
    increment, residual, field, spare = refs[9:]
    levels, rows, cols = source.shape
    norm_zero, norm_one, cross, product_zero, product_one, product_cross = [
        lane_value(scalars[0:1], index) for index in range(6)
    ]
    alpha_zero = norm_zero / (norm_zero + product_zero)
    beta = norm_one / norm_zero
    square = norm_one + 2.0 * beta * cross + beta * beta * norm_zero
    seen = product_one + 2.0 * beta * product_cross + beta * beta * product_zero
    alpha_one = norm_one / (square + seen)
    for level in range(levels):
        direction = image_one[level] + beta * image_zero[level]
        increment[level] = alpha_zero * image_zero[level] + alpha_one * direction
    place(field, source, halo)
    clear_margins(spare)
    spare, field = smooth(field, spare, weights, 8, 48, True)
    for level in range(levels):
        here = residual_one[level]
        direction = here + beta * pick_out(
            right[level, HALO : HALO + rows], right[level + 1, HALO : HALO + rows], level
        )
        image = direction + own_part(field, level, rows)
        residual[level] = here - alpha_one * image


def finish(source, halo, weights, right, residual_one, image_zero, image_one, scalars):
    levels, rows, cols = source.shape
    tall = rows + 2 * HALO
    return pl.pallas_call(
        finish_kernel,
        out_shape=[jax.ShapeDtypeStruct((levels, rows, cols), F32)] * 2,
        in_specs=[VMEM] * 10,
        out_specs=[VMEM] * 2,
        scratch_shapes=[pltpu.VMEM((levels + 1, tall + 2 * EDGE, cols), F32),
            pltpu.VMEM((levels + 1, tall + 2 * EDGE, cols), F32)],
        compiler_params=PARAMS,
        name="finish",
    )(source, *halo, weights, right, residual_one, image_zero, image_one, scalars)


def apply_blocks(values, weights, at):
    high, low = parts(values)
    first = jnp.concatenate([high, low, jnp.zeros((128 - 2 * GROUP, 128), BF16)], axis=0)
    second = jnp.concatenate([high, jnp.zeros((128 - GROUP, 128), BF16)], axis=0)
    right = jnp.concatenate([first, second], axis=1)
    lane = lane_of(128)
    column = jnp.where(lane < 2 * GROUP, lane % GROUP, GROUP)
    kept = jnp.zeros((128, 128), F32)
    for start in range(0, GROUP, 4):
        matrix = weights[at + start : at + start + 4].reshape(4 * 128, 128)
        left = jnp.concatenate(parts(matrix), axis=1)
        product = lax.dot_general(left, right, (((1,), (1,)), ((), ())), preferred_element_type=F32)
        for k in range(4):
            kept = jnp.where(column == start + k, product[k * 128 : (k + 1) * 128], kept)
    kept = kept.T
    return kept[:GROUP] + kept[GROUP : 2 * GROUP]


def start_kernel(capacity, owner, cells, innovations, weights, mask, east, north, *refs):
    parcel, places, products, sides, kept_weights = refs[:5]
    count, held_cells, held_values, held_weights, held_mask, held_faces, held_sides, *moved = refs[5:]
    arrived, left = moved
    held = held_cells.shape[0]
    levels = mask.shape[0]
    steps = held // CHUNK
    moves = [
        (innovations, held_values),
        (cells, held_cells),
        (mask, held_mask),
        (east, held_faces.at[0]),
        (north, held_faces.at[1]),
    ]
    for step in range(steps):
        block = pl.ds(step * CHUNK, CHUNK)
        moves.append((weights.at[block], held_weights.at[block]))
    copies = [
        pltpu.make_async_copy(source, target, arrived.at[index])
        for index, (source, target) in enumerate(moves)
    ]
    returns = []
    for step in range(steps):
        block = pl.ds(step * CHUNK, CHUNK)
        returns.append(
            pltpu.make_async_copy(held_weights.at[block], kept_weights.at[block], left.at[step])
        )
    for copy in copies[: 5 + AHEAD]:
        copy.start()
    parcel[...] = jnp.zeros_like(parcel)
    for index in range(count.shape[0]):
        count[index] = 0
    for index in range(held):
        target = owner[index]
        rank = count[target]
        count[target] = rank + 1
        places[index] = target * capacity + rank
        places[held + index] = target * (capacity + 1) + rank
    for copy in copies[2:5]:
        copy.wait()
    for index in range(2):
        fields = [held_mask[level].astype(F32) * held_faces[index, level] for level in range(levels)]
        for level in range(levels):
            held_faces[index, level] = fields[level]
        held_sides[index] = pack_sides(fields)
    returns += [
        pltpu.make_async_copy(held_faces, products, left.at[steps]),
        pltpu.make_async_copy(held_sides, sides, left.at[steps + 1]),
    ]
    for copy in returns[steps:]:
        copy.start()
    copies[0].wait()
    copies[1].wait()
    for first in range(0, held, GROUP):
        if first % CHUNK == 0:
            step = first // CHUNK
            copies[5 + step].wait()
            if step + AHEAD < steps:
                copies[5 + step + AHEAD].start()
            returns[step].start()
        result = apply_blocks(held_values[first : first + GROUP], held_weights, first)
        cell_rows = held_cells[first : first + GROUP].astype(F32)
        for k in range(GROUP):
            at = places[first + k] + owner[first + k] * capacity
            parcel[pl.ds(at, 1), :] = cell_rows[k : k + 1]
            parcel[pl.ds(at + capacity, 1), :] = result[k : k + 1]
    for copy in returns:
        copy.wait()


def start(owner, cells, innovations, weights, mask, east, north, devices, capacity):
    held, width = cells.shape
    shapes = [(devices * 2 * capacity, width), (2 * held,), (2,) + mask.shape, (2,) + mask.shape[1:]]
    shapes += [weights.shape]
    types = [F32, jnp.int32, F32, F32, F32]
    return pl.pallas_call(
        functools.partial(start_kernel, capacity),
        out_shape=[jax.ShapeDtypeStruct(shape, kind) for shape, kind in zip(shapes, types)],
        in_specs=[SMEM] + [HBM] * 6,
        out_specs=[VMEM, SMEM, HBM, HBM, HBM],
        scratch_shapes=[
            pltpu.SMEM((devices,), jnp.int32),
            pltpu.VMEM((held, width), jnp.int32),
            pltpu.VMEM((held, width), F32),
            pltpu.VMEM((held, width, width), F32),
            pltpu.VMEM(mask.shape, jnp.int32),
            pltpu.VMEM((2,) + mask.shape, F32),
            pltpu.VMEM((2,) + mask.shape[1:], F32),
            pltpu.SemaphoreType.DMA((5 + held // CHUNK,)),
            pltpu.SemaphoreType.DMA((2 + held // CHUNK,)),
        ],
        compiler_params=ROOMLESS,
        name="start",
    )(owner, cells, innovations, weights, mask, east, north)


def weigh_next_kernel(capacity, devices, last, places, returned, sums, weights, *refs):
    held = weights.shape[0]
    if last:
        sums_before, weighted_before, parcel = refs
    else:
        parcel, weighted = refs
    parcel[...] = jnp.zeros_like(parcel)
    total = jnp.zeros((GROUP, 128), F32)
    total_cross = jnp.zeros((GROUP, 128), F32)
    for first in range(0, held, GROUP):
        here = jnp.concatenate(
            [returned[pl.ds(places[first + k], 1), :] for k in range(GROUP)], axis=0
        )
        result = apply_blocks(here, weights, first)
        total += here * result
        if last:
            total_cross += here * weighted_before[first : first + GROUP]
        else:
            weighted[first : first + GROUP] = result
        for k in range(GROUP):
            parcel[pl.ds(places[held + first + k], 1), :] = result[k : k + 1]
    if last:
        scalars = [
            lane_value(sums_before[0:1], 0) / devices,
            lane_value(sums[0:1], 0),
            lane_value(sums[0:1], 1),
            lane_value(sums_before[0:1], 1) / devices,
            jnp.sum(total),
            jnp.sum(total_cross),
        ]
    else:
        scalars = [lane_value(sums[0:1], 0), jnp.sum(total)]
    row = lanes(scalars, 1)
    for target in range(devices):
        at = target * (capacity + 1) + capacity
        parcel[at : at + 1] = row


def weigh_next(places, returned, sums, weights, devices, capacity, before=None):
    held, width = weights.shape[:2]
    last = before is not None
    operands = [places, returned, sums, weights] + (list(before) if last else [])
    out_shape = [jax.ShapeDtypeStruct((devices * (capacity + 1), width), F32)]
    if not last:
        out_shape += [jax.ShapeDtypeStruct((held, width), F32)]
    return pl.pallas_call(
        functools.partial(weigh_next_kernel, capacity, devices, last),
        out_shape=out_shape,
        in_specs=[SMEM] + [VMEM] * (len(operands) - 1),
        out_specs=[VMEM] * len(out_shape),
        compiler_params=PARAMS,
        name="weigh_last" if last else "weigh_next",
    )(*operands)


def swap(block):
    devices = lax.axis_size("lat") * lax.axis_size("lon")
    shares = block.reshape(devices, block.shape[0] // devices, 1, block.shape[1])
    got = lax.all_to_all(shares, ("lat", "lon"), split_axis=0, concat_axis=0, tiled=True)
    return got.reshape(block.shape)


def body(sigma, east_coef, north_coef, mask, innovations, cells, owner, obs_weights):
    devices = lax.axis_size("lat") * lax.axis_size("lon")
    held, width = cells.shape
    capacity = max(2, (2 * held + devices - 1) // devices)

    parcel, places, products, sides, kept_weights = start(
        owner.reshape(held),
        cells,
        innovations,
        obs_weights,
        mask,
        east_coef,
        north_coef,
        devices,
        capacity,
    )
    mixed, down, up, products = exchange_columns(products, sides, True)
    arrived = swap(parcel)
    weights = face_weights(products, exchange_rows(down, up) + (mixed,))

    row_at, col_at, field, sides = scatter_first(arrived, sigma, capacity)
    seen, right, image_zero, sums = observe(
        field, exchange(field, sides), weights, sigma, row_at, col_at
    )
    returned = swap(seen)
    parcel, weighted = weigh_next(places, returned, sums, kept_weights, devices, capacity)
    arrived = swap(parcel)

    field_zero, sides, scalars_zero = scatter_next(arrived, row_at, col_at, sigma, capacity)
    seen, residual_one, image_one, sums = observe(
        field_zero, exchange(field_zero, sides), weights, sigma, row_at, col_at, right, scalars_zero
    )
    returned = swap(seen)
    (parcel,) = weigh_next(
        places, returned, sums, kept_weights, devices, capacity, (scalars_zero, weighted)
    )
    arrived = swap(parcel)

    field, sides, scalars = scatter_next(arrived, row_at, col_at, sigma, capacity, field_zero)
    increment, residual = finish(
        field, exchange(field, sides, True), weights, right, residual_one, image_zero, image_one, scalars
    )
    return (increment, residual)


def solution(mesh):
    return jax.shard_map(
        body,
        mesh=mesh,
        in_specs=(
            P(None, "lat", "lon"),
            P(None, "lat", "lon"),
            P(None, "lat", "lon"),
            P(None, "lat", "lon"),
            P(("lat", "lon"), None),
            P(("lat", "lon"), None),
            P(("lat", "lon"), None),
            P(("lat", "lon"), None, None),
        ),
        out_specs=(P(None, "lat", "lon"), P(None, "lat", "lon")),
        check_vma=False,
    )
```

```python
import functools

import jax
import jax.numpy as jnp
from jax import lax
from jax.experimental import pallas as pl
from jax.experimental.pallas import tpu as pltpu
from jax.sharding import PartitionSpec as P

PASSES = 5
HALO = 16
EDGE = 8
GROUP = 16
CHUNK = 16
AHEAD = 4
F32 = jnp.float32
BF16 = jnp.bfloat16
VMEM = pl.BlockSpec(memory_space=pltpu.VMEM)
HBM = pl.BlockSpec(memory_space=pltpu.HBM)
SMEM = pl.BlockSpec(memory_space=pltpu.SMEM)
PARAMS = pltpu.CompilerParams(vmem_limit_bytes=32 * 1024 * 1024)

ROOMLESS = pltpu.CompilerParams(vmem_limit_bytes=60 * 1024 * 1024)


SNUG = pltpu.CompilerParams(vmem_limit_bytes=52 * 1024 * 1024)


def parts(values):
    high = values.astype(BF16)
    low = (values - high.astype(F32)).astype(BF16)
    return high, low


def lane_of(rows):
    return lax.broadcasted_iota(jnp.int32, (rows, 128), 1)


def pack_sides(fields):
    lane = lane_of(fields[0].shape[0])
    packed = jnp.zeros_like(fields[0])
    for level, field in enumerate(fields):
        start = 2 * HALO * level
        turned = pltpu.roll(field, (start + HALO) % 128, 1)
        packed = jnp.where((lane >= start) & (lane < start + 2 * HALO), turned, packed)
    return packed


def turn_kernel(fields, from_east, from_west, mixed, down, up, *kept):
    levels, rows, _ = fields.shape[-3:]
    for ref in kept:
        ref[...] = fields[...]
    western = lane_of(rows) % (2 * HALO) < HALO
    for index in range(fields.shape[0] if len(fields.shape) == 4 else 1):
        at = (index,) if len(fields.shape) == 4 else ()
        sides = jnp.where(western, from_west[at + (...,)], from_east[at + (...,)])
        mixed[at + (...,)] = sides
        for level in range(levels):
            down[at + (level,)] = fields[at + (level, slice(rows - HALO, rows))]
            up[at + (level,)] = fields[at + (level, slice(0, HALO))]
        down[at + (levels,)] = sides[rows - HALO :]
        up[at + (levels,)] = sides[:HALO]


def exchange(fields, sides):
    mixed, down, up = turn(fields, *exchange_columns(sides))
    return exchange_rows(down, up) + (mixed,)


def exchange_columns(sides):
    wide = lax.axis_size("lon")
    east = [(i, (i + 1) % wide) for i in range(wide)]
    from_west = lax.ppermute(sides, "lon", east)
    from_east = lax.ppermute(sides, "lon", [(to, at) for at, to in east])
    return from_east, from_west


def turn(fields, from_east, from_west, keep=False):
    *lead, levels, rows, cols = fields.shape
    shapes = [(*lead, rows, cols)] + [(*lead, levels + 1, HALO, cols)] * 2
    shapes += [fields.shape] if keep else []
    return pl.pallas_call(
        turn_kernel,
        out_shape=[jax.ShapeDtypeStruct(shape, F32) for shape in shapes],
        in_specs=[VMEM] * 3,
        out_specs=[VMEM] * len(shapes),
        compiler_params=PARAMS,
        name="turn",
    )(fields, from_east, from_west)


def exchange_rows(down, up):
    tall = lax.axis_size("lat")
    first = [(i, i + 1) for i in range(0, tall - 1, 2)]
    second = [(i, i + 1) for i in range(1, tall - 1, 2)]
    even = lax.axis_index("lat") % 2 == 0
    one = lax.ppermute(
        jnp.where(even, down, up), "lat", first + [(to, at) for at, to in first]
    )
    two = lax.ppermute(
        jnp.where(even, up, down), "lat", second + [(to, at) for at, to in second]
    )
    return jnp.where(even, two, one), jnp.where(even, one, two)


def neighbours(tiles):
    lane = lane_of(tiles[0].shape[0])
    later, earlier = tiles[1:] + tiles[:1], tiles[-1:] + tiles[:-1]
    after = [
        pltpu.roll(jnp.where(lane == 0, other, tile), 127, 1) for tile, other in zip(tiles, later)
    ]
    before = [
        pltpu.roll(jnp.where(lane == 127, other, tile), 1, 1) for tile, other in zip(tiles, earlier)
    ]
    return after, before


def lay_out(fields, side):
    lane = lane_of(side.shape[0])
    width = 2 * HALO
    turned = [pltpu.roll(field, width * level + HALO, 1) for level, field in enumerate(fields)]
    tiles = []
    for tile in range(len(fields) + 1):
        left, right = width * tile - HALO, width * tile + HALO
        before = turned[tile - 1] if tile else turned[0]
        after = turned[tile] if tile < len(fields) else turned[-1]
        value = jnp.where(lane < left, before, after)
        tiles.append(jnp.where((lane >= left) & (lane < right), side, value))
    return tiles


def pick_out(first, second, level):
    start = 2 * HALO * level + HALO
    return pltpu.roll(jnp.where(lane_of(first.shape[0]) >= start, first, second), 128 - start, 1)


def place(target, own, halo, lead=()):
    before, after, mixed = halo
    levels = before.shape[-3] - 1
    rows = mixed.shape[-2]
    spans = (
        (EDGE, before, before[lead + (levels,)]),
        (EDGE + HALO, own, mixed[lead + (...,)]),
        (EDGE + HALO + rows, after, after[lead + (levels,)]),
    )
    for start, source, side in spans:
        tiles = lay_out([source[lead + (level,)] for level in range(levels)], side)
        for tile, value in enumerate(tiles):
            target[lead + (tile, slice(start, start + side.shape[0]))] = value
    blank = jnp.zeros((EDGE, 128), F32)
    for tile in range(levels + 1):
        target[lead + (tile, slice(0, EDGE))] = blank
        target[lead + (tile, slice(EDGE + 2 * HALO + rows, 2 * EDGE + 2 * HALO + rows))] = blank


def clear_margins(target):
    blank = jnp.zeros((target.shape[0], EDGE, 128), F32)
    target[:, 0:EDGE] = blank
    target[:, target.shape[1] - EDGE :] = blank


def face_kernel(products, before, after, mixed, weights, padded, faces):
    tiles, tall = weights.shape[1:3]
    for index in range(2):
        place(padded, products, (before, after, mixed), (index,))
    inner = slice(EDGE, EDGE + tall)
    faces[:, 0:EDGE] = jnp.zeros((tiles, EDGE, 128), F32)
    faces[:, EDGE + tall :] = jnp.zeros((tiles, EDGE, 128), F32)
    land = [(padded[0, tile, inner] > 0.0).astype(F32) for tile in range(tiles)]
    land_east, _ = neighbours(land)
    east_face = [padded[0, tile, inner] * land_east[tile] for tile in range(tiles)]
    _, west_face = neighbours(east_face)
    for tile in range(tiles):
        land_north = (padded[0, tile, EDGE + 1 : EDGE + 1 + tall] > 0.0).astype(F32)
        north_face = padded[1, tile, inner] * land_north
        faces[tile, inner] = north_face
        south_face = faces[tile, EDGE - 1 : EDGE - 1 + tall]
        weights[0, tile] = 1.0 - (
            ((east_face[tile] + west_face[tile]) + north_face) + south_face
        )
        weights[1, tile] = east_face[tile]
        weights[2, tile] = west_face[tile]
        weights[3, tile] = north_face
        weights[4, tile] = south_face


def face_weights(products, halo):
    _, levels, rows, cols = products.shape
    tall = rows + 2 * HALO
    return pl.pallas_call(
        face_kernel,
        out_shape=jax.ShapeDtypeStruct((5, levels + 1, tall, cols), F32),
        in_specs=[VMEM] * 4,
        out_specs=VMEM,
        scratch_shapes=[
            pltpu.VMEM((2, levels + 1, tall + 2 * EDGE, cols), F32),
            pltpu.VMEM((levels + 1, tall + 2 * EDGE, cols), F32),
        ],
        compiler_params=PARAMS,
        name="face_weights",
    )(products, *halo)


def sweep(source, target, weights, rows_from, rows_to, block):
    tiles = source.shape[0]

    def step(index, carry):
        first = pl.multiple_of(rows_from + index * block, 8)
        for start in range(0, block, 16):
            count = min(16, block - start)
            at = pl.multiple_of(first + EDGE + start, 8)
            inner = pl.ds(pl.multiple_of(first + start, 8), count)
            here = [source[tile, pl.ds(at, count)] for tile in range(tiles)]
            east, west = neighbours(here)
            for tile in range(tiles):
                above = source[tile, pl.ds(at + 1, count)]
                below = source[tile, pl.ds(at - 1, count)]
                total = weights[0, tile, inner] * here[tile]
                total += weights[1, tile, inner] * east[tile]
                total += weights[2, tile, inner] * west[tile]
                total += weights[3, tile, inner] * above
                total += weights[4, tile, inner] * below
                target[tile, pl.ds(at, count)] = total
        return carry

    lax.fori_loop(0, (rows_to - rows_from) // block, step, 0)


def smooth(field, spare, weights, skip, block, paired):
    tall = weights.shape[2]

    def two(index, carry):
        sweep(field, spare, weights, skip, tall - skip, block)
        sweep(spare, field, weights, skip, tall - skip, block)
        return carry

    if paired:
        lax.fori_loop(0, PASSES // 2, two, 0)
    else:
        for index in range(PASSES // 2):
            two(index, 0)
    sweep(field, spare, weights, skip, tall - skip, block)
    return field, spare


def index_iota(cells):
    return lax.broadcasted_iota(jnp.int32, (cells, 128), 0).astype(F32).astype(BF16)


def spread_row(row, count):
    return jnp.broadcast_to(jnp.broadcast_to(row, (16, 128)).astype(BF16)[0:1], (count, 128))


def one_hot(iota, row):
    count = iota.shape[0]
    return jnp.where(
        iota == spread_row(row, count), jnp.ones((count, 128), BF16), jnp.zeros((count, 128), BF16)
    )


def scatter_into(total, load_rows, slots, half_rows, half_cols, group):
    row_iota = index_iota(half_rows)
    col_iota = index_iota(half_cols)
    total[...] = jnp.zeros_like(total)

    def step(index, carry):
        high_rows, low_rows, columns = [], [], []
        for row_index, col_index, value in load_rows(index):
            high, low = parts(jnp.broadcast_to(value, (16, 128)))
            high = jnp.broadcast_to(high[0:1], (half_rows, 128))
            low = jnp.broadcast_to(low[0:1], (half_rows, 128))
            hit = row_iota == spread_row(row_index, half_rows)
            zero = jnp.zeros((half_rows, 128), BF16)
            high_rows.append(jnp.where(hit, high, zero))
            low_rows.append(jnp.where(hit, low, zero))
            columns.append(one_hot(col_iota, col_index))
        left = jnp.concatenate(high_rows + low_rows, axis=1)
        right = jnp.concatenate(columns + columns, axis=1)
        total[...] += lax.dot_general(
            left, right, (((1,), (1,)), ((), ())), preferred_element_type=F32
        )
        return carry

    lax.fori_loop(0, slots // group, step, 0)


def load_group(index, group, capacity, row_at, col_at, arrived, stride, first_slot):
    base = pl.multiple_of(index * group, group)
    row_block = row_at[pl.ds(base, group)]
    col_block = col_at[pl.ds(base, group)]
    for j in range(group):
        source = index * (group // capacity) + j // capacity
        at = source * stride + first_slot + j % capacity
        yield row_block[j : j + 1], col_block[j : j + 1], arrived[pl.ds(at, 1)]


def split_cells(cells, rows, cols):
    level = cells // (rows * cols)
    row = (cells // cols) % rows
    col = cells % cols
    return (level // 2) * rows + row, (level % 2) * cols + col


def put_field(total, sigma, field, extra=None):
    levels, rows, cols = sigma.shape
    fields = []
    for level in range(levels):
        r, c = level // 2 * rows, level % 2 * cols
        value = total[r : r + rows, c : c + cols]
        value = sigma[level] * value
        if extra is not None:
            value = value + extra(level)
        field[level] = value
        fields.append(value)
    return fields


def scatter_first_kernel(capacity, arrived, sigma, row_at, col_at, field, *refs):
    sides, total = refs
    levels, rows, cols = sigma.shape
    stride = 2 * capacity
    cells = jnp.concatenate(
        [arrived[at : at + capacity] for at in range(0, arrived.shape[0], stride)], axis=0
    )
    row_index, col_index = split_cells(cells.astype(jnp.int32), rows, cols)
    row_at[...] = row_index.astype(F32)
    col_at[...] = col_index.astype(F32)

    def load(index):
        return load_group(index, 64, capacity, row_at, col_at, arrived, stride, capacity)

    scatter_into(total, load, row_at.shape[0], levels // 2 * rows, 2 * cols, 64)
    sides[...] = pack_sides(put_field(total, sigma, field))


def scatter_first(arrived, sigma, capacity):
    levels, rows, cols = sigma.shape
    slots = arrived.shape[0] // 2
    shapes = [(slots, 128), (slots, 128), (levels, rows, cols), (rows, cols)]
    out = pl.pallas_call(
        functools.partial(scatter_first_kernel, capacity),
        out_shape=[jax.ShapeDtypeStruct(shape, F32) for shape in shapes],
        in_specs=[VMEM] * 2,
        out_specs=[VMEM] * len(shapes),
        scratch_shapes=[pltpu.VMEM((levels // 2 * rows, 2 * cols), F32)],
        compiler_params=PARAMS,
        name="scatter_first",
    )(arrived, sigma)
    return out


def lane_value(block, lane):
    return jnp.sum(jnp.where(lane_of(block.shape[0]) == lane, block, 0.0))


def lanes(values, rows):
    lane = lane_of(rows)
    out = jnp.zeros((rows, 128), F32)
    for index, value in enumerate(values):
        out = jnp.where(lane == index, value, out)
    return out


def scatter_next_kernel(capacity, last, arrived, row_at, col_at, sigma, *refs):
    if last:
        previous, field, sides, sums, total = refs
    else:
        previous, (field, sides, sums, total) = None, refs
    levels, rows, cols = sigma.shape
    stride = capacity + 1
    gathered = jnp.concatenate(
        [arrived[at : at + 1] for at in range(capacity, arrived.shape[0], stride)], axis=0
    )
    added = jnp.sum(gathered, axis=0, keepdims=True)
    sums[...] = jnp.broadcast_to(added, (8, 128))

    group = 128 if last else 64

    def load(index):
        return load_group(index, group, capacity, row_at, col_at, arrived, stride, 0)

    scatter_into(
        total, load, row_at.shape[0], levels // 2 * rows, 2 * cols, group
    )
    extra = None
    if last:
        beta = lane_value(added, 1) / lane_value(added, 0)

        def extra(level):
            return beta * previous[level]

    sides[...] = pack_sides(put_field(total, sigma, field, extra))


def scatter_next(arrived, row_at, col_at, sigma, capacity, previous=None):
    levels, rows, cols = sigma.shape
    last = previous is not None
    shapes = [(levels, rows, cols), (rows, cols), (8, 128)]
    operands = [arrived, row_at, col_at, sigma] + ([previous] if last else [])
    out = pl.pallas_call(
        functools.partial(scatter_next_kernel, capacity, last),
        out_shape=[jax.ShapeDtypeStruct(shape, F32) for shape in shapes],
        in_specs=[VMEM] * len(operands),
        out_specs=[VMEM] * len(shapes),
        scratch_shapes=[pltpu.VMEM((levels // 2 * rows, 2 * cols), F32)],
        compiler_params=PARAMS,
        name="scatter_last" if last else "scatter_next",
    )(*operands)
    return out


def gather_from(fields, row_at, col_at, seen, table, group, wide):
    rows, cols = fields[0].shape
    half_rows, half_cols = len(fields) // 2 * rows, 2 * cols
    for level, field in enumerate(fields):
        high, low = parts(field.T)
        c, r = level % 2 * cols, level // 2 * rows
        table[c : c + cols, r : r + rows] = high
        table[c : c + cols, half_rows + r : half_rows + r + rows] = low
    row_iota = index_iota(half_rows)
    sublane = lax.broadcasted_iota(jnp.int32, (8, 128 * wide), 0)

    def step(index, carry):
        base = pl.multiple_of(index * group, group)
        row_block = row_at[pl.ds(base, group)]
        col_block = col_at[pl.ds(base, group)].astype(jnp.int32)
        found = []
        for j in range(0, group, wide):
            hot = jnp.concatenate(
                [one_hot(row_iota, row_block[i : i + 1]) for i in range(j, j + wide)], axis=1
            )
            hot = jnp.concatenate([hot, hot], axis=0)
            lines = jnp.dot(table[...], hot, preferred_element_type=F32)
            wanted = jnp.concatenate([col_block[i : i + 1] for i in range(j, j + wide)], axis=1)
            wanted = jnp.broadcast_to(wanted, (8, 128 * wide))
            tiles = [lines[i : i + 8] for i in range(0, half_cols, 8)]
            bit = 8
            while len(tiles) > 1:
                upper = (wanted & bit) != 0
                tiles = [
                    jnp.where(upper, tiles[i + 1], tiles[i]) for i in range(0, len(tiles), 2)
                ]
                bit = bit * 2
            value = jnp.sum(
                jnp.where((wanted & 7) == sublane, tiles[0], 0.0), axis=0, keepdims=True
            )
            found += [value[:, 128 * i : 128 * (i + 1)] for i in range(wide)]
        seen[pl.ds(base, group)] = jnp.concatenate(found, axis=0)
        return carry

    lax.fori_loop(0, row_at.shape[0] // group, step, 0)


def own_part(field, level, rows):
    inner = slice(EDGE + HALO, EDGE + HALO + rows)
    return pick_out(field[level, inner], field[level + 1, inner], level)


def total_of(pairs):
    added = None
    for left, right in pairs:
        term = left * right
        added = term if added is None else added + term
    return jnp.sum(added)


def observe_first_kernel(source, *refs):
    halo, weights, sigma, row_at, col_at = refs[:3], refs[3], refs[4], refs[5], refs[6]
    seen, right, image, sums, field, spare, table = refs[7:]
    levels, rows, cols = source.shape
    place(field, source, halo)
    clear_margins(spare)
    spare, field = smooth(field, spare, weights, 0, 32, True)
    right[...] = field[:, EDGE : EDGE + rows + 2 * HALO]
    own = [own_part(field, level, rows) for level in range(levels)]
    sums[...] = lanes([total_of([(value, value) for value in own])], 8)
    spare, field = smooth(field, spare, weights, 8, 48, True)
    fields = [sigma[level] * own_part(field, level, rows) for level in range(levels)]
    for level in range(levels):
        image[level] = fields[level]
    gather_from(fields, row_at, col_at, seen, table, 32, 4)


def observe_next_kernel(source, *refs):
    halo, weights, sigma, row_at, col_at = refs[:3], refs[3], refs[4], refs[5], refs[6]
    right, scalars = refs[7:9]
    seen, residual, image, sums, field, spare, table = refs[9:]
    levels, rows, cols = source.shape
    tall = rows + 2 * HALO
    norm, product = lane_value(scalars[0:1], 0), lane_value(scalars[0:1], 1)
    alpha = norm / (norm + product)
    place(field, source, halo)
    clear_margins(spare)
    spare, field = smooth(field, spare, weights, 0, 32, True)

    for tile in range(levels + 1):
        first = right[tile]
        field[tile, EDGE : EDGE + tall] = first - alpha * (first + field[tile, EDGE : EDGE + tall])
    own = [own_part(field, level, rows) for level in range(levels)]
    first = [pick_out(
            right[level, HALO : HALO + rows], right[level + 1, HALO : HALO + rows], level
        ) for level in range(levels)]
    for level in range(levels):
        residual[level] = own[level]
    sums[...] = lanes(
        [total_of([(value, value) for value in own]), total_of(list(zip(own, first)))], 8
    )
    spare, field = smooth(field, spare, weights, 8, 48, True)
    fields = [sigma[level] * own_part(field, level, rows) for level in range(levels)]
    for level in range(levels):
        image[level] = fields[level]
    gather_from(fields, row_at, col_at, seen, table, 64, 8)


def observe(source, halo, weights, sigma, row_at, col_at, right=None, scalars=None):
    levels, rows, cols = sigma.shape
    tall = rows + 2 * HALO
    slots = row_at.shape[0]
    first = right is None
    kept = (levels + 1, tall, cols) if first else (levels, rows, cols)
    shapes = [(slots, 128), kept, (levels, rows, cols), (8, 128)]
    operands = [source, *halo, weights, sigma, row_at, col_at]
    operands += [] if first else [right, scalars]
    return pl.pallas_call(
        observe_first_kernel if first else observe_next_kernel,
        out_shape=[jax.ShapeDtypeStruct(shape, F32) for shape in shapes],
        in_specs=[VMEM] * len(operands),
        out_specs=[VMEM] * len(shapes),
        scratch_shapes=[
            pltpu.VMEM((levels + 1, tall + 2 * EDGE, cols), F32),
            pltpu.VMEM((levels + 1, tall + 2 * EDGE, cols), F32),
            pltpu.VMEM(
                (2 * cols, levels * rows), BF16
            ),
        ],
        compiler_params=PARAMS,
        name="observe_first" if first else "observe_next",
    )(*operands)


def finish_kernel(source, *refs):
    halo, weights, right, residual_one, image_zero, image_one, scalars = refs[:3], *refs[3:9]
    increment, residual, field, spare = refs[9:]
    levels, rows, cols = source.shape
    norm_zero, norm_one, cross, product_zero, product_one, product_cross = [
        lane_value(scalars[0:1], index) for index in range(6)
    ]
    alpha_zero = norm_zero / (norm_zero + product_zero)
    beta = norm_one / norm_zero
    square = norm_one + 2.0 * beta * cross + beta * beta * norm_zero
    seen = product_one + 2.0 * beta * product_cross + beta * beta * product_zero
    alpha_one = norm_one / (square + seen)
    for level in range(levels):
        direction = image_one[level] + beta * image_zero[level]
        increment[level] = alpha_zero * image_zero[level] + alpha_one * direction
    place(field, source, halo)
    clear_margins(spare)
    spare, field = smooth(field, spare, weights, 8, 72, True)
    for level in range(levels):
        here = residual_one[level]
        direction = here + beta * pick_out(
            right[level, HALO : HALO + rows], right[level + 1, HALO : HALO + rows], level
        )
        image = direction + own_part(field, level, rows)
        residual[level] = here - alpha_one * image


def finish(source, halo, weights, right, residual_one, image_zero, image_one, scalars):
    levels, rows, cols = source.shape
    tall = rows + 2 * HALO
    return pl.pallas_call(
        finish_kernel,
        out_shape=[jax.ShapeDtypeStruct((levels, rows, cols), F32)] * 2,
        in_specs=[VMEM] * 10,
        out_specs=[VMEM] * 2,
        scratch_shapes=[pltpu.VMEM((levels + 1, tall + 2 * EDGE, cols), F32),
            pltpu.VMEM((levels + 1, tall + 2 * EDGE, cols), F32)],
        compiler_params=PARAMS,
        name="finish",
    )(source, *halo, weights, right, residual_one, image_zero, image_one, scalars)


def block_columns(values, weights, at):
    high, low = parts(values)
    first = jnp.concatenate([high, low, jnp.zeros((128 - 2 * GROUP, 128), BF16)], axis=0)
    second = jnp.concatenate([high, jnp.zeros((128 - GROUP, 128), BF16)], axis=0)
    right = jnp.concatenate([first, second], axis=1)
    lane = lane_of(128)
    column = jnp.where(lane < 2 * GROUP, lane % GROUP, GROUP)
    kept = jnp.zeros((128, 128), F32)
    for start in range(0, GROUP, 4):
        matrix = weights[at + start : at + start + 4].reshape(4 * 128, 128)
        left = jnp.concatenate(parts(matrix), axis=1)
        product = lax.dot_general(left, right, (((1,), (1,)), ((), ())), preferred_element_type=F32)
        for k in range(4):
            kept = jnp.where(column == start + k, product[k * 128 : (k + 1) * 128], kept)
    return kept


def turned(columns):
    rows = columns.T
    return rows[:GROUP] + rows[GROUP : 2 * GROUP]


def start_kernel(capacity, owner, cells, innovations, weights, mask, east, north, *refs):
    parcel, places, products, sides = refs[:4]
    count, held_cells, held_values, held_weights, held_mask, held_faces, held_sides = refs[4:11]
    columns, arrived, left = refs[11:]
    held = held_cells.shape[0]
    levels = mask.shape[0]
    steps = held // CHUNK
    moves = [
        (innovations, held_values),
        (cells, held_cells),
        (mask, held_mask),
        (east, held_faces.at[0]),
        (north, held_faces.at[1]),
    ]
    for step in range(steps):
        block = pl.ds(step * CHUNK, CHUNK)
        moves.append((weights.at[block], held_weights.at[block]))
    copies = [
        pltpu.make_async_copy(source, target, arrived.at[index])
        for index, (source, target) in enumerate(moves)
    ]
    for copy in copies[: 5 + AHEAD]:
        copy.start()
    parcel[...] = jnp.zeros_like(parcel)
    for index in range(count.shape[0]):
        count[index] = 0
    for index in range(held):
        target = owner[index]
        rank = count[target]
        count[target] = rank + 1
        places[index] = target * capacity + rank
        places[held + index] = target * (capacity + 1) + rank
    for copy in copies[2:5]:
        copy.wait()
    for index in range(2):
        fields = [held_mask[level].astype(F32) * held_faces[index, level] for level in range(levels)]
        for level in range(levels):
            held_faces[index, level] = fields[level]
        held_sides[index] = pack_sides(fields)
    returns = [
        pltpu.make_async_copy(held_faces, products, left.at[0]),
        pltpu.make_async_copy(held_sides, sides, left.at[1]),
    ]
    for copy in returns:
        copy.start()
    copies[0].wait()
    copies[1].wait()
    for first in range(0, held, GROUP):
        if first % CHUNK == 0:
            step = first // CHUNK
            copies[5 + step].wait()
            if step + AHEAD < steps:
                copies[5 + step + AHEAD].start()
        columns[first // GROUP] = block_columns(
            held_values[first : first + GROUP], held_weights, first
        )
    for first in range(0, held, GROUP):
        result = turned(columns[first // GROUP])
        cell_rows = held_cells[first : first + GROUP].astype(F32)
        for k in range(GROUP):
            at = places[first + k] + owner[first + k] * capacity
            parcel[pl.ds(at, 1), :] = cell_rows[k : k + 1]
            parcel[pl.ds(at + capacity, 1), :] = result[k : k + 1]
    for copy in returns:
        copy.wait()


def start(owner, cells, innovations, weights, mask, east, north, devices, capacity):
    held, width = cells.shape
    shapes = [(devices * 2 * capacity, width), (2 * held,), (2,) + mask.shape, (2,) + mask.shape[1:]]
    types = [F32, jnp.int32, F32, F32]
    return pl.pallas_call(
        functools.partial(start_kernel, capacity),
        out_shape=[jax.ShapeDtypeStruct(shape, kind) for shape, kind in zip(shapes, types)],
        in_specs=[SMEM] + [HBM] * 6,
        out_specs=[VMEM, SMEM, HBM, HBM],
        scratch_shapes=[
            pltpu.SMEM((devices,), jnp.int32),
            pltpu.VMEM((held, width), jnp.int32),
            pltpu.VMEM((held, width), F32),
            pltpu.VMEM((held, width, width), F32),
            pltpu.VMEM(mask.shape, jnp.int32),
            pltpu.VMEM((2,) + mask.shape, F32),
            pltpu.VMEM((2,) + mask.shape[1:], F32),
            pltpu.VMEM((held // GROUP, width, width), F32),
            pltpu.SemaphoreType.DMA((5 + held // CHUNK,)),
            pltpu.SemaphoreType.DMA((2,)),
        ],
        compiler_params=ROOMLESS,
        name="start",
    )(owner, cells, innovations, weights, mask, east, north)


def weigh_next_kernel(capacity, devices, last, places, returned, sums, weights, *refs):
    held = weights.shape[0]
    copies = []
    if last:
        sums_before, weighted_before, parcel, values, columns = refs
    else:
        parcel, weighted, values, columns, held_weights, arrived = refs
        for step in range(held // CHUNK):
            block = pl.ds(step * CHUNK, CHUNK)
            copies.append(
                pltpu.make_async_copy(
                    weights.at[block], held_weights.at[block], arrived.at[step]
                )
            )
        for copy in copies[:AHEAD]:
            copy.start()
        weights = held_weights
    parcel[...] = jnp.zeros_like(parcel)
    total = jnp.zeros((GROUP, 128), F32)
    total_cross = jnp.zeros((GROUP, 128), F32)
    for first in range(0, held, GROUP):
        here = jnp.concatenate(
            [returned[pl.ds(places[first + k], 1), :] for k in range(GROUP)], axis=0
        )
        values[first : first + GROUP] = here
        if copies and first % CHUNK == 0:
            step = first // CHUNK
            copies[step].wait()
            if step + AHEAD < len(copies):
                copies[step + AHEAD].start()
        columns[first // GROUP] = block_columns(here, weights, first)
    for first in range(0, held, GROUP):
        here = values[first : first + GROUP]
        result = turned(columns[first // GROUP])
        total += here * result
        if last:
            total_cross += here * weighted_before[first : first + GROUP]
        else:
            weighted[first : first + GROUP] = result
        for k in range(GROUP):
            parcel[pl.ds(places[held + first + k], 1), :] = result[k : k + 1]
    if last:
        scalars = [
            lane_value(sums_before[0:1], 0) / devices,
            lane_value(sums[0:1], 0),
            lane_value(sums[0:1], 1),
            lane_value(sums_before[0:1], 1) / devices,
            jnp.sum(total),
            jnp.sum(total_cross),
        ]
    else:
        scalars = [lane_value(sums[0:1], 0), jnp.sum(total)]
    row = lanes(scalars, 1)
    for target in range(devices):
        at = target * (capacity + 1) + capacity
        parcel[at : at + 1] = row


def weigh_next(places, returned, sums, weights, devices, capacity, before=None):
    held, width = weights.shape[:2]
    last = before is not None
    operands = [places, returned, sums, weights] + (list(before) if last else [])
    out_shape = [jax.ShapeDtypeStruct((devices * (capacity + 1), width), F32)]
    if not last:
        out_shape += [jax.ShapeDtypeStruct((held, width), F32)]
    return pl.pallas_call(
        functools.partial(weigh_next_kernel, capacity, devices, last),
        out_shape=out_shape,
        in_specs=[SMEM, VMEM, VMEM, VMEM if last else HBM] + [VMEM] * (len(operands) - 4),
        out_specs=[VMEM] * len(out_shape),
        scratch_shapes=[
            pltpu.VMEM((held, width), F32),
            pltpu.VMEM((held // GROUP, width, width), F32),
        ]
        + (
            []
            if last
            else [pltpu.VMEM(weights.shape, F32), pltpu.SemaphoreType.DMA((held // CHUNK,))]
        ),
        compiler_params=PARAMS if last else SNUG,
        name="weigh_last" if last else "weigh_next",
    )(*operands)


def swap(block):
    devices = lax.axis_size("lat") * lax.axis_size("lon")
    shares = block.reshape(devices, block.shape[0] // devices, 1, block.shape[1])
    got = lax.all_to_all(shares, ("lat", "lon"), split_axis=0, concat_axis=0, tiled=True)
    return got.reshape(block.shape)


def body(sigma, east_coef, north_coef, mask, innovations, cells, owner, obs_weights):
    devices = lax.axis_size("lat") * lax.axis_size("lon")
    held, width = cells.shape
    capacity = max(2, (2 * held + devices - 1) // devices)

    parcel, places, products, sides = start(
        owner.reshape(held),
        cells,
        innovations,
        obs_weights,
        mask,
        east_coef,
        north_coef,
        devices,
        capacity,
    )
    face_columns = exchange_columns(sides)
    arrived = swap(parcel)

    row_at, col_at, field, sides = scatter_first(arrived, sigma, capacity)
    face_columns, sides = lax.optimization_barrier((face_columns, sides))
    mixed, down, up, products = turn(products, *face_columns, True)
    weights = face_weights(products, exchange_rows(down, up) + (mixed,))
    seen, right, image_zero, sums = observe(
        field, exchange(field, sides), weights, sigma, row_at, col_at
    )
    returned = swap(seen)
    parcel, weighted = weigh_next(places, returned, sums, obs_weights, devices, capacity)
    arrived = swap(parcel)

    field_zero, sides, scalars_zero = scatter_next(arrived, row_at, col_at, sigma, capacity)
    seen, residual_one, image_one, sums = observe(
        field_zero, exchange(field_zero, sides), weights, sigma, row_at, col_at, right, scalars_zero
    )
    returned = swap(seen)
    (parcel,) = weigh_next(
        places, returned, sums, obs_weights, devices, capacity, (scalars_zero, weighted)
    )
    arrived = swap(parcel)

    field, sides, scalars = scatter_next(arrived, row_at, col_at, sigma, capacity, field_zero)
    increment, residual = finish(
        field, exchange(field, sides), weights, right, residual_one, image_zero, image_one, scalars
    )
    return (increment, residual)


def solution(mesh):
    return jax.shard_map(
        body,
        mesh=mesh,
        in_specs=(
            P(None, "lat", "lon"),
            P(None, "lat", "lon"),
            P(None, "lat", "lon"),
            P(None, "lat", "lon"),
            P(("lat", "lon"), None),
            P(("lat", "lon"), None),
            P(("lat", "lon"), None),
            P(("lat", "lon"), None, None),
        ),
        out_specs=(P(None, "lat", "lon"), P(None, "lat", "lon")),
        check_vma=False,
    )
```

```python
import functools

import jax
import jax.numpy as jnp
from jax import lax
from jax.experimental import pallas as pl
from jax.experimental.pallas import tpu as pltpu
from jax.sharding import PartitionSpec as P

PASSES = 5
HALO = 16
EDGE = 8
GROUP = 16
CHUNK = 16
AHEAD = 4
F32 = jnp.float32
BF16 = jnp.bfloat16
VMEM = pl.BlockSpec(memory_space=pltpu.VMEM)
HBM = pl.BlockSpec(memory_space=pltpu.HBM)
SMEM = pl.BlockSpec(memory_space=pltpu.SMEM)
PARAMS = pltpu.CompilerParams(vmem_limit_bytes=32 * 1024 * 1024)

ROOMLESS = pltpu.CompilerParams(vmem_limit_bytes=60 * 1024 * 1024)


SNUG = pltpu.CompilerParams(vmem_limit_bytes=52 * 1024 * 1024)


def parts(values):
    high = values.astype(BF16)
    low = (values - high.astype(F32)).astype(BF16)
    return high, low


def lane_of(rows):
    return lax.broadcasted_iota(jnp.int32, (rows, 128), 1)


def pack_sides(fields):
    lane = lane_of(fields[0].shape[0])
    packed = jnp.zeros_like(fields[0])
    for level, field in enumerate(fields):
        start = 2 * HALO * level
        turned = pltpu.roll(field, (start + HALO) % 128, 1)
        packed = jnp.where((lane >= start) & (lane < start + 2 * HALO), turned, packed)
    return packed


def turn_kernel(count, *refs):
    sources, extra = refs[: 3 * count], refs[3 * count : len(refs) - count - 2]
    *mixed, down, up = refs[len(refs) - count - 2 :]
    row = 0
    if extra:
        row = extra[0].shape[0]
        down[0:row] = extra[0][...]
        up[0:row] = extra[1][...]
    for index in range(count):
        fields, from_east, from_west = sources[3 * index : 3 * index + 3]
        levels, rows, _ = fields.shape[-3:]
        western = lane_of(rows) % (2 * HALO) < HALO
        for at in [(i,) for i in range(fields.shape[0])] if len(fields.shape) == 4 else [()]:
            sides = jnp.where(western, from_west[at + (...,)], from_east[at + (...,)])
            mixed[index][at + (...,)] = sides
            for level in range(levels):
                down[row, level] = fields[at + (level, slice(rows - HALO, rows))]
                up[row, level] = fields[at + (level, slice(0, HALO))]
            down[row, levels] = sides[rows - HALO :]
            up[row, levels] = sides[:HALO]
            row += 1


def exchange(fields, sides):
    mixed, down, up = turn((fields, *exchange_columns(sides)))
    return (*exchange_rows(down, up), mixed)


def exchange_columns(sides):
    wide = lax.axis_size("lon")
    east = [(i, (i + 1) % wide) for i in range(wide)]
    from_west = lax.ppermute(sides, "lon", east)
    from_east = lax.ppermute(sides, "lon", [(to, at) for at, to in east])
    return from_east, from_west


def turn(*groups, rows_ahead=()):
    levels, rows, cols = groups[0][0].shape[-3:]
    shapes = [sides.shape for _, sides, _ in groups]
    total = sum(fields.shape[0] if fields.ndim == 4 else 1 for fields, _, _ in groups)
    total += rows_ahead[0].shape[0] if rows_ahead else 0
    shapes += [(total, levels + 1, HALO, cols)] * 2
    return pl.pallas_call(
        functools.partial(turn_kernel, len(groups)),
        out_shape=[jax.ShapeDtypeStruct(shape, F32) for shape in shapes],
        in_specs=[VMEM] * (3 * len(groups) + len(rows_ahead)),
        out_specs=[VMEM] * len(shapes),
        compiler_params=PARAMS,
        name="turn",
    )(*[array for group in groups for array in group], *rows_ahead)


def exchange_rows(down, up):
    tall = lax.axis_size("lat")
    first = [(i, i + 1) for i in range(0, tall - 1, 2)]
    second = [(i, i + 1) for i in range(1, tall - 1, 2)]
    even = lax.axis_index("lat") % 2 == 0
    one = lax.ppermute(
        jnp.where(even, down, up), "lat", first + [(to, at) for at, to in first]
    )
    two = lax.ppermute(
        jnp.where(even, up, down), "lat", second + [(to, at) for at, to in second]
    )
    return jnp.where(even, two, one), jnp.where(even, one, two)


def neighbours(tiles):
    lane = lane_of(tiles[0].shape[0])
    later, earlier = tiles[1:] + tiles[:1], tiles[-1:] + tiles[:-1]
    after = [
        pltpu.roll(jnp.where(lane == 0, other, tile), 127, 1) for tile, other in zip(tiles, later)
    ]
    before = [
        pltpu.roll(jnp.where(lane == 127, other, tile), 1, 1) for tile, other in zip(tiles, earlier)
    ]
    return after, before


def lay_out(fields, side):
    lane = lane_of(side.shape[0])
    width = 2 * HALO
    turned = [pltpu.roll(field, width * level + HALO, 1) for level, field in enumerate(fields)]
    tiles = []
    for tile in range(len(fields) + 1):
        left, right = width * tile - HALO, width * tile + HALO
        before = turned[tile - 1] if tile else turned[0]
        after = turned[tile] if tile < len(fields) else turned[-1]
        value = jnp.where(lane < left, before, after)
        tiles.append(jnp.where((lane >= left) & (lane < right), side, value))
    return tiles


def pick_out(first, second, level):
    start = 2 * HALO * level + HALO
    return pltpu.roll(jnp.where(lane_of(first.shape[0]) >= start, first, second), 128 - start, 1)


def place(target, own, halo, row, lead=()):
    before, after, mixed = halo
    levels = before.shape[-3] - 1
    rows = mixed.shape[-2]
    spans = (
        (EDGE, before, (row,), before[row, levels]),
        (EDGE + HALO, own, lead, mixed[lead + (...,)]),
        (EDGE + HALO + rows, after, (row,), after[row, levels]),
    )
    for start, source, at, side in spans:
        tiles = lay_out([source[at + (level,)] for level in range(levels)], side)
        for tile, value in enumerate(tiles):
            target[lead + (tile, slice(start, start + side.shape[0]))] = value
    blank = jnp.zeros((EDGE, 128), F32)
    for tile in range(levels + 1):
        target[lead + (tile, slice(0, EDGE))] = blank
        target[lead + (tile, slice(EDGE + 2 * HALO + rows, 2 * EDGE + 2 * HALO + rows))] = blank


def clear_margins(target):
    blank = jnp.zeros((target.shape[0], EDGE, 128), F32)
    target[:, 0:EDGE] = blank
    target[:, target.shape[1] - EDGE :] = blank


def face_kernel(products, before, after, mixed, weights, padded, faces):
    tiles, tall = weights.shape[1:3]
    for index in range(2):
        place(padded, products, (before, after, mixed), index, (index,))
    inner = slice(EDGE, EDGE + tall)
    faces[:, 0:EDGE] = jnp.zeros((tiles, EDGE, 128), F32)
    faces[:, EDGE + tall :] = jnp.zeros((tiles, EDGE, 128), F32)
    land = [(padded[0, tile, inner] > 0.0).astype(F32) for tile in range(tiles)]
    land_east, _ = neighbours(land)
    east_face = [padded[0, tile, inner] * land_east[tile] for tile in range(tiles)]
    _, west_face = neighbours(east_face)
    for tile in range(tiles):
        land_north = (padded[0, tile, EDGE + 1 : EDGE + 1 + tall] > 0.0).astype(F32)
        north_face = padded[1, tile, inner] * land_north
        faces[tile, inner] = north_face
        south_face = faces[tile, EDGE - 1 : EDGE - 1 + tall]
        weights[0, tile] = 1.0 - (
            ((east_face[tile] + west_face[tile]) + north_face) + south_face
        )
        weights[1, tile] = east_face[tile]
        weights[2, tile] = west_face[tile]
        weights[3, tile] = north_face
        weights[4, tile] = south_face


def face_weights(products, halo):
    _, levels, rows, cols = products.shape
    tall = rows + 2 * HALO
    return pl.pallas_call(
        face_kernel,
        out_shape=jax.ShapeDtypeStruct((5, levels + 1, tall, cols), F32),
        in_specs=[VMEM] * 4,
        out_specs=VMEM,
        scratch_shapes=[
            pltpu.VMEM((2, levels + 1, tall + 2 * EDGE, cols), F32),
            pltpu.VMEM((levels + 1, tall + 2 * EDGE, cols), F32),
        ],
        compiler_params=PARAMS,
        name="face_weights",
    )(products, *halo)


def sweep(source, target, weights, rows_from, rows_to, block):
    tiles = source.shape[0]

    def step(index, carry):
        first = pl.multiple_of(rows_from + index * block, 8)
        for start in range(0, block, 16):
            count = min(16, block - start)
            at = pl.multiple_of(first + EDGE + start, 8)
            inner = pl.ds(pl.multiple_of(first + start, 8), count)
            here = [source[tile, pl.ds(at, count)] for tile in range(tiles)]
            east, west = neighbours(here)
            for tile in range(tiles):
                above = source[tile, pl.ds(at + 1, count)]
                below = source[tile, pl.ds(at - 1, count)]
                total = weights[0, tile, inner] * here[tile]
                total += weights[1, tile, inner] * east[tile]
                total += weights[2, tile, inner] * west[tile]
                total += weights[3, tile, inner] * above
                total += weights[4, tile, inner] * below
                target[tile, pl.ds(at, count)] = total
        return carry

    lax.fori_loop(0, (rows_to - rows_from) // block, step, 0)


def smooth(field, spare, weights, skip, block, paired):
    tall = weights.shape[2]

    def two(index, carry):
        sweep(field, spare, weights, skip, tall - skip, block)
        sweep(spare, field, weights, skip, tall - skip, block)
        return carry

    if paired:
        lax.fori_loop(0, PASSES // 2, two, 0)
    else:
        for index in range(PASSES // 2):
            two(index, 0)
    sweep(field, spare, weights, skip, tall - skip, block)
    return field, spare


def index_iota(cells):
    return lax.broadcasted_iota(jnp.int32, (cells, 128), 0).astype(F32).astype(BF16)


def spread_row(row, count):
    return jnp.broadcast_to(jnp.broadcast_to(row, (16, 128)).astype(BF16)[0:1], (count, 128))


def one_hot(iota, row):
    count = iota.shape[0]
    return jnp.where(
        iota == spread_row(row, count), jnp.ones((count, 128), BF16), jnp.zeros((count, 128), BF16)
    )


def scatter_into(total, load_rows, slots, half_rows, half_cols, group):
    row_iota = index_iota(half_rows)
    col_iota = index_iota(half_cols)
    total[...] = jnp.zeros_like(total)

    def step(index, carry):
        high_rows, low_rows, columns = [], [], []
        for row_index, col_index, value in load_rows(index):
            high, low = parts(jnp.broadcast_to(value, (16, 128)))
            high = jnp.broadcast_to(high[0:1], (half_rows, 128))
            low = jnp.broadcast_to(low[0:1], (half_rows, 128))
            hit = row_iota == spread_row(row_index, half_rows)
            zero = jnp.zeros((half_rows, 128), BF16)
            high_rows.append(jnp.where(hit, high, zero))
            low_rows.append(jnp.where(hit, low, zero))
            columns.append(one_hot(col_iota, col_index))
        left = jnp.concatenate(high_rows + low_rows, axis=1)
        right = jnp.concatenate(columns + columns, axis=1)
        total[...] += lax.dot_general(
            left, right, (((1,), (1,)), ((), ())), preferred_element_type=F32
        )
        return carry

    lax.fori_loop(0, slots // group, step, 0)


def load_group(index, group, capacity, row_at, col_at, arrived, stride, first_slot):
    base = pl.multiple_of(index * group, group)
    row_block = row_at[pl.ds(base, group)]
    col_block = col_at[pl.ds(base, group)]
    for j in range(group):
        source = index * (group // capacity) + j // capacity
        at = source * stride + first_slot + j % capacity
        yield row_block[j : j + 1], col_block[j : j + 1], arrived[pl.ds(at, 1)]


def split_cells(cells, rows, cols):
    level = cells // (rows * cols)
    row = (cells // cols) % rows
    col = cells % cols
    return (level // 2) * rows + row, (level % 2) * cols + col


def put_field(total, sigma, field, extra=None):
    levels, rows, cols = sigma.shape
    fields = []
    for level in range(levels):
        r, c = level // 2 * rows, level % 2 * cols
        value = total[r : r + rows, c : c + cols]
        value = sigma[level] * value
        if extra is not None:
            value = value + extra(level)
        field[level] = value
        fields.append(value)
    return fields


def scatter_first_kernel(capacity, arrived, sigma, row_at, col_at, field, *refs):
    sides, total = refs
    levels, rows, cols = sigma.shape
    stride = 2 * capacity
    cells = jnp.concatenate(
        [arrived[at : at + capacity] for at in range(0, arrived.shape[0], stride)], axis=0
    )
    row_index, col_index = split_cells(cells.astype(jnp.int32), rows, cols)
    row_at[...] = row_index.astype(F32)
    col_at[...] = col_index.astype(F32)

    def load(index):
        return load_group(index, 64, capacity, row_at, col_at, arrived, stride, capacity)

    scatter_into(total, load, row_at.shape[0], levels // 2 * rows, 2 * cols, 64)
    sides[...] = pack_sides(put_field(total, sigma, field))


def scatter_first(arrived, sigma, capacity):
    levels, rows, cols = sigma.shape
    slots = arrived.shape[0] // 2
    shapes = [(slots, 128), (slots, 128), (levels, rows, cols), (rows, cols)]
    out = pl.pallas_call(
        functools.partial(scatter_first_kernel, capacity),
        out_shape=[jax.ShapeDtypeStruct(shape, F32) for shape in shapes],
        in_specs=[VMEM] * 2,
        out_specs=[VMEM] * len(shapes),
        scratch_shapes=[pltpu.VMEM((levels // 2 * rows, 2 * cols), F32)],
        compiler_params=PARAMS,
        name="scatter_first",
    )(arrived, sigma)
    return out


def lane_value(block, lane):
    return jnp.sum(jnp.where(lane_of(block.shape[0]) == lane, block, 0.0))


def lanes(values, rows):
    lane = lane_of(rows)
    out = jnp.zeros((rows, 128), F32)
    for index, value in enumerate(values):
        out = jnp.where(lane == index, value, out)
    return out


def scatter_next_kernel(capacity, last, arrived, row_at, col_at, sigma, *refs):
    if last:
        previous, field, sides, sums, total = refs
    else:
        previous, (field, sides, sums, total) = None, refs
    levels, rows, cols = sigma.shape
    stride = capacity + 1
    gathered = jnp.concatenate(
        [arrived[at : at + 1] for at in range(capacity, arrived.shape[0], stride)], axis=0
    )
    added = jnp.sum(gathered, axis=0, keepdims=True)
    sums[...] = jnp.broadcast_to(added, (8, 128))

    group = 128 if last else 64

    def load(index):
        return load_group(index, group, capacity, row_at, col_at, arrived, stride, 0)

    scatter_into(
        total, load, row_at.shape[0], levels // 2 * rows, 2 * cols, group
    )
    extra = None
    if last:
        beta = lane_value(added, 1) / lane_value(added, 0)

        def extra(level):
            return beta * previous[level]

    sides[...] = pack_sides(put_field(total, sigma, field, extra))


def scatter_next(arrived, row_at, col_at, sigma, capacity, previous=None):
    levels, rows, cols = sigma.shape
    last = previous is not None
    shapes = [(levels, rows, cols), (rows, cols), (8, 128)]
    operands = [arrived, row_at, col_at, sigma] + ([previous] if last else [])
    out = pl.pallas_call(
        functools.partial(scatter_next_kernel, capacity, last),
        out_shape=[jax.ShapeDtypeStruct(shape, F32) for shape in shapes],
        in_specs=[VMEM] * len(operands),
        out_specs=[VMEM] * len(shapes),
        scratch_shapes=[pltpu.VMEM((levels // 2 * rows, 2 * cols), F32)],
        compiler_params=PARAMS,
        name="scatter_last" if last else "scatter_next",
    )(*operands)
    return out


def gather_from(fields, row_at, col_at, seen, table, group, wide):
    rows, cols = fields[0].shape
    half_rows, half_cols = len(fields) // 2 * rows, 2 * cols
    for level, field in enumerate(fields):
        high, low = parts(field.T)
        c, r = level % 2 * cols, level // 2 * rows
        table[c : c + cols, r : r + rows] = high
        table[c : c + cols, half_rows + r : half_rows + r + rows] = low
    row_iota = index_iota(half_rows)
    sublane = lax.broadcasted_iota(jnp.int32, (8, 128 * wide), 0)

    def step(index, carry):
        base = pl.multiple_of(index * group, group)
        row_block = row_at[pl.ds(base, group)]
        col_block = col_at[pl.ds(base, group)].astype(jnp.int32)
        found = []
        for j in range(0, group, wide):
            hot = jnp.concatenate(
                [one_hot(row_iota, row_block[i : i + 1]) for i in range(j, j + wide)], axis=1
            )
            hot = jnp.concatenate([hot, hot], axis=0)
            lines = jnp.dot(table[...], hot, preferred_element_type=F32)
            wanted = jnp.concatenate([col_block[i : i + 1] for i in range(j, j + wide)], axis=1)
            wanted = jnp.broadcast_to(wanted, (8, 128 * wide))
            tiles = [lines[i : i + 8] for i in range(0, half_cols, 8)]
            bit = 8
            while len(tiles) > 1:
                upper = (wanted & bit) != 0
                tiles = [
                    jnp.where(upper, tiles[i + 1], tiles[i]) for i in range(0, len(tiles), 2)
                ]
                bit = bit * 2
            value = jnp.sum(
                jnp.where((wanted & 7) == sublane, tiles[0], 0.0), axis=0, keepdims=True
            )
            found += [value[:, 128 * i : 128 * (i + 1)] for i in range(wide)]
        seen[pl.ds(base, group)] = jnp.concatenate(found, axis=0)
        return carry

    lax.fori_loop(0, row_at.shape[0] // group, step, 0)


def own_part(field, level, rows):
    inner = slice(EDGE + HALO, EDGE + HALO + rows)
    return pick_out(field[level, inner], field[level + 1, inner], level)


def total_of(pairs):
    added = None
    for left, right in pairs:
        term = left * right
        added = term if added is None else added + term
    return jnp.sum(added)


def observe_first_kernel(source, *refs):
    halo, weights, sigma, row_at, col_at = refs[:3], refs[3], refs[4], refs[5], refs[6]
    seen, right, image, sums, field, spare, table = refs[7:]
    levels, rows, cols = source.shape
    place(field, source, halo, halo[0].shape[0] - 1)
    clear_margins(spare)
    spare, field = smooth(field, spare, weights, 0, 80, True)
    right[...] = field[:, EDGE : EDGE + rows + 2 * HALO]
    own = [own_part(field, level, rows) for level in range(levels)]
    sums[...] = lanes([total_of([(value, value) for value in own])], 8)
    spare, field = smooth(field, spare, weights, 8, 72, True)
    fields = [sigma[level] * own_part(field, level, rows) for level in range(levels)]
    for level in range(levels):
        image[level] = fields[level]
    gather_from(fields, row_at, col_at, seen, table, 32, 4)


def observe_next_kernel(source, *refs):
    halo, weights, sigma, row_at, col_at = refs[:3], refs[3], refs[4], refs[5], refs[6]
    right, scalars = refs[7:9]
    seen, residual, image, sums, field, spare, table = refs[9:]
    levels, rows, cols = source.shape
    tall = rows + 2 * HALO
    norm, product = lane_value(scalars[0:1], 0), lane_value(scalars[0:1], 1)
    alpha = norm / (norm + product)
    place(field, source, halo, halo[0].shape[0] - 1)
    clear_margins(spare)
    spare, field = smooth(field, spare, weights, 0, 80, True)

    for tile in range(levels + 1):
        first = right[tile]
        field[tile, EDGE : EDGE + tall] = first - alpha * (first + field[tile, EDGE : EDGE + tall])
    own = [own_part(field, level, rows) for level in range(levels)]
    first = [pick_out(
            right[level, HALO : HALO + rows], right[level + 1, HALO : HALO + rows], level
        ) for level in range(levels)]
    for level in range(levels):
        residual[level] = own[level]
    sums[...] = lanes(
        [total_of([(value, value) for value in own]), total_of(list(zip(own, first)))], 8
    )
    spare, field = smooth(field, spare, weights, 8, 72, True)
    fields = [sigma[level] * own_part(field, level, rows) for level in range(levels)]
    for level in range(levels):
        image[level] = fields[level]
    gather_from(fields, row_at, col_at, seen, table, 64, 8)


def observe(source, halo, weights, sigma, row_at, col_at, right=None, scalars=None):
    levels, rows, cols = sigma.shape
    tall = rows + 2 * HALO
    slots = row_at.shape[0]
    first = right is None
    kept = (levels + 1, tall, cols) if first else (levels, rows, cols)
    shapes = [(slots, 128), kept, (levels, rows, cols), (8, 128)]
    operands = [source, *halo, weights, sigma, row_at, col_at]
    operands += [] if first else [right, scalars]
    return pl.pallas_call(
        observe_first_kernel if first else observe_next_kernel,
        out_shape=[jax.ShapeDtypeStruct(shape, F32) for shape in shapes],
        in_specs=[VMEM] * len(operands),
        out_specs=[VMEM] * len(shapes),
        scratch_shapes=[
            pltpu.VMEM((levels + 1, tall + 2 * EDGE, cols), F32),
            pltpu.VMEM((levels + 1, tall + 2 * EDGE, cols), F32),
            pltpu.VMEM(
                (2 * cols, levels * rows), BF16
            ),
        ],
        compiler_params=PARAMS,
        name="observe_first" if first else "observe_next",
    )(*operands)


def finish_kernel(source, *refs):
    halo, weights, right, residual_one, image_zero, image_one, scalars = refs[:3], *refs[3:9]
    increment, residual, field, spare = refs[9:]
    levels, rows, cols = source.shape
    norm_zero, norm_one, cross, product_zero, product_one, product_cross = [
        lane_value(scalars[0:1], index) for index in range(6)
    ]
    alpha_zero = norm_zero / (norm_zero + product_zero)
    beta = norm_one / norm_zero
    square = norm_one + 2.0 * beta * cross + beta * beta * norm_zero
    seen = product_one + 2.0 * beta * product_cross + beta * beta * product_zero
    alpha_one = norm_one / (square + seen)
    for level in range(levels):
        direction = image_one[level] + beta * image_zero[level]
        increment[level] = alpha_zero * image_zero[level] + alpha_one * direction
    place(field, source, halo, halo[0].shape[0] - 1)
    clear_margins(spare)
    spare, field = smooth(field, spare, weights, 8, 72, True)
    for level in range(levels):
        here = residual_one[level]
        direction = here + beta * pick_out(
            right[level, HALO : HALO + rows], right[level + 1, HALO : HALO + rows], level
        )
        image = direction + own_part(field, level, rows)
        residual[level] = here - alpha_one * image


def finish(source, halo, weights, right, residual_one, image_zero, image_one, scalars):
    levels, rows, cols = source.shape
    tall = rows + 2 * HALO
    return pl.pallas_call(
        finish_kernel,
        out_shape=[jax.ShapeDtypeStruct((levels, rows, cols), F32)] * 2,
        in_specs=[VMEM] * 10,
        out_specs=[VMEM] * 2,
        scratch_shapes=[pltpu.VMEM((levels + 1, tall + 2 * EDGE, cols), F32),
            pltpu.VMEM((levels + 1, tall + 2 * EDGE, cols), F32)],
        compiler_params=PARAMS,
        name="finish",
    )(source, *halo, weights, right, residual_one, image_zero, image_one, scalars)


def block_columns(values, weights, at):
    high, low = parts(values)
    first = jnp.concatenate([high, low, jnp.zeros((128 - 2 * GROUP, 128), BF16)], axis=0)
    second = jnp.concatenate([high, jnp.zeros((128 - GROUP, 128), BF16)], axis=0)
    right = jnp.concatenate([first, second], axis=1)
    lane = lane_of(128)
    column = jnp.where(lane < 2 * GROUP, lane % GROUP, GROUP)
    kept = jnp.zeros((128, 128), F32)
    for start in range(0, GROUP, 4):
        matrix = weights[at + start : at + start + 4].reshape(4 * 128, 128)
        left = jnp.concatenate(parts(matrix), axis=1)
        product = lax.dot_general(left, right, (((1,), (1,)), ((), ())), preferred_element_type=F32)
        for k in range(4):
            kept = jnp.where(column == start + k, product[k * 128 : (k + 1) * 128], kept)
    return kept


def turned(columns):
    rows = columns.T
    return rows[:GROUP] + rows[GROUP : 2 * GROUP]


def start_kernel(capacity, owner, cells, innovations, weights, mask, east, north, *refs):
    parcel, places, products, sides = refs[:4]
    count, held_cells, held_values, held_weights, held_mask, held_faces, held_sides = refs[4:11]
    columns, arrived, left = refs[11:]
    held = held_cells.shape[0]
    levels = mask.shape[0]
    steps = held // CHUNK
    moves = [
        (innovations, held_values),
        (cells, held_cells),
        (mask, held_mask),
        (east, held_faces.at[0]),
        (north, held_faces.at[1]),
    ]
    for step in range(steps):
        block = pl.ds(step * CHUNK, CHUNK)
        moves.append((weights.at[block], held_weights.at[block]))
    copies = [
        pltpu.make_async_copy(source, target, arrived.at[index])
        for index, (source, target) in enumerate(moves)
    ]
    for copy in copies[: 5 + AHEAD]:
        copy.start()
    parcel[...] = jnp.zeros_like(parcel)
    for index in range(count.shape[0]):
        count[index] = 0
    for index in range(held):
        target = owner[index]
        rank = count[target]
        count[target] = rank + 1
        places[index] = target * capacity + rank
        places[held + index] = target * (capacity + 1) + rank
    for copy in copies[2:5]:
        copy.wait()
    for index in range(2):
        fields = [held_mask[level].astype(F32) * held_faces[index, level] for level in range(levels)]
        for level in range(levels):
            held_faces[index, level] = fields[level]
        held_sides[index] = pack_sides(fields)
    returns = [
        pltpu.make_async_copy(held_faces, products, left.at[0]),
        pltpu.make_async_copy(held_sides, sides, left.at[1]),
    ]
    for copy in returns:
        copy.start()
    copies[0].wait()
    copies[1].wait()
    for first in range(0, held, GROUP):
        if first % CHUNK == 0:
            step = first // CHUNK
            copies[5 + step].wait()
            if step + AHEAD < steps:
                copies[5 + step + AHEAD].start()
        columns[first // GROUP] = block_columns(
            held_values[first : first + GROUP], held_weights, first
        )
    for first in range(0, held, GROUP):
        result = turned(columns[first // GROUP])
        cell_rows = held_cells[first : first + GROUP].astype(F32)
        for k in range(GROUP):
            at = places[first + k] + owner[first + k] * capacity
            parcel[pl.ds(at, 1), :] = cell_rows[k : k + 1]
            parcel[pl.ds(at + capacity, 1), :] = result[k : k + 1]
    for copy in returns:
        copy.wait()


def start(owner, cells, innovations, weights, mask, east, north, devices, capacity):
    held, width = cells.shape
    shapes = [(devices * 2 * capacity, width), (2 * held,), (2,) + mask.shape, (2,) + mask.shape[1:]]
    types = [F32, jnp.int32, F32, F32]
    return pl.pallas_call(
        functools.partial(start_kernel, capacity),
        out_shape=[jax.ShapeDtypeStruct(shape, kind) for shape, kind in zip(shapes, types)],
        in_specs=[SMEM] + [HBM] * 6,
        out_specs=[VMEM, SMEM, HBM, HBM],
        scratch_shapes=[
            pltpu.SMEM((devices,), jnp.int32),
            pltpu.VMEM((held, width), jnp.int32),
            pltpu.VMEM((held, width), F32),
            pltpu.VMEM((held, width, width), F32),
            pltpu.VMEM(mask.shape, jnp.int32),
            pltpu.VMEM((2,) + mask.shape, F32),
            pltpu.VMEM((2,) + mask.shape[1:], F32),
            pltpu.VMEM((held // GROUP, width, width), F32),
            pltpu.SemaphoreType.DMA((5 + held // CHUNK,)),
            pltpu.SemaphoreType.DMA((2,)),
        ],
        compiler_params=ROOMLESS,
        name="start",
    )(owner, cells, innovations, weights, mask, east, north)


def weigh_next_kernel(capacity, devices, last, places, returned, sums, weights, *refs):
    held = weights.shape[0]
    copies = []
    if last:
        sums_before, weighted_before, parcel, values, columns = refs
    else:
        parcel, weighted, values, columns, held_weights, arrived = refs
        for step in range(held // CHUNK):
            block = pl.ds(step * CHUNK, CHUNK)
            copies.append(
                pltpu.make_async_copy(
                    weights.at[block], held_weights.at[block], arrived.at[step]
                )
            )
        for copy in copies[:AHEAD]:
            copy.start()
        weights = held_weights
    parcel[...] = jnp.zeros_like(parcel)
    total = jnp.zeros((GROUP, 128), F32)
    total_cross = jnp.zeros((GROUP, 128), F32)
    for first in range(0, held, GROUP):
        here = jnp.concatenate(
            [returned[pl.ds(places[first + k], 1), :] for k in range(GROUP)], axis=0
        )
        values[first : first + GROUP] = here
        if copies and first % CHUNK == 0:
            step = first // CHUNK
            copies[step].wait()
            if step + AHEAD < len(copies):
                copies[step + AHEAD].start()
        columns[first // GROUP] = block_columns(here, weights, first)
    for first in range(0, held, GROUP):
        here = values[first : first + GROUP]
        result = turned(columns[first // GROUP])
        total += here * result
        if last:
            total_cross += here * weighted_before[first : first + GROUP]
        else:
            weighted[first : first + GROUP] = result
        for k in range(GROUP):
            parcel[pl.ds(places[held + first + k], 1), :] = result[k : k + 1]
    if last:
        scalars = [
            lane_value(sums_before[0:1], 0) / devices,
            lane_value(sums[0:1], 0),
            lane_value(sums[0:1], 1),
            lane_value(sums_before[0:1], 1) / devices,
            jnp.sum(total),
            jnp.sum(total_cross),
        ]
    else:
        scalars = [lane_value(sums[0:1], 0), jnp.sum(total)]
    row = lanes(scalars, 1)
    for target in range(devices):
        at = target * (capacity + 1) + capacity
        parcel[at : at + 1] = row


def weigh_next(places, returned, sums, weights, devices, capacity, before=None):
    held, width = weights.shape[:2]
    last = before is not None
    operands = [places, returned, sums, weights] + (list(before) if last else [])
    out_shape = [jax.ShapeDtypeStruct((devices * (capacity + 1), width), F32)]
    if not last:
        out_shape += [jax.ShapeDtypeStruct((held, width), F32)]
    return pl.pallas_call(
        functools.partial(weigh_next_kernel, capacity, devices, last),
        out_shape=out_shape,
        in_specs=[SMEM, VMEM, VMEM, VMEM if last else HBM] + [VMEM] * (len(operands) - 4),
        out_specs=[VMEM] * len(out_shape),
        scratch_shapes=[
            pltpu.VMEM((held, width), F32),
            pltpu.VMEM((held // GROUP, width, width), F32),
        ]
        + (
            []
            if last
            else [pltpu.VMEM(weights.shape, F32), pltpu.SemaphoreType.DMA((held // CHUNK,))]
        ),
        compiler_params=PARAMS if last else SNUG,
        name="weigh_last" if last else "weigh_next",
    )(*operands)


def swap(block):
    devices = lax.axis_size("lat") * lax.axis_size("lon")
    shares = block.reshape(devices, block.shape[0] // devices, 1, block.shape[1])
    got = lax.all_to_all(shares, ("lat", "lon"), split_axis=0, concat_axis=0, tiled=True)
    return got.reshape(block.shape)


def body(sigma, east_coef, north_coef, mask, innovations, cells, owner, obs_weights):
    devices = lax.axis_size("lat") * lax.axis_size("lon")
    held, width = cells.shape
    capacity = max(2, (2 * held + devices - 1) // devices)

    parcel, places, products, sides = start(
        owner.reshape(held),
        cells,
        innovations,
        obs_weights,
        mask,
        east_coef,
        north_coef,
        devices,
        capacity,
    )
    face_columns = exchange_columns(sides)
    arrived = swap(parcel)

    row_at, col_at, field, sides = scatter_first(arrived, sigma, capacity)
    face_columns, sides = lax.optimization_barrier((face_columns, sides))
    face_mixed, *face_rows = turn((products, *face_columns))
    mixed, down, up = turn((field, *exchange_columns(sides)), rows_ahead=tuple(face_rows))
    before, after = exchange_rows(down, up)
    weights = face_weights(products, (before, after, face_mixed))
    seen, right, image_zero, sums = observe(
        field, (before, after, mixed), weights, sigma, row_at, col_at
    )
    returned = swap(seen)
    parcel, weighted = weigh_next(places, returned, sums, obs_weights, devices, capacity)
    arrived = swap(parcel)

    field_zero, sides, scalars_zero = scatter_next(arrived, row_at, col_at, sigma, capacity)
    seen, residual_one, image_one, sums = observe(
        field_zero, exchange(field_zero, sides), weights, sigma, row_at, col_at, right, scalars_zero
    )
    returned = swap(seen)
    (parcel,) = weigh_next(
        places, returned, sums, obs_weights, devices, capacity, (scalars_zero, weighted)
    )
    arrived = swap(parcel)

    field, sides, scalars = scatter_next(arrived, row_at, col_at, sigma, capacity, field_zero)
    increment, residual = finish(
        field, exchange(field, sides), weights, right, residual_one, image_zero, image_one, scalars
    )
    return (increment, residual)


def solution(mesh):
    return jax.shard_map(
        body,
        mesh=mesh,
        in_specs=(
            P(None, "lat", "lon"),
            P(None, "lat", "lon"),
            P(None, "lat", "lon"),
            P(None, "lat", "lon"),
            P(("lat", "lon"), None),
            P(("lat", "lon"), None),
            P(("lat", "lon"), None),
            P(("lat", "lon"), None, None),
        ),
        out_specs=(P(None, "lat", "lon"), P(None, "lat", "lon")),
        check_vma=False,
    )
```

```python
import functools

import jax
import jax.numpy as jnp
from jax import lax
from jax.experimental import pallas as pl
from jax.experimental.pallas import tpu as pltpu
from jax.sharding import PartitionSpec as P

PASSES = 5
HALO = 16
EDGE = 8
GROUP = 16
CHUNK = 16
AHEAD = 4
F32 = jnp.float32
BF16 = jnp.bfloat16
VMEM = pl.BlockSpec(memory_space=pltpu.VMEM)
HBM = pl.BlockSpec(memory_space=pltpu.HBM)
SMEM = pl.BlockSpec(memory_space=pltpu.SMEM)
PARAMS = pltpu.CompilerParams(vmem_limit_bytes=32 * 1024 * 1024)

ROOMLESS = pltpu.CompilerParams(vmem_limit_bytes=60 * 1024 * 1024)


SNUG = pltpu.CompilerParams(vmem_limit_bytes=52 * 1024 * 1024)


def parts(values):
    high = values.astype(BF16)
    low = (values - high.astype(F32)).astype(BF16)
    return high, low


def lane_of(rows):
    return lax.broadcasted_iota(jnp.int32, (rows, 128), 1)


def pack_sides(fields):
    lane = lane_of(fields[0].shape[0])
    packed = jnp.zeros_like(fields[0])
    for level, field in enumerate(fields):
        start = 2 * HALO * level
        turned = pltpu.roll(field, (start + HALO) % 128, 1)
        packed = jnp.where((lane >= start) & (lane < start + 2 * HALO), turned, packed)
    half = packed.shape[0] // 2
    low, high = packed[:half], packed[half:]
    western = lane[:half] % (2 * HALO) < HALO
    return (
        jnp.where(western, low, pltpu.roll(high, HALO, 1)),
        jnp.where(western, pltpu.roll(low, 128 - HALO, 1), high),
    )


def unpack_sides(from_east, from_west):
    western = lane_of(from_east.shape[0]) % (2 * HALO) < HALO
    low = jnp.where(western, from_west, pltpu.roll(from_east, HALO, 1))
    high = jnp.where(western, pltpu.roll(from_west, 128 - HALO, 1), from_east)
    return jnp.concatenate([low, high], axis=0)


def turn_kernel(count, ahead, *refs):
    sources, extra = refs[: 3 * count], refs[3 * count : 3 * count + ahead]
    *mixed, down, up = refs[3 * count + ahead : 4 * count + ahead + 2]
    for kept in refs[4 * count + ahead + 2 :]:
        kept[...] = sources[0][...]
    row = 0
    if extra:
        row = extra[0].shape[0]
        down[0:row] = extra[0][...]
        up[0:row] = extra[1][...]
    for index in range(count):
        fields, from_east, from_west = sources[3 * index : 3 * index + 3]
        levels, rows, _ = fields.shape[-3:]
        for at in [(i,) for i in range(fields.shape[0])] if len(fields.shape) == 4 else [()]:
            sides = unpack_sides(from_east[at + (...,)], from_west[at + (...,)])
            mixed[index][at + (...,)] = sides
            for level in range(levels):
                down[row, level] = fields[at + (level, slice(rows - HALO, rows))]
                up[row, level] = fields[at + (level, slice(0, HALO))]
            down[row, levels] = sides[rows - HALO :]
            up[row, levels] = sides[:HALO]
            row += 1


def exchange(fields, sides):
    mixed, down, up = turn((fields, *exchange_columns(sides)))
    return (*exchange_rows(down, up), mixed)


def exchange_columns(sides):
    wide = lax.axis_size("lon")
    east = [(i, (i + 1) % wide) for i in range(wide)]
    from_west = lax.ppermute(sides[0], "lon", east)
    from_east = lax.ppermute(sides[1], "lon", [(to, at) for at, to in east])
    return from_east, from_west


def turn(*groups, rows_ahead=(), keep=False):
    levels, rows, cols = groups[0][0].shape[-3:]
    shapes = [fields.shape[:-3] + (rows, cols) for fields, _, _ in groups]
    total = sum(fields.shape[0] if fields.ndim == 4 else 1 for fields, _, _ in groups)
    total += rows_ahead[0].shape[0] if rows_ahead else 0
    shapes += [(total, levels + 1, HALO, cols)] * 2
    shapes += [groups[0][0].shape] if keep else []
    return pl.pallas_call(
        functools.partial(turn_kernel, len(groups), len(rows_ahead)),
        out_shape=[jax.ShapeDtypeStruct(shape, F32) for shape in shapes],
        in_specs=[VMEM] * (3 * len(groups) + len(rows_ahead)),
        out_specs=[VMEM] * len(shapes),
        compiler_params=PARAMS,
        name="turn",
    )(*[array for group in groups for array in group], *rows_ahead)


def exchange_rows(down, up):
    tall = lax.axis_size("lat")
    first = [(i, i + 1) for i in range(0, tall - 1, 2)]
    second = [(i, i + 1) for i in range(1, tall - 1, 2)]
    even = lax.axis_index("lat") % 2 == 0
    one = lax.ppermute(
        jnp.where(even, down, up), "lat", first + [(to, at) for at, to in first]
    )
    two = lax.ppermute(
        jnp.where(even, up, down), "lat", second + [(to, at) for at, to in second]
    )
    return jnp.where(even, two, one), jnp.where(even, one, two)


def neighbours(tiles):
    lane = lane_of(tiles[0].shape[0])
    later, earlier = tiles[1:] + tiles[:1], tiles[-1:] + tiles[:-1]
    after = [
        pltpu.roll(jnp.where(lane == 0, other, tile), 127, 1) for tile, other in zip(tiles, later)
    ]
    before = [
        pltpu.roll(jnp.where(lane == 127, other, tile), 1, 1) for tile, other in zip(tiles, earlier)
    ]
    return after, before


def lay_out(fields, side):
    lane = lane_of(side.shape[0])
    width = 2 * HALO
    turned = [pltpu.roll(field, width * level + HALO, 1) for level, field in enumerate(fields)]
    tiles = []
    for tile in range(len(fields) + 1):
        left, right = width * tile - HALO, width * tile + HALO
        before = turned[tile - 1] if tile else turned[0]
        after = turned[tile] if tile < len(fields) else turned[-1]
        value = jnp.where(lane < left, before, after)
        tiles.append(jnp.where((lane >= left) & (lane < right), side, value))
    return tiles


def pick_out(first, second, level):
    start = 2 * HALO * level + HALO
    return pltpu.roll(jnp.where(lane_of(first.shape[0]) >= start, first, second), 128 - start, 1)


def place(target, own, halo, row, lead=()):
    before, after, mixed = halo
    levels = before.shape[-3] - 1
    rows = mixed.shape[-2]
    spans = (
        (EDGE, before, (row,), before[row, levels]),
        (EDGE + HALO, own, lead, mixed[lead + (...,)]),
        (EDGE + HALO + rows, after, (row,), after[row, levels]),
    )
    for start, source, at, side in spans:
        tiles = lay_out([source[at + (level,)] for level in range(levels)], side)
        for tile, value in enumerate(tiles):
            target[lead + (tile, slice(start, start + side.shape[0]))] = value
    blank = jnp.zeros((EDGE, 128), F32)
    for tile in range(levels + 1):
        target[lead + (tile, slice(0, EDGE))] = blank
        target[lead + (tile, slice(EDGE + 2 * HALO + rows, 2 * EDGE + 2 * HALO + rows))] = blank


def clear_margins(target):
    blank = jnp.zeros((target.shape[0], EDGE, 128), F32)
    target[:, 0:EDGE] = blank
    target[:, target.shape[1] - EDGE :] = blank


def face_kernel(products, before, after, mixed, weights, padded, faces):
    tiles, tall = weights.shape[1:3]
    for index in range(2):
        place(padded, products, (before, after, mixed), index, (index,))
    inner = slice(EDGE, EDGE + tall)
    faces[:, 0:EDGE] = jnp.zeros((tiles, EDGE, 128), F32)
    faces[:, EDGE + tall :] = jnp.zeros((tiles, EDGE, 128), F32)
    land = [(padded[0, tile, inner] > 0.0).astype(F32) for tile in range(tiles)]
    land_east, _ = neighbours(land)
    east_face = [padded[0, tile, inner] * land_east[tile] for tile in range(tiles)]
    _, west_face = neighbours(east_face)
    for tile in range(tiles):
        land_north = (padded[0, tile, EDGE + 1 : EDGE + 1 + tall] > 0.0).astype(F32)
        north_face = padded[1, tile, inner] * land_north
        faces[tile, inner] = north_face
        south_face = faces[tile, EDGE - 1 : EDGE - 1 + tall]
        weights[0, tile] = 1.0 - (
            ((east_face[tile] + west_face[tile]) + north_face) + south_face
        )
        weights[1, tile] = east_face[tile]
        weights[2, tile] = west_face[tile]
        weights[3, tile] = north_face
        weights[4, tile] = south_face


def face_weights(products, halo):
    _, levels, rows, cols = products.shape
    tall = rows + 2 * HALO
    return pl.pallas_call(
        face_kernel,
        out_shape=jax.ShapeDtypeStruct((5, levels + 1, tall, cols), F32),
        in_specs=[VMEM] * 4,
        out_specs=VMEM,
        scratch_shapes=[
            pltpu.VMEM((2, levels + 1, tall + 2 * EDGE, cols), F32),
            pltpu.VMEM((levels + 1, tall + 2 * EDGE, cols), F32),
        ],
        compiler_params=PARAMS,
        name="face_weights",
    )(products, *halo)


def sweep(source, target, weights, rows_from, rows_to, block):
    tiles = source.shape[0]

    def step(index, carry):
        first = pl.multiple_of(rows_from + index * block, 8)
        for start in range(0, block, 16):
            count = min(16, block - start)
            at = pl.multiple_of(first + EDGE + start, 8)
            inner = pl.ds(pl.multiple_of(first + start, 8), count)
            here = [source[tile, pl.ds(at, count)] for tile in range(tiles)]
            east, west = neighbours(here)
            for tile in range(tiles):
                above = source[tile, pl.ds(at + 1, count)]
                below = source[tile, pl.ds(at - 1, count)]
                total = weights[0, tile, inner] * here[tile]
                total += weights[1, tile, inner] * east[tile]
                total += weights[2, tile, inner] * west[tile]
                total += weights[3, tile, inner] * above
                total += weights[4, tile, inner] * below
                target[tile, pl.ds(at, count)] = total
        return carry

    lax.fori_loop(0, (rows_to - rows_from) // block, step, 0)


def smooth(field, spare, weights, skip, block, paired):
    tall = weights.shape[2]

    def two(index, carry):
        sweep(field, spare, weights, skip, tall - skip, block)
        sweep(spare, field, weights, skip, tall - skip, block)
        return carry

    if paired:
        lax.fori_loop(0, PASSES // 2, two, 0)
    else:
        for index in range(PASSES // 2):
            two(index, 0)
    sweep(field, spare, weights, skip, tall - skip, block)
    return field, spare


def index_iota(cells):
    return lax.broadcasted_iota(jnp.int32, (cells, 128), 0).astype(F32).astype(BF16)


def spread_row(row, count):
    return jnp.broadcast_to(jnp.broadcast_to(row, (16, 128)).astype(BF16)[0:1], (count, 128))


def one_hot(iota, row):
    count = iota.shape[0]
    return jnp.where(
        iota == spread_row(row, count), jnp.ones((count, 128), BF16), jnp.zeros((count, 128), BF16)
    )


def scatter_into(total, load_rows, slots, half_rows, half_cols, group):
    row_iota = index_iota(half_rows)
    col_iota = index_iota(half_cols)
    total[...] = jnp.zeros_like(total)

    def step(index, carry):
        high_rows, low_rows, columns = [], [], []
        for row_index, col_index, value in load_rows(index):
            high, low = parts(jnp.broadcast_to(value, (16, 128)))
            high = jnp.broadcast_to(high[0:1], (half_rows, 128))
            low = jnp.broadcast_to(low[0:1], (half_rows, 128))
            hit = row_iota == spread_row(row_index, half_rows)
            zero = jnp.zeros((half_rows, 128), BF16)
            high_rows.append(jnp.where(hit, high, zero))
            low_rows.append(jnp.where(hit, low, zero))
            columns.append(one_hot(col_iota, col_index))
        left = jnp.concatenate(high_rows + low_rows, axis=1)
        right = jnp.concatenate(columns + columns, axis=1)
        total[...] += lax.dot_general(
            left, right, (((1,), (1,)), ((), ())), preferred_element_type=F32
        )
        return carry

    lax.fori_loop(0, slots // group, step, 0)


def load_group(index, group, capacity, row_at, col_at, arrived, stride, first_slot):
    base = pl.multiple_of(index * group, group)
    row_block = row_at[pl.ds(base, group)]
    col_block = col_at[pl.ds(base, group)]
    for j in range(group):
        source = index * (group // capacity) + j // capacity
        at = source * stride + first_slot + j % capacity
        yield row_block[j : j + 1], col_block[j : j + 1], arrived[pl.ds(at, 1)]


def split_cells(cells, rows, cols):
    level = cells // (rows * cols)
    row = (cells // cols) % rows
    col = cells % cols
    return (level // 2) * rows + row, (level % 2) * cols + col


def put_field(total, sigma, field, extra=None):
    levels, rows, cols = sigma.shape
    fields = []
    for level in range(levels):
        r, c = level // 2 * rows, level % 2 * cols
        value = total[r : r + rows, c : c + cols]
        value = sigma[level] * value
        if extra is not None:
            value = value + extra(level)
        field[level] = value
        fields.append(value)
    return fields


def scatter_first_kernel(capacity, arrived, sigma, row_at, col_at, field, *refs):
    eastward, westward, total = refs
    levels, rows, cols = sigma.shape
    stride = 2 * capacity
    cells = jnp.concatenate(
        [arrived[at : at + capacity] for at in range(0, arrived.shape[0], stride)], axis=0
    )
    row_index, col_index = split_cells(cells.astype(jnp.int32), rows, cols)
    row_at[...] = row_index.astype(F32)
    col_at[...] = col_index.astype(F32)

    def load(index):
        return load_group(index, 64, capacity, row_at, col_at, arrived, stride, capacity)

    scatter_into(total, load, row_at.shape[0], levels // 2 * rows, 2 * cols, 64)
    eastward[...], westward[...] = pack_sides(put_field(total, sigma, field))


def scatter_first(arrived, sigma, capacity):
    levels, rows, cols = sigma.shape
    slots = arrived.shape[0] // 2
    shapes = [(slots, 128), (slots, 128), (levels, rows, cols)] + [(rows // 2, cols)] * 2
    out = pl.pallas_call(
        functools.partial(scatter_first_kernel, capacity),
        out_shape=[jax.ShapeDtypeStruct(shape, F32) for shape in shapes],
        in_specs=[VMEM] * 2,
        out_specs=[VMEM] * len(shapes),
        scratch_shapes=[pltpu.VMEM((levels // 2 * rows, 2 * cols), F32)],
        compiler_params=PARAMS,
        name="scatter_first",
    )(arrived, sigma)
    return out


def lane_value(block, lane):
    return jnp.sum(jnp.where(lane_of(block.shape[0]) == lane, block, 0.0))


def lanes(values, rows):
    lane = lane_of(rows)
    out = jnp.zeros((rows, 128), F32)
    for index, value in enumerate(values):
        out = jnp.where(lane == index, value, out)
    return out


def scatter_next_kernel(capacity, last, arrived, row_at, col_at, sigma, *refs):
    if last:
        previous, field, eastward, westward, sums, total = refs
    else:
        previous, (field, eastward, westward, sums, total) = None, refs
    levels, rows, cols = sigma.shape
    stride = capacity + 1
    gathered = jnp.concatenate(
        [arrived[at : at + 1] for at in range(capacity, arrived.shape[0], stride)], axis=0
    )
    added = jnp.sum(gathered, axis=0, keepdims=True)
    sums[...] = jnp.broadcast_to(added, (8, 128))

    group = 128 if last else 64

    def load(index):
        return load_group(index, group, capacity, row_at, col_at, arrived, stride, 0)

    scatter_into(
        total, load, row_at.shape[0], levels // 2 * rows, 2 * cols, group
    )
    extra = None
    if last:
        beta = lane_value(added, 1) / lane_value(added, 0)

        def extra(level):
            return beta * previous[level]

    eastward[...], westward[...] = pack_sides(put_field(total, sigma, field, extra))


def scatter_next(arrived, row_at, col_at, sigma, capacity, previous=None):
    levels, rows, cols = sigma.shape
    last = previous is not None
    shapes = [(levels, rows, cols)] + [(rows // 2, cols)] * 2 + [(8, 128)]
    operands = [arrived, row_at, col_at, sigma] + ([previous] if last else [])
    out = pl.pallas_call(
        functools.partial(scatter_next_kernel, capacity, last),
        out_shape=[jax.ShapeDtypeStruct(shape, F32) for shape in shapes],
        in_specs=[VMEM] * len(operands),
        out_specs=[VMEM] * len(shapes),
        scratch_shapes=[pltpu.VMEM((levels // 2 * rows, 2 * cols), F32)],
        compiler_params=PARAMS,
        name="scatter_last" if last else "scatter_next",
    )(*operands)
    return out


def gather_from(fields, row_at, col_at, seen, table, group, wide):
    rows, cols = fields[0].shape
    half_rows, half_cols = len(fields) // 2 * rows, 2 * cols
    for level, field in enumerate(fields):
        high, low = parts(field.T)
        c, r = level % 2 * cols, level // 2 * rows
        table[c : c + cols, r : r + rows] = high
        table[c : c + cols, half_rows + r : half_rows + r + rows] = low
    row_iota = index_iota(half_rows)
    sublane = lax.broadcasted_iota(jnp.int32, (8, 128 * wide), 0)

    def step(index, carry):
        base = pl.multiple_of(index * group, group)
        row_block = row_at[pl.ds(base, group)]
        col_block = col_at[pl.ds(base, group)].astype(jnp.int32)
        found = []
        for j in range(0, group, wide):
            hot = jnp.concatenate(
                [one_hot(row_iota, row_block[i : i + 1]) for i in range(j, j + wide)], axis=1
            )
            hot = jnp.concatenate([hot, hot], axis=0)
            lines = jnp.dot(table[...], hot, preferred_element_type=F32)
            wanted = jnp.concatenate([col_block[i : i + 1] for i in range(j, j + wide)], axis=1)
            wanted = jnp.broadcast_to(wanted, (8, 128 * wide))
            tiles = [lines[i : i + 8] for i in range(0, half_cols, 8)]
            bit = 8
            while len(tiles) > 1:
                upper = (wanted & bit) != 0
                tiles = [
                    jnp.where(upper, tiles[i + 1], tiles[i]) for i in range(0, len(tiles), 2)
                ]
                bit = bit * 2
            value = jnp.sum(
                jnp.where((wanted & 7) == sublane, tiles[0], 0.0), axis=0, keepdims=True
            )
            found += [value[:, 128 * i : 128 * (i + 1)] for i in range(wide)]
        seen[pl.ds(base, group)] = jnp.concatenate(found, axis=0)
        return carry

    lax.fori_loop(0, row_at.shape[0] // group, step, 0)


def own_part(field, level, rows):
    inner = slice(EDGE + HALO, EDGE + HALO + rows)
    return pick_out(field[level, inner], field[level + 1, inner], level)


def total_of(pairs):
    added = None
    for left, right in pairs:
        term = left * right
        added = term if added is None else added + term
    return jnp.sum(added)


def observe_first_kernel(source, *refs):
    halo, weights, sigma, row_at, col_at = refs[:3], refs[3], refs[4], refs[5], refs[6]
    seen, right, image, sums, field, spare, table = refs[7:]
    levels, rows, cols = source.shape
    place(field, source, halo, halo[0].shape[0] - 1)
    clear_margins(spare)
    spare, field = smooth(field, spare, weights, 0, 80, True)
    right[...] = field[:, EDGE : EDGE + rows + 2 * HALO]
    own = [own_part(field, level, rows) for level in range(levels)]
    sums[...] = lanes([total_of([(value, value) for value in own])], 8)
    spare, field = smooth(field, spare, weights, 8, 72, True)
    fields = [sigma[level] * own_part(field, level, rows) for level in range(levels)]
    for level in range(levels):
        image[level] = fields[level]
    gather_from(fields, row_at, col_at, seen, table, 32, 4)


def observe_next_kernel(source, *refs):
    halo, weights, sigma, row_at, col_at = refs[:3], refs[3], refs[4], refs[5], refs[6]
    right, scalars = refs[7:9]
    seen, residual, image, sums, field, spare, table = refs[9:]
    levels, rows, cols = source.shape
    tall = rows + 2 * HALO
    norm, product = lane_value(scalars[0:1], 0), lane_value(scalars[0:1], 1)
    alpha = norm / (norm + product)
    place(field, source, halo, halo[0].shape[0] - 1)
    clear_margins(spare)
    spare, field = smooth(field, spare, weights, 0, 160, True)

    for tile in range(levels + 1):
        first = right[tile]
        field[tile, EDGE : EDGE + tall] = first - alpha * (first + field[tile, EDGE : EDGE + tall])
    own = [own_part(field, level, rows) for level in range(levels)]
    first = [pick_out(
            right[level, HALO : HALO + rows], right[level + 1, HALO : HALO + rows], level
        ) for level in range(levels)]
    for level in range(levels):
        residual[level] = own[level]
    sums[...] = lanes(
        [total_of([(value, value) for value in own]), total_of(list(zip(own, first)))], 8
    )
    spare, field = smooth(field, spare, weights, 8, 144, True)
    fields = [sigma[level] * own_part(field, level, rows) for level in range(levels)]
    for level in range(levels):
        image[level] = fields[level]
    gather_from(fields, row_at, col_at, seen, table, 64, 8)


def observe(source, halo, weights, sigma, row_at, col_at, right=None, scalars=None):
    levels, rows, cols = sigma.shape
    tall = rows + 2 * HALO
    slots = row_at.shape[0]
    first = right is None
    kept = (levels + 1, tall, cols) if first else (levels, rows, cols)
    shapes = [(slots, 128), kept, (levels, rows, cols), (8, 128)]
    operands = [source, *halo, weights, sigma, row_at, col_at]
    operands += [] if first else [right, scalars]
    return pl.pallas_call(
        observe_first_kernel if first else observe_next_kernel,
        out_shape=[jax.ShapeDtypeStruct(shape, F32) for shape in shapes],
        in_specs=[VMEM] * len(operands),
        out_specs=[VMEM] * len(shapes),
        scratch_shapes=[
            pltpu.VMEM((levels + 1, tall + 2 * EDGE, cols), F32),
            pltpu.VMEM((levels + 1, tall + 2 * EDGE, cols), F32),
            pltpu.VMEM(
                (2 * cols, levels * rows), BF16
            ),
        ],
        compiler_params=PARAMS,
        name="observe_first" if first else "observe_next",
    )(*operands)


def finish_kernel(source, *refs):
    halo, weights, right, residual_one, image_zero, image_one, scalars = refs[:3], *refs[3:9]
    increment, residual, field, spare = refs[9:]
    levels, rows, cols = source.shape
    norm_zero, norm_one, cross, product_zero, product_one, product_cross = [
        lane_value(scalars[0:1], index) for index in range(6)
    ]
    alpha_zero = norm_zero / (norm_zero + product_zero)
    beta = norm_one / norm_zero
    square = norm_one + 2.0 * beta * cross + beta * beta * norm_zero
    seen = product_one + 2.0 * beta * product_cross + beta * beta * product_zero
    alpha_one = norm_one / (square + seen)
    for level in range(levels):
        direction = image_one[level] + beta * image_zero[level]
        increment[level] = alpha_zero * image_zero[level] + alpha_one * direction
    place(field, source, halo, halo[0].shape[0] - 1)
    clear_margins(spare)
    spare, field = smooth(field, spare, weights, 8, 144, True)
    for level in range(levels):
        here = residual_one[level]
        direction = here + beta * pick_out(
            right[level, HALO : HALO + rows], right[level + 1, HALO : HALO + rows], level
        )
        image = direction + own_part(field, level, rows)
        residual[level] = here - alpha_one * image


def finish(source, halo, weights, right, residual_one, image_zero, image_one, scalars):
    levels, rows, cols = source.shape
    tall = rows + 2 * HALO
    return pl.pallas_call(
        finish_kernel,
        out_shape=[jax.ShapeDtypeStruct((levels, rows, cols), F32)] * 2,
        in_specs=[VMEM] * 10,
        out_specs=[VMEM] * 2,
        scratch_shapes=[pltpu.VMEM((levels + 1, tall + 2 * EDGE, cols), F32),
            pltpu.VMEM((levels + 1, tall + 2 * EDGE, cols), F32)],
        compiler_params=PARAMS,
        name="finish",
    )(source, *halo, weights, right, residual_one, image_zero, image_one, scalars)


def block_columns(values, weights, at):
    high, low = parts(values)
    first = jnp.concatenate([high, low, jnp.zeros((128 - 2 * GROUP, 128), BF16)], axis=0)
    second = jnp.concatenate([high, jnp.zeros((128 - GROUP, 128), BF16)], axis=0)
    right = jnp.concatenate([first, second], axis=1)
    lane = lane_of(128)
    column = jnp.where(lane < 2 * GROUP, lane % GROUP, GROUP)
    kept = jnp.zeros((128, 128), F32)
    for start in range(0, GROUP, 4):
        matrix = weights[at + start : at + start + 4].reshape(4 * 128, 128)
        left = jnp.concatenate(parts(matrix), axis=1)
        product = lax.dot_general(left, right, (((1,), (1,)), ((), ())), preferred_element_type=F32)
        for k in range(4):
            kept = jnp.where(column == start + k, product[k * 128 : (k + 1) * 128], kept)
    return kept


def turned(columns):
    rows = columns.T
    return rows[:GROUP] + rows[GROUP : 2 * GROUP]


def start_kernel(capacity, owner, cells, innovations, weights, mask, east, north, *refs):
    parcel, places, products, eastward, westward = refs[:5]
    count, held_cells, held_values, held_weights, held_mask, held_faces, held_sides = refs[5:12]
    columns, arrived, left = refs[12:]
    held = held_cells.shape[0]
    levels = mask.shape[0]
    steps = held // CHUNK
    moves = [
        (innovations, held_values),
        (cells, held_cells),
        (mask, held_mask),
        (east, held_faces.at[0]),
        (north, held_faces.at[1]),
    ]
    for step in range(steps):
        block = pl.ds(step * CHUNK, CHUNK)
        moves.append((weights.at[block], held_weights.at[block]))
    copies = [
        pltpu.make_async_copy(source, target, arrived.at[index])
        for index, (source, target) in enumerate(moves)
    ]
    for copy in copies[: 5 + AHEAD]:
        copy.start()
    parcel[...] = jnp.zeros_like(parcel)
    for index in range(count.shape[0]):
        count[index] = 0
    for index in range(held):
        target = owner[index]
        rank = count[target]
        count[target] = rank + 1
        places[index] = target * capacity + rank
        places[held + index] = target * (capacity + 1) + rank
    for copy in copies[2:5]:
        copy.wait()
    for index in range(2):
        fields = [held_mask[level].astype(F32) * held_faces[index, level] for level in range(levels)]
        for level in range(levels):
            held_faces[index, level] = fields[level]
        held_sides[0, index], held_sides[1, index] = pack_sides(fields)
    returns = [
        pltpu.make_async_copy(held_faces, products, left.at[0]),
        pltpu.make_async_copy(held_sides.at[0], eastward, left.at[1]),
        pltpu.make_async_copy(held_sides.at[1], westward, left.at[2]),
    ]
    for copy in returns:
        copy.start()
    copies[0].wait()
    copies[1].wait()
    for first in range(0, held, GROUP):
        if first % CHUNK == 0:
            step = first // CHUNK
            copies[5 + step].wait()
            if step + AHEAD < steps:
                copies[5 + step + AHEAD].start()
        columns[first // GROUP] = block_columns(
            held_values[first : first + GROUP], held_weights, first
        )
    for first in range(0, held, GROUP):
        result = turned(columns[first // GROUP])
        cell_rows = held_cells[first : first + GROUP].astype(F32)
        for k in range(GROUP):
            at = places[first + k] + owner[first + k] * capacity
            parcel[pl.ds(at, 1), :] = cell_rows[k : k + 1]
            parcel[pl.ds(at + capacity, 1), :] = result[k : k + 1]
    for copy in returns:
        copy.wait()


def start(owner, cells, innovations, weights, mask, east, north, devices, capacity):
    held, width = cells.shape
    rows, cols = mask.shape[1:]
    shapes = [(devices * 2 * capacity, width), (2 * held,), (2,) + mask.shape]
    shapes += [(2, rows // 2, cols)] * 2
    types = [F32, jnp.int32, F32, F32, F32]
    return pl.pallas_call(
        functools.partial(start_kernel, capacity),
        out_shape=[jax.ShapeDtypeStruct(shape, kind) for shape, kind in zip(shapes, types)],
        in_specs=[SMEM] + [HBM] * 6,
        out_specs=[VMEM, SMEM, HBM, HBM, HBM],
        scratch_shapes=[
            pltpu.SMEM((devices,), jnp.int32),
            pltpu.VMEM((held, width), jnp.int32),
            pltpu.VMEM((held, width), F32),
            pltpu.VMEM((held, width, width), F32),
            pltpu.VMEM(mask.shape, jnp.int32),
            pltpu.VMEM((2,) + mask.shape, F32),
            pltpu.VMEM((2, 2, rows // 2, cols), F32),
            pltpu.VMEM((held // GROUP, width, width), F32),
            pltpu.SemaphoreType.DMA((5 + held // CHUNK,)),
            pltpu.SemaphoreType.DMA((3,)),
        ],
        compiler_params=ROOMLESS,
        name="start",
    )(owner, cells, innovations, weights, mask, east, north)


def weigh_next_kernel(capacity, devices, last, places, returned, sums, weights, *refs):
    held = weights.shape[0]
    copies = []
    if last:
        sums_before, weighted_before, parcel, values, columns = refs
    else:
        parcel, weighted, values, columns, held_weights, arrived = refs
        for step in range(held // CHUNK):
            block = pl.ds(step * CHUNK, CHUNK)
            copies.append(
                pltpu.make_async_copy(
                    weights.at[block], held_weights.at[block], arrived.at[step]
                )
            )
        for copy in copies[:AHEAD]:
            copy.start()
        weights = held_weights
    parcel[...] = jnp.zeros_like(parcel)
    total = jnp.zeros((GROUP, 128), F32)
    total_cross = jnp.zeros((GROUP, 128), F32)
    for first in range(0, held, GROUP):
        here = jnp.concatenate(
            [returned[pl.ds(places[first + k], 1), :] for k in range(GROUP)], axis=0
        )
        values[first : first + GROUP] = here
        if copies and first % CHUNK == 0:
            step = first // CHUNK
            copies[step].wait()
            if step + AHEAD < len(copies):
                copies[step + AHEAD].start()
        columns[first // GROUP] = block_columns(here, weights, first)
    for first in range(0, held, GROUP):
        here = values[first : first + GROUP]
        result = turned(columns[first // GROUP])
        total += here * result
        if last:
            total_cross += here * weighted_before[first : first + GROUP]
        else:
            weighted[first : first + GROUP] = result
        for k in range(GROUP):
            parcel[pl.ds(places[held + first + k], 1), :] = result[k : k + 1]
    if last:
        scalars = [
            lane_value(sums_before[0:1], 0) / devices,
            lane_value(sums[0:1], 0),
            lane_value(sums[0:1], 1),
            lane_value(sums_before[0:1], 1) / devices,
            jnp.sum(total),
            jnp.sum(total_cross),
        ]
    else:
        scalars = [lane_value(sums[0:1], 0), jnp.sum(total)]
    row = lanes(scalars, 1)
    for target in range(devices):
        at = target * (capacity + 1) + capacity
        parcel[at : at + 1] = row


def weigh_next(places, returned, sums, weights, devices, capacity, before=None):
    held, width = weights.shape[:2]
    last = before is not None
    operands = [places, returned, sums, weights] + (list(before) if last else [])
    out_shape = [jax.ShapeDtypeStruct((devices * (capacity + 1), width), F32)]
    if not last:
        out_shape += [jax.ShapeDtypeStruct((held, width), F32)]
    return pl.pallas_call(
        functools.partial(weigh_next_kernel, capacity, devices, last),
        out_shape=out_shape,
        in_specs=[SMEM, VMEM, VMEM, VMEM if last else HBM] + [VMEM] * (len(operands) - 4),
        out_specs=[VMEM] * len(out_shape),
        scratch_shapes=[
            pltpu.VMEM((held, width), F32),
            pltpu.VMEM((held // GROUP, width, width), F32),
        ]
        + (
            []
            if last
            else [pltpu.VMEM(weights.shape, F32), pltpu.SemaphoreType.DMA((held // CHUNK,))]
        ),
        compiler_params=PARAMS if last else SNUG,
        name="weigh_last" if last else "weigh_next",
    )(*operands)


def swap(block):
    devices = lax.axis_size("lat") * lax.axis_size("lon")
    shares = block.reshape(devices, block.shape[0] // devices, 1, block.shape[1])
    got = lax.all_to_all(shares, ("lat", "lon"), split_axis=0, concat_axis=0, tiled=True)
    return got.reshape(block.shape)


def body(sigma, east_coef, north_coef, mask, innovations, cells, owner, obs_weights):
    devices = lax.axis_size("lat") * lax.axis_size("lon")
    held, width = cells.shape
    capacity = max(2, (2 * held + devices - 1) // devices)

    parcel, places, products, *sides = start(
        owner.reshape(held),
        cells,
        innovations,
        obs_weights,
        mask,
        east_coef,
        north_coef,
        devices,
        capacity,
    )
    face_columns = exchange_columns(sides)
    arrived = swap(parcel)

    row_at, col_at, field, *sides = scatter_first(arrived, sigma, capacity)
    face_columns, sides = lax.optimization_barrier((face_columns, sides))
    face_mixed, *face_rows, products = turn((products, *face_columns), keep=True)
    mixed, down, up = turn((field, *exchange_columns(sides)), rows_ahead=tuple(face_rows))
    before, after = exchange_rows(down, up)
    weights = face_weights(products, (before, after, face_mixed))
    seen, right, image_zero, sums = observe(
        field, (before, after, mixed), weights, sigma, row_at, col_at
    )
    returned = swap(seen)
    parcel, weighted = weigh_next(places, returned, sums, obs_weights, devices, capacity)
    arrived = swap(parcel)

    field_zero, *sides, scalars_zero = scatter_next(arrived, row_at, col_at, sigma, capacity)
    seen, residual_one, image_one, sums = observe(
        field_zero, exchange(field_zero, sides), weights, sigma, row_at, col_at, right, scalars_zero
    )
    returned = swap(seen)
    (parcel,) = weigh_next(
        places, returned, sums, obs_weights, devices, capacity, (scalars_zero, weighted)
    )
    arrived = swap(parcel)

    field, *sides, scalars = scatter_next(arrived, row_at, col_at, sigma, capacity, field_zero)
    increment, residual = finish(
        field, exchange(field, sides), weights, right, residual_one, image_zero, image_one, scalars
    )
    return (increment, residual)


def solution(mesh):
    return jax.shard_map(
        body,
        mesh=mesh,
        in_specs=(
            P(None, "lat", "lon"),
            P(None, "lat", "lon"),
            P(None, "lat", "lon"),
            P(None, "lat", "lon"),
            P(("lat", "lon"), None),
            P(("lat", "lon"), None),
            P(("lat", "lon"), None),
            P(("lat", "lon"), None, None),
        ),
        out_specs=(P(None, "lat", "lon"), P(None, "lat", "lon")),
        check_vma=False,
    )
```

```python
import functools

import jax
import jax.numpy as jnp
from jax import lax
from jax.experimental import pallas as pl
from jax.experimental.pallas import tpu as pltpu
from jax.sharding import PartitionSpec as P

PASSES = 5
HALO = 16
EDGE = 8
GROUP = 16
CHUNK = 16
AHEAD = 4
F32 = jnp.float32
BF16 = jnp.bfloat16
VMEM = pl.BlockSpec(memory_space=pltpu.VMEM)
HBM = pl.BlockSpec(memory_space=pltpu.HBM)
SMEM = pl.BlockSpec(memory_space=pltpu.SMEM)
PARAMS = pltpu.CompilerParams(vmem_limit_bytes=32 * 1024 * 1024)

ROOMLESS = pltpu.CompilerParams(vmem_limit_bytes=60 * 1024 * 1024)


SNUG = pltpu.CompilerParams(vmem_limit_bytes=52 * 1024 * 1024)


def parts(values):
    high = values.astype(BF16)
    low = (values - high.astype(F32)).astype(BF16)
    return high, low


def lane_of(rows):
    return lax.broadcasted_iota(jnp.int32, (rows, 128), 1)


def pack_sides(fields):
    lane = lane_of(fields[0].shape[0])
    packed = jnp.zeros_like(fields[0])
    for level, field in enumerate(fields):
        start = 2 * HALO * level
        turned = pltpu.roll(field, (start + HALO) % 128, 1)
        packed = jnp.where((lane >= start) & (lane < start + 2 * HALO), turned, packed)
    half = packed.shape[0] // 2
    low, high = packed[:half], packed[half:]
    western = lane[:half] % (2 * HALO) < HALO
    return (
        jnp.where(western, low, pltpu.roll(high, HALO, 1)),
        jnp.where(western, pltpu.roll(low, 128 - HALO, 1), high),
    )


def unpack_sides(from_east, from_west):
    western = lane_of(from_east.shape[0]) % (2 * HALO) < HALO
    low = jnp.where(western, from_west, pltpu.roll(from_east, HALO, 1))
    high = jnp.where(western, pltpu.roll(from_west, 128 - HALO, 1), from_east)
    return jnp.concatenate([low, high], axis=0)


def turn_kernel(count, ahead, *refs):
    sources, extra = refs[: 3 * count], refs[3 * count : 3 * count + ahead]
    *mixed, down, up = refs[3 * count + ahead : 4 * count + ahead + 2]
    for kept in refs[4 * count + ahead + 2 :]:
        kept[...] = sources[0][...]
    row = 0
    if extra:
        row = extra[0].shape[0]
        down[0:row] = extra[0][...]
        up[0:row] = extra[1][...]
    for index in range(count):
        fields, from_east, from_west = sources[3 * index : 3 * index + 3]
        levels, rows, _ = fields.shape[-3:]
        for at in [(i,) for i in range(fields.shape[0])] if len(fields.shape) == 4 else [()]:
            sides = unpack_sides(from_east[at + (...,)], from_west[at + (...,)])
            mixed[index][at + (...,)] = sides
            for level in range(levels):
                down[row, level] = fields[at + (level, slice(rows - HALO, rows))]
                up[row, level] = fields[at + (level, slice(0, HALO))]
            down[row, levels] = sides[rows - HALO :]
            up[row, levels] = sides[:HALO]
            row += 1


def exchange(fields, sides):
    mixed, down, up = turn((fields, *exchange_columns(sides)))
    return (*exchange_rows(down, up), mixed)


def exchange_columns(sides):
    wide = lax.axis_size("lon")
    east = [(i, (i + 1) % wide) for i in range(wide)]
    from_west = lax.ppermute(sides[0], "lon", east)
    from_east = lax.ppermute(sides[1], "lon", [(to, at) for at, to in east])
    return from_east, from_west


def turn(*groups, rows_ahead=(), keep=False):
    levels, rows, cols = groups[0][0].shape[-3:]
    shapes = [fields.shape[:-3] + (rows, cols) for fields, _, _ in groups]
    total = sum(fields.shape[0] if fields.ndim == 4 else 1 for fields, _, _ in groups)
    total += rows_ahead[0].shape[0] if rows_ahead else 0
    shapes += [(total, levels + 1, HALO, cols)] * 2
    shapes += [groups[0][0].shape] if keep else []
    return pl.pallas_call(
        functools.partial(turn_kernel, len(groups), len(rows_ahead)),
        out_shape=[jax.ShapeDtypeStruct(shape, F32) for shape in shapes],
        in_specs=[VMEM] * (3 * len(groups) + len(rows_ahead)),
        out_specs=[VMEM] * len(shapes),
        compiler_params=PARAMS,
        name="turn",
    )(*[array for group in groups for array in group], *rows_ahead)


def exchange_rows(down, up):
    tall = lax.axis_size("lat")
    first = [(i, i + 1) for i in range(0, tall - 1, 2)]
    second = [(i, i + 1) for i in range(1, tall - 1, 2)]
    even = lax.axis_index("lat") % 2 == 0
    one = lax.ppermute(
        jnp.where(even, down, up), "lat", first + [(to, at) for at, to in first]
    )
    two = lax.ppermute(
        jnp.where(even, up, down), "lat", second + [(to, at) for at, to in second]
    )
    return jnp.where(even, two, one), jnp.where(even, one, two)


def neighbours(tiles):
    lane = lane_of(tiles[0].shape[0])
    later, earlier = tiles[1:] + tiles[:1], tiles[-1:] + tiles[:-1]
    after = [
        pltpu.roll(jnp.where(lane == 0, other, tile), 127, 1) for tile, other in zip(tiles, later)
    ]
    before = [
        pltpu.roll(jnp.where(lane == 127, other, tile), 1, 1) for tile, other in zip(tiles, earlier)
    ]
    return after, before


def lay_out(fields, side):
    lane = lane_of(side.shape[0])
    width = 2 * HALO
    turned = [pltpu.roll(field, width * level + HALO, 1) for level, field in enumerate(fields)]
    tiles = []
    for tile in range(len(fields) + 1):
        left, right = width * tile - HALO, width * tile + HALO
        before = turned[tile - 1] if tile else turned[0]
        after = turned[tile] if tile < len(fields) else turned[-1]
        value = jnp.where(lane < left, before, after)
        tiles.append(jnp.where((lane >= left) & (lane < right), side, value))
    return tiles


def pick_out(first, second, level):
    start = 2 * HALO * level + HALO
    return pltpu.roll(jnp.where(lane_of(first.shape[0]) >= start, first, second), 128 - start, 1)


def place(target, own, halo, row, lead=()):
    before, after, mixed = halo
    levels = before.shape[-3] - 1
    rows = mixed.shape[-2]
    spans = (
        (EDGE, before, (row,), before[row, levels]),
        (EDGE + HALO, own, lead, mixed[lead + (...,)]),
        (EDGE + HALO + rows, after, (row,), after[row, levels]),
    )
    for start, source, at, side in spans:
        tiles = lay_out([source[at + (level,)] for level in range(levels)], side)
        for tile, value in enumerate(tiles):
            target[lead + (tile, slice(start, start + side.shape[0]))] = value
    blank = jnp.zeros((EDGE, 128), F32)
    for tile in range(levels + 1):
        target[lead + (tile, slice(0, EDGE))] = blank
        target[lead + (tile, slice(EDGE + 2 * HALO + rows, 2 * EDGE + 2 * HALO + rows))] = blank


def clear_margins(target):
    blank = jnp.zeros((target.shape[0], EDGE, 128), F32)
    target[:, 0:EDGE] = blank
    target[:, target.shape[1] - EDGE :] = blank


def face_kernel(products, before, after, mixed, weights, padded, faces):
    tiles, tall = weights.shape[1:3]
    for index in range(2):
        place(padded, products, (before, after, mixed), index, (index,))
    inner = slice(EDGE, EDGE + tall)
    faces[:, 0:EDGE] = jnp.zeros((tiles, EDGE, 128), F32)
    faces[:, EDGE + tall :] = jnp.zeros((tiles, EDGE, 128), F32)
    land = [(padded[0, tile, inner] > 0.0).astype(F32) for tile in range(tiles)]
    land_east, _ = neighbours(land)
    east_face = [padded[0, tile, inner] * land_east[tile] for tile in range(tiles)]
    _, west_face = neighbours(east_face)
    for tile in range(tiles):
        land_north = (padded[0, tile, EDGE + 1 : EDGE + 1 + tall] > 0.0).astype(F32)
        north_face = padded[1, tile, inner] * land_north
        faces[tile, inner] = north_face
        south_face = faces[tile, EDGE - 1 : EDGE - 1 + tall]
        weights[0, tile] = 1.0 - (
            ((east_face[tile] + west_face[tile]) + north_face) + south_face
        )
        weights[1, tile] = east_face[tile]
        weights[2, tile] = west_face[tile]
        weights[3, tile] = north_face
        weights[4, tile] = south_face


def face_weights(products, halo):
    _, levels, rows, cols = products.shape
    tall = rows + 2 * HALO
    return pl.pallas_call(
        face_kernel,
        out_shape=jax.ShapeDtypeStruct((5, levels + 1, tall, cols), F32),
        in_specs=[VMEM] * 4,
        out_specs=VMEM,
        scratch_shapes=[
            pltpu.VMEM((2, levels + 1, tall + 2 * EDGE, cols), F32),
            pltpu.VMEM((levels + 1, tall + 2 * EDGE, cols), F32),
        ],
        compiler_params=PARAMS,
        name="face_weights",
    )(products, *halo)


def sweep(source, target, weights, rows_from, rows_to, block):
    tiles = source.shape[0]

    def step(index, carry):
        first = pl.multiple_of(rows_from + index * block, 8)
        for start in range(0, block, 16):
            count = min(16, block - start)
            at = pl.multiple_of(first + EDGE + start, 8)
            inner = pl.ds(pl.multiple_of(first + start, 8), count)
            here = [source[tile, pl.ds(at, count)] for tile in range(tiles)]
            east, west = neighbours(here)
            for tile in range(tiles):
                above = source[tile, pl.ds(at + 1, count)]
                below = source[tile, pl.ds(at - 1, count)]
                total = weights[0, tile, inner] * here[tile]
                total += weights[1, tile, inner] * east[tile]
                total += weights[2, tile, inner] * west[tile]
                total += weights[3, tile, inner] * above
                total += weights[4, tile, inner] * below
                target[tile, pl.ds(at, count)] = total
        return carry

    lax.fori_loop(0, (rows_to - rows_from) // block, step, 0)


def smooth(field, spare, weights, wide):
    tall = weights.shape[2]
    inner, own = slice(8, tall - 8), slice(HALO, tall - HALO)

    def sweep_rows(source, target, rows):
        sweep(source, target, weights, rows.start, rows.stop, rows.stop - rows.start)

    def two(index, carry):
        one, other = (spare, field) if wide else (field, spare)
        sweep_rows(one, other, inner)
        sweep_rows(other, one, inner)
        return carry

    if wide:
        sweep_rows(field, spare, slice(0, tall))
        lax.fori_loop(0, PASSES // 2, two, 0)
    else:
        lax.fori_loop(0, PASSES // 2, two, 0)
        sweep_rows(field, spare, own)
    return field, spare


def index_iota(cells):
    return lax.broadcasted_iota(jnp.int32, (cells, 128), 0).astype(F32).astype(BF16)


def spread_row(row, count):
    return jnp.broadcast_to(jnp.broadcast_to(row, (16, 128)).astype(BF16)[0:1], (count, 128))


def one_hot(iota, row):
    count = iota.shape[0]
    return jnp.where(
        iota == spread_row(row, count), jnp.ones((count, 128), BF16), jnp.zeros((count, 128), BF16)
    )


def scatter_into(total, load_rows, slots, half_rows, half_cols, group):
    row_iota = index_iota(half_rows)
    col_iota = index_iota(half_cols)
    total[...] = jnp.zeros_like(total)

    def step(index, carry):
        high_rows, low_rows, columns = [], [], []
        for row_index, col_index, value in load_rows(index):
            high, low = parts(jnp.broadcast_to(value, (16, 128)))
            high = jnp.broadcast_to(high[0:1], (half_rows, 128))
            low = jnp.broadcast_to(low[0:1], (half_rows, 128))
            hit = row_iota == spread_row(row_index, half_rows)
            zero = jnp.zeros((half_rows, 128), BF16)
            high_rows.append(jnp.where(hit, high, zero))
            low_rows.append(jnp.where(hit, low, zero))
            columns.append(one_hot(col_iota, col_index))
        left = jnp.concatenate(high_rows + low_rows, axis=1)
        right = jnp.concatenate(columns + columns, axis=1)
        total[...] += lax.dot_general(
            left, right, (((1,), (1,)), ((), ())), preferred_element_type=F32
        )
        return carry

    lax.fori_loop(0, slots // group, step, 0)


def load_group(index, group, capacity, row_at, col_at, arrived, stride, first_slot):
    base = pl.multiple_of(index * group, group)
    row_block = row_at[pl.ds(base, group)]
    col_block = col_at[pl.ds(base, group)]
    for j in range(group):
        source = index * (group // capacity) + j // capacity
        at = source * stride + first_slot + j % capacity
        yield row_block[j : j + 1], col_block[j : j + 1], arrived[pl.ds(at, 1)]


def split_cells(cells, rows, cols):
    level = cells // (rows * cols)
    row = (cells // cols) % rows
    col = cells % cols
    return (level // 2) * rows + row, (level % 2) * cols + col


def put_field(total, sigma, field, extra=None):
    levels, rows, cols = sigma.shape
    fields = []
    for level in range(levels):
        r, c = level // 2 * rows, level % 2 * cols
        value = total[r : r + rows, c : c + cols]
        value = sigma[level] * value
        if extra is not None:
            value = value + extra(level)
        field[level] = value
        fields.append(value)
    return fields


def scatter_first_kernel(capacity, arrived, sigma, row_at, col_at, field, *refs):
    eastward, westward, total = refs
    levels, rows, cols = sigma.shape
    stride = 2 * capacity
    cells = jnp.concatenate(
        [arrived[at : at + capacity] for at in range(0, arrived.shape[0], stride)], axis=0
    )
    row_index, col_index = split_cells(cells.astype(jnp.int32), rows, cols)
    row_at[...] = row_index.astype(F32)
    col_at[...] = col_index.astype(F32)

    def load(index):
        return load_group(index, 64, capacity, row_at, col_at, arrived, stride, capacity)

    scatter_into(total, load, row_at.shape[0], levels // 2 * rows, 2 * cols, 64)
    eastward[...], westward[...] = pack_sides(put_field(total, sigma, field))


def scatter_first(arrived, sigma, capacity):
    levels, rows, cols = sigma.shape
    slots = arrived.shape[0] // 2
    shapes = [(slots, 128), (slots, 128), (levels, rows, cols)] + [(rows // 2, cols)] * 2
    out = pl.pallas_call(
        functools.partial(scatter_first_kernel, capacity),
        out_shape=[jax.ShapeDtypeStruct(shape, F32) for shape in shapes],
        in_specs=[VMEM] * 2,
        out_specs=[VMEM] * len(shapes),
        scratch_shapes=[pltpu.VMEM((levels // 2 * rows, 2 * cols), F32)],
        compiler_params=PARAMS,
        name="scatter_first",
    )(arrived, sigma)
    return out


def lane_value(block, lane):
    return jnp.sum(jnp.where(lane_of(block.shape[0]) == lane, block, 0.0))


def lanes(values, rows):
    lane = lane_of(rows)
    out = jnp.zeros((rows, 128), F32)
    for index, value in enumerate(values):
        out = jnp.where(lane == index, value, out)
    return out


def scatter_next_kernel(capacity, last, arrived, row_at, col_at, sigma, *refs):
    if last:
        previous, field, eastward, westward, sums, total = refs
    else:
        previous, (field, eastward, westward, sums, total) = None, refs
    levels, rows, cols = sigma.shape
    stride = capacity + 1
    gathered = jnp.concatenate(
        [arrived[at : at + 1] for at in range(capacity, arrived.shape[0], stride)], axis=0
    )
    added = jnp.sum(gathered, axis=0, keepdims=True)
    sums[...] = jnp.broadcast_to(added, (8, 128))

    group = 128 if last else 64

    def load(index):
        return load_group(index, group, capacity, row_at, col_at, arrived, stride, 0)

    scatter_into(
        total, load, row_at.shape[0], levels // 2 * rows, 2 * cols, group
    )
    extra = None
    if last:
        beta = lane_value(added, 1) / lane_value(added, 0)

        def extra(level):
            return beta * previous[level]

    eastward[...], westward[...] = pack_sides(put_field(total, sigma, field, extra))


def scatter_next(arrived, row_at, col_at, sigma, capacity, previous=None):
    levels, rows, cols = sigma.shape
    last = previous is not None
    shapes = [(levels, rows, cols)] + [(rows // 2, cols)] * 2 + [(8, 128)]
    operands = [arrived, row_at, col_at, sigma] + ([previous] if last else [])
    out = pl.pallas_call(
        functools.partial(scatter_next_kernel, capacity, last),
        out_shape=[jax.ShapeDtypeStruct(shape, F32) for shape in shapes],
        in_specs=[VMEM] * len(operands),
        out_specs=[VMEM] * len(shapes),
        scratch_shapes=[pltpu.VMEM((levels // 2 * rows, 2 * cols), F32)],
        compiler_params=PARAMS,
        name="scatter_last" if last else "scatter_next",
    )(*operands)
    return out


def gather_from(fields, row_at, col_at, seen, table, group, wide):
    rows, cols = fields[0].shape
    half_rows, half_cols = len(fields) // 2 * rows, 2 * cols
    for level, field in enumerate(fields):
        high, low = parts(field.T)
        c, r = level % 2 * cols, level // 2 * rows
        table[c : c + cols, r : r + rows] = high
        table[c : c + cols, half_rows + r : half_rows + r + rows] = low
    row_iota = index_iota(half_rows)
    sublane = lax.broadcasted_iota(jnp.int32, (8, 128 * wide), 0)

    def step(index, carry):
        base = pl.multiple_of(index * group, group)
        row_block = row_at[pl.ds(base, group)]
        col_block = col_at[pl.ds(base, group)].astype(jnp.int32)
        found = []
        for j in range(0, group, wide):
            hot = jnp.concatenate(
                [one_hot(row_iota, row_block[i : i + 1]) for i in range(j, j + wide)], axis=1
            )
            hot = jnp.concatenate([hot, hot], axis=0)
            lines = jnp.dot(table[...], hot, preferred_element_type=F32)
            wanted = jnp.concatenate([col_block[i : i + 1] for i in range(j, j + wide)], axis=1)
            wanted = jnp.broadcast_to(wanted, (8, 128 * wide))
            tiles = [lines[i : i + 8] for i in range(0, half_cols, 8)]
            bit = 8
            while len(tiles) > 1:
                upper = (wanted & bit) != 0
                tiles = [
                    jnp.where(upper, tiles[i + 1], tiles[i]) for i in range(0, len(tiles), 2)
                ]
                bit = bit * 2
            value = jnp.sum(
                jnp.where((wanted & 7) == sublane, tiles[0], 0.0), axis=0, keepdims=True
            )
            found += [value[:, 128 * i : 128 * (i + 1)] for i in range(wide)]
        seen[pl.ds(base, group)] = jnp.concatenate(found, axis=0)
        return carry

    lax.fori_loop(0, row_at.shape[0] // group, step, 0)


def own_part(field, level, rows):
    inner = slice(EDGE + HALO, EDGE + HALO + rows)
    return pick_out(field[level, inner], field[level + 1, inner], level)


def total_of(pairs):
    added = None
    for left, right in pairs:
        term = left * right
        added = term if added is None else added + term
    return jnp.sum(added)


def observe_first_kernel(source, *refs):
    halo, weights, sigma, row_at, col_at = refs[:3], refs[3], refs[4], refs[5], refs[6]
    seen, right, image, sums, field, spare, table = refs[7:]
    levels, rows, cols = source.shape
    place(field, source, halo, halo[0].shape[0] - 1)
    clear_margins(spare)
    spare, field = smooth(field, spare, weights, True)
    right[...] = field[:, EDGE : EDGE + rows + 2 * HALO]
    own = [own_part(field, level, rows) for level in range(levels)]
    sums[...] = lanes([total_of([(value, value) for value in own])], 8)
    spare, field = smooth(field, spare, weights, False)
    fields = [sigma[level] * own_part(field, level, rows) for level in range(levels)]
    for level in range(levels):
        image[level] = fields[level]
    gather_from(fields, row_at, col_at, seen, table, 64, 8)


def observe_next_kernel(source, *refs):
    halo, weights, sigma, row_at, col_at = refs[:3], refs[3], refs[4], refs[5], refs[6]
    right, scalars = refs[7:9]
    seen, residual, image, sums, field, spare, table = refs[9:]
    levels, rows, cols = source.shape
    tall = rows + 2 * HALO
    norm, product = lane_value(scalars[0:1], 0), lane_value(scalars[0:1], 1)
    alpha = norm / (norm + product)
    place(field, source, halo, halo[0].shape[0] - 1)
    clear_margins(spare)
    spare, field = smooth(field, spare, weights, True)

    for tile in range(levels + 1):
        first = right[tile]
        field[tile, EDGE : EDGE + tall] = first - alpha * (first + field[tile, EDGE : EDGE + tall])
    own = [own_part(field, level, rows) for level in range(levels)]
    first = [pick_out(
            right[level, HALO : HALO + rows], right[level + 1, HALO : HALO + rows], level
        ) for level in range(levels)]
    for level in range(levels):
        residual[level] = own[level]
    sums[...] = lanes(
        [total_of([(value, value) for value in own]), total_of(list(zip(own, first)))], 8
    )
    spare, field = smooth(field, spare, weights, False)
    fields = [sigma[level] * own_part(field, level, rows) for level in range(levels)]
    for level in range(levels):
        image[level] = fields[level]
    gather_from(fields, row_at, col_at, seen, table, 64, 8)


def observe(source, halo, weights, sigma, row_at, col_at, right=None, scalars=None):
    levels, rows, cols = sigma.shape
    tall = rows + 2 * HALO
    slots = row_at.shape[0]
    first = right is None
    kept = (levels + 1, tall, cols) if first else (levels, rows, cols)
    shapes = [(slots, 128), kept, (levels, rows, cols), (8, 128)]
    operands = [source, *halo, weights, sigma, row_at, col_at]
    operands += [] if first else [right, scalars]
    return pl.pallas_call(
        observe_first_kernel if first else observe_next_kernel,
        out_shape=[jax.ShapeDtypeStruct(shape, F32) for shape in shapes],
        in_specs=[VMEM] * len(operands),
        out_specs=[VMEM] * len(shapes),
        scratch_shapes=[
            pltpu.VMEM((levels + 1, tall + 2 * EDGE, cols), F32),
            pltpu.VMEM((levels + 1, tall + 2 * EDGE, cols), F32),
            pltpu.VMEM(
                (2 * cols, levels * rows), BF16
            ),
        ],
        compiler_params=PARAMS,
        name="observe_first" if first else "observe_next",
    )(*operands)


def finish_kernel(source, *refs):
    halo, weights, right, residual_one, image_zero, image_one, scalars = refs[:3], *refs[3:9]
    increment, residual, field, spare = refs[9:]
    levels, rows, cols = source.shape
    norm_zero, norm_one, cross, product_zero, product_one, product_cross = [
        lane_value(scalars[0:1], index) for index in range(6)
    ]
    alpha_zero = norm_zero / (norm_zero + product_zero)
    beta = norm_one / norm_zero
    square = norm_one + 2.0 * beta * cross + beta * beta * norm_zero
    seen = product_one + 2.0 * beta * product_cross + beta * beta * product_zero
    alpha_one = norm_one / (square + seen)
    for level in range(levels):
        direction = image_one[level] + beta * image_zero[level]
        increment[level] = alpha_zero * image_zero[level] + alpha_one * direction
    place(field, source, halo, halo[0].shape[0] - 1)
    clear_margins(spare)
    spare, field = smooth(field, spare, weights, False)
    for level in range(levels):
        here = residual_one[level]
        direction = here + beta * pick_out(
            right[level, HALO : HALO + rows], right[level + 1, HALO : HALO + rows], level
        )
        image = direction + own_part(field, level, rows)
        residual[level] = here - alpha_one * image


def finish(source, halo, weights, right, residual_one, image_zero, image_one, scalars):
    levels, rows, cols = source.shape
    tall = rows + 2 * HALO
    return pl.pallas_call(
        finish_kernel,
        out_shape=[jax.ShapeDtypeStruct((levels, rows, cols), F32)] * 2,
        in_specs=[VMEM] * 10,
        out_specs=[VMEM] * 2,
        scratch_shapes=[pltpu.VMEM((levels + 1, tall + 2 * EDGE, cols), F32),
            pltpu.VMEM((levels + 1, tall + 2 * EDGE, cols), F32)],
        compiler_params=PARAMS,
        name="finish",
    )(source, *halo, weights, right, residual_one, image_zero, image_one, scalars)


def block_columns(values, weights, at):
    high, low = parts(values)
    first = jnp.concatenate([high, low, jnp.zeros((128 - 2 * GROUP, 128), BF16)], axis=0)
    second = jnp.concatenate([high, jnp.zeros((128 - GROUP, 128), BF16)], axis=0)
    right = jnp.concatenate([first, second], axis=1)
    lane = lane_of(128)
    column = jnp.where(lane < 2 * GROUP, lane % GROUP, GROUP)
    kept = jnp.zeros((128, 128), F32)
    for start in range(0, GROUP, 4):
        matrix = weights[at + start : at + start + 4].reshape(4 * 128, 128)
        left = jnp.concatenate(parts(matrix), axis=1)
        product = lax.dot_general(left, right, (((1,), (1,)), ((), ())), preferred_element_type=F32)
        for k in range(4):
            kept = jnp.where(column == start + k, product[k * 128 : (k + 1) * 128], kept)
    return kept


def turned(columns):
    rows = columns.T
    return rows[:GROUP] + rows[GROUP : 2 * GROUP]


def start_kernel(capacity, owner, cells, innovations, weights, mask, east, north, *refs):
    parcel, places, products, eastward, westward = refs[:5]
    count, held_cells, held_values, held_weights, held_mask, held_faces, held_sides = refs[5:12]
    columns, arrived, left = refs[12:]
    held = held_cells.shape[0]
    levels = mask.shape[0]
    steps = held // CHUNK
    moves = [
        (innovations, held_values),
        (cells, held_cells),
        (mask, held_mask),
        (east, held_faces.at[0]),
        (north, held_faces.at[1]),
    ]
    for step in range(steps):
        block = pl.ds(step * CHUNK, CHUNK)
        moves.append((weights.at[block], held_weights.at[block]))
    copies = [
        pltpu.make_async_copy(source, target, arrived.at[index])
        for index, (source, target) in enumerate(moves)
    ]
    for copy in copies[: 5 + AHEAD]:
        copy.start()
    parcel[...] = jnp.zeros_like(parcel)
    for index in range(count.shape[0]):
        count[index] = 0
    for index in range(held):
        target = owner[index]
        rank = count[target]
        count[target] = rank + 1
        places[index] = target * capacity + rank
        places[held + index] = target * (capacity + 1) + rank
    for copy in copies[2:5]:
        copy.wait()
    for index in range(2):
        fields = [held_mask[level].astype(F32) * held_faces[index, level] for level in range(levels)]
        for level in range(levels):
            held_faces[index, level] = fields[level]
        held_sides[0, index], held_sides[1, index] = pack_sides(fields)
    returns = [
        pltpu.make_async_copy(held_faces, products, left.at[0]),
        pltpu.make_async_copy(held_sides.at[0], eastward, left.at[1]),
        pltpu.make_async_copy(held_sides.at[1], westward, left.at[2]),
    ]
    for copy in returns:
        copy.start()
    copies[0].wait()
    copies[1].wait()
    for first in range(0, held, GROUP):
        if first % CHUNK == 0:
            step = first // CHUNK
            copies[5 + step].wait()
            if step + AHEAD < steps:
                copies[5 + step + AHEAD].start()
        columns[first // GROUP] = block_columns(
            held_values[first : first + GROUP], held_weights, first
        )
    for first in range(0, held, GROUP):
        result = turned(columns[first // GROUP])
        cell_rows = held_cells[first : first + GROUP].astype(F32)
        for k in range(GROUP):
            at = places[first + k] + owner[first + k] * capacity
            parcel[pl.ds(at, 1), :] = cell_rows[k : k + 1]
            parcel[pl.ds(at + capacity, 1), :] = result[k : k + 1]
    for copy in returns:
        copy.wait()


def start(owner, cells, innovations, weights, mask, east, north, devices, capacity):
    held, width = cells.shape
    rows, cols = mask.shape[1:]
    shapes = [(devices * 2 * capacity, width), (2 * held,), (2,) + mask.shape]
    shapes += [(2, rows // 2, cols)] * 2
    types = [F32, jnp.int32, F32, F32, F32]
    return pl.pallas_call(
        functools.partial(start_kernel, capacity),
        out_shape=[jax.ShapeDtypeStruct(shape, kind) for shape, kind in zip(shapes, types)],
        in_specs=[SMEM] + [HBM] * 6,
        out_specs=[VMEM, SMEM, HBM, HBM, HBM],
        scratch_shapes=[
            pltpu.SMEM((devices,), jnp.int32),
            pltpu.VMEM((held, width), jnp.int32),
            pltpu.VMEM((held, width), F32),
            pltpu.VMEM((held, width, width), F32),
            pltpu.VMEM(mask.shape, jnp.int32),
            pltpu.VMEM((2,) + mask.shape, F32),
            pltpu.VMEM((2, 2, rows // 2, cols), F32),
            pltpu.VMEM((held // GROUP, width, width), F32),
            pltpu.SemaphoreType.DMA((5 + held // CHUNK,)),
            pltpu.SemaphoreType.DMA((3,)),
        ],
        compiler_params=ROOMLESS,
        name="start",
    )(owner, cells, innovations, weights, mask, east, north)


def weigh_next_kernel(capacity, devices, last, places, returned, sums, weights, *refs):
    held = weights.shape[0]
    copies = []
    if last:
        sums_before, weighted_before, parcel, values, columns = refs
    else:
        parcel, weighted, values, columns, held_weights, arrived = refs
        for step in range(held // CHUNK):
            block = pl.ds(step * CHUNK, CHUNK)
            copies.append(
                pltpu.make_async_copy(
                    weights.at[block], held_weights.at[block], arrived.at[step]
                )
            )
        for copy in copies[:AHEAD]:
            copy.start()
        weights = held_weights
    parcel[...] = jnp.zeros_like(parcel)
    total = jnp.zeros((GROUP, 128), F32)
    total_cross = jnp.zeros((GROUP, 128), F32)
    for first in range(0, held, GROUP):
        here = jnp.concatenate(
            [returned[pl.ds(places[first + k], 1), :] for k in range(GROUP)], axis=0
        )
        values[first : first + GROUP] = here
        if copies and first % CHUNK == 0:
            step = first // CHUNK
            copies[step].wait()
            if step + AHEAD < len(copies):
                copies[step + AHEAD].start()
        columns[first // GROUP] = block_columns(here, weights, first)
    for first in range(0, held, GROUP):
        here = values[first : first + GROUP]
        result = turned(columns[first // GROUP])
        total += here * result
        if last:
            total_cross += here * weighted_before[first : first + GROUP]
        else:
            weighted[first : first + GROUP] = result
        for k in range(GROUP):
            parcel[pl.ds(places[held + first + k], 1), :] = result[k : k + 1]
    if last:
        scalars = [
            lane_value(sums_before[0:1], 0) / devices,
            lane_value(sums[0:1], 0),
            lane_value(sums[0:1], 1),
            lane_value(sums_before[0:1], 1) / devices,
            jnp.sum(total),
            jnp.sum(total_cross),
        ]
    else:
        scalars = [lane_value(sums[0:1], 0), jnp.sum(total)]
    row = lanes(scalars, 1)
    for target in range(devices):
        at = target * (capacity + 1) + capacity
        parcel[at : at + 1] = row


def weigh_next(places, returned, sums, weights, devices, capacity, before=None):
    held, width = weights.shape[:2]
    last = before is not None
    operands = [places, returned, sums, weights] + (list(before) if last else [])
    out_shape = [jax.ShapeDtypeStruct((devices * (capacity + 1), width), F32)]
    if not last:
        out_shape += [jax.ShapeDtypeStruct((held, width), F32)]
    return pl.pallas_call(
        functools.partial(weigh_next_kernel, capacity, devices, last),
        out_shape=out_shape,
        in_specs=[SMEM, VMEM, VMEM, VMEM if last else HBM] + [VMEM] * (len(operands) - 4),
        out_specs=[VMEM] * len(out_shape),
        scratch_shapes=[
            pltpu.VMEM((held, width), F32),
            pltpu.VMEM((held // GROUP, width, width), F32),
        ]
        + (
            []
            if last
            else [pltpu.VMEM(weights.shape, F32), pltpu.SemaphoreType.DMA((held // CHUNK,))]
        ),
        compiler_params=PARAMS if last else SNUG,
        name="weigh_last" if last else "weigh_next",
    )(*operands)


def swap(block):
    devices = lax.axis_size("lat") * lax.axis_size("lon")
    shares = block.reshape(devices, block.shape[0] // devices, 1, block.shape[1])
    got = lax.all_to_all(shares, ("lat", "lon"), split_axis=0, concat_axis=0, tiled=True)
    return got.reshape(block.shape)


def body(sigma, east_coef, north_coef, mask, innovations, cells, owner, obs_weights):
    devices = lax.axis_size("lat") * lax.axis_size("lon")
    held, width = cells.shape
    capacity = max(2, (2 * held + devices - 1) // devices)

    parcel, places, products, *sides = start(
        owner.reshape(held),
        cells,
        innovations,
        obs_weights,
        mask,
        east_coef,
        north_coef,
        devices,
        capacity,
    )
    face_columns = exchange_columns(sides)
    arrived = swap(parcel)

    row_at, col_at, field, *sides = scatter_first(arrived, sigma, capacity)
    face_columns, sides = lax.optimization_barrier((face_columns, sides))
    face_mixed, *face_rows, products = turn((products, *face_columns), keep=True)
    mixed, down, up = turn((field, *exchange_columns(sides)), rows_ahead=tuple(face_rows))
    before, after = exchange_rows(down, up)
    weights = face_weights(products, (before, after, face_mixed))
    seen, right, image_zero, sums = observe(
        field, (before, after, mixed), weights, sigma, row_at, col_at
    )
    returned = swap(seen)
    parcel, weighted = weigh_next(places, returned, sums, obs_weights, devices, capacity)
    arrived = swap(parcel)

    field_zero, *sides, scalars_zero = scatter_next(arrived, row_at, col_at, sigma, capacity)
    seen, residual_one, image_one, sums = observe(
        field_zero, exchange(field_zero, sides), weights, sigma, row_at, col_at, right, scalars_zero
    )
    returned = swap(seen)
    (parcel,) = weigh_next(
        places, returned, sums, obs_weights, devices, capacity, (scalars_zero, weighted)
    )
    arrived = swap(parcel)

    field, *sides, scalars = scatter_next(arrived, row_at, col_at, sigma, capacity, field_zero)
    increment, residual = finish(
        field, exchange(field, sides), weights, right, residual_one, image_zero, image_one, scalars
    )
    return (increment, residual)


def solution(mesh):
    return jax.shard_map(
        body,
        mesh=mesh,
        in_specs=(
            P(None, "lat", "lon"),
            P(None, "lat", "lon"),
            P(None, "lat", "lon"),
            P(None, "lat", "lon"),
            P(("lat", "lon"), None),
            P(("lat", "lon"), None),
            P(("lat", "lon"), None),
            P(("lat", "lon"), None, None),
        ),
        out_specs=(P(None, "lat", "lon"), P(None, "lat", "lon")),
        check_vma=False,
    )
```

```python
import functools

import jax
import jax.numpy as jnp
from jax import lax
from jax.experimental import pallas as pl
from jax.experimental.pallas import tpu as pltpu
from jax.sharding import PartitionSpec as P

PASSES = 5
HALO = 16
EDGE = 8
GROUP = 16
CHUNK = 16
AHEAD = 4
F32 = jnp.float32
BF16 = jnp.bfloat16
VMEM = pl.BlockSpec(memory_space=pltpu.VMEM)
HBM = pl.BlockSpec(memory_space=pltpu.HBM)
SMEM = pl.BlockSpec(memory_space=pltpu.SMEM)
PARAMS = pltpu.CompilerParams(vmem_limit_bytes=32 * 1024 * 1024)

ROOMLESS = pltpu.CompilerParams(vmem_limit_bytes=60 * 1024 * 1024)


SNUG = pltpu.CompilerParams(vmem_limit_bytes=52 * 1024 * 1024)


def parts(values):
    high = values.astype(BF16)
    low = (values - high.astype(F32)).astype(BF16)
    return high, low


def lane_of(rows):
    return lax.broadcasted_iota(jnp.int32, (rows, 128), 1)


def pack_sides(fields):
    lane = lane_of(fields[0].shape[0])
    packed = jnp.zeros_like(fields[0])
    for level, field in enumerate(fields):
        start = 2 * HALO * level
        turned = pltpu.roll(field, (start + HALO) % 128, 1)
        packed = jnp.where((lane >= start) & (lane < start + 2 * HALO), turned, packed)
    half = packed.shape[0] // 2
    low, high = packed[:half], packed[half:]
    western = lane[:half] % (2 * HALO) < HALO
    return (
        jnp.where(western, low, pltpu.roll(high, HALO, 1)),
        jnp.where(western, pltpu.roll(low, 128 - HALO, 1), high),
    )


def unpack_sides(from_east, from_west):
    western = lane_of(from_east.shape[0]) % (2 * HALO) < HALO
    low = jnp.where(western, from_west, pltpu.roll(from_east, HALO, 1))
    high = jnp.where(western, pltpu.roll(from_west, 128 - HALO, 1), from_east)
    return jnp.concatenate([low, high], axis=0)


def turn_kernel(count, ahead, *refs):
    sources, extra = refs[: 3 * count], refs[3 * count : 3 * count + ahead]
    *mixed, down, up = refs[3 * count + ahead : 4 * count + ahead + 2]
    for kept in refs[4 * count + ahead + 2 :]:
        kept[...] = sources[0][...]
    row = 0
    if extra:
        row = extra[0].shape[0]
        down[0:row] = extra[0][...]
        up[0:row] = extra[1][...]
    for index in range(count):
        fields, from_east, from_west = sources[3 * index : 3 * index + 3]
        levels, rows, _ = fields.shape[-3:]
        for at in [(i,) for i in range(fields.shape[0])] if len(fields.shape) == 4 else [()]:
            sides = unpack_sides(from_east[at + (...,)], from_west[at + (...,)])
            mixed[index][at + (...,)] = sides
            for level in range(levels):
                down[row, level] = fields[at + (level, slice(rows - HALO, rows))]
                up[row, level] = fields[at + (level, slice(0, HALO))]
            down[row, levels] = sides[rows - HALO :]
            up[row, levels] = sides[:HALO]
            row += 1


def exchange(fields, sides):
    mixed, down, up = turn((fields, *exchange_columns(sides)))
    return (*exchange_rows(down, up), mixed)


def exchange_columns(sides):
    wide = lax.axis_size("lon")
    east = [(i, (i + 1) % wide) for i in range(wide)]
    from_west = lax.ppermute(sides[0], "lon", east)
    from_east = lax.ppermute(sides[1], "lon", [(to, at) for at, to in east])
    return from_east, from_west


def turn(*groups, rows_ahead=(), keep=False):
    levels, rows, cols = groups[0][0].shape[-3:]
    shapes = [fields.shape[:-3] + (rows, cols) for fields, _, _ in groups]
    total = sum(fields.shape[0] if fields.ndim == 4 else 1 for fields, _, _ in groups)
    total += rows_ahead[0].shape[0] if rows_ahead else 0
    shapes += [(total, levels + 1, HALO, cols)] * 2
    shapes += [groups[0][0].shape] if keep else []
    return pl.pallas_call(
        functools.partial(turn_kernel, len(groups), len(rows_ahead)),
        out_shape=[jax.ShapeDtypeStruct(shape, F32) for shape in shapes],
        in_specs=[VMEM] * (3 * len(groups) + len(rows_ahead)),
        out_specs=[VMEM] * len(shapes),
        compiler_params=PARAMS,
        name="turn",
    )(*[array for group in groups for array in group], *rows_ahead)


def exchange_rows(down, up):
    tall = lax.axis_size("lat")
    first = [(i, i + 1) for i in range(0, tall - 1, 2)]
    second = [(i, i + 1) for i in range(1, tall - 1, 2)]
    even = lax.axis_index("lat") % 2 == 0
    one = lax.ppermute(
        jnp.where(even, down, up), "lat", first + [(to, at) for at, to in first]
    )
    two = lax.ppermute(
        jnp.where(even, up, down), "lat", second + [(to, at) for at, to in second]
    )
    return jnp.where(even, two, one), jnp.where(even, one, two)


def neighbours(tiles):
    lane = lane_of(tiles[0].shape[0])
    later, earlier = tiles[1:] + tiles[:1], tiles[-1:] + tiles[:-1]
    after = [
        pltpu.roll(jnp.where(lane == 0, other, tile), 127, 1) for tile, other in zip(tiles, later)
    ]
    before = [
        pltpu.roll(jnp.where(lane == 127, other, tile), 1, 1) for tile, other in zip(tiles, earlier)
    ]
    return after, before


def lay_out(fields, side):
    lane = lane_of(side.shape[0])
    width = 2 * HALO
    turned = [pltpu.roll(field, width * level + HALO, 1) for level, field in enumerate(fields)]
    tiles = []
    for tile in range(len(fields) + 1):
        left, right = width * tile - HALO, width * tile + HALO
        before = turned[tile - 1] if tile else turned[0]
        after = turned[tile] if tile < len(fields) else turned[-1]
        value = jnp.where(lane < left, before, after)
        tiles.append(jnp.where((lane >= left) & (lane < right), side, value))
    return tiles


def pick_out(first, second, level):
    start = 2 * HALO * level + HALO
    return pltpu.roll(jnp.where(lane_of(first.shape[0]) >= start, first, second), 128 - start, 1)


def place(target, own, halo, row, lead=()):
    before, after, mixed = halo
    levels = before.shape[-3] - 1
    rows = mixed.shape[-2]
    spans = (
        (EDGE, before, (row,), before[row, levels]),
        (EDGE + HALO, own, lead, mixed[lead + (...,)]),
        (EDGE + HALO + rows, after, (row,), after[row, levels]),
    )
    for start, source, at, side in spans:
        tiles = lay_out([source[at + (level,)] for level in range(levels)], side)
        for tile, value in enumerate(tiles):
            target[lead + (tile, slice(start, start + side.shape[0]))] = value
    blank = jnp.zeros((EDGE, 128), F32)
    for tile in range(levels + 1):
        target[lead + (tile, slice(0, EDGE))] = blank
        target[lead + (tile, slice(EDGE + 2 * HALO + rows, 2 * EDGE + 2 * HALO + rows))] = blank


def clear_margins(target):
    blank = jnp.zeros((target.shape[0], EDGE, 128), F32)
    target[:, 0:EDGE] = blank
    target[:, target.shape[1] - EDGE :] = blank


def face_kernel(products, before, after, mixed, weights, padded, faces):
    tiles, tall = weights.shape[1:3]
    for index in range(2):
        place(padded, products, (before, after, mixed), index, (index,))
    inner = slice(EDGE, EDGE + tall)
    faces[:, 0:EDGE] = jnp.zeros((tiles, EDGE, 128), F32)
    faces[:, EDGE + tall :] = jnp.zeros((tiles, EDGE, 128), F32)
    land = [(padded[0, tile, inner] > 0.0).astype(F32) for tile in range(tiles)]
    land_east, _ = neighbours(land)
    east_face = [padded[0, tile, inner] * land_east[tile] for tile in range(tiles)]
    _, west_face = neighbours(east_face)
    for tile in range(tiles):
        land_north = (padded[0, tile, EDGE + 1 : EDGE + 1 + tall] > 0.0).astype(F32)
        north_face = padded[1, tile, inner] * land_north
        faces[tile, inner] = north_face
        south_face = faces[tile, EDGE - 1 : EDGE - 1 + tall]
        weights[0, tile] = 1.0 - (
            ((east_face[tile] + west_face[tile]) + north_face) + south_face
        )
        weights[1, tile] = east_face[tile]
        weights[2, tile] = west_face[tile]
        weights[3, tile] = north_face
        weights[4, tile] = south_face


def face_weights(products, halo):
    _, levels, rows, cols = products.shape
    tall = rows + 2 * HALO
    return pl.pallas_call(
        face_kernel,
        out_shape=jax.ShapeDtypeStruct((5, levels + 1, tall, cols), F32),
        in_specs=[VMEM] * 4,
        out_specs=VMEM,
        scratch_shapes=[
            pltpu.VMEM((2, levels + 1, tall + 2 * EDGE, cols), F32),
            pltpu.VMEM((levels + 1, tall + 2 * EDGE, cols), F32),
        ],
        compiler_params=PARAMS,
        name="face_weights",
    )(products, *halo)


def sweep(source, target, weights, rows_from, rows_to, block):
    tiles = source.shape[0]

    def step(index, carry):
        first = pl.multiple_of(rows_from + index * block, 8)
        for start in range(0, block, 16):
            count = min(16, block - start)
            at = pl.multiple_of(first + EDGE + start, 8)
            inner = pl.ds(pl.multiple_of(first + start, 8), count)
            here = [source[tile, pl.ds(at, count)] for tile in range(tiles)]
            east, west = neighbours(here)
            for tile in range(tiles):
                above = source[tile, pl.ds(at + 1, count)]
                below = source[tile, pl.ds(at - 1, count)]
                total = weights[0, tile, inner] * here[tile]
                total += weights[1, tile, inner] * east[tile]
                total += weights[2, tile, inner] * west[tile]
                total += weights[3, tile, inner] * above
                total += weights[4, tile, inner] * below
                target[tile, pl.ds(at, count)] = total
        return carry

    lax.fori_loop(0, (rows_to - rows_from) // block, step, 0)


def smooth(field, spare, weights, wide):
    tall = weights.shape[2]
    inner, own = slice(8, tall - 8), slice(HALO, tall - HALO)

    def sweep_rows(source, target, rows):
        sweep(source, target, weights, rows.start, rows.stop, rows.stop - rows.start)

    def two(index, carry):
        one, other = (spare, field) if wide else (field, spare)
        sweep_rows(one, other, inner)
        sweep_rows(other, one, inner)
        return carry

    if wide:
        sweep_rows(field, spare, slice(0, tall))
        lax.fori_loop(0, PASSES // 2, two, 0)
    else:
        lax.fori_loop(0, PASSES // 2, two, 0)
        sweep_rows(field, spare, own)
    return field, spare


def index_iota(cells):
    return lax.broadcasted_iota(jnp.int32, (cells, 128), 0).astype(F32).astype(BF16)


def spread_row(row, count):
    return jnp.broadcast_to(jnp.broadcast_to(row, (16, 128)).astype(BF16)[0:1], (count, 128))


def one_hot(iota, row):
    count = iota.shape[0]
    return jnp.where(
        iota == spread_row(row, count), jnp.ones((count, 128), BF16), jnp.zeros((count, 128), BF16)
    )


def scatter_into(total, load_rows, slots, half_rows, half_cols, group):
    row_iota = index_iota(half_rows)
    col_iota = index_iota(half_cols)
    total[...] = jnp.zeros_like(total)

    def step(index, carry):
        high_rows, low_rows, columns = [], [], []
        for row_index, col_index, value in load_rows(index):
            high, low = parts(jnp.broadcast_to(value, (16, 128)))
            high = jnp.broadcast_to(high[0:1], (half_rows, 128))
            low = jnp.broadcast_to(low[0:1], (half_rows, 128))
            hit = row_iota == spread_row(row_index, half_rows)
            zero = jnp.zeros((half_rows, 128), BF16)
            high_rows.append(jnp.where(hit, high, zero))
            low_rows.append(jnp.where(hit, low, zero))
            columns.append(one_hot(col_iota, col_index))
        left = jnp.concatenate(high_rows + low_rows, axis=1)
        right = jnp.concatenate(columns + columns, axis=1)
        total[...] += lax.dot_general(
            left, right, (((1,), (1,)), ((), ())), preferred_element_type=F32
        )
        return carry

    lax.fori_loop(0, slots // group, step, 0)


def load_group(index, group, capacity, row_at, col_at, arrived, stride, first_slot):
    base = pl.multiple_of(index * group, group)
    row_block = row_at[pl.ds(base, group)]
    col_block = col_at[pl.ds(base, group)]
    for j in range(group):
        source = index * (group // capacity) + j // capacity
        at = source * stride + first_slot + j % capacity
        yield row_block[j : j + 1], col_block[j : j + 1], arrived[pl.ds(at, 1)]


def split_cells(cells, rows, cols):
    level = cells // (rows * cols)
    row = (cells // cols) % rows
    col = cells % cols
    return (level // 2) * rows + row, (level % 2) * cols + col


def put_field(total, sigma, field, extra=None):
    levels, rows, cols = sigma.shape
    fields = []
    for level in range(levels):
        r, c = level // 2 * rows, level % 2 * cols
        value = total[r : r + rows, c : c + cols]
        value = sigma[level] * value
        if extra is not None:
            value = value + extra(level)
        field[level] = value
        fields.append(value)
    return fields


def scatter_first_kernel(capacity, arrived, sigma, row_at, col_at, field, *refs):
    eastward, westward, total = refs
    levels, rows, cols = sigma.shape
    stride = 2 * capacity
    cells = jnp.concatenate(
        [arrived[at : at + capacity] for at in range(0, arrived.shape[0], stride)], axis=0
    )
    row_index, col_index = split_cells(cells.astype(jnp.int32), rows, cols)
    row_at[...] = row_index.astype(F32)
    col_at[...] = col_index.astype(F32)

    def load(index):
        return load_group(index, 128, capacity, row_at, col_at, arrived, stride, capacity)

    scatter_into(total, load, row_at.shape[0], levels // 2 * rows, 2 * cols, 128)
    eastward[...], westward[...] = pack_sides(put_field(total, sigma, field))


def scatter_first(arrived, sigma, capacity):
    levels, rows, cols = sigma.shape
    slots = arrived.shape[0] // 2
    shapes = [(slots, 128), (slots, 128), (levels, rows, cols)] + [(rows // 2, cols)] * 2
    out = pl.pallas_call(
        functools.partial(scatter_first_kernel, capacity),
        out_shape=[jax.ShapeDtypeStruct(shape, F32) for shape in shapes],
        in_specs=[VMEM] * 2,
        out_specs=[VMEM] * len(shapes),
        scratch_shapes=[pltpu.VMEM((levels // 2 * rows, 2 * cols), F32)],
        compiler_params=PARAMS,
        name="scatter_first",
    )(arrived, sigma)
    return out


def lane_value(block, lane):
    return jnp.sum(jnp.where(lane_of(block.shape[0]) == lane, block, 0.0))


def lanes(values, rows):
    lane = lane_of(rows)
    out = jnp.zeros((rows, 128), F32)
    for index, value in enumerate(values):
        out = jnp.where(lane == index, value, out)
    return out


def scatter_next_kernel(capacity, last, arrived, row_at, col_at, sigma, *refs):
    if last:
        previous, field, eastward, westward, sums, total = refs
    else:
        previous, (field, eastward, westward, sums, total) = None, refs
    levels, rows, cols = sigma.shape
    stride = capacity + 1
    gathered = jnp.concatenate(
        [arrived[at : at + 1] for at in range(capacity, arrived.shape[0], stride)], axis=0
    )
    added = jnp.sum(gathered, axis=0, keepdims=True)
    sums[...] = jnp.broadcast_to(added, (8, 128))

    group = 128

    def load(index):
        return load_group(index, group, capacity, row_at, col_at, arrived, stride, 0)

    scatter_into(
        total, load, row_at.shape[0], levels // 2 * rows, 2 * cols, group
    )
    extra = None
    if last:
        beta = lane_value(added, 1) / lane_value(added, 0)

        def extra(level):
            return beta * previous[level]

    eastward[...], westward[...] = pack_sides(put_field(total, sigma, field, extra))


def scatter_next(arrived, row_at, col_at, sigma, capacity, previous=None):
    levels, rows, cols = sigma.shape
    last = previous is not None
    shapes = [(levels, rows, cols)] + [(rows // 2, cols)] * 2 + [(8, 128)]
    operands = [arrived, row_at, col_at, sigma] + ([previous] if last else [])
    out = pl.pallas_call(
        functools.partial(scatter_next_kernel, capacity, last),
        out_shape=[jax.ShapeDtypeStruct(shape, F32) for shape in shapes],
        in_specs=[VMEM] * len(operands),
        out_specs=[VMEM] * len(shapes),
        scratch_shapes=[pltpu.VMEM((levels // 2 * rows, 2 * cols), F32)],
        compiler_params=PARAMS,
        name="scatter_last" if last else "scatter_next",
    )(*operands)
    return out


def gather_from(fields, row_at, col_at, seen, table, group, wide):
    rows, cols = fields[0].shape
    half_rows, half_cols = len(fields) // 2 * rows, 2 * cols
    for level, field in enumerate(fields):
        high, low = parts(field.T)
        c, r = level % 2 * cols, level // 2 * rows
        table[c : c + cols, r : r + rows] = high
        table[c : c + cols, half_rows + r : half_rows + r + rows] = low
    row_iota = index_iota(half_rows)
    sublane = lax.broadcasted_iota(jnp.int32, (8, 128 * wide), 0)

    def step(index, carry):
        base = pl.multiple_of(index * group, group)
        row_block = row_at[pl.ds(base, group)]
        col_block = col_at[pl.ds(base, group)].astype(jnp.int32)
        found = []
        for j in range(0, group, wide):
            hot = jnp.concatenate(
                [one_hot(row_iota, row_block[i : i + 1]) for i in range(j, j + wide)], axis=1
            )
            hot = jnp.concatenate([hot, hot], axis=0)
            lines = jnp.dot(table[...], hot, preferred_element_type=F32)
            wanted = jnp.concatenate([col_block[i : i + 1] for i in range(j, j + wide)], axis=1)
            wanted = jnp.broadcast_to(wanted, (8, 128 * wide))
            tiles = [lines[i : i + 8] for i in range(0, half_cols, 8)]
            bit = 8
            while len(tiles) > 1:
                upper = (wanted & bit) != 0
                tiles = [
                    jnp.where(upper, tiles[i + 1], tiles[i]) for i in range(0, len(tiles), 2)
                ]
                bit = bit * 2
            value = jnp.sum(
                jnp.where((wanted & 7) == sublane, tiles[0], 0.0), axis=0, keepdims=True
            )
            found += [value[:, 128 * i : 128 * (i + 1)] for i in range(wide)]
        seen[pl.ds(base, group)] = jnp.concatenate(found, axis=0)
        return carry

    lax.fori_loop(0, row_at.shape[0] // group, step, 0)


def own_part(field, level, rows):
    inner = slice(EDGE + HALO, EDGE + HALO + rows)
    return pick_out(field[level, inner], field[level + 1, inner], level)


def total_of(pairs):
    added = None
    for left, right in pairs:
        term = left * right
        added = term if added is None else added + term
    return jnp.sum(added)


def observe_first_kernel(source, *refs):
    halo, weights, sigma, row_at, col_at = refs[:3], refs[3], refs[4], refs[5], refs[6]
    seen, right, image, sums, field, spare, table = refs[7:]
    levels, rows, cols = source.shape
    place(field, source, halo, halo[0].shape[0] - 1)
    clear_margins(spare)
    spare, field = smooth(field, spare, weights, True)
    right[...] = field[:, EDGE : EDGE + rows + 2 * HALO]
    own = [own_part(field, level, rows) for level in range(levels)]
    sums[...] = lanes([total_of([(value, value) for value in own])], 8)
    spare, field = smooth(field, spare, weights, False)
    fields = [sigma[level] * own_part(field, level, rows) for level in range(levels)]
    for level in range(levels):
        image[level] = fields[level]
    gather_from(fields, row_at, col_at, seen, table, 64, 8)


def observe_next_kernel(source, *refs):
    halo, weights, sigma, row_at, col_at = refs[:3], refs[3], refs[4], refs[5], refs[6]
    right, scalars = refs[7:9]
    seen, residual, image, sums, field, spare, table = refs[9:]
    levels, rows, cols = source.shape
    tall = rows + 2 * HALO
    norm, product = lane_value(scalars[0:1], 0), lane_value(scalars[0:1], 1)
    alpha = norm / (norm + product)
    place(field, source, halo, halo[0].shape[0] - 1)
    clear_margins(spare)
    spare, field = smooth(field, spare, weights, True)

    for tile in range(levels + 1):
        first = right[tile]
        field[tile, EDGE : EDGE + tall] = first - alpha * (first + field[tile, EDGE : EDGE + tall])
    own = [own_part(field, level, rows) for level in range(levels)]
    first = [pick_out(
            right[level, HALO : HALO + rows], right[level + 1, HALO : HALO + rows], level
        ) for level in range(levels)]
    for level in range(levels):
        residual[level] = own[level]
    sums[...] = lanes(
        [total_of([(value, value) for value in own]), total_of(list(zip(own, first)))], 8
    )
    spare, field = smooth(field, spare, weights, False)
    fields = [sigma[level] * own_part(field, level, rows) for level in range(levels)]
    for level in range(levels):
        image[level] = fields[level]
    gather_from(fields, row_at, col_at, seen, table, 128, 8)


def observe(source, halo, weights, sigma, row_at, col_at, right=None, scalars=None):
    levels, rows, cols = sigma.shape
    tall = rows + 2 * HALO
    slots = row_at.shape[0]
    first = right is None
    kept = (levels + 1, tall, cols) if first else (levels, rows, cols)
    shapes = [(slots, 128), kept, (levels, rows, cols), (8, 128)]
    operands = [source, *halo, weights, sigma, row_at, col_at]
    operands += [] if first else [right, scalars]
    return pl.pallas_call(
        observe_first_kernel if first else observe_next_kernel,
        out_shape=[jax.ShapeDtypeStruct(shape, F32) for shape in shapes],
        in_specs=[VMEM] * len(operands),
        out_specs=[VMEM] * len(shapes),
        scratch_shapes=[
            pltpu.VMEM((levels + 1, tall + 2 * EDGE, cols), F32),
            pltpu.VMEM((levels + 1, tall + 2 * EDGE, cols), F32),
            pltpu.VMEM(
                (2 * cols, levels * rows), BF16
            ),
        ],
        compiler_params=PARAMS,
        name="observe_first" if first else "observe_next",
    )(*operands)


def finish_kernel(source, *refs):
    halo, weights, right, residual_one, image_zero, image_one, scalars = refs[:3], *refs[3:9]
    increment, residual, field, spare = refs[9:]
    levels, rows, cols = source.shape
    norm_zero, norm_one, cross, product_zero, product_one, product_cross = [
        lane_value(scalars[0:1], index) for index in range(6)
    ]
    alpha_zero = norm_zero / (norm_zero + product_zero)
    beta = norm_one / norm_zero
    square = norm_one + 2.0 * beta * cross + beta * beta * norm_zero
    seen = product_one + 2.0 * beta * product_cross + beta * beta * product_zero
    alpha_one = norm_one / (square + seen)
    for level in range(levels):
        direction = image_one[level] + beta * image_zero[level]
        increment[level] = alpha_zero * image_zero[level] + alpha_one * direction
    place(field, source, halo, halo[0].shape[0] - 1)
    clear_margins(spare)
    spare, field = smooth(field, spare, weights, False)
    for level in range(levels):
        here = residual_one[level]
        direction = here + beta * pick_out(
            right[level, HALO : HALO + rows], right[level + 1, HALO : HALO + rows], level
        )
        image = direction + own_part(field, level, rows)
        residual[level] = here - alpha_one * image


def finish(source, halo, weights, right, residual_one, image_zero, image_one, scalars):
    levels, rows, cols = source.shape
    tall = rows + 2 * HALO
    return pl.pallas_call(
        finish_kernel,
        out_shape=[jax.ShapeDtypeStruct((levels, rows, cols), F32)] * 2,
        in_specs=[VMEM] * 10,
        out_specs=[VMEM] * 2,
        scratch_shapes=[pltpu.VMEM((levels + 1, tall + 2 * EDGE, cols), F32),
            pltpu.VMEM((levels + 1, tall + 2 * EDGE, cols), F32)],
        compiler_params=PARAMS,
        name="finish",
    )(source, *halo, weights, right, residual_one, image_zero, image_one, scalars)


def block_columns(values, weights, at):
    high, low = parts(values)
    first = jnp.concatenate([high, low, jnp.zeros((128 - 2 * GROUP, 128), BF16)], axis=0)
    second = jnp.concatenate([high, jnp.zeros((128 - GROUP, 128), BF16)], axis=0)
    right = jnp.concatenate([first, second], axis=1)
    lane = lane_of(128)
    column = jnp.where(lane < 2 * GROUP, lane % GROUP, GROUP)
    kept = jnp.zeros((128, 128), F32)
    for start in range(0, GROUP, 4):
        matrix = weights[at + start : at + start + 4].reshape(4 * 128, 128)
        left = jnp.concatenate(parts(matrix), axis=1)
        product = lax.dot_general(left, right, (((1,), (1,)), ((), ())), preferred_element_type=F32)
        for k in range(4):
            kept = jnp.where(column == start + k, product[k * 128 : (k + 1) * 128], kept)
    return kept


def turned(columns):
    rows = columns.T
    return rows[:GROUP] + rows[GROUP : 2 * GROUP]


def start_kernel(capacity, owner, cells, innovations, weights, mask, east, north, *refs):
    parcel, places, products, eastward, westward = refs[:5]
    count, held_cells, held_values, held_weights, held_mask, held_faces, held_sides = refs[5:12]
    columns, arrived, left = refs[12:]
    held = held_cells.shape[0]
    levels = mask.shape[0]
    steps = held // CHUNK
    moves = [
        (innovations, held_values),
        (cells, held_cells),
        (mask, held_mask),
        (east, held_faces.at[0]),
        (north, held_faces.at[1]),
    ]
    for step in range(steps):
        block = pl.ds(step * CHUNK, CHUNK)
        moves.append((weights.at[block], held_weights.at[block]))
    copies = [
        pltpu.make_async_copy(source, target, arrived.at[index])
        for index, (source, target) in enumerate(moves)
    ]
    for copy in copies[: 5 + AHEAD]:
        copy.start()
    parcel[...] = jnp.zeros_like(parcel)
    for index in range(count.shape[0]):
        count[index] = 0
    for index in range(held):
        target = owner[index]
        rank = count[target]
        count[target] = rank + 1
        places[index] = target * capacity + rank
        places[held + index] = target * (capacity + 1) + rank
    for copy in copies[2:5]:
        copy.wait()
    for index in range(2):
        fields = [held_mask[level].astype(F32) * held_faces[index, level] for level in range(levels)]
        for level in range(levels):
            held_faces[index, level] = fields[level]
        held_sides[0, index], held_sides[1, index] = pack_sides(fields)
    returns = [
        pltpu.make_async_copy(held_faces, products, left.at[0]),
        pltpu.make_async_copy(held_sides.at[0], eastward, left.at[1]),
        pltpu.make_async_copy(held_sides.at[1], westward, left.at[2]),
    ]
    for copy in returns:
        copy.start()
    copies[0].wait()
    copies[1].wait()
    for first in range(0, held, GROUP):
        if first % CHUNK == 0:
            step = first // CHUNK
            copies[5 + step].wait()
            if step + AHEAD < steps:
                copies[5 + step + AHEAD].start()
        columns[first // GROUP] = block_columns(
            held_values[first : first + GROUP], held_weights, first
        )
    for first in range(0, held, GROUP):
        result = turned(columns[first // GROUP])
        cell_rows = held_cells[first : first + GROUP].astype(F32)
        for k in range(GROUP):
            at = places[first + k] + owner[first + k] * capacity
            parcel[pl.ds(at, 1), :] = cell_rows[k : k + 1]
            parcel[pl.ds(at + capacity, 1), :] = result[k : k + 1]
    for copy in returns:
        copy.wait()


def start(owner, cells, innovations, weights, mask, east, north, devices, capacity):
    held, width = cells.shape
    rows, cols = mask.shape[1:]
    shapes = [(devices * 2 * capacity, width), (2 * held,), (2,) + mask.shape]
    shapes += [(2, rows // 2, cols)] * 2
    types = [F32, jnp.int32, F32, F32, F32]
    return pl.pallas_call(
        functools.partial(start_kernel, capacity),
        out_shape=[jax.ShapeDtypeStruct(shape, kind) for shape, kind in zip(shapes, types)],
        in_specs=[SMEM] + [HBM] * 6,
        out_specs=[VMEM, SMEM, HBM, HBM, HBM],
        scratch_shapes=[
            pltpu.SMEM((devices,), jnp.int32),
            pltpu.VMEM((held, width), jnp.int32),
            pltpu.VMEM((held, width), F32),
            pltpu.VMEM((held, width, width), F32),
            pltpu.VMEM(mask.shape, jnp.int32),
            pltpu.VMEM((2,) + mask.shape, F32),
            pltpu.VMEM((2, 2, rows // 2, cols), F32),
            pltpu.VMEM((held // GROUP, width, width), F32),
            pltpu.SemaphoreType.DMA((5 + held // CHUNK,)),
            pltpu.SemaphoreType.DMA((3,)),
        ],
        compiler_params=ROOMLESS,
        name="start",
    )(owner, cells, innovations, weights, mask, east, north)


def weigh_next_kernel(capacity, devices, last, places, returned, sums, weights, *refs):
    held = weights.shape[0]
    copies = []
    if last:
        sums_before, weighted_before, parcel, values, columns = refs
    else:
        parcel, weighted, values, columns, held_weights, arrived = refs
        for step in range(held // CHUNK):
            block = pl.ds(step * CHUNK, CHUNK)
            copies.append(
                pltpu.make_async_copy(
                    weights.at[block], held_weights.at[block], arrived.at[step]
                )
            )
        for copy in copies[:AHEAD]:
            copy.start()
        weights = held_weights
    parcel[...] = jnp.zeros_like(parcel)
    total = jnp.zeros((GROUP, 128), F32)
    total_cross = jnp.zeros((GROUP, 128), F32)
    for first in range(0, held, GROUP):
        here = jnp.concatenate(
            [returned[pl.ds(places[first + k], 1), :] for k in range(GROUP)], axis=0
        )
        values[first : first + GROUP] = here
        if copies and first % CHUNK == 0:
            step = first // CHUNK
            copies[step].wait()
            if step + AHEAD < len(copies):
                copies[step + AHEAD].start()
        columns[first // GROUP] = block_columns(here, weights, first)
    for first in range(0, held, GROUP):
        here = values[first : first + GROUP]
        result = turned(columns[first // GROUP])
        total += here * result
        if last:
            total_cross += here * weighted_before[first : first + GROUP]
        else:
            weighted[first : first + GROUP] = result
        for k in range(GROUP):
            parcel[pl.ds(places[held + first + k], 1), :] = result[k : k + 1]
    if last:
        scalars = [
            lane_value(sums_before[0:1], 0) / devices,
            lane_value(sums[0:1], 0),
            lane_value(sums[0:1], 1),
            lane_value(sums_before[0:1], 1) / devices,
            jnp.sum(total),
            jnp.sum(total_cross),
        ]
    else:
        scalars = [lane_value(sums[0:1], 0), jnp.sum(total)]
    row = lanes(scalars, 1)
    for target in range(devices):
        at = target * (capacity + 1) + capacity
        parcel[at : at + 1] = row


def weigh_next(places, returned, sums, weights, devices, capacity, before=None):
    held, width = weights.shape[:2]
    last = before is not None
    operands = [places, returned, sums, weights] + (list(before) if last else [])
    out_shape = [jax.ShapeDtypeStruct((devices * (capacity + 1), width), F32)]
    if not last:
        out_shape += [jax.ShapeDtypeStruct((held, width), F32)]
    return pl.pallas_call(
        functools.partial(weigh_next_kernel, capacity, devices, last),
        out_shape=out_shape,
        in_specs=[SMEM, VMEM, VMEM, VMEM if last else HBM] + [VMEM] * (len(operands) - 4),
        out_specs=[VMEM] * len(out_shape),
        scratch_shapes=[
            pltpu.VMEM((held, width), F32),
            pltpu.VMEM((held // GROUP, width, width), F32),
        ]
        + (
            []
            if last
            else [pltpu.VMEM(weights.shape, F32), pltpu.SemaphoreType.DMA((held // CHUNK,))]
        ),
        compiler_params=PARAMS if last else SNUG,
        name="weigh_last" if last else "weigh_next",
    )(*operands)


def swap(block):
    devices = lax.axis_size("lat") * lax.axis_size("lon")
    shares = block.reshape(devices, block.shape[0] // devices, 1, block.shape[1])
    got = lax.all_to_all(shares, ("lat", "lon"), split_axis=0, concat_axis=0, tiled=True)
    return got.reshape(block.shape)


def body(sigma, east_coef, north_coef, mask, innovations, cells, owner, obs_weights):
    devices = lax.axis_size("lat") * lax.axis_size("lon")
    held, width = cells.shape
    capacity = max(2, (2 * held + devices - 1) // devices)

    parcel, places, products, *sides = start(
        owner.reshape(held),
        cells,
        innovations,
        obs_weights,
        mask,
        east_coef,
        north_coef,
        devices,
        capacity,
    )
    face_columns = exchange_columns(sides)
    arrived = swap(parcel)

    row_at, col_at, field, *sides = scatter_first(arrived, sigma, capacity)
    face_columns, sides = lax.optimization_barrier((face_columns, sides))
    face_mixed, *face_rows, products = turn((products, *face_columns), keep=True)
    mixed, down, up = turn((field, *exchange_columns(sides)), rows_ahead=tuple(face_rows))
    before, after = exchange_rows(down, up)
    weights = face_weights(products, (before, after, face_mixed))
    seen, right, image_zero, sums = observe(
        field, (before, after, mixed), weights, sigma, row_at, col_at
    )
    returned = swap(seen)
    parcel, weighted = weigh_next(places, returned, sums, obs_weights, devices, capacity)
    arrived = swap(parcel)

    field_zero, *sides, scalars_zero = scatter_next(arrived, row_at, col_at, sigma, capacity)
    seen, residual_one, image_one, sums = observe(
        field_zero, exchange(field_zero, sides), weights, sigma, row_at, col_at, right, scalars_zero
    )
    returned = swap(seen)
    (parcel,) = weigh_next(
        places, returned, sums, obs_weights, devices, capacity, (scalars_zero, weighted)
    )
    arrived = swap(parcel)

    field, *sides, scalars = scatter_next(arrived, row_at, col_at, sigma, capacity, field_zero)
    increment, residual = finish(
        field, exchange(field, sides), weights, right, residual_one, image_zero, image_one, scalars
    )
    return (increment, residual)


def solution(mesh):
    return jax.shard_map(
        body,
        mesh=mesh,
        in_specs=(
            P(None, "lat", "lon"),
            P(None, "lat", "lon"),
            P(None, "lat", "lon"),
            P(None, "lat", "lon"),
            P(("lat", "lon"), None),
            P(("lat", "lon"), None),
            P(("lat", "lon"), None),
            P(("lat", "lon"), None, None),
        ),
        out_specs=(P(None, "lat", "lon"), P(None, "lat", "lon")),
        check_vma=False,
    )
```
